32 devices in a mesh: grp: 8 (over z, y), lvl: 4 (over x, core).
Axes of the slice: x: 2, y: 2, z: 4, core: 2. Of those that a mesh axis runs over, the one named last changes fastest.
Arguments:
- latents: bfloat16 [8192, 1024], P(('grp', 'lvl')), may hold values from -6 to 6
- blocks: bfloat16 [64, 256, 1024], P(('grp', 'lvl')), may hold values from -6 to 6
- neighbours: int32 [64, 2], P(('grp', 'lvl')), may hold values from 0 to 1
- fill: int32 [64], P(('grp', 'lvl')), may hold values from 64 to 256
- cotangent: bfloat16 [8192, 1024], P(('grp', 'lvl')), may hold values from -6 to 6
- latent_gain: float32 [1024], replicated, may hold values from 0.5 to 1.5
- latent_shift: float32 [1024], replicated, may hold values from -1 to 1
- block_gain: float32 [1024], replicated, may hold values from 0.5 to 1.5
- block_shift: float32 [1024], replicated, may hold values from -1 to 1
- cross_query: bfloat16 [1024, 1024], replicated, may hold values from -0.1875 to 0.1875
- cross_key: bfloat16 [1024, 1024], replicated, may hold values from -0.1875 to 0.1875
- cross_value: bfloat16 [1024, 1024], replicated, may hold values from -0.1875 to 0.1875
- cross_output: bfloat16 [1024, 1024], replicated, may hold values from -0.75 to 0.75
- self_gain: float32 [1024], replicated, may hold values from 0.5 to 1.5
- self_shift: float32 [1024], replicated, may hold values from -1 to 1
- self_query: bfloat16 [1024, 1024], replicated, may hold values from -0.1875 to 0.1875
- self_key: bfloat16 [1024, 1024], replicated, may hold values from -0.1875 to 0.1875
- self_value: bfloat16 [1024, 1024], replicated, may hold values from -0.1875 to 0.1875
- self_output: bfloat16 [1024, 1024], replicated, may hold values from -1 to 1
- hidden_gain: float32 [1024], replicated, may hold values from 0.5 to 1.5
- hidden_shift: float32 [1024], replicated, may hold values from -1 to 1
- hidden_expand: bfloat16 [1024, 4096], replicated, may hold values from -0.1875 to 0.1875
- hidden_reduce: bfloat16 [4096, 1024], replicated, may hold values from -0.09375 to 0.09375
Outputs:
- updated: bfloat16 [8192, 1024], P(('grp', 'lvl'))
- latent_delta: bfloat16 [8192, 1024], P(('grp', 'lvl'))
- block_delta: bfloat16 [64, 256, 1024], P(('grp', 'lvl'))
- latent_gain_delta: float32 [1024], P(('grp', 'lvl'))
- latent_shift_delta: float32 [1024], P(('grp', 'lvl'))
- block_gain_delta: float32 [1024], P(('grp', 'lvl'))
- block_shift_delta: float32 [1024], P(('grp', 'lvl'))
- cross_query_delta: float32 [1024, 1024], P(('grp', 'lvl'))
- cross_key_delta: float32 [1024, 1024], P(('grp', 'lvl'))
- cross_value_delta: float32 [1024, 1024], P(('grp', 'lvl'))
- cross_output_delta: float32 [1024, 1024], P(('grp', 'lvl'))
- self_gain_delta: float32 [1024], P(('grp', 'lvl'))
- self_shift_delta: float32 [1024], P(('grp', 'lvl'))
- self_query_delta: float32 [1024, 1024], P(('grp', 'lvl'))
- self_key_delta: float32 [1024, 1024], P(('grp', 'lvl'))
- self_value_delta: float32 [1024, 1024], P(('grp', 'lvl'))
- self_output_delta: float32 [1024, 1024], P(('grp', 'lvl'))
- hidden_gain_delta: float32 [1024], P(('grp', 'lvl'))
- hidden_shift_delta: float32 [1024], P(('grp', 'lvl'))
- hidden_expand_delta: float32 [1024, 4096], P(('grp', 'lvl'))
- hidden_reduce_delta: float32 [4096, 1024], P(('grp', 'lvl'))
The draws below stay inside these ranges and needn't reach their ends.
Inputs may be any that keep to these rules, and one draw needn't show every extreme that they name: `neighbours`: each index is one of the 2 blocks of the group's own run; a block may be read twice by one group. `fill`: every block has at least one live slot.
All inputs are finite; a program needn't handle non-finite values.
Results may differ from the reference program's by a relative error of at most 0.017.
Values may be sent and summed in bfloat16 or wider, within the bound.
No kernel may reach another device: no remote copies, remote signals or barrier semaphores. Data moves between devices by JAX's collectives and lax.ppermute only.
A program may use at most 256 MiB of HBM per device.

```python
import jax
import jax.numpy as jnp
from jax import lax

D = 1024
H = 8
FF = 4096
LAT = 128
NB = 256
READS = 2
G_DEV = 2
BLOCKS = 64
TOKENS = 8192
N_GRP = 8
N_LVL = 4
DEVICES = 32


def set_ends(values, rng, least, high):
    dims = values.shape
    spot = [jax.random.randint(jax.random.fold_in(rng, axis), (), 0, dims[axis]) for axis in range(len(dims))]
    values = values.at[tuple(spot)].set(least)
    longest = dims.index(max(dims))
    spot[longest] = (spot[longest] + 1) % dims[longest]
    return values.at[tuple(spot)].set(high)


def steps_of(own_key, shape, split, smallest, high):
    level = 1.0
    for axis_at, shards_of in split:
        steps = jax.random.uniform(jax.random.fold_in(jax.random.fold_in(own_key, 6), axis_at), (shards_of,), jnp.float32, smallest / len(split), high / len(split))
        level = level * jnp.repeat(jnp.exp(steps), shape[axis_at] // shards_of).reshape((-1,) + (1,) * (len(shape) - 1 - axis_at))
    return level


def gaussian(rng, shape, deviation, bound, cuts=(), kind=jnp.bfloat16):
    values = jax.random.normal(rng, shape, jnp.float32) * deviation
    if len(cuts) > 0:
        values = steps_of(rng, shape, cuts, -0.22, 0.18) * values
    return jnp.clip(values, min=-bound, max=bound).astype(kind)


def setup_inputs(seed: int = 0) -> dict:
    key_list = jax.random.split(jax.random.key(seed), 24)
    return {
        "latents": gaussian(key_list[0], (TOKENS, D), 1.0, 6.0, ((0, 32),)),
        "blocks": gaussian(key_list[1], (BLOCKS, NB, D), 1.0, 6.0, ((0, 32),)),
        "neighbours": set_ends(jax.random.randint(key_list[2], (BLOCKS, READS), 0, G_DEV), jax.random.fold_in(key_list[2], 1), 0, G_DEV - 1).astype(jnp.int32),
        "fill": set_ends(jax.random.randint(key_list[3], (BLOCKS,), NB // 4, NB + 1), jax.random.fold_in(key_list[3], 1), NB // 4, NB).astype(jnp.int32),
        "cotangent": gaussian(key_list[4], (TOKENS, D), 1.0, 6.0, ((0, 32),)),
        "latent_gain": jnp.clip(1.0 + 0.1 * jax.random.normal(key_list[5], (D,), jnp.float32), 0.5, 1.5),
        "latent_shift": gaussian(key_list[6], (D,), 0.2, 1.0, (), jnp.float32),
        "block_gain": jnp.clip(1.0 + 0.1 * jax.random.normal(key_list[7], (D,), jnp.float32), 0.5, 1.5),
        "block_shift": gaussian(key_list[8], (D,), 0.2, 1.0, (), jnp.float32),
        "cross_query": gaussian(key_list[9], (D, D), D ** -0.5, 0.1875),
        "cross_key": gaussian(key_list[10], (D, D), D ** -0.5, 0.1875),
        "cross_value": gaussian(key_list[11], (D, D), D ** -0.5, 0.1875),
        "cross_output": gaussian(key_list[12], (D, D), (D // 16) ** -0.5, 0.75),
        "self_gain": jnp.clip(1.0 + 0.1 * jax.random.normal(key_list[13], (D,), jnp.float32), 0.5, 1.5),
        "self_shift": gaussian(key_list[14], (D,), 0.2, 1.0, (), jnp.float32),
        "self_query": gaussian(key_list[15], (D, D), D ** -0.5, 0.1875),
        "self_key": gaussian(key_list[16], (D, D), D ** -0.5, 0.1875),
        "self_value": gaussian(key_list[17], (D, D), D ** -0.5, 0.1875),
        "self_output": gaussian(key_list[18], (D, D), (D // 32) ** -0.5, 1.0),
        "hidden_gain": jnp.clip(1.0 + 0.1 * jax.random.normal(key_list[19], (D,), jnp.float32), 0.5, 1.5),
        "hidden_shift": gaussian(key_list[20], (D,), 0.2, 1.0, (), jnp.float32),
        "hidden_expand": gaussian(key_list[21], (D, FF), D ** -0.5, 0.1875),
        "hidden_reduce": gaussian(key_list[22], (FF, D), FF ** -0.5, 0.09375),
    }


EPS = 1e-05
NEG = -1e+30

@jax.custom_vjp
def low(v):
    return lax.optimization_barrier(v.astype(jnp.bfloat16)).astype(jnp.float32)

@jax.custom_vjp
def low_back(v):
    return v

def low_keep(v):
    return (low(v), None)

def low_pass(kept, grad):
    return (grad,)

def back_keep(v):
    return (v, None)

def back_low(kept, grad):
    return (low(grad),)
low.defvjp(low_keep, low_pass)
low_back.defvjp(back_keep, back_low)

def normed(values, norm_gain, norm_shift):
    center = values - lax.optimization_barrier(jnp.mean(values, axis=-1, keepdims=True))
    spread = lax.optimization_barrier(jnp.mean(center * center, axis=-1, keepdims=True))
    return center * lax.rsqrt(spread + EPS) * norm_gain + norm_shift

def product(left_side, right_side):
    return jnp.dot(left_side, right_side, precision=lax.Precision.HIGHEST)

def cross_device(pieces):
    queries, block_keys, block_values, neighbours, fill = pieces
    head_size = D // H
    picked_keys = block_keys[neighbours].reshape(G_DEV, READS * NB, H, head_size)
    picked_values = block_values[neighbours].reshape(G_DEV, READS * NB, H, head_size)
    positions = jnp.arange(NB, dtype=jnp.int32)
    live_keys = (positions[None, None, :] < fill[neighbours][:, :, None]).reshape(G_DEV, READS * NB)
    scores = jnp.einsum('gqhd,gkhd->ghqk', queries, picked_keys, precision=lax.Precision.HIGHEST)
    scores = low_back(scores * head_size ** (-0.5))
    scores = jnp.where(live_keys[:, None, None, :], scores, NEG)
    attention = low(jax.nn.softmax(scores, axis=-1))
    return jnp.einsum('ghqk,gkhd->gqhd', attention, picked_values, precision=lax.Precision.HIGHEST)

def self_one(pieces):
    queries, set_keys, set_values = pieces
    head_size = D // H
    scores = low_back(product(queries, set_keys.T) * head_size ** (-0.5))
    attention = low(jax.nn.softmax(scores, axis=-1))
    return product(attention, set_values)

def forward(latents, blocks, latent_gain, latent_shift, block_gain, block_shift, cross_query, cross_key, cross_value, cross_output, self_gain, self_shift, self_query, self_key, self_value, self_output, hidden_gain, hidden_shift, hidden_expand, hidden_reduce, neighbours, fill):
    head_size = D // H
    length = N_LVL * G_DEV * LAT
    latent_in = low(normed(latents, latent_gain, latent_shift))
    block_in = low(normed(blocks.reshape(BLOCKS * NB, D), block_gain, block_shift))
    cross_queries = low_back(low(product(latent_in, cross_query)))
    block_keys = low_back(low(product(block_in, cross_key)))
    block_values = low_back(low(product(block_in, cross_value)))
    mixture = lax.map(jax.checkpoint(cross_device), (cross_queries.reshape(DEVICES, G_DEV, LAT, H, head_size), block_keys.reshape(DEVICES, G_DEV, NB, H, head_size), block_values.reshape(DEVICES, G_DEV, NB, H, head_size), neighbours.reshape(DEVICES, G_DEV, READS), fill.reshape(DEVICES, G_DEV)))
    cross_mixed = low_back(low(mixture.reshape(TOKENS, D)))
    after_cross = latents + low_back(product(cross_mixed, cross_output))
    self_in = low(normed(after_cross, self_gain, self_shift))

    def heads_of(values):
        return values.reshape(N_GRP, length, H, head_size).transpose(0, 2, 1, 3).reshape(N_GRP * H, length, head_size)
    self_queries = low_back(low(product(self_in, self_query)))
    self_keys = low_back(low(product(self_in, self_key)))
    self_values = low_back(low(product(self_in, self_value)))
    mixture = lax.map(jax.checkpoint(self_one), (heads_of(self_queries), heads_of(self_keys), heads_of(self_values)))
    self_mixed = mixture.reshape(N_GRP, H, length, head_size).transpose(0, 2, 1, 3).reshape(TOKENS, D)
    self_mixed = low_back(low(self_mixed))
    after_self = after_cross + low_back(product(self_mixed, self_output))
    hidden_in = low(normed(after_self, hidden_gain, hidden_shift))
    pre_act = low_back(product(hidden_in, hidden_expand))
    activated = low(jax.nn.gelu(pre_act))
    return after_self + low_back(product(activated, hidden_reduce))

def reference(latents, blocks, neighbours, fill, cotangent, latent_gain, latent_shift, block_gain, block_shift, cross_query, cross_key, cross_value, cross_output, self_gain, self_shift, self_query, self_key, self_value, self_output, hidden_gain, hidden_shift, hidden_expand, hidden_reduce):
    floats = [latents, blocks, latent_gain, latent_shift, block_gain, block_shift, cross_query, cross_key, cross_value, cross_output, self_gain, self_shift, self_query, self_key, self_value, self_output, hidden_gain, hidden_shift, hidden_expand, hidden_reduce]
    floats = [item.astype(jnp.float32) for item in floats]

    def closed(*params):
        return forward(*params, neighbours, fill)
    result, pullback = jax.vjp(closed, *floats)
    deltas = pullback(cotangent.astype(jnp.float32))
    return (result.astype(jnp.bfloat16), deltas[0].astype(jnp.bfloat16), deltas[1].astype(jnp.bfloat16), deltas[2], deltas[3], deltas[4], deltas[5], deltas[6], deltas[7], deltas[8], deltas[9], deltas[10], deltas[11], deltas[12], deltas[13], deltas[14], deltas[15], deltas[16], deltas[17], deltas[18], deltas[19])
```

```python
import functools

import jax
import jax.numpy as jnp
from jax import lax
from jax.experimental import pallas as pl
from jax.experimental.pallas import tpu as pltpu
from jax.sharding import PartitionSpec as P

H = 8


EPS = 1e-05
NEG = -1e30
BF = jnp.bfloat16
F32 = jnp.float32
VMEM_BYTES = 56 * 1024 * 1024
SQRT_2_PI = 0.7978845608028654
CUBIC = 0.044715


def nn(a, b):
    return lax.dot_general(a, b, (((1,), (0,)), ((), ())), preferred_element_type=F32)


def nt(a, b):
    return lax.dot_general(a, b, (((1,), (1,)), ((), ())), preferred_element_type=F32)


def tn(a, b):
    return lax.dot_general(a, b, (((0,), (0,)), ((), ())), preferred_element_type=F32)


def flip(v):
    return jnp.transpose(v)


def hat(v):
    center = v - jnp.mean(v, axis=-1, keepdims=True)
    scale = lax.rsqrt(jnp.mean(center * center, axis=-1, keepdims=True) + EPS)
    return center * scale, scale


def norm_back(dy, v, gain):
    unit, scale = hat(v)
    t = dy * gain
    side = scale * (
        t
        - jnp.mean(t, axis=-1, keepdims=True)
        - unit * jnp.mean(t * unit, axis=-1, keepdims=True)
    )
    return side, jnp.sum(dy * unit, axis=0, keepdims=True), jnp.sum(dy, axis=0, keepdims=True)


def gelu_parts(x):
    square = x * x
    t = jnp.tanh(SQRT_2_PI * x * (1.0 + CUBIC * square))
    half = 0.5 + 0.5 * t
    act = x * half
    slope = half + (0.5 * SQRT_2_PI) * x * (1.0 - t * t) * (1.0 + (3.0 * CUBIC) * square)
    return act, slope


def counts_by_row(nb, fill, rows, groups, block_rows, reads):
    keys = groups * block_rows
    key = lax.broadcasted_iota(jnp.int32, (rows, keys), 1)
    row = lax.broadcasted_iota(jnp.int32, (rows, keys), 0)
    per = rows // groups
    out = jnp.zeros((rows, keys), F32)
    for g in range(groups):
        for m in range(groups):
            times = jnp.int32(0)
            for n in range(reads):
                times = times + (nb[g * reads + n] == m).astype(jnp.int32)
            live = (key >= m * block_rows) & (key < m * block_rows + fill[m])
            here = live & (row >= g * per) & (row < (g + 1) * per)
            out = jnp.where(here, times.astype(F32), out)
    return out


def counts_by_key(nb, fill, rows, groups, block_rows, reads):
    keys = groups * block_rows
    key = lax.broadcasted_iota(jnp.int32, (keys, rows), 0)
    row = lax.broadcasted_iota(jnp.int32, (keys, rows), 1)
    per = rows // groups
    out = jnp.zeros((keys, rows), F32)
    for g in range(groups):
        for m in range(groups):
            times = jnp.int32(0)
            for n in range(reads):
                times = times + (nb[g * reads + n] == m).astype(jnp.int32)
            live = (key >= m * block_rows) & (key < m * block_rows + fill[m])
            here = live & (row >= g * per) & (row < (g + 1) * per)
            out = jnp.where(here, times.astype(F32), out)
    return out


def params():
    return pltpu.CompilerParams(
        vmem_limit_bytes=VMEM_BYTES, dimension_semantics=("arbitrary",)
    )


def whole(shape):
    zeros = (0,) * len(shape)
    return pl.BlockSpec(shape, lambda i, *_: zeros)


def call(kernel, name, grid, scalars, ins, outs, scratch, flops, nbytes):
    return pl.pallas_call(
        kernel,
        name=name,
        grid_spec=pltpu.PrefetchScalarGridSpec(
            num_scalar_prefetch=len(scalars),
            grid=(grid,),
            in_specs=[spec for _, spec in ins],
            out_specs=[spec for _, _, spec in outs],
            scratch_shapes=scratch,
        ),
        out_shape=[jax.ShapeDtypeStruct(shape, dtype) for shape, dtype, _ in outs],
        compiler_params=params(),
        cost_estimate=pl.CostEstimate(flops=flops, bytes_accessed=nbytes, transcendentals=0),
    )(*scalars, *[array for array, _ in ins])


def cross_forward_kernel(
    groups, reads, nb, fill, lat, blk, lg, lb, bg, bb, sg, sb, wq, wk, wv, wo,
    cq, ck, cv, co, ac, self_in, lat_in, blk_in, acc, cnt,
):
    i = pl.program_id(0)
    rows, width = lat.shape
    keys = blk.shape[0]
    scale = (width // H) ** -0.5
    head = width // H

    @pl.when(i == 0)
    def _():
        lat_in[...] = (hat(lat[...].astype(F32))[0] * lg[...] + lb[...]).astype(BF)
        blk_in[...] = (hat(blk[...].astype(F32))[0] * bg[...] + bb[...]).astype(BF)
        acc[...] = lat[...].astype(F32)
        cnt[...] = counts_by_row(nb, fill, rows, groups, keys // groups, reads)

    q = nn(lat_in[...], wq[...]).astype(BF)
    k = nn(blk_in[...], wk[...]).astype(BF)
    v = nn(blk_in[...], wv[...]).astype(BF)
    cq[...] = q
    ck[...] = k
    cv[...] = v
    times = cnt[...]
    seen = times > 0.0
    mixed = []
    for h in range(q.shape[1] // head):
        cut = slice(h * head, (h + 1) * head)
        s = jnp.where(seen, nt(q[:, cut], k[:, cut]) * scale, NEG)
        e = jnp.exp(s - jnp.max(s, axis=-1, keepdims=True))
        total = jnp.sum(e * times, axis=-1, keepdims=True)
        p = (e * (1.0 / total)).astype(BF) * times.astype(BF)
        mixed.append(nn(p, v[:, cut]).astype(BF))
    mixed = jnp.concatenate(mixed, axis=1)
    co[...] = mixed
    acc[...] += nn(mixed, wo[...])

    @pl.when(i == pl.num_programs(0) - 1)
    def _():
        after = acc[...]
        ac[...] = after
        self_in[...] = (hat(after)[0] * sg[...] + sb[...]).astype(BF)


def flip_rows_kernel(n, order, *refs):
    ins, outs, tmp = refs[:n], refs[n : 2 * n], refs[2 * n :]
    chunks = order.shape[0]
    for src, dst, t in zip(ins, outs, tmp, strict=True):
        t[...] = flip(src[...])
        size = t.shape[0] // chunks
        for p in range(chunks):
            at = pl.multiple_of(order[p] * size, size)
            dst[p * size : (p + 1) * size, :] = t[pl.ds(at, size), :]


def self_forward_kernel(ids, a0, a1, a2, a3, wq, wk, wv, q, k, v, o0, o1, o2):
    rows, width = a0.shape
    head = width // H
    scale = head**-0.5
    for j, a in enumerate((a0, a1, a2, a3)):
        here = slice(j * rows, (j + 1) * rows)
        x = a[...]
        q[here, :] = nn(x, wq[...]).astype(BF)
        k[here, :] = nn(x, wk[...]).astype(BF)
        v[here, :] = nn(x, wv[...]).astype(BF)
    for j in range(4):
        mixed = []
        for h in range(q.shape[1] // head):
            cut = slice(h * head, (h + 1) * head)
            s = nt(q[j * rows : (j + 1) * rows, cut], k[:, cut]) * scale
            e = jnp.exp(s - jnp.max(s, axis=-1, keepdims=True))
            p = (e * (1.0 / jnp.sum(e, axis=-1, keepdims=True))).astype(BF)
            mixed.append(nn(p, v[:, cut]).astype(BF))
        mixed = jnp.concatenate(mixed, axis=1)
        if j == 0:
            o0[...] = mixed
        elif j == 1:
            o1[...] = mixed
        else:
            o2[(j - 2) * rows : (j - 1) * rows, :] = mixed


def self_out_kernel(ids, ac, o0, o1, o2, o3, wo, hg, hb, after, hidden_in, so):
    cols = o0.shape[1]
    for j, o in enumerate((o0, o1, o2, o3)):
        at = pl.multiple_of((ids[1] ^ j) * cols, cols)
        so[:, pl.ds(at, cols)] = o[...]
    v = ac[...] + nn(so[...], wo[...])
    after[...] = v
    hidden_in[...] = (hat(v)[0] * hg[...] + hb[...]).astype(BF)


def ff_local_kernel(
    hidden_in, gy, after, hg, wexp, wred, updated, gate, das, vecs, up, dh
):
    i = pl.program_id(0)

    @pl.when(i == 0)
    def _():
        up[...] = after[...]
        dh[...] = jnp.zeros_like(dh)

    pre = nn(hidden_in[...], wexp[...])
    dact = nt(gy[...], wred[...])
    act, slope = gelu_parts(pre)
    up[...] += nn(act.astype(BF), wred[...])
    dh[...] += nt((dact * slope).astype(BF), wexp[...])

    @pl.when(i == pl.num_programs(0) - 1)
    def _():
        updated[...] = up[...].astype(BF)
        side, dg, db = norm_back(dh[...], after[...], hg[...])
        total = gy[...].astype(F32) + side
        das[...] = total
        gate[...] = total.astype(BF)
        vecs[0:1, :] = dg
        vecs[1:2, :] = db


def ff_weights_kernel(n, ids, *refs):
    hs, gs = refs[:n], refs[n : 2 * n]
    wexp = refs[2 * n : 2 * n + 4]
    wred = refs[2 * n + 4 : 2 * n + 8]
    red_keep, red_send, exp_keep, exp_send = refs[2 * n + 8 : 2 * n + 12]
    h_all, g_all, we, wr, red, exp, sem = refs[2 * n + 12 :]
    copies = []
    for src, dst, which in ((hs, h_all, 0), (gs, g_all, 1)):
        at = 0
        for k, piece in enumerate(src):
            size = piece.shape[0]
            copies.append(
                pltpu.make_async_copy(piece, dst.at[pl.ds(at, size)], sem.at[which, k])
            )
            at += size
    for c in copies:
        c.start()
    unit = wexp[0].shape[1]
    for q in range(4):
        we[q * unit : (q + 1) * unit, :] = flip(wexp[q][...])
        wr[q * unit : (q + 1) * unit, :] = wred[q][...]
    red[...] = jnp.zeros_like(red)
    exp[...] = jnp.zeros_like(exp)
    for c in copies:
        c.wait()
    tile = 256

    def step(t, carry):
        rows = pl.ds(pl.multiple_of(t * tile, tile), tile)
        h = h_all[rows, :]
        g = g_all[rows, :]
        act, slope = gelu_parts(nt(we[...], h))
        dpre = (nt(wr[...], g) * slope).astype(BF)
        red[...] += nn(act.astype(BF), g)
        exp[...] += nn(dpre, h)
        return carry

    lax.fori_loop(0, h_all.shape[0] // tile, step, 0)
    half = 2 * unit
    red_keep[...] = red[0:half, :].astype(BF)
    red_send[...] = red[half:, :].astype(BF)
    span = exp.shape[1] // 4
    for p in range(4):
        z = ids[4 + p]
        lanes = pl.ds(pl.multiple_of(z * span, span), span)
        out = exp_keep if p < 2 else exp_send
        low = (p % 2) * unit
        for q in range(4):
            to = pl.ds(pl.multiple_of(ids[4 + q] * span, span), span)
            out[low : low + unit, to] = exp[q * unit : (q + 1) * unit, lanes].astype(BF)


def self_backward_kernel(
    ids, g0, g1, g2, g3, q, k, v, wo, wq, wk, wv, flipped, keep, send, do, dq, dk, dv
):
    rows, width = g0.shape
    head = width // H
    scale = head**-0.5
    for j, g in enumerate((g0, g1, g2, g3)):
        do[j * rows : (j + 1) * rows, :] = nt(g[...], wo[...]).astype(BF)
    cols = q.shape[1]
    tile = 256
    for h in range(cols // head):
        cut = slice(h * head, (h + 1) * head)
        kh = k[:, cut]
        vh = v[:, cut]
        kt = flip(kh)
        key_sum = jnp.zeros((k.shape[0], head), F32)
        value_sum = jnp.zeros((k.shape[0], head), F32)
        for t in range(q.shape[0] // tile):
            here = slice(t * tile, (t + 1) * tile)
            qt = q[here, cut]
            dt = do[here, cut]
            s = nt(kh, qt) * scale
            e = jnp.exp(s - jnp.max(s, axis=0, keepdims=True))
            p = e * (1.0 / jnp.sum(e, axis=0, keepdims=True))
            dp = nt(vh, dt)
            ds = (p * (dp - jnp.sum(p * dp, axis=0, keepdims=True))).astype(BF)
            value_sum += nn(p.astype(BF), dt)
            key_sum += nn(ds, qt)
            back = (nn(kt, ds) * scale).astype(BF)
            flipped[cut, here] = back
            dq[here, cut] = flip(back)
        dk[:, cut] = (key_sum * scale).astype(BF)
        dv[:, cut] = value_sum.astype(BF)
    flipped[cols : 2 * cols, :] = flip(dk[...])
    flipped[2 * cols : 3 * cols, :] = flip(dv[...])
    for j in range(4):
        here = slice(j * rows, (j + 1) * rows)
        side = nt(dq[here, :], wq[...]) + nt(dk[here, :], wk[...]) + nt(dv[here, :], wv[...])
        out = send if j % 2 else keep
        low = (j // 2) * rows
        out[low : low + rows, :] = side.astype(BF)


def self_weights_kernel(ids, flipped, a0, a1, a2, a3, out):
    rows = a0.shape[0]
    total = None
    for j, a in enumerate((a0, a1, a2, a3)):
        part = nn(flipped[:, j * rows : (j + 1) * rows], a[...])
        total = part if total is None else total + part
    blocks, _, span = out.shape
    for b in range(blocks):
        out[b ^ ids[0]] = total[:, b * span : (b + 1) * span].astype(BF)


def cross_backward_kernel(
    groups, reads, nb, fill, keep, rcv, xr, das, ac, sg, wo, cq, ck, cv,
    dac, gate, vecs, dq, dk, dv, cnt,
):
    i = pl.program_id(0)
    rows, width = das.shape
    keys = ck.shape[0]
    head = width // H
    scale = head**-0.5

    @pl.when(i == 0)
    def _():
        dy = keep[...].astype(F32) + rcv[...].astype(F32) + xr[...].astype(F32)
        side, dg, db = norm_back(dy, ac[...], sg[...])
        total = das[...] + side
        dac[...] = total
        gate[...] = total.astype(BF)
        vecs[0:1, :] = dg
        vecs[1:2, :] = db
        cnt[...] = counts_by_key(nb, fill, rows, groups, keys // groups, reads)

    do = nt(gate[...], wo[...]).astype(BF)
    times = cnt[...]
    seen = times > 0.0
    for h in range(cq.shape[1] // head):
        cut = slice(h * head, (h + 1) * head)
        qh = cq[:, cut]
        kh = ck[:, cut]
        dh = do[:, cut]
        s = jnp.where(seen, nt(kh, qh) * scale, NEG)
        e = jnp.exp(s - jnp.max(s, axis=0, keepdims=True))
        p = e * (1.0 / jnp.sum(e * times, axis=0, keepdims=True))
        dp = nt(cv[:, cut], dh)
        delta = jnp.sum(p * dp * times, axis=0, keepdims=True)
        ds = (p * (dp - delta)).astype(BF) * times.astype(BF)
        dv[:, cut] = nn(p.astype(BF) * times.astype(BF), dh).astype(BF)
        dk[:, cut] = (nn(ds, qh) * scale).astype(BF)
        dq[:, cut] = flip((nn(flip(kh), ds) * scale).astype(BF))


def cross_inputs_kernel(
    dq, dk, dv, wq, wk, wv, lat, blk, lg, bg, dac, dlat, dblk, vecs, la, ba
):
    i = pl.program_id(0)

    @pl.when(i == 0)
    def _():
        la[...] = jnp.zeros_like(la)
        ba[...] = jnp.zeros_like(ba)

    la[...] += nt(dq[...], wq[...])
    ba[...] += nt(dk[...], wk[...]) + nt(dv[...], wv[...])

    @pl.when(i == pl.num_programs(0) - 1)
    def _():
        side, dg, db = norm_back(la[...], lat[...].astype(F32), lg[...])
        dlat[...] = (dac[...] + side).astype(BF)
        vecs[0:1, :] = dg
        vecs[1:2, :] = db
        side, dg, db = norm_back(ba[...], blk[...].astype(F32), bg[...])
        dblk[...] = side.astype(BF)
        vecs[2:3, :] = dg
        vecs[3:4, :] = db


def products_kernel(pairs, n_left, *refs):
    n = len(pairs)
    lefts, rights = refs[:n_left], refs[n_left : n_left + n]
    outs = refs[n_left + n :]
    for k, at in enumerate(pairs):
        r = nn(lefts[at][...], rights[k][...])
        half = r.shape[0] // 2
        outs[2 * k][...] = r[:half].astype(BF)
        outs[2 * k + 1][...] = r[half:].astype(BF)


def products(name, lefts, pairs, rights):
    depth, width = lefts[0].shape[0], rights[0].shape[1]
    span = width // 4
    ins = [(a, whole(a.shape)) for a in lefts]
    ins += [(b, pl.BlockSpec((b.shape[0], span), lambda i: (0, i))) for b in rights]
    outs = []
    for _ in pairs:
        outs += [((depth // 2, width), BF, pl.BlockSpec((depth // 2, span), lambda i: (0, i)))] * 2
    flops = sum(2 * depth * width * b.shape[0] for b in rights)
    return call(
        functools.partial(products_kernel, pairs, len(lefts)),
        name, 4, [], ins, outs, [], flops, 2 * depth * width * len(pairs) * 2,
    )


def flip_rows(name, order, arrays):
    ins = [(a, whole(a.shape)) for a in arrays]
    outs = [(a.shape[::-1], BF, whole(a.shape[::-1])) for a in arrays]
    scratch = [pltpu.VMEM(a.shape[::-1], BF) for a in arrays]
    size = sum(a.shape[0] * a.shape[1] for a in arrays)
    return call(
        functools.partial(flip_rows_kernel, len(arrays)),
        name, 1, [order], ins, outs, scratch, size, 4 * size,
    )


def swap(values, axis, bit):
    size = lax.axis_size(axis)
    return lax.ppermute(values, axis, [(i, i ^ bit) for i in range(size)])


CORE = ("lvl", 1)
ACROSS = ("lvl", 2)
BESIDE = ("grp", 1)
NEAR = ("grp", 2)
FAR = ("grp", 4)


def gather_set(own):
    across = swap(own, *ACROSS)
    return own, swap(own, *CORE), across, swap(across, *CORE)


def gather_plane(own):
    half = own.shape[0] // 2
    across = swap(own, *ACROSS)
    beside = swap(own, *BESIDE)
    corner_a = swap(across[:half], *BESIDE)
    corner_b = swap(beside[half:], *ACROSS)
    mine = (own, across, beside, corner_a, corner_b)
    return mine + tuple(swap(v, *CORE) for v in mine)


def scatter_sum(keep, send, order):
    link, _ = order[0]
    got = swap(send, *link)
    depth, width = keep.shape
    left = [bit for _, bit in order[1:]]
    n = len(left)
    shape = (2,) * n + (depth >> n, width)
    keep, got = keep.reshape(shape), got.reshape(shape)
    for link, bit in order[1:]:
        axis = sorted(left).index(bit)
        left.remove(bit)
        pick = lambda a, at: lax.index_in_dim(a, at, axis, keepdims=False)
        send = (pick(keep, 1).astype(F32) + pick(got, 1).astype(F32)).astype(BF)
        keep = (pick(keep, 0).astype(F32) + pick(got, 0).astype(F32)).astype(BF)
        got = swap(send, *link)
    return keep.astype(F32) + got.astype(F32)


ORDER_A = ((CORE, None), (ACROSS, 0), (BESIDE, 1), (NEAR, 2), (FAR, 3))
ORDER_B = ((CORE, None), (BESIDE, 1), (NEAR, 2), (FAR, 3), (ACROSS, 0))
ORDER_C = ((CORE, None), (NEAR, 2), (FAR, 3), (ACROSS, 0), (BESIDE, 1))


def tiled(
    latents, blocks, neighbours, fill, cotangent,
    latent_gain, latent_shift, block_gain, block_shift,
    cross_query, cross_key, cross_value, cross_output,
    self_gain, self_shift, self_query, self_key, self_value, self_output,
    hidden_gain, hidden_shift, hidden_expand, hidden_reduce,
):
    rows, width = latents.shape
    groups, block_rows, _ = blocks.shape
    keys = groups * block_rows
    reads = neighbours.shape[1]
    hidden = hidden_expand.shape[1]
    n_grp, n_lvl = lax.axis_size("grp"), lax.axis_size("lvl")
    n_dev = n_grp * n_lvl
    g = lax.axis_index("grp").astype(jnp.int32)
    l = lax.axis_index("lvl").astype(jnp.int32)
    me = g * n_lvl + l
    depth = g // 2
    plane = (g % 2) * n_lvl + l
    ids = jnp.stack([g, l, me, plane, depth, depth ^ 2, depth ^ 1, depth ^ 3]).astype(jnp.int32)
    bits = n_dev.bit_length() - 1
    turned = [int(format(p, f"0{bits}b")[::-1], 2) for p in range(n_dev)]
    order = jnp.array(turned, jnp.int32) ^ me
    unit = hidden // n_dev

    vec = lambda v: v.reshape(1, width)
    vspec = whole((1, width))
    nb = neighbours.reshape(groups * reads)
    blk = blocks.reshape(keys, width)
    pair = width // 4
    cols = pl.BlockSpec((width, pair), lambda i, *_: (0, i))
    rspec = pl.BlockSpec((pair, width), lambda i, *_: (i, 0))
    mine = pl.BlockSpec((width, pair), lambda i, ids: (0, ids[1]))
    mine_rows = pl.BlockSpec((pair, width), lambda i, ids: (ids[1], 0))
    row_full = whole((rows, width))
    key_full = whole((keys, width))
    row_part = pl.BlockSpec((rows, pair), lambda i, *_: (0, i))
    key_part = pl.BlockSpec((keys, pair), lambda i, *_: (0, i))
    set_rows = n_lvl * rows

    gy_all = gather_plane(cotangent)

    cq, ck, cv, co, after_cross, self_in, latent_in, block_in = call(
        functools.partial(cross_forward_kernel, groups, reads),
        "cross_forward", 4, [nb, fill],
        [(latents, row_full), (blk, key_full)]
        + [(vec(v), vspec) for v in (latent_gain, latent_shift, block_gain, block_shift, self_gain, self_shift)]
        + [(cross_query, cols), (cross_key, cols), (cross_value, cols), (cross_output, rspec)],
        [
            ((rows, width), BF, row_part), ((keys, width), BF, key_part), ((keys, width), BF, key_part),
            ((rows, width), BF, row_part), ((rows, width), F32, row_full), ((rows, width), BF, row_full),
            ((rows, width), BF, row_full), ((keys, width), BF, key_full),
        ],
        [pltpu.VMEM((rows, width), F32), pltpu.VMEM((rows, keys), F32)],
        2 * width * width * (2 * rows + 2 * keys) + 4 * rows * keys * width, 14 << 20,
    )

    set_in = gather_set(self_in)
    set_spec = [whole((rows, width))] * 4
    part = (set_rows, pair)
    q, k, v, o0, o1, o2 = call(
        self_forward_kernel, "self_forward", 1, [ids],
        list(zip(set_in, set_spec))
        + [(self_query, mine), (self_key, mine), (self_value, mine)],
        [(part, BF, whole(part))] * 3
        + [((rows, pair), BF, whole((rows, pair)))] * 2
        + [((2 * rows, pair), BF, whole((2 * rows, pair)))],
        [], 6 * set_rows * width * pair + 4 * set_rows * set_rows * pair, 7 << 20,
    )
    latent_flip, block_flip, co_flip = flip_rows("flip_cross", order, [latent_in, block_in, co])

    across = swap(o2, *ACROSS)
    pieces = (o0, swap(o1, *CORE), across[:rows], swap(across[rows:], *CORE))
    after_self, hidden_in, so = call(
        self_out_kernel, "self_out", 1, [ids],
        [(after_cross, row_full)] + [(p, whole((rows, pair))) for p in pieces]
        + [(self_output, whole((width, width))), (vec(hidden_gain), vspec), (vec(hidden_shift), vspec)],
        [((rows, width), F32, row_full), ((rows, width), BF, row_full), ((rows, width), BF, row_full)],
        [], 2 * rows * width * width, 6 << 20,
    )

    hidden_all = gather_plane(hidden_in)
    step = 512
    updated, gate, after_self_delta, hidden_vecs = call(
        ff_local_kernel, "ff_local", hidden // step, [],
        [
            (hidden_in, row_full), (cotangent, row_full), (after_self, row_full), (vec(hidden_gain), vspec),
            (hidden_expand, pl.BlockSpec((width, step), lambda i: (0, i))),
            (hidden_reduce, pl.BlockSpec((step, width), lambda i: (i, 0))),
        ],
        [
            ((rows, width), BF, row_full), ((rows, width), BF, row_full),
            ((rows, width), F32, row_full), ((2, width), F32, whole((2, width))),
        ],
        [pltpu.VMEM((rows, width), F32)] * 2,
        8 * rows * width * hidden, 20 << 20,
    )
    gate_all = gather_set(gate)

    plane_rows = 2 * set_rows
    n_piece = len(hidden_all)
    any_spec = pl.BlockSpec(memory_space=pl.ANY)
    half = (2 * unit, width)

    def unit_cols(p):
        return pl.BlockSpec((width, unit), lambda i, ids: (0, ids[4 + p] * 2 * n_lvl + ids[3]))

    def unit_rows(p):
        return pl.BlockSpec((unit, width), lambda i, ids: (ids[4 + p] * 2 * n_lvl + ids[3], 0))

    red_keep, red_send, exp_keep, exp_send = call(
        functools.partial(ff_weights_kernel, n_piece), "ff_weights", 1, [ids],
        [(a, any_spec) for a in hidden_all] + [(a, any_spec) for a in gy_all]
        + [(hidden_expand, unit_cols(p)) for p in range(4)]
        + [(hidden_reduce, unit_rows(p)) for p in range(4)],
        [(half, BF, whole(half))] * 4,
        [
            pltpu.VMEM((plane_rows, width), BF), pltpu.VMEM((plane_rows, width), BF),
            pltpu.VMEM((4 * unit, width), BF), pltpu.VMEM((4 * unit, width), BF),
            pltpu.VMEM((4 * unit, width), F32), pltpu.VMEM((4 * unit, width), F32),
            pltpu.SemaphoreType.DMA((2, n_piece)),
        ],
        8 * plane_rows * width * 4 * unit, 14 << 20,
    )
    ff_order = ((NEAR, None), (FAR, 0))
    reduce_delta = scatter_sum(red_keep, red_send, ff_order)
    expand_sum = scatter_sum(exp_keep, exp_send, ff_order)

    flipped, self_keep, self_send = call(
        self_backward_kernel, "self_backward", 1, [ids],
        list(zip(gate_all, set_spec)) + [(a, whole(part)) for a in (q, k, v)]
        + [(self_output, mine_rows), (self_query, mine), (self_key, mine), (self_value, mine)],
        [((3 * pair, set_rows), BF, whole((3 * pair, set_rows)))]
        + [((2 * rows, width), BF, whole((2 * rows, width)))] * 2,
        [pltpu.VMEM(part, BF)] * 4,
        8 * set_rows * width * pair + 10 * set_rows * set_rows * pair, 10 << 20,
    )
    self_got = swap(self_send, *CORE)
    self_pass = (self_keep[rows:].astype(F32) + self_got[rows:].astype(F32)).astype(BF)
    self_across = swap(self_pass, *ACROSS)

    span = width // n_grp
    (self_stack,) = call(
        self_weights_kernel, "self_weights", 1, [ids],
        [(flipped, whole(flipped.shape))] + list(zip(set_in, set_spec)),
        [((n_grp, 3 * pair, span), BF, whole((n_grp, 3 * pair, span)))],
        [], 6 * set_rows * width * pair, 8 << 20,
    )
    so_flip, = flip_rows("flip_self", order, [so])
    so_keep, so_send = products("self_output_weights", [so_flip], (0,), [gate])

    half_rows = pl.BlockSpec((rows, width), lambda i, *_: (0, 0))
    after_cross_delta, cross_gate, self_vecs, dcq, dck, dcv = call(
        functools.partial(cross_backward_kernel, groups, reads),
        "cross_backward", 4, [nb, fill],
        [
            (self_keep, half_rows), (self_got, half_rows), (self_across, row_full),
            (after_self_delta, row_full), (after_cross, row_full), (vec(self_gain), vspec),
            (cross_output, rspec), (cq, row_part), (ck, key_part), (cv, key_part),
        ],
        [
            ((rows, width), F32, row_full), ((rows, width), BF, row_full), ((2, width), F32, whole((2, width))),
            ((rows, width), BF, row_part), ((keys, width), BF, key_part), ((keys, width), BF, key_part),
        ],
        [pltpu.VMEM((keys, rows), F32)],
        2 * rows * width * width + 10 * rows * keys * width, 12 << 20,
    )
    co_keep, co_send = products("cross_output_weights", [co_flip], (0,), [cross_gate])
    cq_keep, cq_send, ck_keep, ck_send, cv_keep, cv_send = products(
        "cross_weights", [latent_flip, block_flip], (0, 1, 1), [dcq, dck, dcv]
    )
    latent_delta, block_delta, cross_vecs = call(
        cross_inputs_kernel, "cross_inputs", 4, [],
        [
            (dcq, row_part), (dck, key_part), (dcv, key_part),
            (cross_query, cols), (cross_key, cols), (cross_value, cols),
            (latents, row_full), (blk, key_full), (vec(latent_gain), vspec), (vec(block_gain), vspec),
            (after_cross_delta, row_full),
        ],
        [((rows, width), BF, row_full), ((keys, width), BF, key_full), ((4, width), F32, whole((4, width)))],
        [pltpu.VMEM((rows, width), F32), pltpu.VMEM((keys, width), F32)],
        2 * width * width * (rows + 2 * keys), 12 << 20,
    )

    self_output_delta = scatter_sum(so_keep, so_send, ORDER_A)
    cross_output_delta = scatter_sum(co_keep, co_send, ORDER_A)
    cross_query_delta = scatter_sum(cq_keep, cq_send, ORDER_A)
    cross_key_delta = scatter_sum(ck_keep, ck_send, ORDER_B)
    cross_value_delta = scatter_sum(cv_keep, cv_send, ORDER_C)

    stack = self_stack.reshape(2, 2, 2, 3 * pair, span)
    got = swap(stack[:, :, 1], *BESIDE)
    kept = stack[:, :, 0]
    for link in (NEAR, FAR):
        send = (kept[:, 1].astype(F32) + got[:, 1].astype(F32)).astype(BF) if link is NEAR else (
            kept[1].astype(F32) + got[1].astype(F32)
        ).astype(BF)
        kept = (kept[:, 0].astype(F32) + got[:, 0].astype(F32)).astype(BF) if link is NEAR else (
            kept[0].astype(F32) + got[0].astype(F32)
        ).astype(BF)
        got = swap(send, *link)
    stack = (kept.astype(F32) + got.astype(F32)).astype(BF)
    chunk = width // n_dev
    parts = stack.reshape(3, pair, n_lvl, chunk).transpose(2, 0, 3, 1)
    parts = lax.all_to_all(parts, "lvl", split_axis=0, concat_axis=0, tiled=True)
    parts = parts.transpose(1, 2, 0, 3).reshape(3, chunk, width).astype(F32)

    n_plane = 2 * n_lvl
    expand = expand_sum.astype(BF).reshape(unit, n_grp // 2, n_plane, chunk)
    expand = expand.transpose(2, 3, 1, 0)
    groups_of = [[d * n_plane + s for s in range(n_plane)] for d in range(n_grp // 2)]
    expand = lax.all_to_all(
        expand, ("grp", "lvl"), split_axis=0, concat_axis=0, axis_index_groups=groups_of, tiled=True
    )
    expand_delta = expand.transpose(1, 2, 0, 3).reshape(chunk, hidden).astype(F32)

    vecs = jnp.concatenate([cross_vecs, self_vecs, hidden_vecs], axis=0)
    vecs = vecs.reshape(8, n_dev, chunk).transpose(1, 0, 2).reshape(n_dev, 8 * chunk)
    vecs = lax.psum_scatter(vecs, ("grp", "lvl"), scatter_dimension=0, tiled=True).reshape(8, chunk)

    return (
        updated, latent_delta, block_delta.reshape(groups, block_rows, width),
        vecs[0], vecs[1], vecs[2], vecs[3],
        cross_query_delta, cross_key_delta, cross_value_delta, cross_output_delta,
        vecs[4], vecs[5],
        parts[0], parts[1], parts[2], self_output_delta,
        vecs[6], vecs[7],
        expand_delta, reduce_delta,
    )


def normed(values, norm_gain, norm_shift):
    center = values - jnp.mean(values, axis=-1, keepdims=True)
    spread = jnp.mean(center * center, axis=-1, keepdims=True)
    return center * lax.rsqrt(spread + EPS) * norm_gain + norm_shift


def to_half(values):
    return values.astype(jnp.bfloat16)


def matmul(left_side, right_side):
    return jnp.dot(left_side, right_side, preferred_element_type=jnp.float32)


def left_outer(left_side, right_side):
    return lax.dot_general(
        left_side, right_side, (((0,), (0,)), ((), ())), preferred_element_type=jnp.float32
    )


def right_outer(left_side, right_side):
    return lax.dot_general(
        left_side, right_side, (((1,), (1,)), ((), ())), preferred_element_type=jnp.float32
    )


def self_forward(query_heads, key_heads, value_heads, score_scale):
    length, local_heads, head_size = query_heads.shape
    block_rows = min(512, length)
    query_blocks = query_heads.reshape(length // block_rows, block_rows, local_heads, head_size)

    def one_block(query_block):
        scores = (
            jnp.einsum("qhd,khd->hqk", query_block, key_heads, preferred_element_type=jnp.float32)
            * score_scale
        )
        row_top = jnp.max(scores, axis=-1, keepdims=True)
        raised = jnp.exp(scores - row_top)
        row_total = jnp.sum(raised, axis=-1, keepdims=True)
        attention = raised / row_total
        mixture = jnp.einsum(
            "hqk,khd->qhd", to_half(attention), value_heads, preferred_element_type=jnp.float32
        )
        return (to_half(mixture), row_top + jnp.log(row_total))

    mixture, log_total = lax.map(one_block, query_blocks)
    return (mixture.reshape(length, local_heads, head_size), log_total)


def self_backward(query_heads, key_heads, value_heads, mixed_delta, log_total, score_scale):
    length, local_heads, head_size = query_heads.shape
    block_rows = min(512, length)
    query_blocks = query_heads.reshape(length // block_rows, block_rows, local_heads, head_size)
    delta_blocks = mixed_delta.reshape(length // block_rows, block_rows, local_heads, head_size)

    def one_block(running, pieces):
        key_sum, value_sum = running
        query_block, delta_block, log_block = pieces
        scores = (
            jnp.einsum("qhd,khd->hqk", query_block, key_heads, preferred_element_type=jnp.float32)
            * score_scale
        )
        attention = jnp.exp(scores - log_block)
        value_sum = value_sum + jnp.einsum(
            "hqk,qhd->khd", to_half(attention), delta_block, preferred_element_type=jnp.float32
        )
        weight_delta = jnp.einsum(
            "qhd,khd->hqk", delta_block, value_heads, preferred_element_type=jnp.float32
        )
        score_delta = to_half(
            attention * (weight_delta - jnp.sum(attention * weight_delta, axis=-1, keepdims=True))
        )
        query_delta = to_half(
            jnp.einsum("hqk,khd->qhd", score_delta, key_heads, preferred_element_type=jnp.float32)
            * score_scale
        )
        key_sum = (
            key_sum
            + jnp.einsum(
                "hqk,qhd->khd", score_delta, query_block, preferred_element_type=jnp.float32
            )
            * score_scale
        )
        return ((key_sum, value_sum), query_delta)

    zero_start = jnp.zeros(key_heads.shape, jnp.float32)
    (key_sum, value_sum), query_delta = lax.scan(
        one_block, (zero_start, zero_start), (query_blocks, delta_blocks, log_total)
    )
    return (
        query_delta.reshape(length, local_heads, head_size),
        to_half(key_sum),
        to_half(value_sum),
    )


def cross_forward(cross_queries, block_keys, block_values, neighbours, fill, score_scale):
    groups, latent_rows, head_count, head_size = cross_queries.shape
    block_rows = block_keys.shape[1]
    reads = neighbours.shape[1]
    picked_keys = block_keys[neighbours].reshape(groups, reads * block_rows, head_count, head_size)
    picked_values = block_values[neighbours].reshape(
        groups, reads * block_rows, head_count, head_size
    )
    positions = jnp.arange(block_rows, dtype=jnp.int32)
    live_keys = (positions[None, None, :] < fill[neighbours][:, :, None]).reshape(
        groups, reads * block_rows
    )
    scores = (
        jnp.einsum(
            "gqhd,gkhd->ghqk", cross_queries, picked_keys, preferred_element_type=jnp.float32
        )
        * score_scale
    )
    scores = jnp.where(live_keys[:, None, None, :], scores, NEG)
    attention = jax.nn.softmax(scores, axis=-1)
    return (attention, picked_keys, picked_values)


def plain(
    latents,
    blocks,
    neighbours,
    fill,
    cotangent,
    latent_gain,
    latent_shift,
    block_gain,
    block_shift,
    cross_query,
    cross_key,
    cross_value,
    cross_output,
    self_gain,
    self_shift,
    self_query,
    self_key,
    self_value,
    self_output,
    hidden_gain,
    hidden_shift,
    hidden_expand,
    hidden_reduce,
):
    rows = latents.shape[0]
    width = latents.shape[1]
    groups = blocks.shape[0]
    block_rows = blocks.shape[1]
    reads = neighbours.shape[1]
    head_size = width // H
    score_scale = head_size ** (-0.5)
    latent_float = latents.astype(jnp.float32)
    latent_norm, latent_pull = jax.vjp(normed, latent_float, latent_gain, latent_shift)
    latent_in = to_half(latent_norm)
    block_float = blocks.reshape(groups * block_rows, width).astype(jnp.float32)
    block_norm, block_pull = jax.vjp(normed, block_float, block_gain, block_shift)
    block_in = to_half(block_norm)
    cross_queries = to_half(matmul(latent_in, cross_query)).reshape(
        groups, rows // groups, H, head_size
    )
    block_keys = to_half(matmul(block_in, cross_key)).reshape(groups, block_rows, H, head_size)
    block_values = to_half(matmul(block_in, cross_value)).reshape(groups, block_rows, H, head_size)
    attention, picked_keys, picked_values = cross_forward(
        cross_queries, block_keys, block_values, neighbours, fill, score_scale
    )
    attention_half = to_half(attention)
    cross_mixed = to_half(
        jnp.einsum(
            "ghqk,gkhd->gqhd", attention_half, picked_values, preferred_element_type=jnp.float32
        )
    ).reshape(rows, width)
    after_cross = latent_float + matmul(cross_mixed, cross_output)
    self_norm, self_pull = jax.vjp(normed, after_cross, self_gain, self_shift)
    self_in = to_half(self_norm)
    self_queries = to_half(matmul(self_in, self_query)).reshape(rows, H, head_size)
    self_keys = to_half(matmul(self_in, self_key)).reshape(rows, H, head_size)
    self_values = to_half(matmul(self_in, self_value)).reshape(rows, H, head_size)
    query_heads, key_heads, value_heads = (
        lax.all_to_all(self_queries, "lvl", split_axis=1, concat_axis=0, tiled=True),
        lax.all_to_all(self_keys, "lvl", split_axis=1, concat_axis=0, tiled=True),
        lax.all_to_all(self_values, "lvl", split_axis=1, concat_axis=0, tiled=True),
    )
    head_mixed, log_total = self_forward(query_heads, key_heads, value_heads, score_scale)
    self_mixed = lax.all_to_all(head_mixed, "lvl", split_axis=0, concat_axis=1, tiled=True).reshape(
        rows, width
    )
    after_self = after_cross + matmul(self_mixed, self_output)
    hidden_norm, hidden_pull = jax.vjp(normed, after_self, hidden_gain, hidden_shift)
    hidden_in = to_half(hidden_norm)
    pre_act = matmul(hidden_in, hidden_expand)
    activated, act_pull = jax.vjp(jax.nn.gelu, pre_act)
    act_half = to_half(activated)
    updated = to_half(after_self + matmul(act_half, hidden_reduce))
    reduce_delta = left_outer(act_half, cotangent)
    act_delta = right_outer(cotangent, hidden_reduce)
    pre_delta = to_half(act_pull(act_delta)[0])
    expand_delta = left_outer(hidden_in, pre_delta)
    hidden_delta = right_outer(pre_delta, hidden_expand)
    self_side, hidden_gain_delta, hidden_shift_delta = hidden_pull(hidden_delta)
    after_self_delta = cotangent.astype(jnp.float32) + self_side
    self_gate = to_half(after_self_delta)
    self_output_delta = left_outer(self_mixed, self_gate)
    mixed_delta = to_half(right_outer(self_gate, self_output)).reshape(rows, H, head_size)
    head_delta = lax.all_to_all(mixed_delta, "lvl", split_axis=1, concat_axis=0, tiled=True)
    query_back, key_back, value_back = self_backward(
        query_heads, key_heads, value_heads, head_delta, log_total, score_scale
    )
    query_local, key_local, value_local = (
        lax.all_to_all(query_back, "lvl", split_axis=0, concat_axis=1, tiled=True),
        lax.all_to_all(key_back, "lvl", split_axis=0, concat_axis=1, tiled=True),
        lax.all_to_all(value_back, "lvl", split_axis=0, concat_axis=1, tiled=True),
    )
    query_local = query_local.reshape(rows, width)
    key_local = key_local.reshape(rows, width)
    value_local = value_local.reshape(rows, width)
    self_query_delta = left_outer(self_in, query_local)
    self_key_delta = left_outer(self_in, key_local)
    self_value_delta = left_outer(self_in, value_local)
    self_delta = (
        right_outer(query_local, self_query)
        + right_outer(key_local, self_key)
        + right_outer(value_local, self_value)
    )
    cross_side, self_gain_delta, self_shift_delta = self_pull(self_delta)
    after_cross_delta = after_self_delta + cross_side
    cross_gate = to_half(after_cross_delta)
    cross_output_delta = left_outer(cross_mixed, cross_gate)
    cross_delta = to_half(right_outer(cross_gate, cross_output)).reshape(
        groups, rows // groups, H, head_size
    )
    weight_delta = jnp.einsum(
        "gqhd,gkhd->ghqk", cross_delta, picked_values, preferred_element_type=jnp.float32
    )
    picked_value_delta = jnp.einsum(
        "ghqk,gqhd->gkhd", attention_half, cross_delta, preferred_element_type=jnp.float32
    )
    score_delta = to_half(
        attention * (weight_delta - jnp.sum(attention * weight_delta, axis=-1, keepdims=True))
    )
    cross_query_back = to_half(
        jnp.einsum("ghqk,gkhd->gqhd", score_delta, picked_keys, preferred_element_type=jnp.float32)
        * score_scale
    ).reshape(rows, width)
    picked_key_delta = (
        jnp.einsum(
            "ghqk,gqhd->gkhd", score_delta, cross_queries, preferred_element_type=jnp.float32
        )
        * score_scale
    )
    chosen = (
        neighbours.reshape(groups * reads)[:, None] == jnp.arange(groups, dtype=jnp.int32)[None, :]
    ).astype(jnp.float32)
    key_rows = picked_key_delta.reshape(groups * reads, block_rows * width)
    value_rows = picked_value_delta.reshape(groups * reads, block_rows * width)
    block_key_back = to_half(left_outer_exact(chosen, key_rows)).reshape(groups * block_rows, width)
    block_value_back = to_half(left_outer_exact(chosen, value_rows)).reshape(
        groups * block_rows, width
    )
    cross_query_delta = left_outer(latent_in, cross_query_back)
    cross_key_delta = left_outer(block_in, block_key_back)
    cross_value_delta = left_outer(block_in, block_value_back)
    block_side = right_outer(block_key_back, cross_key) + right_outer(block_value_back, cross_value)
    block_input_delta, block_gain_delta, block_shift_delta = block_pull(block_side)
    latent_side = right_outer(cross_query_back, cross_query)
    latent_input_delta, latent_gain_delta, latent_shift_delta = latent_pull(latent_side)
    latent_delta = to_half(after_cross_delta + latent_input_delta)
    block_delta = to_half(block_input_delta).reshape(groups, block_rows, width)
    summed = (
        lax.psum_scatter(latent_gain_delta, ("grp", "lvl"), scatter_dimension=0, tiled=True),
        lax.psum_scatter(latent_shift_delta, ("grp", "lvl"), scatter_dimension=0, tiled=True),
        lax.psum_scatter(block_gain_delta, ("grp", "lvl"), scatter_dimension=0, tiled=True),
        lax.psum_scatter(block_shift_delta, ("grp", "lvl"), scatter_dimension=0, tiled=True),
        lax.psum_scatter(cross_query_delta, ("grp", "lvl"), scatter_dimension=0, tiled=True),
        lax.psum_scatter(cross_key_delta, ("grp", "lvl"), scatter_dimension=0, tiled=True),
        lax.psum_scatter(cross_value_delta, ("grp", "lvl"), scatter_dimension=0, tiled=True),
        lax.psum_scatter(cross_output_delta, ("grp", "lvl"), scatter_dimension=0, tiled=True),
        lax.psum_scatter(self_gain_delta, ("grp", "lvl"), scatter_dimension=0, tiled=True),
        lax.psum_scatter(self_shift_delta, ("grp", "lvl"), scatter_dimension=0, tiled=True),
        lax.psum_scatter(self_query_delta, ("grp", "lvl"), scatter_dimension=0, tiled=True),
        lax.psum_scatter(self_key_delta, ("grp", "lvl"), scatter_dimension=0, tiled=True),
        lax.psum_scatter(self_value_delta, ("grp", "lvl"), scatter_dimension=0, tiled=True),
        lax.psum_scatter(self_output_delta, ("grp", "lvl"), scatter_dimension=0, tiled=True),
        lax.psum_scatter(hidden_gain_delta, ("grp", "lvl"), scatter_dimension=0, tiled=True),
        lax.psum_scatter(hidden_shift_delta, ("grp", "lvl"), scatter_dimension=0, tiled=True),
        lax.psum_scatter(expand_delta, ("grp", "lvl"), scatter_dimension=0, tiled=True),
        lax.psum_scatter(reduce_delta, ("grp", "lvl"), scatter_dimension=0, tiled=True),
    )
    return (
        updated,
        latent_delta,
        block_delta,
        summed[0],
        summed[1],
        summed[2],
        summed[3],
        summed[4],
        summed[5],
        summed[6],
        summed[7],
        summed[8],
        summed[9],
        summed[10],
        summed[11],
        summed[12],
        summed[13],
        summed[14],
        summed[15],
        summed[16],
        summed[17],
    )


def left_outer_exact(left_side, right_side):
    return lax.dot_general(
        left_side,
        right_side,
        (((0,), (0,)), ((), ())),
        precision=lax.Precision.HIGHEST,
        preferred_element_type=jnp.float32,
    )

def fits(shape, latents, hidden_expand):
    n_dev = shape["grp"] * shape["lvl"]
    return (
        shape["grp"] == 8
        and shape["lvl"] == 4
        and latents.shape[1] % (16 * n_dev) == 0
        and hidden_expand.shape[1] % (128 * n_dev) == 0
    )


def on_device(shape, *args):
    return (tiled if fits(shape, args[0], args[21]) else plain)(*args)


def solution(mesh):
    placed = (
        P(("grp", "lvl"), None),
        P(("grp", "lvl"), None, None),
        P(("grp", "lvl"), None),
        P(("grp", "lvl")),
        P(("grp", "lvl"), None),
        P(),
        P(),
        P(),
        P(),
        P(),
        P(),
        P(),
        P(),
        P(),
        P(),
        P(),
        P(),
        P(),
        P(),
        P(),
        P(),
        P(),
        P(),
    )
    return jax.shard_map(
        functools.partial(on_device, mesh.shape),
        mesh=mesh,
        in_specs=placed,
        out_specs=(
            P(("grp", "lvl"), None),
            P(("grp", "lvl"), None),
            P(("grp", "lvl"), None, None),
            P(("grp", "lvl")),
            P(("grp", "lvl")),
            P(("grp", "lvl")),
            P(("grp", "lvl")),
            P(("grp", "lvl"), None),
            P(("grp", "lvl"), None),
            P(("grp", "lvl"), None),
            P(("grp", "lvl"), None),
            P(("grp", "lvl")),
            P(("grp", "lvl")),
            P(("grp", "lvl"), None),
            P(("grp", "lvl"), None),
            P(("grp", "lvl"), None),
            P(("grp", "lvl"), None),
            P(("grp", "lvl")),
            P(("grp", "lvl")),
            P(("grp", "lvl"), None),
            P(("grp", "lvl"), None),
        ),
        check_vma=False,
    )
```

```python
import functools

import jax
import jax.numpy as jnp
from jax import lax
from jax.experimental import pallas as pl
from jax.experimental.pallas import tpu as pltpu
from jax.sharding import PartitionSpec as P

H = 8


EPS = 1e-05
NEG = -1e30
BF = jnp.bfloat16
F32 = jnp.float32
LOG2_E = 1.4426950408889634
SQRT_2_PI = 0.7978845608028654
CUBIC = 0.044715


def nn(a, b):
    return lax.dot_general(a, b, (((1,), (0,)), ((), ())), preferred_element_type=F32)


def nt(a, b):
    return lax.dot_general(a, b, (((1,), (1,)), ((), ())), preferred_element_type=F32)


def tn(a, b):
    return lax.dot_general(a, b, (((0,), (0,)), ((), ())), preferred_element_type=F32)


def flip(v):
    return jnp.transpose(v)


def hat(v):
    center = v - jnp.mean(v, axis=-1, keepdims=True)
    scale = lax.rsqrt(jnp.mean(center * center, axis=-1, keepdims=True) + EPS)
    return center * scale, scale


def norm_back(dy, v, gain):
    unit, scale = hat(v)
    t = dy * gain
    side = scale * (
        t
        - jnp.mean(t, axis=-1, keepdims=True)
        - unit * jnp.mean(t * unit, axis=-1, keepdims=True)
    )
    return side, jnp.sum(dy * unit, axis=0, keepdims=True), jnp.sum(dy, axis=0, keepdims=True)


def gelu_parts(x):
    square = x * x
    t = jnp.tanh(SQRT_2_PI * x * (1.0 + CUBIC * square))
    half = 0.5 + 0.5 * t
    act = x * half
    slope = half + (0.5 * SQRT_2_PI) * x * (1.0 - t * t) * (1.0 + (3.0 * CUBIC) * square)
    return act, slope


def counts_by_row(nb, fill, rows, groups, block_rows, reads):
    keys = groups * block_rows
    key = lax.broadcasted_iota(jnp.int32, (rows, keys), 1)
    row = lax.broadcasted_iota(jnp.int32, (rows, keys), 0)
    per = rows // groups
    out = jnp.zeros((rows, keys), F32)
    for g in range(groups):
        for m in range(groups):
            times = jnp.int32(0)
            for n in range(reads):
                times = times + (nb[g * reads + n] == m).astype(jnp.int32)
            live = (key >= m * block_rows) & (key < m * block_rows + fill[m])
            here = live & (row >= g * per) & (row < (g + 1) * per)
            out = jnp.where(here, times.astype(F32), out)
    return out


def counts_by_key(nb, fill, rows, groups, block_rows, reads):
    keys = groups * block_rows
    key = lax.broadcasted_iota(jnp.int32, (keys, rows), 0)
    row = lax.broadcasted_iota(jnp.int32, (keys, rows), 1)
    per = rows // groups
    out = jnp.zeros((keys, rows), F32)
    for g in range(groups):
        for m in range(groups):
            times = jnp.int32(0)
            for n in range(reads):
                times = times + (nb[g * reads + n] == m).astype(jnp.int32)
            live = (key >= m * block_rows) & (key < m * block_rows + fill[m])
            here = live & (row >= g * per) & (row < (g + 1) * per)
            out = jnp.where(here, times.astype(F32), out)
    return out


def whole(shape):
    zeros = (0,) * len(shape)
    return pl.BlockSpec(shape, lambda i, *_: zeros)


def near_core(array):
    return pltpu.with_memory_space_constraint(array, pltpu.VMEM)


def call(kernel, name, grid, scalars, ins, outs, scratch, flops, nbytes, vmem=56, after=()):
    first = len(scalars) + len(ins)

    def body(*refs):
        kernel(*refs[:first], *refs[first + len(after) :])

    arrays = [near_core(item[0]) if len(item) > 2 else item[0] for item in ins]
    shapes = [(pltpu.VMEM if len(item) > 3 else jax.ShapeDtypeStruct)(item[0], item[1]) for item in outs]
    return pl.pallas_call(
        body,
        name=name,
        grid_spec=pltpu.PrefetchScalarGridSpec(
            num_scalar_prefetch=len(scalars),
            grid=(grid,),
            in_specs=[item[1] for item in ins] + [pl.BlockSpec(memory_space=pl.ANY)] * len(after),
            out_specs=[item[2] for item in outs],
            scratch_shapes=scratch,
        ),
        out_shape=shapes,
        compiler_params=pltpu.CompilerParams(
            vmem_limit_bytes=vmem * 1024 * 1024, dimension_semantics=("arbitrary",)
        ),
        cost_estimate=pl.CostEstimate(flops=1, bytes_accessed=1, transcendentals=0),
    )(*scalars, *arrays, *after)


def tie(array, after):
    spec = pl.BlockSpec(memory_space=pl.ANY)
    return pl.pallas_call(
        lambda *refs: None,
        name="tie",
        in_specs=[spec] * (1 + len(after)),
        out_specs=spec,
        out_shape=jax.ShapeDtypeStruct(array.shape, array.dtype),
        input_output_aliases={0: 0},
    )(array, *after)


def cross_forward_kernel(
    groups, reads, nb, fill, lat, blk, lg, lb, bg, bb, sg, sb, wq, wk, wv, wo,
    cq, ck, cv, co, ac, self_in, lat_in, blk_in, acc, cnt,
):
    i = pl.program_id(0)
    rows, width = lat.shape
    keys = blk.shape[0]
    scale = (width // H) ** -0.5
    head = width // H

    @pl.when(i == 0)
    def _():
        lat_in[...] = (hat(lat[...].astype(F32))[0] * lg[...] + lb[...]).astype(BF)
        blk_in[...] = (hat(blk[...].astype(F32))[0] * bg[...] + bb[...]).astype(BF)
        acc[...] = lat[...].astype(F32)
        cnt[...] = counts_by_row(nb, fill, rows, groups, keys // groups, reads)

    q = nn(lat_in[...], wq[...]).astype(BF)
    k = nn(blk_in[...], wk[...]).astype(BF)
    v = nn(blk_in[...], wv[...]).astype(BF)
    cq[...] = q
    ck[...] = k
    cv[...] = v
    times = cnt[...]
    seen = times > 0.0
    mixed = []
    for h in range(q.shape[1] // head):
        cut = slice(h * head, (h + 1) * head)
        s = jnp.where(seen, nt(q[:, cut], k[:, cut]), NEG)
        e = jnp.exp2((s - jnp.max(s, axis=-1, keepdims=True)) * (scale * LOG2_E))
        total = jnp.sum(e * times, axis=-1, keepdims=True)
        p = (e * (1.0 / total)).astype(BF) * times.astype(BF)
        mixed.append(nn(p, v[:, cut]).astype(BF))
    mixed = jnp.concatenate(mixed, axis=1)
    co[...] = mixed
    acc[...] += nn(mixed, wo[...])

    @pl.when(i == pl.num_programs(0) - 1)
    def _():
        after = acc[...]
        ac[...] = after
        self_in[...] = (hat(after)[0] * sg[...] + sb[...]).astype(BF)


def flip_rows_kernel(plan, orders, *refs):
    n = 1 + max(src for src, _ in plan)
    ins, outs, tmp = refs[:n], refs[n : n + len(plan)], refs[n + len(plan) :]
    chunks = orders.shape[1]
    for src, t in zip(ins, tmp, strict=True):
        t[...] = flip(src[...])
    for dst, (src, which) in zip(outs, plan, strict=True):
        t = tmp[src]
        size = t.shape[0] // chunks
        for p in range(chunks):
            at = pl.multiple_of(orders[which, p] * size, size)
            dst[p * size : (p + 1) * size, :] = t[pl.ds(at, size), :]


def self_forward_kernel(ids, a0, a1, a2, a3, wq, wk, wv, q, k, v, o0, o1, o2):
    rows, width = a0.shape
    head = width // H
    scale = head**-0.5
    for j, a in enumerate((a0, a1, a2, a3)):
        here = slice(j * rows, (j + 1) * rows)
        x = a[...]
        q[here, :] = nn(x, wq[...]).astype(BF)
        k[here, :] = nn(x, wk[...]).astype(BF)
        v[here, :] = nn(x, wv[...]).astype(BF)
    for j in range(4):
        mixed = []
        for h in range(q.shape[1] // head):
            cut = slice(h * head, (h + 1) * head)
            s = nt(q[j * rows : (j + 1) * rows, cut], k[:, cut])
            e = jnp.exp2((s - jnp.max(s, axis=-1, keepdims=True)) * (scale * LOG2_E))
            p = (e * (1.0 / jnp.sum(e, axis=-1, keepdims=True))).astype(BF)
            mixed.append(nn(p, v[:, cut]).astype(BF))
        mixed = jnp.concatenate(mixed, axis=1)
        if j == 0:
            o0[...] = mixed
        elif j == 1:
            o1[...] = mixed
        else:
            o2[(j - 2) * rows : (j - 1) * rows, :] = mixed


def self_out_kernel(ids, ac, o0, o1, o2, o3, wo, hg, hb, after, hidden_in, so):
    cols = o0.shape[1]
    for j, o in enumerate((o0, o1, o2, o3)):
        at = pl.multiple_of((ids[1] ^ j) * cols, cols)
        so[:, pl.ds(at, cols)] = o[...]
    v = ac[...] + nn(so[...], wo[...])
    after[...] = v
    hidden_in[...] = (hat(v)[0] * hg[...] + hb[...]).astype(BF)


def ff_local_kernel(
    hidden_in, gy, after, hg, wexp, wred, updated, gate, das, vecs, up, dh
):
    i = pl.program_id(0)

    @pl.when(i == 0)
    def _():
        up[...] = after[...]
        dh[...] = jnp.zeros_like(dh)

    pre = nn(hidden_in[...], wexp[...])
    dact = nt(gy[...], wred[...])
    act, slope = gelu_parts(pre)
    up[...] += nn(act.astype(BF), wred[...])
    dh[...] += nt((dact * slope).astype(BF), wexp[...])

    @pl.when(i == pl.num_programs(0) - 1)
    def _():
        updated[...] = up[...].astype(BF)
        side, dg, db = norm_back(dh[...], after[...], hg[...])
        total = gy[...].astype(F32) + side
        das[...] = total
        gate[...] = total.astype(BF)
        vecs[0:1, :] = dg
        vecs[1:2, :] = db


def ff_sums(we, wr, h, g, red, exp, fresh):
    act, slope = gelu_parts(nt(we[...], h))
    dpre = (nt(wr[...], g) * slope).astype(BF)
    if fresh:
        red[...] = nn(act.astype(BF), g)
        exp[...] = nn(dpre, h)
    else:
        red[...] += nn(act.astype(BF), g)
        exp[...] += nn(dpre, h)


def ff_weights_a_kernel(ids, *refs):
    hs, gs = refs[:4], refs[4:8]
    wexp, wred = refs[8:12], refs[12:16]
    red, exp, we, wr, h_all, g_all, sem = refs[16:]
    rows = hs[0].shape[0]
    copies = [
        pltpu.make_async_copy(piece, dst.at[pl.ds(k * rows, rows)], sem.at[which, k])
        for which, (src, dst) in enumerate(((hs, h_all), (gs, g_all)))
        for k, piece in enumerate(src)
    ]
    for c in copies:
        c.start()
    unit = wexp[0].shape[1]
    for q in range(4):
        we[q * unit : (q + 1) * unit, :] = flip(wexp[q][...])
        wr[q * unit : (q + 1) * unit, :] = wred[q][...]
    for t in range(2):
        for k in (2 * t, 2 * t + 1, 2 * t + 4, 2 * t + 5):
            copies[k].wait()
        here = slice(2 * t * rows, 2 * (t + 1) * rows)
        ff_sums(we, wr, h_all[here, :], g_all[here, :], red, exp, t == 0)


def ff_weights_b_kernel(ids, *refs):
    hs, gs = refs[:4], refs[4:8]
    red_in, exp_in, we, wr, keep, send, red, exp, h_all, g_all, sem = refs[8:]
    rows = hs[0].shape[0]
    copies = [
        pltpu.make_async_copy(piece, dst.at[pl.ds(k * rows, rows)], sem.at[which, k])
        for which, (src, dst) in enumerate(((hs, h_all), (gs, g_all)))
        for k, piece in enumerate(src)
    ]
    for c in copies:
        c.start()
    red[...] = red_in[...]
    exp[...] = exp_in[...]
    unit = we.shape[0] // 4
    for t in range(2):
        for k in (2 * t, 2 * t + 1, 2 * t + 4, 2 * t + 5):
            copies[k].wait()
        here = slice(2 * t * rows, 2 * (t + 1) * rows)
        ff_sums(we, wr, h_all[here, :], g_all[here, :], red, exp, False)
    span = exp.shape[1] // 4
    for p in range(4):
        lanes = pl.ds(pl.multiple_of(ids[4 + p] * span, span), span)
        out = keep if p < 2 else send
        low = (p % 2) * 2 * unit
        out[low : low + unit, :] = red[p * unit : (p + 1) * unit, :].astype(BF)
        for q in range(4):
            to = pl.ds(pl.multiple_of(ids[4 + q] * span, span), span)
            out[low + unit : low + 2 * unit, to] = exp[q * unit : (q + 1) * unit, lanes].astype(BF)


def self_backward_kernel(
    ids, g0, g1, g2, g3, q, k, v, wo, wq, wk, wv, flipped, keep, send, do, dq, dk, dv
):
    rows, width = g0.shape
    head = width // H
    scale = head**-0.5
    for j, g in enumerate((g0, g1, g2, g3)):
        do[j * rows : (j + 1) * rows, :] = nt(g[...], wo[...]).astype(BF)
    cols = q.shape[1]
    tile = 256
    for h in range(cols // head):
        cut = slice(h * head, (h + 1) * head)
        kh = k[:, cut]
        vh = v[:, cut]
        kt = flip(kh)
        key_sum = jnp.zeros((k.shape[0], head), F32)
        value_sum = jnp.zeros((k.shape[0], head), F32)
        for t in range(q.shape[0] // tile):
            here = slice(t * tile, (t + 1) * tile)
            qt = q[here, cut]
            dt = do[here, cut]
            s = nt(kh, qt)
            e = jnp.exp2((s - jnp.max(s, axis=0, keepdims=True)) * (scale * LOG2_E))
            p = e * (1.0 / jnp.sum(e, axis=0, keepdims=True))
            dp = nt(vh, dt)
            ds = (p * (dp - jnp.sum(p * dp, axis=0, keepdims=True))).astype(BF)
            value_sum += nn(p.astype(BF), dt)
            key_sum += nn(ds, qt)
            back = (nn(kt, ds) * scale).astype(BF)
            flipped[cut, here] = back
            dq[here, cut] = flip(back)
        dk[:, cut] = (key_sum * scale).astype(BF)
        dv[:, cut] = value_sum.astype(BF)
    flipped[cols : 2 * cols, :] = flip(dk[...])
    flipped[2 * cols : 3 * cols, :] = flip(dv[...])
    for j in range(4):
        here = slice(j * rows, (j + 1) * rows)
        side = nt(dq[here, :], wq[...]) + nt(dk[here, :], wk[...]) + nt(dv[here, :], wv[...])
        out = send if j % 2 else keep
        low = (j // 2) * rows
        out[low : low + rows, :] = side.astype(BF)


def self_weights_kernel(ids, flipped, *refs):
    ins, gates, mixed = refs[0:4], refs[4:8], refs[8:12]
    keep, send, total = refs[12:]
    rows = ins[0].shape[0]
    three = flipped.shape[0]
    for low, high, parts in (
        (0, three, [(flipped[:, j * rows : (j + 1) * rows], ins[j][...]) for j in range(4)]),
        (three, total.shape[0], [(flip(gates[j][...]), mixed[j][...]) for j in range(4)]),
    ):
        acc = None
        for left, right in parts:
            part = nn(left, right)
            acc = part if acc is None else acc + part
        total[low:high, :] = acc
    depth, span = total.shape[0], keep.shape[1]
    blocks = total.shape[1] // span
    for p in range(blocks):
        out = keep if p < blocks // 2 else send
        low = (p % (blocks // 2)) * depth
        lanes = pl.ds(pl.multiple_of(ids[8 + p] * span, span), span)
        out[low : low + depth, :] = total[:, lanes].astype(BF)


def cross_backward_kernel(
    groups, reads, nb, fill, keep, rcv, xr, das, ac, sg, wo, cq, ck, cv,
    dac, gate, vecs, dq, dk, dv, cnt,
):
    i = pl.program_id(0)
    rows, width = das.shape
    keys = ck.shape[0]
    head = width // H
    scale = head**-0.5

    @pl.when(i == 0)
    def _():
        dy = keep[...].astype(F32) + rcv[...].astype(F32) + xr[...].astype(F32)
        side, dg, db = norm_back(dy, ac[...], sg[...])
        total = das[...] + side
        dac[...] = total
        gate[...] = total.astype(BF)
        vecs[0:1, :] = dg
        vecs[1:2, :] = db
        cnt[...] = counts_by_key(nb, fill, rows, groups, keys // groups, reads)

    do = nt(gate[...], wo[...]).astype(BF)
    times = cnt[...]
    seen = times > 0.0
    for h in range(cq.shape[1] // head):
        cut = slice(h * head, (h + 1) * head)
        qh = cq[:, cut]
        kh = ck[:, cut]
        dh = do[:, cut]
        s = jnp.where(seen, nt(kh, qh), NEG)
        e = jnp.exp2((s - jnp.max(s, axis=0, keepdims=True)) * (scale * LOG2_E))
        p = e * (1.0 / jnp.sum(e * times, axis=0, keepdims=True))
        dp = nt(cv[:, cut], dh)
        delta = jnp.sum(p * dp * times, axis=0, keepdims=True)
        ds = (p * (dp - delta)).astype(BF) * times.astype(BF)
        dv[:, cut] = nn(p.astype(BF) * times.astype(BF), dh).astype(BF)
        dk[:, cut] = (nn(ds, qh) * scale).astype(BF)
        dq[:, cut] = flip((nn(flip(kh), ds) * scale).astype(BF))


def cross_inputs_kernel(
    orders, dq, dk, dv, wq, wk, wv, lat, blk, lg, bg, dac, sv, hv, dlat, dblk, keep, send, la, ba, vecs, turned
):
    i = pl.program_id(0)

    @pl.when(i == 0)
    def _():
        la[...] = jnp.zeros_like(la)
        ba[...] = jnp.zeros_like(ba)

    la[...] += nt(dq[...], wq[...])
    ba[...] += nt(dk[...], wk[...]) + nt(dv[...], wv[...])

    @pl.when(i == pl.num_programs(0) - 1)
    def _():
        vecs[...] = jnp.zeros_like(vecs)
        side, dg, db = norm_back(la[...], lat[...].astype(F32), lg[...])
        dlat[...] = (dac[...] + side).astype(BF)
        vecs[0:1, :] = dg
        vecs[1:2, :] = db
        side, dg, db = norm_back(ba[...], blk[...].astype(F32), bg[...])
        dblk[...] = side.astype(BF)
        vecs[2:3, :] = dg
        vecs[3:4, :] = db
        vecs[4:6, :] = sv[...]
        vecs[6:8, :] = hv[...]
        turned[...] = flip(vecs[...])
        chunks = orders.shape[1]
        size = turned.shape[0] // chunks
        half = chunks // 2
        for p in range(chunks):
            at = pl.multiple_of(orders[2, p] * size, size)
            out = keep if p < half else send
            low = (p % half) * size
            out[low : low + size, :] = turned[pl.ds(at, size), :].astype(BF)


def cross_weights_kernel(n, parts, *refs):
    lefts, rights = refs[:n], refs[n : 2 * n]
    outs = refs[2 * n :]
    i = pl.program_id(0)
    for chain, members in enumerate(parts):
        for half in range(2):

            @pl.when((i < 2) if half else (i >= 2))
            def _(chain=chain, members=members, half=half):
                out = outs[2 * chain + half]
                at = 0
                for m in members:
                    r = nn(lefts[m][...], rights[m][...])
                    out[:, at : at + r.shape[1]] = r.astype(BF)
                    at += r.shape[1]


def combine_kernel(widths, *refs):
    total = sum(len(w) for w in widths)
    ins, outs = refs[: 4 * total], refs[4 * total :]
    n = 0
    for k, parts in enumerate(widths):
        at = 0
        for width in parts:
            a, b, c, d = ins[4 * n : 4 * n + 4]
            outs[2 * k][:, at : at + width] = (a[...].astype(F32) + b[...].astype(F32)).astype(BF)
            outs[2 * k + 1][:, at : at + width] = (c[...].astype(F32) + d[...].astype(F32)).astype(BF)
            at += width
            n += 1


def combine(name, chains, steps, after=()):
    ins, outs = [], []
    size = 0
    for parts in chains:
        depth = parts[0][0].shape[0]
        part = depth // 2 // steps
        for kept, got in parts:
            width = kept.shape[1]
            top = pl.BlockSpec((part, width), lambda i: (i, 0))
            low = pl.BlockSpec((part, width), lambda i: (i + steps, 0))
            ins += [(kept, top), (got, top), (kept, low), (got, low)]
        width = sum(kept.shape[1] for kept, _ in parts)
        outs += [((depth // 2, width), BF, pl.BlockSpec((part, width), lambda i: (i, 0)))] * 2
        size += depth * width
    widths = tuple(tuple(kept.shape[1] for kept, _ in parts) for parts in chains)
    out = call(
        functools.partial(combine_kernel, widths), name, steps, [], ins, outs, [],
        size, 6 * size, after=after,
    )
    return [tuple(out[2 * k : 2 * k + 2]) for k in range(len(chains))]


def add_kernel(a, b, out):
    out[...] = (a[...].astype(F32) + b[...].astype(F32)).astype(BF)


def pack_kernel(ff_kept, ff_got, set_kept, set_got, reduce_delta, out):
    unit, width = reduce_delta.shape
    reduce_delta[...] = ff_kept[0:unit, :].astype(F32) + ff_got[0:unit, :].astype(F32)
    rest = ff_kept[unit:, :].astype(F32) + ff_got[unit:, :].astype(F32)
    devices, chunk, _ = out.shape
    span = devices * chunk
    parts = width // span
    for q in range(parts):
        t = flip(rest[:, q * span : (q + 1) * span]).astype(BF)
        for d in range(devices):
            out[d, :, q * unit : (q + 1) * unit] = t[d * chunk : (d + 1) * chunk, :]
    t = flip(set_kept[...].astype(F32) + set_got[...].astype(F32)).astype(BF)
    n_set = t.shape[0] // chunk
    for d in range(devices):
        at = (d % n_set) * chunk
        out[d, :, parts * unit :] = t[at : at + chunk, :]


def place_kernel(unit, n_set, ids, got, expand, *outs):
    devices, _, width = got.shape
    parts = expand.shape[1] // (devices * unit)
    for q in range(parts):
        for d in range(devices):
            at = (q * devices + d) * unit
            expand[:, at : at + unit] = got[d, :, q * unit : (q + 1) * unit].astype(F32)
    cols = (width - parts * unit) // len(outs)
    for d in range(n_set):
        mine = got[(ids[0] % (devices // n_set)) * n_set + d]
        for m, out in enumerate(outs):
            at = parts * unit + m * cols
            out[:, d * cols : (d + 1) * cols] = mine[:, at : at + cols].astype(F32)


def cross_last_kernel(parts, n, *refs):
    ins, outs, vecs = refs[: 2 * n], refs[2 * n : 2 * n + 4], refs[2 * n + 4 :]
    done = [0] * len(outs)
    for chain, members in enumerate(parts):
        total = ins[2 * chain][...].astype(F32) + ins[2 * chain + 1][...].astype(F32)
        at = 0
        for which, cols in members:
            if which < len(outs):
                outs[which][:, done[which] : done[which] + cols] = total[:, at : at + cols]
                done[which] += cols
            else:
                t = flip(total[:, at : at + cols])
                for k, out in enumerate(vecs):
                    out[...] = t[k : k + 1, :]
            at += cols


def swap(values, axis, bit):
    size = lax.axis_size(axis)
    return lax.ppermute(values, axis, [(i, i ^ bit) for i in range(size)])


CORE = ("lvl", 1)
ACROSS = ("lvl", 2)
BESIDE = ("grp", 1)
NEAR = ("grp", 2)
FAR = ("grp", 4)


def gather_set(own, wait=lambda across: across):
    across = wait(swap(own, *ACROSS))
    return own, swap(own, *CORE), across, swap(across, *CORE)


def places(links, n_lvl):
    weights = [bit * (n_lvl if axis == "grp" else 1) for axis, bit in links]
    n = len(weights)
    return [
        sum(w for k, w in enumerate(weights) if p >> (n - 1 - k) & 1) for p in range(1 << n)
    ]


CHAINS = (
    (CORE, ACROSS, BESIDE, NEAR, FAR),
    (CORE, BESIDE, NEAR, FAR, ACROSS),
    (CORE, NEAR, FAR, ACROSS, BESIDE),
)


def tiled(
    latents, blocks, neighbours, fill, cotangent,
    latent_gain, latent_shift, block_gain, block_shift,
    cross_query, cross_key, cross_value, cross_output,
    self_gain, self_shift, self_query, self_key, self_value, self_output,
    hidden_gain, hidden_shift, hidden_expand, hidden_reduce,
):
    rows, width = latents.shape
    groups, block_rows, _ = blocks.shape
    keys = groups * block_rows
    reads = neighbours.shape[1]
    hidden = hidden_expand.shape[1]
    n_grp, n_lvl = lax.axis_size("grp"), lax.axis_size("lvl")
    n_dev = n_grp * n_lvl
    n_plane = 2 * n_lvl
    g = lax.axis_index("grp").astype(jnp.int32)
    l = lax.axis_index("lvl").astype(jnp.int32)
    me = g * n_lvl + l
    depth = g // 2
    plane = (g % 2) * n_lvl + l
    ids = jnp.stack(
        [g, l, me, plane, depth, depth ^ 2, depth ^ 1, depth ^ 3] + [g ^ p for p in (0, 4, 2, 6, 1, 5, 3, 7)]
    ).astype(jnp.int32)
    orders = jnp.array([places(links, n_lvl) for links in CHAINS], jnp.int32) ^ me
    unit = hidden // n_dev
    chunk = width // n_dev

    vec = lambda v: v.reshape(1, width)
    vspec = whole((1, width))
    nb = neighbours.reshape(groups * reads)
    blk = blocks.reshape(keys, width)
    pair = width // 4
    cols = pl.BlockSpec((width, pair), lambda i, *_: (0, i))
    rspec = pl.BlockSpec((pair, width), lambda i, *_: (i, 0))
    mine = pl.BlockSpec((width, pair), lambda i, ids: (0, ids[1]))
    mine_rows = pl.BlockSpec((pair, width), lambda i, ids: (ids[1], 0))
    row_full = whole((rows, width))
    key_full = whole((keys, width))
    row_part = pl.BlockSpec((rows, pair), lambda i, *_: (0, i))
    key_part = pl.BlockSpec((keys, pair), lambda i, *_: (0, i))
    set_rows = n_lvl * rows

    full = lambda a: whole(a.shape)
    cot_across, cot_beside = swap(cotangent, *ACROSS), swap(cotangent, *BESIDE)

    cq, ck, cv, co, after_cross, self_in, latent_in, block_in = call(
        functools.partial(cross_forward_kernel, groups, reads),
        "cross_forward", 4, [nb, fill],
        [(latents, row_full), (blk, key_full)]
        + [(vec(v), vspec) for v in (latent_gain, latent_shift, block_gain, block_shift, self_gain, self_shift)]
        + [(cross_query, cols), (cross_key, cols), (cross_value, cols), (cross_output, rspec)],
        [
            ((rows, width), BF, row_part), ((keys, width), BF, key_part), ((keys, width), BF, key_part),
            ((rows, width), BF, row_part), ((rows, width), F32, row_full), ((rows, width), BF, row_full),
            ((rows, width), BF, row_full), ((keys, width), BF, key_full),
        ],
        [pltpu.VMEM((rows, width), F32), pltpu.VMEM((rows, keys), F32)],
        2 * width * width * (2 * rows + 2 * keys) + 4 * rows * keys * width, 14 << 20,
    )

    set_spec = [whole((rows, width))] * 4
    part = (set_rows, pair)
    plan = ((0, 0), (1, 1), (1, 2), (2, 0), (2, 1), (2, 2))
    sources = (latent_in, block_in, co)
    flips = call(
        functools.partial(flip_rows_kernel, plan), "flip_cross", 1, [orders],
        [(a, full(a)) for a in sources],
        [(sources[k].shape[::-1], BF, whole(sources[k].shape[::-1])) for k, _ in plan],
        [pltpu.VMEM(a.shape[::-1], BF) for a in sources],
        1 << 21, 8 << 20,
    )
    self_in = tie(self_in, [cot_across, cot_beside])
    set_in = gather_set(self_in, lambda across: tie(across, [flips[0]]))
    cot_corner = swap(cot_across, *BESIDE)
    q, k, v, o0, o1, o2 = call(
        self_forward_kernel, "self_forward", 1, [ids],
        list(zip(set_in, set_spec))
        + [(self_query, mine), (self_key, mine), (self_value, mine)],
        [(part, BF, whole(part))] * 3
        + [((rows, pair), BF, whole((rows, pair)))] * 2
        + [((2 * rows, pair), BF, whole((2 * rows, pair)))],
        [], 6 * set_rows * width * pair + 4 * set_rows * set_rows * pair, 7 << 20,
        after=[flips[0]],
    )

    across = swap(tie(o2, [cot_corner]), *ACROSS)
    cots = [cotangent, cot_across, cot_beside, cot_corner]
    cots_core = [swap(a, *CORE) for a in cots]
    o_spec = whole((rows, pair))
    pieces = (o0, swap(o1, *CORE), across, swap(across[rows:], *CORE))
    after_self, hidden_in, so = call(
        self_out_kernel, "self_out", 1, [ids],
        [(after_cross, row_full)] + [(p, o_spec) for p in pieces]
        + [(self_output, whole((width, width))), (vec(hidden_gain), vspec), (vec(hidden_shift), vspec)],
        [((rows, width), F32, row_full), ((rows, width), BF, row_full), ((rows, width), BF, row_full)],
        [], 2 * rows * width * width, 6 << 20, after=cots_core,
    )

    hid_across, hid_beside = swap(hidden_in, *ACROSS), swap(hidden_in, *BESIDE)
    step = 512
    updated, gate, after_self_delta, hidden_vecs = call(
        ff_local_kernel, "ff_local", hidden // step, [],
        [
            (hidden_in, row_full), (cotangent, row_full), (after_self, row_full), (vec(hidden_gain), vspec),
            (hidden_expand, pl.BlockSpec((width, step), lambda i: (0, i))),
            (hidden_reduce, pl.BlockSpec((step, width), lambda i: (i, 0))),
        ],
        [
            ((rows, width), BF, row_full), ((rows, width), BF, row_full),
            ((rows, width), F32, row_full), ((2, width), F32, whole((2, width))),
        ],
        [pltpu.VMEM((rows, width), F32)] * 2,
        8 * rows * width * hidden, 20 << 20,
    )
    gate = tie(gate, [hid_across, hid_beside])
    hid_corner = swap(hid_across, *BESIDE)

    any_spec = pl.BlockSpec(memory_space=pl.ANY)

    def unit_cols(p):
        return pl.BlockSpec((width, unit), lambda i, ids: (0, ids[4 + p] * n_plane + ids[3]))

    def unit_rows(p):
        return pl.BlockSpec((unit, width), lambda i, ids: (ids[4 + p] * n_plane + ids[3], 0))

    mine_units = (4 * unit, width)
    half_units = [((4 * unit, width), F32, whole(mine_units), 0)] * 2 + [(mine_units, BF, whole(mine_units), 0)] * 2
    own_hid = [hidden_in, hid_across, swap(hidden_in, *CORE), swap(hid_across, *CORE)]
    own_cot = [cotangent, cot_across, cots_core[0], cots_core[1]]
    ff_flops = 8 * set_rows * width * 4 * unit
    copied = [
        pltpu.VMEM((set_rows, width), BF), pltpu.VMEM((set_rows, width), BF), pltpu.SemaphoreType.DMA((2, 4)),
    ]
    ff_part = call(
        ff_weights_a_kernel, "ff_weights_a", 1, [ids],
        [(a, any_spec) for a in own_hid + own_cot]
        + [(hidden_expand, unit_cols(p)) for p in range(4)]
        + [(hidden_reduce, unit_rows(p)) for p in range(4)],
        half_units, copied, ff_flops, 14 << 20, after=[gate],
    )

    gate_all = gather_set(gate, lambda across: tie(across, [ff_part[0], hid_corner]))
    flipped, self_keep, self_send = call(
        self_backward_kernel, "self_backward", 1, [ids],
        list(zip(gate_all, set_spec)) + [(a, whole(part)) for a in (q, k, v)]
        + [(self_output, mine_rows), (self_query, mine), (self_key, mine), (self_value, mine)],
        [((3 * pair, set_rows), BF, whole((3 * pair, set_rows)))]
        + [((2 * rows, width), BF, whole((2 * rows, width)))] * 2,
        [pltpu.VMEM(part, BF)] * 4,
        8 * set_rows * width * pair + 10 * set_rows * set_rows * pair, 10 << 20,
    )
    so = tie(so, [gate_all[2]])
    so_across = swap(so, *ACROSS)
    self_send = tie(self_send, [so_across])
    self_got = swap(self_send, *CORE)
    so_all = (so, swap(so, *CORE), so_across, swap(so_across, *CORE))
    lower = pl.BlockSpec((rows // 2, width), lambda i: (i + 2, 0))
    (self_pass,) = call(
        add_kernel, "self_pass", 2, [], [(self_keep, lower), (self_got, lower)],
        [((rows, width), BF, pl.BlockSpec((rows // 2, width), lambda i: (i, 0)))],
        [], rows * width, 6 * rows * width,
    )
    self_across = swap(self_pass, *ACROSS)

    other_hid = [hid_beside, hid_corner, swap(hid_beside, *CORE), swap(hid_corner, *CORE)]
    other_cot = [cot_beside, cot_corner, cots_core[2], cots_core[3]]
    ff_keep, ff_send = call(
        ff_weights_b_kernel, "ff_weights_b", 1, [ids],
        [(a, any_spec) for a in other_hid + other_cot] + [(a, full(a), 0) for a in ff_part],
        [(mine_units, BF, whole(mine_units))] * 2,
        [pltpu.VMEM(mine_units, F32)] * 2 + copied, ff_flops, 14 << 20, after=[self_pass],
    )
    ff_got = swap(ff_send, *NEAR)

    span = width // n_grp
    stack = (n_grp // 2 * 4 * pair, span)
    stack_keep, stack_send = call(
        self_weights_kernel, "self_weights", 1, [ids],
        [(flipped, full(flipped))] + list(zip(set_in, set_spec))
        + [(a, pl.BlockSpec((rows, pair), lambda i, ids: (0, ids[1]))) for a in gate_all]
        + list(zip(so_all, set_spec)),
        [(stack, BF, whole(stack))] * 2,
        [pltpu.VMEM((4 * pair, width), F32)],
        8 * set_rows * width * pair, 8 << 20, after=[ff_send],
    )
    stack_send = tie(stack_send, [self_across])
    stack_got = swap(stack_send, *BESIDE)

    half_rows = pl.BlockSpec((rows, width), lambda i, *_: (0, 0))
    after_cross_delta, cross_gate, self_vecs, dcq, dck, dcv = call(
        functools.partial(cross_backward_kernel, groups, reads),
        "cross_backward", 4, [nb, fill],
        [
            (self_keep, half_rows), (self_got, half_rows), (self_across, row_full),
            (after_self_delta, row_full), (after_cross, row_full), (vec(self_gain), vspec),
            (cross_output, rspec), (cq, row_part), (ck, key_part), (cv, key_part),
        ],
        [
            ((rows, width), F32, row_full), ((rows, width), BF, row_full), ((2, width), F32, whole((2, width))),
            ((rows, width), BF, row_part), ((keys, width), BF, key_part), ((keys, width), BF, key_part),
        ],
        [pltpu.VMEM((keys, rows), F32)],
        2 * rows * width * width + 10 * rows * keys * width, 12 << 20, after=[stack_send],
    )

    ((ff_keep, ff_send),) = combine("ff_sum", [[(ff_keep, ff_got)]], 2, after=[dcq])
    ff_got = swap(ff_send, *FAR)

    third = 3 * width // 8
    lefts = (flips[0], flips[3], flips[1], flips[4], flips[2], flips[5])
    rights = [
        (dcq, full(dcq)), (cross_gate, pl.BlockSpec((rows, third), lambda i: (0, 0))),
        (dck, full(dck)), (cross_gate, pl.BlockSpec((rows, third), lambda i: (0, 1))),
        (dcv, full(dcv)), (cross_gate, pl.BlockSpec((rows, width - 2 * third), lambda i: (0, 3))),
    ]
    tile = width // 4
    wide = [width + third, width + third, 2 * width - 2 * third]
    outs = []
    for n in wide:
        outs.append(((width // 2, n), BF, pl.BlockSpec((tile, n), lambda i: (jnp.maximum(i - 2, 0), 0))))
        outs.append(((width // 2, n), BF, pl.BlockSpec((tile, n), lambda i: (jnp.minimum(i, 1), 0))))
    sums = call(
        functools.partial(cross_weights_kernel, 6, ((0, 1), (2, 3), (4, 5))), "cross_weights", 4, [],
        [(a, pl.BlockSpec((tile, a.shape[1]), lambda i: ((i + 2) % 4, 0))) for a in lefts] + rights,
        outs, [], 2 * width * width * (2 * rows + 2 * keys), 16 << 20, after=[ff_send],
    )
    kept, sent = sums[0::2], sums[1::2]
    got = [swap(tie(a, [stack_got]), *CORE) for a in sent]
    ((stack_keep, stack_send),) = combine("self_sum_y", [[(stack_keep, stack_got)]], 2, after=[sent[0]])
    stack_got = swap(stack_send, *NEAR)

    marks = 128
    latent_delta, block_delta, vec_keep, vec_send = call(
        cross_inputs_kernel, "cross_inputs", 4, [orders],
        [
            (dcq, row_part), (dck, key_part), (dcv, key_part),
            (cross_query, cols), (cross_key, cols), (cross_value, cols),
            (latents, row_full), (blk, key_full), (vec(latent_gain), vspec), (vec(block_gain), vspec),
            (after_cross_delta, row_full), (self_vecs, full(self_vecs)), (hidden_vecs, full(hidden_vecs)),
        ],
        [((rows, width), BF, row_full), ((keys, width), BF, key_full)]
        + [((width // 2, marks), BF, whole((width // 2, marks)))] * 2,
        [
            pltpu.VMEM((rows, width), F32), pltpu.VMEM((keys, width), F32),
            pltpu.VMEM((marks, width), F32), pltpu.VMEM((width, marks), F32),
        ],
        2 * width * width * (rows + 2 * keys), 12 << 20, after=[stack_send],
    )
    vec_got = swap(tie(vec_send, [ff_got]), *CORE)
    chains = [[pair_] for pair_ in zip(kept, got)]
    chains[2].append((vec_keep, vec_got))
    pairs = combine("cross_sum_core", chains, 4)
    got = [swap(send, *CHAINS[n][1]) for n, (_, send) in enumerate(pairs)]

    ((stack_keep, stack_send),) = combine("self_sum_near", [[(stack_keep, stack_got)]], 2, after=[pairs[0][1]])
    stack_got = swap(stack_send, *FAR)
    for stage in (2, 3, 4):
        pairs = combine(
            f"cross_sum_{stage}", [[(kept, a)] for (kept, _), a in zip(pairs, got)], 1, after=[stack_send]
        )
        got = [swap(send, *CHAINS[n][stage]) for n, (_, send) in enumerate(pairs)]
        if stage == 2:
            piece = (unit, width)
            mixed = (n_plane, chunk, 4 * unit + 4 * pair)
            reduce_delta, turned = call(
                pack_kernel, "pack", 1, [],
                [(a, full(a)) for a in (ff_keep, ff_got, stack_keep, stack_got)],
                [(piece, F32, whole(piece)), (mixed, BF, whole(mixed))],
                [], 1 << 18, 2 << 20, after=[pairs[0][1]],
            )
            stack_send = reduce_delta
            groups_of = [[d * n_plane + s for s in range(n_plane)] for d in range(n_grp // 2)]
            turned = lax.all_to_all(
                turned, ("grp", "lvl"), split_axis=0, concat_axis=0, axis_index_groups=groups_of, tiled=True
            )
    members = (
        ((0, width), (3, third)), ((1, width), (3, third)), ((2, width), (3, width - 2 * third), (4, marks)),
    )
    ins = []
    for (kept, _), a in zip(pairs, got):
        ins += [(kept, full(kept)), (a, full(a))]
    last = call(
        functools.partial(cross_last_kernel, members, 3), "cross_last", 1, [], ins,
        [((chunk, width), F32, whole((chunk, width)))] * 4 + [((1, chunk), F32, whole((1, chunk)))] * 8,
        [], 1 << 18, 1 << 20,
    )
    placed = call(
        functools.partial(place_kernel, unit, n_lvl), "place", 1, [ids], [(turned, full(turned))],
        [((chunk, hidden), F32, whole((chunk, hidden)))] + [((chunk, width), F32, whole((chunk, width)))] * 4,
        [], 1 << 18, 1 << 20,
    )
    vecs = [a.reshape(chunk) for a in last[4:]]

    return (
        updated, latent_delta, block_delta.reshape(groups, block_rows, width),
        vecs[0], vecs[1], vecs[2], vecs[3],
        last[0], last[1], last[2], last[3],
        vecs[4], vecs[5],
        placed[1], placed[2], placed[3], placed[4],
        vecs[6], vecs[7],
        placed[0], reduce_delta,
    )


def normed(values, norm_gain, norm_shift):
    center = values - jnp.mean(values, axis=-1, keepdims=True)
    spread = jnp.mean(center * center, axis=-1, keepdims=True)
    return center * lax.rsqrt(spread + EPS) * norm_gain + norm_shift


def to_half(values):
    return values.astype(jnp.bfloat16)


def matmul(left_side, right_side):
    return jnp.dot(left_side, right_side, preferred_element_type=jnp.float32)


def left_outer(left_side, right_side):
    return lax.dot_general(
        left_side, right_side, (((0,), (0,)), ((), ())), preferred_element_type=jnp.float32
    )


def right_outer(left_side, right_side):
    return lax.dot_general(
        left_side, right_side, (((1,), (1,)), ((), ())), preferred_element_type=jnp.float32
    )


def self_forward(query_heads, key_heads, value_heads, score_scale):
    length, local_heads, head_size = query_heads.shape
    block_rows = min(512, length)
    query_blocks = query_heads.reshape(length // block_rows, block_rows, local_heads, head_size)

    def one_block(query_block):
        scores = (
            jnp.einsum("qhd,khd->hqk", query_block, key_heads, preferred_element_type=jnp.float32)
            * score_scale
        )
        row_top = jnp.max(scores, axis=-1, keepdims=True)
        raised = jnp.exp(scores - row_top)
        row_total = jnp.sum(raised, axis=-1, keepdims=True)
        attention = raised / row_total
        mixture = jnp.einsum(
            "hqk,khd->qhd", to_half(attention), value_heads, preferred_element_type=jnp.float32
        )
        return (to_half(mixture), row_top + jnp.log(row_total))

    mixture, log_total = lax.map(one_block, query_blocks)
    return (mixture.reshape(length, local_heads, head_size), log_total)


def self_backward(query_heads, key_heads, value_heads, mixed_delta, log_total, score_scale):
    length, local_heads, head_size = query_heads.shape
    block_rows = min(512, length)
    query_blocks = query_heads.reshape(length // block_rows, block_rows, local_heads, head_size)
    delta_blocks = mixed_delta.reshape(length // block_rows, block_rows, local_heads, head_size)

    def one_block(running, pieces):
        key_sum, value_sum = running
        query_block, delta_block, log_block = pieces
        scores = (
            jnp.einsum("qhd,khd->hqk", query_block, key_heads, preferred_element_type=jnp.float32)
            * score_scale
        )
        attention = jnp.exp(scores - log_block)
        value_sum = value_sum + jnp.einsum(
            "hqk,qhd->khd", to_half(attention), delta_block, preferred_element_type=jnp.float32
        )
        weight_delta = jnp.einsum(
            "qhd,khd->hqk", delta_block, value_heads, preferred_element_type=jnp.float32
        )
        score_delta = to_half(
            attention * (weight_delta - jnp.sum(attention * weight_delta, axis=-1, keepdims=True))
        )
        query_delta = to_half(
            jnp.einsum("hqk,khd->qhd", score_delta, key_heads, preferred_element_type=jnp.float32)
            * score_scale
        )
        key_sum = (
            key_sum
            + jnp.einsum(
                "hqk,qhd->khd", score_delta, query_block, preferred_element_type=jnp.float32
            )
            * score_scale
        )
        return ((key_sum, value_sum), query_delta)

    zero_start = jnp.zeros(key_heads.shape, jnp.float32)
    (key_sum, value_sum), query_delta = lax.scan(
        one_block, (zero_start, zero_start), (query_blocks, delta_blocks, log_total)
    )
    return (
        query_delta.reshape(length, local_heads, head_size),
        to_half(key_sum),
        to_half(value_sum),
    )


def cross_forward(cross_queries, block_keys, block_values, neighbours, fill, score_scale):
    groups, latent_rows, head_count, head_size = cross_queries.shape
    block_rows = block_keys.shape[1]
    reads = neighbours.shape[1]
    picked_keys = block_keys[neighbours].reshape(groups, reads * block_rows, head_count, head_size)
    picked_values = block_values[neighbours].reshape(
        groups, reads * block_rows, head_count, head_size
    )
    positions = jnp.arange(block_rows, dtype=jnp.int32)
    live_keys = (positions[None, None, :] < fill[neighbours][:, :, None]).reshape(
        groups, reads * block_rows
    )
    scores = (
        jnp.einsum(
            "gqhd,gkhd->ghqk", cross_queries, picked_keys, preferred_element_type=jnp.float32
        )
        * score_scale
    )
    scores = jnp.where(live_keys[:, None, None, :], scores, NEG)
    attention = jax.nn.softmax(scores, axis=-1)
    return (attention, picked_keys, picked_values)


def plain(
    latents,
    blocks,
    neighbours,
    fill,
    cotangent,
    latent_gain,
    latent_shift,
    block_gain,
    block_shift,
    cross_query,
    cross_key,
    cross_value,
    cross_output,
    self_gain,
    self_shift,
    self_query,
    self_key,
    self_value,
    self_output,
    hidden_gain,
    hidden_shift,
    hidden_expand,
    hidden_reduce,
):
    rows = latents.shape[0]
    width = latents.shape[1]
    groups = blocks.shape[0]
    block_rows = blocks.shape[1]
    reads = neighbours.shape[1]
    head_size = width // H
    score_scale = head_size ** (-0.5)
    latent_float = latents.astype(jnp.float32)
    latent_norm, latent_pull = jax.vjp(normed, latent_float, latent_gain, latent_shift)
    latent_in = to_half(latent_norm)
    block_float = blocks.reshape(groups * block_rows, width).astype(jnp.float32)
    block_norm, block_pull = jax.vjp(normed, block_float, block_gain, block_shift)
    block_in = to_half(block_norm)
    cross_queries = to_half(matmul(latent_in, cross_query)).reshape(
        groups, rows // groups, H, head_size
    )
    block_keys = to_half(matmul(block_in, cross_key)).reshape(groups, block_rows, H, head_size)
    block_values = to_half(matmul(block_in, cross_value)).reshape(groups, block_rows, H, head_size)
    attention, picked_keys, picked_values = cross_forward(
        cross_queries, block_keys, block_values, neighbours, fill, score_scale
    )
    attention_half = to_half(attention)
    cross_mixed = to_half(
        jnp.einsum(
            "ghqk,gkhd->gqhd", attention_half, picked_values, preferred_element_type=jnp.float32
        )
    ).reshape(rows, width)
    after_cross = latent_float + matmul(cross_mixed, cross_output)
    self_norm, self_pull = jax.vjp(normed, after_cross, self_gain, self_shift)
    self_in = to_half(self_norm)
    self_queries = to_half(matmul(self_in, self_query)).reshape(rows, H, head_size)
    self_keys = to_half(matmul(self_in, self_key)).reshape(rows, H, head_size)
    self_values = to_half(matmul(self_in, self_value)).reshape(rows, H, head_size)
    query_heads, key_heads, value_heads = (
        lax.all_to_all(self_queries, "lvl", split_axis=1, concat_axis=0, tiled=True),
        lax.all_to_all(self_keys, "lvl", split_axis=1, concat_axis=0, tiled=True),
        lax.all_to_all(self_values, "lvl", split_axis=1, concat_axis=0, tiled=True),
    )
    head_mixed, log_total = self_forward(query_heads, key_heads, value_heads, score_scale)
    self_mixed = lax.all_to_all(head_mixed, "lvl", split_axis=0, concat_axis=1, tiled=True).reshape(
        rows, width
    )
    after_self = after_cross + matmul(self_mixed, self_output)
    hidden_norm, hidden_pull = jax.vjp(normed, after_self, hidden_gain, hidden_shift)
    hidden_in = to_half(hidden_norm)
    pre_act = matmul(hidden_in, hidden_expand)
    activated, act_pull = jax.vjp(jax.nn.gelu, pre_act)
    act_half = to_half(activated)
    updated = to_half(after_self + matmul(act_half, hidden_reduce))
    reduce_delta = left_outer(act_half, cotangent)
    act_delta = right_outer(cotangent, hidden_reduce)
    pre_delta = to_half(act_pull(act_delta)[0])
    expand_delta = left_outer(hidden_in, pre_delta)
    hidden_delta = right_outer(pre_delta, hidden_expand)
    self_side, hidden_gain_delta, hidden_shift_delta = hidden_pull(hidden_delta)
    after_self_delta = cotangent.astype(jnp.float32) + self_side
    self_gate = to_half(after_self_delta)
    self_output_delta = left_outer(self_mixed, self_gate)
    mixed_delta = to_half(right_outer(self_gate, self_output)).reshape(rows, H, head_size)
    head_delta = lax.all_to_all(mixed_delta, "lvl", split_axis=1, concat_axis=0, tiled=True)
    query_back, key_back, value_back = self_backward(
        query_heads, key_heads, value_heads, head_delta, log_total, score_scale
    )
    query_local, key_local, value_local = (
        lax.all_to_all(query_back, "lvl", split_axis=0, concat_axis=1, tiled=True),
        lax.all_to_all(key_back, "lvl", split_axis=0, concat_axis=1, tiled=True),
        lax.all_to_all(value_back, "lvl", split_axis=0, concat_axis=1, tiled=True),
    )
    query_local = query_local.reshape(rows, width)
    key_local = key_local.reshape(rows, width)
    value_local = value_local.reshape(rows, width)
    self_query_delta = left_outer(self_in, query_local)
    self_key_delta = left_outer(self_in, key_local)
    self_value_delta = left_outer(self_in, value_local)
    self_delta = (
        right_outer(query_local, self_query)
        + right_outer(key_local, self_key)
        + right_outer(value_local, self_value)
    )
    cross_side, self_gain_delta, self_shift_delta = self_pull(self_delta)
    after_cross_delta = after_self_delta + cross_side
    cross_gate = to_half(after_cross_delta)
    cross_output_delta = left_outer(cross_mixed, cross_gate)
    cross_delta = to_half(right_outer(cross_gate, cross_output)).reshape(
        groups, rows // groups, H, head_size
    )
    weight_delta = jnp.einsum(
        "gqhd,gkhd->ghqk", cross_delta, picked_values, preferred_element_type=jnp.float32
    )
    picked_value_delta = jnp.einsum(
        "ghqk,gqhd->gkhd", attention_half, cross_delta, preferred_element_type=jnp.float32
    )
    score_delta = to_half(
        attention * (weight_delta - jnp.sum(attention * weight_delta, axis=-1, keepdims=True))
    )
    cross_query_back = to_half(
        jnp.einsum("ghqk,gkhd->gqhd", score_delta, picked_keys, preferred_element_type=jnp.float32)
        * score_scale
    ).reshape(rows, width)
    picked_key_delta = (
        jnp.einsum(
            "ghqk,gqhd->gkhd", score_delta, cross_queries, preferred_element_type=jnp.float32
        )
        * score_scale
    )
    chosen = (
        neighbours.reshape(groups * reads)[:, None] == jnp.arange(groups, dtype=jnp.int32)[None, :]
    ).astype(jnp.float32)
    key_rows = picked_key_delta.reshape(groups * reads, block_rows * width)
    value_rows = picked_value_delta.reshape(groups * reads, block_rows * width)
    block_key_back = to_half(left_outer_exact(chosen, key_rows)).reshape(groups * block_rows, width)
    block_value_back = to_half(left_outer_exact(chosen, value_rows)).reshape(
        groups * block_rows, width
    )
    cross_query_delta = left_outer(latent_in, cross_query_back)
    cross_key_delta = left_outer(block_in, block_key_back)
    cross_value_delta = left_outer(block_in, block_value_back)
    block_side = right_outer(block_key_back, cross_key) + right_outer(block_value_back, cross_value)
    block_input_delta, block_gain_delta, block_shift_delta = block_pull(block_side)
    latent_side = right_outer(cross_query_back, cross_query)
    latent_input_delta, latent_gain_delta, latent_shift_delta = latent_pull(latent_side)
    latent_delta = to_half(after_cross_delta + latent_input_delta)
    block_delta = to_half(block_input_delta).reshape(groups, block_rows, width)
    summed = (
        lax.psum_scatter(latent_gain_delta, ("grp", "lvl"), scatter_dimension=0, tiled=True),
        lax.psum_scatter(latent_shift_delta, ("grp", "lvl"), scatter_dimension=0, tiled=True),
        lax.psum_scatter(block_gain_delta, ("grp", "lvl"), scatter_dimension=0, tiled=True),
        lax.psum_scatter(block_shift_delta, ("grp", "lvl"), scatter_dimension=0, tiled=True),
        lax.psum_scatter(cross_query_delta, ("grp", "lvl"), scatter_dimension=0, tiled=True),
        lax.psum_scatter(cross_key_delta, ("grp", "lvl"), scatter_dimension=0, tiled=True),
        lax.psum_scatter(cross_value_delta, ("grp", "lvl"), scatter_dimension=0, tiled=True),
        lax.psum_scatter(cross_output_delta, ("grp", "lvl"), scatter_dimension=0, tiled=True),
        lax.psum_scatter(self_gain_delta, ("grp", "lvl"), scatter_dimension=0, tiled=True),
        lax.psum_scatter(self_shift_delta, ("grp", "lvl"), scatter_dimension=0, tiled=True),
        lax.psum_scatter(self_query_delta, ("grp", "lvl"), scatter_dimension=0, tiled=True),
        lax.psum_scatter(self_key_delta, ("grp", "lvl"), scatter_dimension=0, tiled=True),
        lax.psum_scatter(self_value_delta, ("grp", "lvl"), scatter_dimension=0, tiled=True),
        lax.psum_scatter(self_output_delta, ("grp", "lvl"), scatter_dimension=0, tiled=True),
        lax.psum_scatter(hidden_gain_delta, ("grp", "lvl"), scatter_dimension=0, tiled=True),
        lax.psum_scatter(hidden_shift_delta, ("grp", "lvl"), scatter_dimension=0, tiled=True),
        lax.psum_scatter(expand_delta, ("grp", "lvl"), scatter_dimension=0, tiled=True),
        lax.psum_scatter(reduce_delta, ("grp", "lvl"), scatter_dimension=0, tiled=True),
    )
    return (
        updated,
        latent_delta,
        block_delta,
        summed[0],
        summed[1],
        summed[2],
        summed[3],
        summed[4],
        summed[5],
        summed[6],
        summed[7],
        summed[8],
        summed[9],
        summed[10],
        summed[11],
        summed[12],
        summed[13],
        summed[14],
        summed[15],
        summed[16],
        summed[17],
    )


def left_outer_exact(left_side, right_side):
    return lax.dot_general(
        left_side,
        right_side,
        (((0,), (0,)), ((), ())),
        precision=lax.Precision.HIGHEST,
        preferred_element_type=jnp.float32,
    )

def fits(shape, latents, hidden_expand):
    n_dev = shape["grp"] * shape["lvl"]
    return (
        shape["grp"] == 8
        and shape["lvl"] == 4
        and latents.shape[1] % (16 * n_dev) == 0
        and hidden_expand.shape[1] % (128 * n_dev) == 0
    )


def on_device(shape, *args):
    return (tiled if fits(shape, args[0], args[21]) else plain)(*args)


def solution(mesh):
    placed = (
        P(("grp", "lvl"), None),
        P(("grp", "lvl"), None, None),
        P(("grp", "lvl"), None),
        P(("grp", "lvl")),
        P(("grp", "lvl"), None),
        P(),
        P(),
        P(),
        P(),
        P(),
        P(),
        P(),
        P(),
        P(),
        P(),
        P(),
        P(),
        P(),
        P(),
        P(),
        P(),
        P(),
        P(),
    )
    return jax.shard_map(
        functools.partial(on_device, mesh.shape),
        mesh=mesh,
        in_specs=placed,
        out_specs=(
            P(("grp", "lvl"), None),
            P(("grp", "lvl"), None),
            P(("grp", "lvl"), None, None),
            P(("grp", "lvl")),
            P(("grp", "lvl")),
            P(("grp", "lvl")),
            P(("grp", "lvl")),
            P(("grp", "lvl"), None),
            P(("grp", "lvl"), None),
            P(("grp", "lvl"), None),
            P(("grp", "lvl"), None),
            P(("grp", "lvl")),
            P(("grp", "lvl")),
            P(("grp", "lvl"), None),
            P(("grp", "lvl"), None),
            P(("grp", "lvl"), None),
            P(("grp", "lvl"), None),
            P(("grp", "lvl")),
            P(("grp", "lvl")),
            P(("grp", "lvl"), None),
            P(("grp", "lvl"), None),
        ),
        check_vma=False,
    )
```

```python
import functools

import jax
import jax.numpy as jnp
from jax import lax
from jax.experimental import pallas as pl
from jax.experimental.pallas import tpu as pltpu
from jax.sharding import PartitionSpec as P

H = 8


EPS = 1e-05
NEG = -1e30
BF = jnp.bfloat16
F32 = jnp.float32
VMEM_MB = 30
V = True
LOG2_E = 1.4426950408889634
SQRT_2_PI = 0.7978845608028654
CUBIC = 0.044715


def nn(a, b):
    return lax.dot_general(a, b, (((1,), (0,)), ((), ())), preferred_element_type=F32)


def nt(a, b):
    return lax.dot_general(a, b, (((1,), (1,)), ((), ())), preferred_element_type=F32)


def tn(a, b):
    return lax.dot_general(a, b, (((0,), (0,)), ((), ())), preferred_element_type=F32)


def flip(v):
    return jnp.transpose(v)


def hat(v):
    center = v - jnp.mean(v, axis=-1, keepdims=True)
    scale = lax.rsqrt(jnp.mean(center * center, axis=-1, keepdims=True) + EPS)
    return center * scale, scale


def norm_back(dy, v, gain):
    unit, scale = hat(v)
    t = dy * gain
    side = scale * (
        t
        - jnp.mean(t, axis=-1, keepdims=True)
        - unit * jnp.mean(t * unit, axis=-1, keepdims=True)
    )
    return side, jnp.sum(dy * unit, axis=0, keepdims=True), jnp.sum(dy, axis=0, keepdims=True)


def gelu_parts(x):
    square = x * x
    t = jnp.tanh(SQRT_2_PI * x * (1.0 + CUBIC * square))
    half = 0.5 + 0.5 * t
    act = x * half
    slope = half + (0.5 * SQRT_2_PI) * x * (1.0 - t * t) * (1.0 + (3.0 * CUBIC) * square)
    return act, slope


def counts_by_row(nb, fill, rows, groups, block_rows, reads):
    keys = groups * block_rows
    key = lax.broadcasted_iota(jnp.int32, (rows, keys), 1)
    row = lax.broadcasted_iota(jnp.int32, (rows, keys), 0)
    per = rows // groups
    out = jnp.zeros((rows, keys), F32)
    for g in range(groups):
        for m in range(groups):
            times = jnp.int32(0)
            for n in range(reads):
                times = times + (nb[g * reads + n] == m).astype(jnp.int32)
            live = (key >= m * block_rows) & (key < m * block_rows + fill[m])
            here = live & (row >= g * per) & (row < (g + 1) * per)
            out = jnp.where(here, times.astype(F32), out)
    return out


def counts_by_key(nb, fill, rows, groups, block_rows, reads):
    keys = groups * block_rows
    key = lax.broadcasted_iota(jnp.int32, (keys, rows), 0)
    row = lax.broadcasted_iota(jnp.int32, (keys, rows), 1)
    per = rows // groups
    out = jnp.zeros((keys, rows), F32)
    for g in range(groups):
        for m in range(groups):
            times = jnp.int32(0)
            for n in range(reads):
                times = times + (nb[g * reads + n] == m).astype(jnp.int32)
            live = (key >= m * block_rows) & (key < m * block_rows + fill[m])
            here = live & (row >= g * per) & (row < (g + 1) * per)
            out = jnp.where(here, times.astype(F32), out)
    return out


def whole(shape):
    zeros = (0,) * len(shape)
    return pl.BlockSpec(shape, lambda i, *_: zeros)


def near_core(array):
    return pltpu.with_memory_space_constraint(array, pltpu.VMEM)


def far_off(array):
    return pltpu.with_memory_space_constraint(array, pltpu.HBM)


def call(kernel, name, grid, scalars, ins, outs, scratch, flops, nbytes, vmem=VMEM_MB, after=()):
    first = len(scalars) + len(ins)

    def body(*refs):
        kernel(*refs[:first], *refs[first + len(after) :])

    arrays = [near_core(item[0]) if len(item) > 2 else far_off(item[0]) for item in ins]
    shapes = [(pltpu.VMEM if len(item) > 3 else pltpu.HBM)(item[0], item[1]) for item in outs]
    return pl.pallas_call(
        body,
        name=name,
        grid_spec=pltpu.PrefetchScalarGridSpec(
            num_scalar_prefetch=len(scalars),
            grid=(grid,),
            in_specs=[item[1] for item in ins] + [pl.BlockSpec(memory_space=pl.ANY)] * len(after),
            out_specs=[item[2] for item in outs],
            scratch_shapes=scratch,
        ),
        out_shape=shapes,
        compiler_params=pltpu.CompilerParams(
            vmem_limit_bytes=vmem * 1024 * 1024, dimension_semantics=("arbitrary",)
        ),
        cost_estimate=pl.CostEstimate(flops=1, bytes_accessed=1, transcendentals=0),
    )(*scalars, *arrays, *after)


def tie(array, after):
    spec = pl.BlockSpec(memory_space=pl.ANY)
    array = near_core(array)
    return pl.pallas_call(
        lambda *refs: None,
        name="tie",
        in_specs=[spec] * (1 + len(after)),
        out_specs=spec,
        out_shape=pltpu.VMEM(array.shape, array.dtype),
        input_output_aliases={0: 0},
        compiler_params=pltpu.CompilerParams(vmem_limit_bytes=1024 * 1024),
    )(array, *after)


def cross_forward_kernel(
    groups, reads, nb, fill, lat, blk, lg, lb, bg, bb, sg, sb, wq, wk, wv, wo,
    cq, ck, cv, co, ac, self_in, lat_in, blk_in, acc, cnt,
):
    i = pl.program_id(0)
    rows, width = lat.shape
    keys = blk.shape[0]
    scale = (width // H) ** -0.5
    head = width // H

    @pl.when(i == 0)
    def _():
        lat_in[...] = (hat(lat[...].astype(F32))[0] * lg[...] + lb[...]).astype(BF)
        blk_in[...] = (hat(blk[...].astype(F32))[0] * bg[...] + bb[...]).astype(BF)
        acc[...] = lat[...].astype(F32)
        cnt[...] = counts_by_row(nb, fill, rows, groups, keys // groups, reads)

    q = nn(lat_in[...], wq[...]).astype(BF)
    k = nn(blk_in[...], wk[...]).astype(BF)
    v = nn(blk_in[...], wv[...]).astype(BF)
    cq[...] = q
    ck[...] = k
    cv[...] = v
    times = cnt[...]
    seen = times > 0.0
    mixed = []
    for h in range(q.shape[1] // head):
        cut = slice(h * head, (h + 1) * head)
        s = jnp.where(seen, nt(q[:, cut], k[:, cut]), NEG)
        e = jnp.exp2((s - jnp.max(s, axis=-1, keepdims=True)) * (scale * LOG2_E))
        total = jnp.sum(e * times, axis=-1, keepdims=True)
        p = (e * (1.0 / total)).astype(BF) * times.astype(BF)
        mixed.append(nn(p, v[:, cut]).astype(BF))
    mixed = jnp.concatenate(mixed, axis=1)
    co[...] = mixed
    acc[...] += nn(mixed, wo[...])

    @pl.when(i == pl.num_programs(0) - 1)
    def _():
        after = acc[...]
        ac[...] = after
        self_in[...] = (hat(after)[0] * sg[...] + sb[...]).astype(BF)


def flip_rows_kernel(plan, orders, *refs):
    n = 1 + max(src for src, _ in plan)
    ins, outs, tmp = refs[:n], refs[n : n + len(plan)], refs[n + len(plan) :]
    chunks = orders.shape[1]
    for src, t in zip(ins, tmp, strict=True):
        t[...] = flip(src[...])
    for dst, (src, which) in zip(outs, plan, strict=True):
        t = tmp[src]
        size = t.shape[0] // chunks
        for p in range(chunks):
            at = pl.multiple_of(orders[which, p] * size, size)
            dst[p * size : (p + 1) * size, :] = t[pl.ds(at, size), :]


def self_forward_kernel(ids, a0, a1, a2, a3, wq, wk, wv, q, k, v, o0, o1, o2):
    rows, width = a0.shape
    head = width // H
    scale = head**-0.5
    for j, a in enumerate((a0, a1, a2, a3)):
        here = slice(j * rows, (j + 1) * rows)
        x = a[...]
        q[here, :] = nn(x, wq[...]).astype(BF)
        k[here, :] = nn(x, wk[...]).astype(BF)
        v[here, :] = nn(x, wv[...]).astype(BF)
    for j in range(4):
        mixed = []
        for h in range(q.shape[1] // head):
            cut = slice(h * head, (h + 1) * head)
            s = nt(q[j * rows : (j + 1) * rows, cut], k[:, cut])
            e = jnp.exp2((s - jnp.max(s, axis=-1, keepdims=True)) * (scale * LOG2_E))
            p = (e * (1.0 / jnp.sum(e, axis=-1, keepdims=True))).astype(BF)
            mixed.append(nn(p, v[:, cut]).astype(BF))
        mixed = jnp.concatenate(mixed, axis=1)
        if j == 0:
            o0[...] = mixed
        elif j == 1:
            o1[...] = mixed
        else:
            o2[(j - 2) * rows : (j - 1) * rows, :] = mixed


def self_out_kernel(ids, ac, o0, o1, o2, o3, wo, hg, hb, after, hidden_in, so):
    cols = o0.shape[1]
    for j, o in enumerate((o0, o1, o2, o3)):
        at = pl.multiple_of((ids[1] ^ j) * cols, cols)
        so[:, pl.ds(at, cols)] = o[...]
    v = ac[...] + nn(so[...], wo[...])
    after[...] = v
    hidden_in[...] = (hat(v)[0] * hg[...] + hb[...]).astype(BF)


def cot_back_kernel(gy, wred, out):
    out[...] = nt(gy[...], wred[...])


def cot_units_kernel(ids, *refs):
    gs, wexp, wred = refs[:8], refs[8:12], refs[12:16]
    own, other, we, wr = refs[16:]
    unit = wexp[0].shape[1]
    for q in range(4):
        we[q * unit : (q + 1) * unit, :] = flip(wexp[q][...])
        wr[q * unit : (q + 1) * unit, :] = wred[q][...]
    rows = gs[0].shape[0]
    for k, g in enumerate(gs):
        out = own if k < 4 else other
        at = (k % 4) * rows
        out[:, at : at + rows] = nt(wr[...], g[...])


def ff_local_kernel(
    hidden_in, gy, after, hg, dact, wexp, wred, updated, gate, das, vecs, up, dh
):
    i = pl.program_id(0)

    @pl.when(i == 0)
    def _():
        up[...] = after[...]
        dh[...] = jnp.zeros_like(dh)

    act, slope = gelu_parts(nn(hidden_in[...], wexp[...]))
    up[...] += nn(act.astype(BF), wred[...])
    dh[...] += nt((dact[...] * slope).astype(BF), wexp[...])

    @pl.when(i == pl.num_programs(0) - 1)
    def _():
        updated[...] = up[...].astype(BF)
        side, dg, db = norm_back(dh[...], after[...], hg[...])
        total = gy[...].astype(F32) + side
        das[...] = total
        gate[...] = total.astype(BF)
        vecs[0:1, :] = dg
        vecs[1:2, :] = db


def ff_sums(we, dact, h, g, red, exp, fresh):
    act, slope = gelu_parts(nt(we[...], h))
    dpre = (dact * slope).astype(BF)
    if fresh:
        red[...] = nn(act.astype(BF), g)
        exp[...] = nn(dpre, h)
    else:
        red[...] += nn(act.astype(BF), g)
        exp[...] += nn(dpre, h)


def ff_tokens(refs, dact, we, red, exp, h_all, g_all, sem, fresh):
    hs, gs = refs[:4], refs[4:8]
    rows = hs[0].shape[0]
    copies = [
        pltpu.make_async_copy(piece, dst.at[pl.ds(k * rows, rows)], sem.at[which, k])
        for which, (src, dst) in enumerate(((hs, h_all), (gs, g_all)))
        for k, piece in enumerate(src)
    ]
    for c in copies:
        c.start()
    for t in range(2):
        for k in (2 * t, 2 * t + 1, 2 * t + 4, 2 * t + 5):
            copies[k].wait()
        here = slice(2 * t * rows, 2 * (t + 1) * rows)
        ff_sums(we, dact[:, here], h_all[here, :], g_all[here, :], red, exp, fresh and t == 0)


def ff_weights_a_kernel(*refs):
    dact, we, red, exp, h_all, g_all, sem = refs[8:]
    ff_tokens(refs, dact, we, red, exp, h_all, g_all, sem, True)


def ff_weights_b_kernel(ids, *refs):
    red_in, exp_in, dact, we, keep, send, red, exp, h_all, g_all, sem = refs[8:]
    red[...] = red_in[...]
    exp[...] = exp_in[...]
    ff_tokens(refs, dact, we, red, exp, h_all, g_all, sem, False)
    unit = we.shape[0] // 4
    half = 2 * unit
    width = red.shape[1]
    keep[:, 0:width] = red[0:half, :].astype(BF)
    send[:, 0:width] = red[half:, :].astype(BF)
    span = width // 8
    for p in range(4):
        out = keep if p < 2 else send
        low = (p % 2) * unit
        for q in range(4):
            for z in range(2):
                lanes = pl.ds(pl.multiple_of((ids[8 + p] + 2 * z) * span, span), span)
                to = pl.ds(pl.multiple_of(width + (2 * ids[12 + q] + z) * span, span), span)
                out[low : low + unit, to] = exp[q * unit : (q + 1) * unit, lanes].astype(BF)


def self_backward_kernel(
    ids, g0, g1, g2, g3, q, k, v, wo, wq, wk, wv, flipped, keep, send, do, dq, dk, dv
):
    rows, width = g0.shape
    head = width // H
    scale = head**-0.5
    for j, g in enumerate((g0, g1, g2, g3)):
        do[j * rows : (j + 1) * rows, :] = nt(g[...], wo[...]).astype(BF)
    cols = q.shape[1]
    tile = 256
    for h in range(cols // head):
        cut = slice(h * head, (h + 1) * head)
        kh = k[:, cut]
        vh = v[:, cut]
        kt = flip(kh)
        key_sum = jnp.zeros((k.shape[0], head), F32)
        value_sum = jnp.zeros((k.shape[0], head), F32)
        for t in range(q.shape[0] // tile):
            here = slice(t * tile, (t + 1) * tile)
            qt = q[here, cut]
            dt = do[here, cut]
            s = nt(kh, qt)
            e = jnp.exp2((s - jnp.max(s, axis=0, keepdims=True)) * (scale * LOG2_E))
            p = e * (1.0 / jnp.sum(e, axis=0, keepdims=True))
            dp = nt(vh, dt)
            ds = (p * (dp - jnp.sum(p * dp, axis=0, keepdims=True))).astype(BF)
            value_sum += nn(p.astype(BF), dt)
            key_sum += nn(ds, qt)
            back = (nn(kt, ds) * scale).astype(BF)
            flipped[cut, here] = back
            dq[here, cut] = flip(back)
        dk[:, cut] = (key_sum * scale).astype(BF)
        dv[:, cut] = value_sum.astype(BF)
    flipped[cols : 2 * cols, :] = flip(dk[...])
    flipped[2 * cols : 3 * cols, :] = flip(dv[...])
    for j in range(4):
        here = slice(j * rows, (j + 1) * rows)
        side = nt(dq[here, :], wq[...]) + nt(dk[here, :], wk[...]) + nt(dv[here, :], wv[...])
        out = send if j % 2 else keep
        low = (j // 2) * rows
        out[low : low + rows, :] = side.astype(BF)


def self_weights_kernel(ids, flipped, *refs):
    ins, gates, mixed = refs[0:4], refs[4:8], refs[8:12]
    keep, send, total = refs[12:]
    rows = ins[0].shape[0]
    three = flipped.shape[0]
    for low, high, parts in (
        (0, three, [(flipped[:, j * rows : (j + 1) * rows], ins[j][...]) for j in range(4)]),
        (three, total.shape[0], [(flip(gates[j][...]), mixed[j][...]) for j in range(4)]),
    ):
        acc = None
        for left, right in parts:
            part = nn(left, right)
            acc = part if acc is None else acc + part
        total[low:high, :] = acc
    depth, span = total.shape[0], keep.shape[1]
    blocks = total.shape[1] // span
    for p in range(blocks):
        out = keep if p < blocks // 2 else send
        low = (p % (blocks // 2)) * depth
        lanes = pl.ds(pl.multiple_of(ids[16 + p] * span, span), span)
        out[low : low + depth, :] = total[:, lanes].astype(BF)


def cross_backward_kernel(
    groups, reads, nb, fill, keep, rcv, xr, das, ac, sg, wo, cq, ck, cv,
    dac, gate, vecs, dq, dk, dv, cnt,
):
    i = pl.program_id(0)
    rows, width = das.shape
    keys = ck.shape[0]
    head = width // H
    scale = head**-0.5

    @pl.when(i == 0)
    def _():
        dy = keep[...].astype(F32) + rcv[...].astype(F32) + xr[...].astype(F32)
        side, dg, db = norm_back(dy, ac[...], sg[...])
        total = das[...] + side
        dac[...] = total
        gate[...] = total.astype(BF)
        vecs[0:1, :] = dg
        vecs[1:2, :] = db
        cnt[...] = counts_by_key(nb, fill, rows, groups, keys // groups, reads)

    do = nt(gate[...], wo[...]).astype(BF)
    times = cnt[...]
    seen = times > 0.0
    for h in range(cq.shape[1] // head):
        cut = slice(h * head, (h + 1) * head)
        qh = cq[:, cut]
        kh = ck[:, cut]
        dh = do[:, cut]
        s = jnp.where(seen, nt(kh, qh), NEG)
        e = jnp.exp2((s - jnp.max(s, axis=0, keepdims=True)) * (scale * LOG2_E))
        p = e * (1.0 / jnp.sum(e * times, axis=0, keepdims=True))
        dp = nt(cv[:, cut], dh)
        delta = jnp.sum(p * dp * times, axis=0, keepdims=True)
        ds = (p * (dp - delta)).astype(BF) * times.astype(BF)
        dv[:, cut] = nn(p.astype(BF) * times.astype(BF), dh).astype(BF)
        dk[:, cut] = (nn(ds, qh) * scale).astype(BF)
        dq[:, cut] = flip((nn(flip(kh), ds) * scale).astype(BF))


def cross_inputs_kernel(
    orders, dq, dk, dv, wq, wk, wv, lat, blk, lg, bg, dac, sv, hv, dlat, dblk, *rest
):
    i = pl.program_id(0)
    outs, (la, ba, vecs, turned) = rest[:-4], rest[-4:]

    @pl.when(i == 0)
    def _():
        la[...] = jnp.zeros_like(la)
        ba[...] = jnp.zeros_like(ba)

    la[...] += nt(dq[...], wq[...])
    ba[...] += nt(dk[...], wk[...]) + nt(dv[...], wv[...])

    @pl.when(i == pl.num_programs(0) - 1)
    def _():
        vecs[...] = jnp.zeros_like(vecs)
        side, dg, db = norm_back(la[...], lat[...].astype(F32), lg[...])
        dlat[...] = (dac[...] + side).astype(BF)
        vecs[0:1, :] = dg
        vecs[1:2, :] = db
        side, dg, db = norm_back(ba[...], blk[...].astype(F32), bg[...])
        dblk[...] = side.astype(BF)
        vecs[2:3, :] = dg
        vecs[3:4, :] = db
        vecs[4:6, :] = sv[...]
        vecs[6:8, :] = hv[...]
        turned[...] = flip(vecs[...])
        chunks = orders.shape[1]
        size = turned.shape[0] // chunks
        part = chunks // len(outs)
        for p in range(chunks):
            at = pl.multiple_of(orders[2, p] * size, size)
            low = (p % part) * size
            outs[p // part][low : low + size, :] = turned[pl.ds(at, size), :].astype(BF)


def cross_weights_kernel(n, parts, *refs):
    lefts, rights = refs[:n], refs[n : 2 * n]
    outs = refs[2 * n :]
    i = pl.program_id(0)
    for chain, members in enumerate(parts):
        for half in range(2):

            @pl.when((i < 2) if half else (i >= 2))
            def _(chain=chain, members=members, half=half):
                out = outs[2 * chain + half]
                at = 0
                for m in members:
                    r = nn(lefts[m][...], rights[m][...])
                    out[:, at : at + r.shape[1]] = r.astype(BF)
                    at += r.shape[1]


def combine_kernel(terms, *refs):
    total = sum(sum(parts) for parts in terms)
    ins, outs = refs[: 2 * total], refs[2 * total :]
    n = 0
    for k, parts in enumerate(terms):
        at = 0
        for count in parts:
            tops, lows = ins[n : n + 2 * count : 2], ins[n + 1 : n + 2 * count : 2]
            width = tops[0].shape[1]
            for out, refs_ in ((outs[2 * k], tops), (outs[2 * k + 1], lows)):
                acc = refs_[0][...].astype(F32)
                for ref in refs_[1:]:
                    acc = acc + ref[...].astype(F32)
                out[:, at : at + width] = acc.astype(BF)
            at += width
            n += 2 * count


def combine(name, chains, steps, after=()):
    ins, outs = [], []
    for parts in chains:
        depth = parts[0][0].shape[0]
        part = depth // 2 // steps
        for terms in parts:
            for a in terms:
                top = pl.BlockSpec((part, a.shape[1]), lambda i: (i, 0))
                low = pl.BlockSpec((part, a.shape[1]), lambda i: (i + steps, 0))
                ins += [(a, top, V), (a, low, V)]
        width = sum(terms[0].shape[1] for terms in parts)
        outs += [((depth // 2, width), BF, pl.BlockSpec((part, width), lambda i: (i, 0)), V)] * 2
    counts = tuple(tuple(len(terms) for terms in parts) for parts in chains)
    out = call(
        functools.partial(combine_kernel, counts), name, steps, [], ins, outs, [], 1, 1, after=after
    )
    return [tuple(out[2 * k : 2 * k + 2]) for k in range(len(chains))]


def add_kernel(a, b, out):
    out[...] = (a[...].astype(F32) + b[...].astype(F32)).astype(BF)


def pack_kernel(ff_kept, ff_got, set_kept, set_got, reduce_delta, out):
    unit, width = reduce_delta.shape
    reduce_delta[...] = ff_kept[:, 0:width].astype(F32) + ff_got[:, 0:width].astype(F32)
    rest = ff_kept[:, width:].astype(F32) + ff_got[:, width:].astype(F32)
    devices, chunk, _ = out.shape
    span = devices * chunk
    parts = width // span
    for q in range(parts):
        t = flip(rest[:, q * span : (q + 1) * span]).astype(BF)
        for d in range(devices):
            out[d, :, q * unit : (q + 1) * unit] = t[d * chunk : (d + 1) * chunk, :]
    t = flip(set_kept[...].astype(F32) + set_got[...].astype(F32)).astype(BF)
    n_set = t.shape[0] // chunk
    for d in range(devices):
        at = (d % n_set) * chunk
        out[d, :, parts * unit :] = t[at : at + chunk, :]


def place_kernel(unit, n_set, ids, got, expand, *outs):
    devices, _, width = got.shape
    parts = expand.shape[1] // (devices * unit)
    for q in range(parts):
        for d in range(devices):
            at = ((q // 2) * 2 * devices + (d // n_set) * devices + (q % 2) * n_set + d % n_set) * unit
            expand[:, at : at + unit] = got[d, :, q * unit : (q + 1) * unit].astype(F32)
    cols = (width - parts * unit) // len(outs)
    for d in range(n_set):
        mine = got[ids[3] * n_set + d]
        for m, out in enumerate(outs):
            at = parts * unit + m * cols
            out[:, d * cols : (d + 1) * cols] = mine[:, at : at + cols].astype(F32)


def cross_last_kernel(parts, n, *refs):
    ins, outs, vecs = refs[: 2 * n], refs[2 * n : 2 * n + 4], refs[2 * n + 4 :]
    done = [0] * len(outs)
    for chain, members in enumerate(parts):
        total = ins[2 * chain][...].astype(F32) + ins[2 * chain + 1][...].astype(F32)
        at = 0
        for which, cols in members:
            if which < len(outs):
                outs[which][:, done[which] : done[which] + cols] = total[:, at : at + cols]
                done[which] += cols
            else:
                t = flip(total[:, at : at + cols])
                for k, out in enumerate(vecs):
                    out[...] = t[k : k + 1, :]
            at += cols


def swap(values, axis, bit):
    size = lax.axis_size(axis)
    return lax.ppermute(values, axis, [(i, i ^ bit) for i in range(size)])


CORE = ("lvl", 1)
ACROSS = ("lvl", 2)
BESIDE = ("grp", 1)
NEAR = ("grp", 2)
FAR = ("grp", 4)


def gather_set(own, wait=lambda across: across):
    across = wait(swap(own, *ACROSS))
    return own, swap(own, *CORE), across, swap(across, *CORE)


def places(links, n_lvl):
    weights = [bit * (n_lvl if axis == "grp" else 1) for axis, bit in links]
    n = len(weights)
    return [
        sum(w for k, w in enumerate(weights) if p >> (n - 1 - k) & 1) for p in range(1 << n)
    ]


CHAINS = (
    (CORE, ACROSS, BESIDE, NEAR, FAR),
    (CORE, BESIDE, NEAR, ACROSS, FAR),
    (CORE, NEAR, ACROSS, FAR, BESIDE),
)


def tiled(
    latents, blocks, neighbours, fill, cotangent,
    latent_gain, latent_shift, block_gain, block_shift,
    cross_query, cross_key, cross_value, cross_output,
    self_gain, self_shift, self_query, self_key, self_value, self_output,
    hidden_gain, hidden_shift, hidden_expand, hidden_reduce,
):
    rows, width = latents.shape
    groups, block_rows, _ = blocks.shape
    keys = groups * block_rows
    reads = neighbours.shape[1]
    hidden = hidden_expand.shape[1]
    n_grp, n_lvl = lax.axis_size("grp"), lax.axis_size("lvl")
    n_dev = n_grp * n_lvl
    n_plane = 2 * n_lvl
    g = lax.axis_index("grp").astype(jnp.int32)
    l = lax.axis_index("lvl").astype(jnp.int32)
    me = g * n_lvl + l
    per = n_lvl
    steps = [0, FAR[1], BESIDE[1], FAR[1] | BESIDE[1]]
    bare = g & ~NEAR[1]
    ids = jnp.stack(
        [g, l, me, (g & NEAR[1]) // NEAR[1]]
        + [me ^ (p * per) for p in steps]
        + [bare ^ p for p in steps]
        + [((bare ^ p) // FAR[1]) * 2 + ((bare ^ p) & 1) for p in steps]
        + [g ^ p for p in (0, 4, 1, 5, 2, 6, 3, 7)]
    ).astype(jnp.int32)
    orders = jnp.array([places(links, n_lvl) for links in CHAINS], jnp.int32) ^ me
    unit = hidden // n_dev
    chunk = width // n_dev

    vec = lambda v: v.reshape(1, width)
    vspec = whole((1, width))
    nb = neighbours.reshape(groups * reads)
    blk = blocks.reshape(keys, width)
    pair = width // 4
    cols = pl.BlockSpec((width, pair), lambda i, *_: (0, i))
    rspec = pl.BlockSpec((pair, width), lambda i, *_: (i, 0))
    mine = pl.BlockSpec((width, pair), lambda i, ids: (0, ids[1]))
    mine_rows = pl.BlockSpec((pair, width), lambda i, ids: (ids[1], 0))
    row_full = whole((rows, width))
    key_full = whole((keys, width))
    row_part = pl.BlockSpec((rows, pair), lambda i, *_: (0, i))
    key_part = pl.BlockSpec((keys, pair), lambda i, *_: (0, i))
    set_rows = n_lvl * rows

    full = lambda a: whole(a.shape)
    cot_across, cot_near = swap(cotangent, *ACROSS), swap(cotangent, *NEAR)

    cq, ck, cv, co, after_cross, self_in, latent_in, block_in = call(
        functools.partial(cross_forward_kernel, groups, reads),
        "cross_forward", 4, [nb, fill],
        [(latents, row_full), (blk, key_full)]
        + [(vec(v), vspec) for v in (latent_gain, latent_shift, block_gain, block_shift, self_gain, self_shift)]
        + [(cross_query, cols), (cross_key, cols), (cross_value, cols), (cross_output, rspec)],
        [
            ((rows, width), BF, row_part), ((keys, width), BF, key_part),
            ((keys, width), BF, key_part), ((rows, width), BF, row_part),
            ((rows, width), F32, row_full), ((rows, width), BF, row_full, V),
            ((rows, width), BF, row_full), ((keys, width), BF, key_full),
        ],
        [pltpu.VMEM((rows, width), F32), pltpu.VMEM((rows, keys), F32)],
        2 * width * width * (2 * rows + 2 * keys) + 4 * rows * keys * width, 14 << 20,
    )

    set_of = lambda pieces: [(a, whole((rows, width)), V) for a in pieces]
    part = (set_rows, pair)
    plan = ((0, 0), (1, 1), (1, 2), (2, 0), (2, 1), (2, 2))
    sources = (latent_in, block_in, co)
    flips = call(
        functools.partial(flip_rows_kernel, plan), "flip_cross", 1, [orders],
        [(a, full(a)) for a in sources],
        [(sources[k].shape[::-1], BF, whole(sources[k].shape[::-1])) for k, _ in plan],
        [pltpu.VMEM(a.shape[::-1], BF) for a in sources],
        1 << 21, 8 << 20,
    )
    cot_corner = swap(cot_across, *NEAR)
    (dact,) = call(
        cot_back_kernel, "cot_back", 4, [],
        [(cotangent, row_full), (hidden_reduce, pl.BlockSpec((hidden // 4, width), lambda i: (i, 0)))],
        [((rows, hidden), F32, pl.BlockSpec((rows, hidden // 4), lambda i: (0, i)), V)],
        [], 1, 1, after=[far_off(flips[0])],
    )
    self_in = tie(self_in, [cot_across, cot_near])
    set_in = gather_set(self_in, lambda across: tie(across, [dact]))
    q, k, v, o0, o1, o2 = call(
        self_forward_kernel, "self_forward", 1, [ids],
        set_of(set_in)
        + [(self_query, mine), (self_key, mine), (self_value, mine)],
        [(part, BF, whole(part))] * 3
        + [((rows, pair), BF, whole((rows, pair)), V)] * 2
        + [((2 * rows, pair), BF, whole((2 * rows, pair)), V)],
        [], 6 * set_rows * width * pair + 4 * set_rows * set_rows * pair, 7 << 20,
        after=[dact],
    )

    across = swap(tie(o2, [cot_corner]), *ACROSS)
    cots = [cotangent, cot_across, cot_near, cot_corner]
    cots_core = [swap(a, *CORE) for a in cots]
    own_cot = [cotangent, cot_across, cots_core[0], cots_core[1]]
    other_cot = [cot_near, cot_corner, cots_core[2], cots_core[3]]

    def unit_cols(p):
        return pl.BlockSpec((width, unit), lambda i, ids: (0, ids[4 + p]))

    def unit_rows(p):
        return pl.BlockSpec((unit, width), lambda i, ids: (ids[4 + p], 0))

    mine_units = (4 * unit, width)
    by_token = (4 * unit, set_rows)
    dact_own, dact_other, mine_expand = call(
        cot_units_kernel, "cot_units", 1, [ids],
        [(own_cot[0], row_full)] + [(a, row_full, V) for a in own_cot[1:] + other_cot]
        + [(hidden_expand, unit_cols(p)) for p in range(4)]
        + [(hidden_reduce, unit_rows(p)) for p in range(4)],
        [(by_token, F32, whole(by_token), V)] * 2 + [(mine_units, BF, whole(mine_units), V)],
        [pltpu.VMEM(mine_units, BF)], 1, 1, after=[o0],
    )
    across = tie(across, [mine_expand])
    o_spec = whole((rows, pair))
    pieces = (o0, swap(o1, *CORE), across, swap(across[rows:], *CORE))
    after_self, hidden_in, so = call(
        self_out_kernel, "self_out", 1, [ids],
        [(after_cross, row_full)] + [(p, o_spec, V) for p in pieces]
        + [(self_output, whole((width, width))), (vec(hidden_gain), vspec), (vec(hidden_shift), vspec)],
        [((rows, width), F32, row_full, V), ((rows, width), BF, row_full, V), ((rows, width), BF, row_full, V)],
        [], 2 * rows * width * width, 6 << 20, after=[mine_expand],
    )

    hid_across, hid_near = swap(hidden_in, *ACROSS), swap(hidden_in, *NEAR)
    step = 512
    updated, gate, after_self_delta, hidden_vecs = call(
        ff_local_kernel, "ff_local", hidden // step, [],
        [
            (hidden_in, row_full, V), (cotangent, row_full), (after_self, row_full, V), (vec(hidden_gain), vspec),
            (dact, pl.BlockSpec((rows, step), lambda i: (0, i)), V),
            (hidden_expand, pl.BlockSpec((width, step), lambda i: (0, i))),
            (hidden_reduce, pl.BlockSpec((step, width), lambda i: (i, 0))),
        ],
        [
            ((rows, width), BF, row_full), ((rows, width), BF, row_full, V),
            ((rows, width), F32, row_full), ((2, width), F32, whole((2, width))),
        ],
        [pltpu.VMEM((rows, width), F32)] * 2,
        8 * rows * width * hidden, 20 << 20,
    )
    gate = tie(gate, [hid_across, hid_near])
    hid_corner = swap(hid_across, *NEAR)

    any_spec = pl.BlockSpec(memory_space=pl.ANY)

    own_hid = [hidden_in, hid_across, swap(hidden_in, *CORE), swap(hid_across, *CORE)]
    ff_flops = 8 * set_rows * width * 4 * unit
    copied = [
        pltpu.VMEM((set_rows, width), BF), pltpu.VMEM((set_rows, width), BF), pltpu.SemaphoreType.DMA((2, 4)),
    ]
    ff_part = call(
        ff_weights_a_kernel, "ff_weights_a", 1, [],
        [(a, any_spec, V) for a in own_hid] + [(own_cot[0], any_spec)] + [(a, any_spec, V) for a in own_cot[1:]]
        + [(a, full(a), V) for a in (dact_own, mine_expand)],
        [(mine_units, F32, whole(mine_units), V)] * 2, copied, ff_flops, 14 << 20, after=[gate],
    )

    gate_all = gather_set(gate, lambda across: tie(across, [ff_part[0], hid_corner]))
    flipped, self_keep, self_send = call(
        self_backward_kernel, "self_backward", 1, [ids],
        set_of(gate_all) + [(a, whole(part)) for a in (q, k, v)]
        + [(self_output, mine_rows), (self_query, mine), (self_key, mine), (self_value, mine)],
        [((3 * pair, set_rows), BF, whole((3 * pair, set_rows)))]
        + [((2 * rows, width), BF, whole((2 * rows, width)), V)] * 2,
        [pltpu.VMEM(part, BF)] * 4,
        8 * set_rows * width * pair + 10 * set_rows * set_rows * pair, 10 << 20,
    )
    so = tie(so, [gate_all[2]])
    so_across = swap(so, *ACROSS)
    self_send = tie(self_send, [so_across])
    self_got = swap(self_send, *CORE)
    so_all = (so, swap(so, *CORE), so_across, swap(so_across, *CORE))
    lower = pl.BlockSpec((rows // 2, width), lambda i: (i + 2, 0))
    (self_pass,) = call(
        add_kernel, "self_pass", 2, [], [(self_keep, lower, V), (self_got, lower, V)],
        [((rows, width), BF, pl.BlockSpec((rows // 2, width), lambda i: (i, 0)), V)],
        [], rows * width, 6 * rows * width,
    )
    self_across = swap(self_pass, *ACROSS)

    other_hid = [hid_near, hid_corner, swap(hid_near, *CORE), swap(hid_corner, *CORE)]
    half = (2 * unit, 2 * width)
    ff_keep, ff_send = call(
        ff_weights_b_kernel, "ff_weights_b", 1, [ids],
        [(a, any_spec, V) for a in other_hid + other_cot] + [(a, full(a), V) for a in (*ff_part, dact_other, mine_expand)],
        [(half, BF, whole(half), V)] * 2,
        [pltpu.VMEM(mine_units, F32)] * 2 + copied, ff_flops, 14 << 20, after=[self_pass],
    )
    ff_got = swap(ff_send, *BESIDE)

    span = width // n_grp
    stack = (n_grp // 2 * 4 * pair, span)
    stack_keep, stack_send = call(
        self_weights_kernel, "self_weights", 1, [ids],
        [(flipped, full(flipped))] + set_of(set_in)
        + [(a, pl.BlockSpec((rows, pair), lambda i, ids: (0, ids[1])), V) for a in gate_all]
        + set_of(so_all),
        [(stack, BF, whole(stack), V)] * 2,
        [pltpu.VMEM((4 * pair, width), F32)],
        8 * set_rows * width * pair, 8 << 20, after=[ff_send],
    )
    stack_send = tie(stack_send, [self_across])
    stack_got = swap(stack_send, *NEAR)

    half_rows = pl.BlockSpec((rows, width), lambda i, *_: (0, 0))
    after_cross_delta, cross_gate, self_vecs, dcq, dck, dcv = call(
        functools.partial(cross_backward_kernel, groups, reads),
        "cross_backward", 4, [nb, fill],
        [
            (self_keep, half_rows, V), (self_got, half_rows, V), (self_across, row_full, V),
            (after_self_delta, row_full), (after_cross, row_full), (vec(self_gain), vspec),
            (cross_output, rspec), (cq, row_part), (ck, key_part), (cv, key_part),
        ],
        [
            ((rows, width), F32, row_full), ((rows, width), BF, row_full, V), ((2, width), F32, whole((2, width))),
            ((rows, width), BF, row_part, V), ((keys, width), BF, key_part, V), ((keys, width), BF, key_part, V),
        ],
        [pltpu.VMEM((keys, rows), F32)],
        2 * rows * width * width + 10 * rows * keys * width, 12 << 20, after=[stack_send],
    )

    third = 3 * width // 8
    lefts = (flips[0], flips[3], flips[1], flips[4], flips[2], flips[5])
    rights = [
        (dcq, full(dcq), V), (cross_gate, pl.BlockSpec((rows, third), lambda i: (0, 0)), V),
        (dck, full(dck), V), (cross_gate, pl.BlockSpec((rows, third), lambda i: (0, 1)), V),
        (dcv, full(dcv), V), (cross_gate, pl.BlockSpec((rows, width - 2 * third), lambda i: (0, 3)), V),
    ]
    tile = width // 4
    wide = [width + third, width + third, 2 * width - 2 * third]
    outs = []
    for n in wide:
        outs.append(((width // 2, n), BF, pl.BlockSpec((tile, n), lambda i: (jnp.maximum(i - 2, 0), 0)), V))
        outs.append(((width // 2, n), BF, pl.BlockSpec((tile, n), lambda i: (jnp.minimum(i, 1), 0)), V))
    sums = call(
        functools.partial(cross_weights_kernel, 6, ((0, 1), (2, 3), (4, 5))), "cross_weights", 4, [],
        [(a, pl.BlockSpec((tile, a.shape[1]), lambda i: ((i + 2) % 4, 0))) for a in lefts] + rights,
        outs, [], 2 * width * width * (2 * rows + 2 * keys), 16 << 20,
    )
    kept, sent = sums[0::2], sums[1::2]
    got = [swap(tie(a, [stack_got]), *CORE) for a in sent]
    ((ff_keep, ff_send),) = combine("ff_sum", [[(ff_keep, ff_got)]], 1, after=[sent[0]])
    ff_got = swap(ff_send, *FAR)
    ((stack_keep, stack_send),) = combine("self_sum_near", [[(stack_keep, stack_got)]], 2, after=[ff_send])
    stack_got = swap(stack_send, *BESIDE)

    pairs = combine("cross_sum_core", [[p] for p in zip(kept, got)], 4, after=[stack_send])
    got = [swap(send, *CHAINS[n][1]) for n, (_, send) in enumerate(pairs)]

    marks = 128
    quarter = (width // 4, marks)
    latent_delta, block_delta, *vecs = call(
        cross_inputs_kernel, "cross_inputs", 4, [orders],
        [
            (dcq, row_part, V), (dck, key_part, V), (dcv, key_part, V),
            (cross_query, cols), (cross_key, cols), (cross_value, cols),
            (latents, row_full), (blk, key_full), (vec(latent_gain), vspec), (vec(block_gain), vspec),
            (after_cross_delta, row_full), (self_vecs, full(self_vecs)), (hidden_vecs, full(hidden_vecs)),
        ],
        [((rows, width), BF, row_full), ((keys, width), BF, key_full)] + [(quarter, BF, whole(quarter), V)] * 4,
        [
            pltpu.VMEM((rows, width), F32), pltpu.VMEM((keys, width), F32),
            pltpu.VMEM((marks, width), F32), pltpu.VMEM((width, marks), F32),
        ],
        2 * width * width * (rows + 2 * keys), 12 << 20, after=[pairs[0][1]],
    )
    both = NEAR[1] * n_lvl + CORE[1]
    vecs = [tie(a, [ff_got]) for a in vecs]
    vecs = (
        vecs[0], swap(vecs[1], *NEAR), swap(vecs[2], *CORE),
        lax.ppermute(vecs[3], ("grp", "lvl"), [(i, i ^ both) for i in range(n_dev)]),
    )
    ((stack_keep, stack_send),) = combine("self_sum_y", [[(stack_keep, stack_got)]], 2, after=[vecs[0]])
    stack_got = swap(stack_send, *FAR)
    for stage in (2, 3, 4):
        chains = [[(kept, a)] for (kept, _), a in zip(pairs, got)]
        if stage == 2:
            chains[2].append(vecs)
        pairs = combine(f"cross_sum_{stage}", chains, 1, after=[stack_send])
        got = [swap(send, *CHAINS[n][stage]) for n, (_, send) in enumerate(pairs)]
        if stage == 3:
            piece = (unit, width)
            mixed = (n_plane, chunk, 4 * unit + 4 * pair)
            reduce_delta, turned = call(
                pack_kernel, "pack", 1, [],
                [
                    (a, full(a), V)
                    for a in (ff_keep, ff_got, stack_keep, stack_got)
                ],
                [(piece, F32, whole(piece)), (mixed, BF, whole(mixed), V)],
                [], 1 << 18, 2 << 20, after=[pairs[0][1]],
            )
            stack_send = turned
            planes = [
                [(d ^ z) * n_lvl + k for z in (0, NEAR[1]) for k in range(n_lvl)]
                for d in range(n_grp)
                if not d & NEAR[1]
            ]
            got_all = lax.all_to_all(
                turned, ("grp", "lvl"), split_axis=0, concat_axis=0, axis_index_groups=planes, tiled=True
            )
    members = (
        ((0, width), (3, third)), ((1, width), (3, third)), ((2, width), (3, width - 2 * third), (4, marks)),
    )
    ins = []
    for (kept, _), a in zip(pairs, got):
        ins += [(kept, full(kept), V), (a, full(a), V)]
    last = call(
        functools.partial(cross_last_kernel, members, 3), "cross_last", 1, [], ins,
        [((chunk, width), F32, whole((chunk, width)))] * 4 + [((1, chunk), F32, whole((1, chunk)))] * 8,
        [], 1 << 18, 1 << 20,
    )
    placed = call(
        functools.partial(place_kernel, unit, n_lvl), "place", 1, [ids], [(got_all, full(got_all), V)],
        [((chunk, hidden), F32, whole((chunk, hidden)))] + [((chunk, width), F32, whole((chunk, width)))] * 4,
        [], 1 << 18, 1 << 20,
    )
    vecs = [a.reshape(chunk) for a in last[4:]]

    return (
        updated, latent_delta, block_delta.reshape(groups, block_rows, width),
        vecs[0], vecs[1], vecs[2], vecs[3],
        last[0], last[1], last[2], last[3],
        vecs[4], vecs[5],
        placed[1], placed[2], placed[3], placed[4],
        vecs[6], vecs[7],
        placed[0], reduce_delta,
    )


def normed(values, norm_gain, norm_shift):
    center = values - jnp.mean(values, axis=-1, keepdims=True)
    spread = jnp.mean(center * center, axis=-1, keepdims=True)
    return center * lax.rsqrt(spread + EPS) * norm_gain + norm_shift


def to_half(values):
    return values.astype(jnp.bfloat16)


def matmul(left_side, right_side):
    return jnp.dot(left_side, right_side, preferred_element_type=jnp.float32)


def left_outer(left_side, right_side):
    return lax.dot_general(
        left_side, right_side, (((0,), (0,)), ((), ())), preferred_element_type=jnp.float32
    )


def right_outer(left_side, right_side):
    return lax.dot_general(
        left_side, right_side, (((1,), (1,)), ((), ())), preferred_element_type=jnp.float32
    )


def self_forward(query_heads, key_heads, value_heads, score_scale):
    length, local_heads, head_size = query_heads.shape
    block_rows = min(512, length)
    query_blocks = query_heads.reshape(length // block_rows, block_rows, local_heads, head_size)

    def one_block(query_block):
        scores = (
            jnp.einsum("qhd,khd->hqk", query_block, key_heads, preferred_element_type=jnp.float32)
            * score_scale
        )
        row_top = jnp.max(scores, axis=-1, keepdims=True)
        raised = jnp.exp(scores - row_top)
        row_total = jnp.sum(raised, axis=-1, keepdims=True)
        attention = raised / row_total
        mixture = jnp.einsum(
            "hqk,khd->qhd", to_half(attention), value_heads, preferred_element_type=jnp.float32
        )
        return (to_half(mixture), row_top + jnp.log(row_total))

    mixture, log_total = lax.map(one_block, query_blocks)
    return (mixture.reshape(length, local_heads, head_size), log_total)


def self_backward(query_heads, key_heads, value_heads, mixed_delta, log_total, score_scale):
    length, local_heads, head_size = query_heads.shape
    block_rows = min(512, length)
    query_blocks = query_heads.reshape(length // block_rows, block_rows, local_heads, head_size)
    delta_blocks = mixed_delta.reshape(length // block_rows, block_rows, local_heads, head_size)

    def one_block(running, pieces):
        key_sum, value_sum = running
        query_block, delta_block, log_block = pieces
        scores = (
            jnp.einsum("qhd,khd->hqk", query_block, key_heads, preferred_element_type=jnp.float32)
            * score_scale
        )
        attention = jnp.exp(scores - log_block)
        value_sum = value_sum + jnp.einsum(
            "hqk,qhd->khd", to_half(attention), delta_block, preferred_element_type=jnp.float32
        )
        weight_delta = jnp.einsum(
            "qhd,khd->hqk", delta_block, value_heads, preferred_element_type=jnp.float32
        )
        score_delta = to_half(
            attention * (weight_delta - jnp.sum(attention * weight_delta, axis=-1, keepdims=True))
        )
        query_delta = to_half(
            jnp.einsum("hqk,khd->qhd", score_delta, key_heads, preferred_element_type=jnp.float32)
            * score_scale
        )
        key_sum = (
            key_sum
            + jnp.einsum(
                "hqk,qhd->khd", score_delta, query_block, preferred_element_type=jnp.float32
            )
            * score_scale
        )
        return ((key_sum, value_sum), query_delta)

    zero_start = jnp.zeros(key_heads.shape, jnp.float32)
    (key_sum, value_sum), query_delta = lax.scan(
        one_block, (zero_start, zero_start), (query_blocks, delta_blocks, log_total)
    )
    return (
        query_delta.reshape(length, local_heads, head_size),
        to_half(key_sum),
        to_half(value_sum),
    )


def cross_forward(cross_queries, block_keys, block_values, neighbours, fill, score_scale):
    groups, latent_rows, head_count, head_size = cross_queries.shape
    block_rows = block_keys.shape[1]
    reads = neighbours.shape[1]
    picked_keys = block_keys[neighbours].reshape(groups, reads * block_rows, head_count, head_size)
    picked_values = block_values[neighbours].reshape(
        groups, reads * block_rows, head_count, head_size
    )
    positions = jnp.arange(block_rows, dtype=jnp.int32)
    live_keys = (positions[None, None, :] < fill[neighbours][:, :, None]).reshape(
        groups, reads * block_rows
    )
    scores = (
        jnp.einsum(
            "gqhd,gkhd->ghqk", cross_queries, picked_keys, preferred_element_type=jnp.float32
        )
        * score_scale
    )
    scores = jnp.where(live_keys[:, None, None, :], scores, NEG)
    attention = jax.nn.softmax(scores, axis=-1)
    return (attention, picked_keys, picked_values)


def plain(
    latents,
    blocks,
    neighbours,
    fill,
    cotangent,
    latent_gain,
    latent_shift,
    block_gain,
    block_shift,
    cross_query,
    cross_key,
    cross_value,
    cross_output,
    self_gain,
    self_shift,
    self_query,
    self_key,
    self_value,
    self_output,
    hidden_gain,
    hidden_shift,
    hidden_expand,
    hidden_reduce,
):
    rows = latents.shape[0]
    width = latents.shape[1]
    groups = blocks.shape[0]
    block_rows = blocks.shape[1]
    reads = neighbours.shape[1]
    head_size = width // H
    score_scale = head_size ** (-0.5)
    latent_float = latents.astype(jnp.float32)
    latent_norm, latent_pull = jax.vjp(normed, latent_float, latent_gain, latent_shift)
    latent_in = to_half(latent_norm)
    block_float = blocks.reshape(groups * block_rows, width).astype(jnp.float32)
    block_norm, block_pull = jax.vjp(normed, block_float, block_gain, block_shift)
    block_in = to_half(block_norm)
    cross_queries = to_half(matmul(latent_in, cross_query)).reshape(
        groups, rows // groups, H, head_size
    )
    block_keys = to_half(matmul(block_in, cross_key)).reshape(groups, block_rows, H, head_size)
    block_values = to_half(matmul(block_in, cross_value)).reshape(groups, block_rows, H, head_size)
    attention, picked_keys, picked_values = cross_forward(
        cross_queries, block_keys, block_values, neighbours, fill, score_scale
    )
    attention_half = to_half(attention)
    cross_mixed = to_half(
        jnp.einsum(
            "ghqk,gkhd->gqhd", attention_half, picked_values, preferred_element_type=jnp.float32
        )
    ).reshape(rows, width)
    after_cross = latent_float + matmul(cross_mixed, cross_output)
    self_norm, self_pull = jax.vjp(normed, after_cross, self_gain, self_shift)
    self_in = to_half(self_norm)
    self_queries = to_half(matmul(self_in, self_query)).reshape(rows, H, head_size)
    self_keys = to_half(matmul(self_in, self_key)).reshape(rows, H, head_size)
    self_values = to_half(matmul(self_in, self_value)).reshape(rows, H, head_size)
    query_heads, key_heads, value_heads = (
        lax.all_to_all(self_queries, "lvl", split_axis=1, concat_axis=0, tiled=True),
        lax.all_to_all(self_keys, "lvl", split_axis=1, concat_axis=0, tiled=True),
        lax.all_to_all(self_values, "lvl", split_axis=1, concat_axis=0, tiled=True),
    )
    head_mixed, log_total = self_forward(query_heads, key_heads, value_heads, score_scale)
    self_mixed = lax.all_to_all(head_mixed, "lvl", split_axis=0, concat_axis=1, tiled=True).reshape(
        rows, width
    )
    after_self = after_cross + matmul(self_mixed, self_output)
    hidden_norm, hidden_pull = jax.vjp(normed, after_self, hidden_gain, hidden_shift)
    hidden_in = to_half(hidden_norm)
    pre_act = matmul(hidden_in, hidden_expand)
    activated, act_pull = jax.vjp(jax.nn.gelu, pre_act)
    act_half = to_half(activated)
    updated = to_half(after_self + matmul(act_half, hidden_reduce))
    reduce_delta = left_outer(act_half, cotangent)
    act_delta = right_outer(cotangent, hidden_reduce)
    pre_delta = to_half(act_pull(act_delta)[0])
    expand_delta = left_outer(hidden_in, pre_delta)
    hidden_delta = right_outer(pre_delta, hidden_expand)
    self_side, hidden_gain_delta, hidden_shift_delta = hidden_pull(hidden_delta)
    after_self_delta = cotangent.astype(jnp.float32) + self_side
    self_gate = to_half(after_self_delta)
    self_output_delta = left_outer(self_mixed, self_gate)
    mixed_delta = to_half(right_outer(self_gate, self_output)).reshape(rows, H, head_size)
    head_delta = lax.all_to_all(mixed_delta, "lvl", split_axis=1, concat_axis=0, tiled=True)
    query_back, key_back, value_back = self_backward(
        query_heads, key_heads, value_heads, head_delta, log_total, score_scale
    )
    query_local, key_local, value_local = (
        lax.all_to_all(query_back, "lvl", split_axis=0, concat_axis=1, tiled=True),
        lax.all_to_all(key_back, "lvl", split_axis=0, concat_axis=1, tiled=True),
        lax.all_to_all(value_back, "lvl", split_axis=0, concat_axis=1, tiled=True),
    )
    query_local = query_local.reshape(rows, width)
    key_local = key_local.reshape(rows, width)
    value_local = value_local.reshape(rows, width)
    self_query_delta = left_outer(self_in, query_local)
    self_key_delta = left_outer(self_in, key_local)
    self_value_delta = left_outer(self_in, value_local)
    self_delta = (
        right_outer(query_local, self_query)
        + right_outer(key_local, self_key)
        + right_outer(value_local, self_value)
    )
    cross_side, self_gain_delta, self_shift_delta = self_pull(self_delta)
    after_cross_delta = after_self_delta + cross_side
    cross_gate = to_half(after_cross_delta)
    cross_output_delta = left_outer(cross_mixed, cross_gate)
    cross_delta = to_half(right_outer(cross_gate, cross_output)).reshape(
        groups, rows // groups, H, head_size
    )
    weight_delta = jnp.einsum(
        "gqhd,gkhd->ghqk", cross_delta, picked_values, preferred_element_type=jnp.float32
    )
    picked_value_delta = jnp.einsum(
        "ghqk,gqhd->gkhd", attention_half, cross_delta, preferred_element_type=jnp.float32
    )
    score_delta = to_half(
        attention * (weight_delta - jnp.sum(attention * weight_delta, axis=-1, keepdims=True))
    )
    cross_query_back = to_half(
        jnp.einsum("ghqk,gkhd->gqhd", score_delta, picked_keys, preferred_element_type=jnp.float32)
        * score_scale
    ).reshape(rows, width)
    picked_key_delta = (
        jnp.einsum(
            "ghqk,gqhd->gkhd", score_delta, cross_queries, preferred_element_type=jnp.float32
        )
        * score_scale
    )
    chosen = (
        neighbours.reshape(groups * reads)[:, None] == jnp.arange(groups, dtype=jnp.int32)[None, :]
    ).astype(jnp.float32)
    key_rows = picked_key_delta.reshape(groups * reads, block_rows * width)
    value_rows = picked_value_delta.reshape(groups * reads, block_rows * width)
    block_key_back = to_half(left_outer_exact(chosen, key_rows)).reshape(groups * block_rows, width)
    block_value_back = to_half(left_outer_exact(chosen, value_rows)).reshape(
        groups * block_rows, width
    )
    cross_query_delta = left_outer(latent_in, cross_query_back)
    cross_key_delta = left_outer(block_in, block_key_back)
    cross_value_delta = left_outer(block_in, block_value_back)
    block_side = right_outer(block_key_back, cross_key) + right_outer(block_value_back, cross_value)
    block_input_delta, block_gain_delta, block_shift_delta = block_pull(block_side)
    latent_side = right_outer(cross_query_back, cross_query)
    latent_input_delta, latent_gain_delta, latent_shift_delta = latent_pull(latent_side)
    latent_delta = to_half(after_cross_delta + latent_input_delta)
    block_delta = to_half(block_input_delta).reshape(groups, block_rows, width)
    summed = (
        lax.psum_scatter(latent_gain_delta, ("grp", "lvl"), scatter_dimension=0, tiled=True),
        lax.psum_scatter(latent_shift_delta, ("grp", "lvl"), scatter_dimension=0, tiled=True),
        lax.psum_scatter(block_gain_delta, ("grp", "lvl"), scatter_dimension=0, tiled=True),
        lax.psum_scatter(block_shift_delta, ("grp", "lvl"), scatter_dimension=0, tiled=True),
        lax.psum_scatter(cross_query_delta, ("grp", "lvl"), scatter_dimension=0, tiled=True),
        lax.psum_scatter(cross_key_delta, ("grp", "lvl"), scatter_dimension=0, tiled=True),
        lax.psum_scatter(cross_value_delta, ("grp", "lvl"), scatter_dimension=0, tiled=True),
        lax.psum_scatter(cross_output_delta, ("grp", "lvl"), scatter_dimension=0, tiled=True),
        lax.psum_scatter(self_gain_delta, ("grp", "lvl"), scatter_dimension=0, tiled=True),
        lax.psum_scatter(self_shift_delta, ("grp", "lvl"), scatter_dimension=0, tiled=True),
        lax.psum_scatter(self_query_delta, ("grp", "lvl"), scatter_dimension=0, tiled=True),
        lax.psum_scatter(self_key_delta, ("grp", "lvl"), scatter_dimension=0, tiled=True),
        lax.psum_scatter(self_value_delta, ("grp", "lvl"), scatter_dimension=0, tiled=True),
        lax.psum_scatter(self_output_delta, ("grp", "lvl"), scatter_dimension=0, tiled=True),
        lax.psum_scatter(hidden_gain_delta, ("grp", "lvl"), scatter_dimension=0, tiled=True),
        lax.psum_scatter(hidden_shift_delta, ("grp", "lvl"), scatter_dimension=0, tiled=True),
        lax.psum_scatter(expand_delta, ("grp", "lvl"), scatter_dimension=0, tiled=True),
        lax.psum_scatter(reduce_delta, ("grp", "lvl"), scatter_dimension=0, tiled=True),
    )
    return (
        updated,
        latent_delta,
        block_delta,
        summed[0],
        summed[1],
        summed[2],
        summed[3],
        summed[4],
        summed[5],
        summed[6],
        summed[7],
        summed[8],
        summed[9],
        summed[10],
        summed[11],
        summed[12],
        summed[13],
        summed[14],
        summed[15],
        summed[16],
        summed[17],
    )


def left_outer_exact(left_side, right_side):
    return lax.dot_general(
        left_side,
        right_side,
        (((0,), (0,)), ((), ())),
        precision=lax.Precision.HIGHEST,
        preferred_element_type=jnp.float32,
    )

def fits(shape, latents, hidden_expand):
    n_dev = shape["grp"] * shape["lvl"]
    return (
        shape["grp"] == 8
        and shape["lvl"] == 4
        and latents.shape[1] % (16 * n_dev) == 0
        and hidden_expand.shape[1] % (128 * n_dev) == 0
    )


def on_device(shape, *args):
    return (tiled if fits(shape, args[0], args[21]) else plain)(*args)


def solution(mesh):
    placed = (
        P(("grp", "lvl"), None),
        P(("grp", "lvl"), None, None),
        P(("grp", "lvl"), None),
        P(("grp", "lvl")),
        P(("grp", "lvl"), None),
        P(),
        P(),
        P(),
        P(),
        P(),
        P(),
        P(),
        P(),
        P(),
        P(),
        P(),
        P(),
        P(),
        P(),
        P(),
        P(),
        P(),
        P(),
    )
    return jax.shard_map(
        functools.partial(on_device, mesh.shape),
        mesh=mesh,
        in_specs=placed,
        out_specs=(
            P(("grp", "lvl"), None),
            P(("grp", "lvl"), None),
            P(("grp", "lvl"), None, None),
            P(("grp", "lvl")),
            P(("grp", "lvl")),
            P(("grp", "lvl")),
            P(("grp", "lvl")),
            P(("grp", "lvl"), None),
            P(("grp", "lvl"), None),
            P(("grp", "lvl"), None),
            P(("grp", "lvl"), None),
            P(("grp", "lvl")),
            P(("grp", "lvl")),
            P(("grp", "lvl"), None),
            P(("grp", "lvl"), None),
            P(("grp", "lvl"), None),
            P(("grp", "lvl"), None),
            P(("grp", "lvl")),
            P(("grp", "lvl")),
            P(("grp", "lvl"), None),
            P(("grp", "lvl"), None),
        ),
        check_vma=False,
    )
```

```python
import functools

import jax
import jax.numpy as jnp
from jax import lax
from jax.experimental import pallas as pl
from jax.experimental.pallas import tpu as pltpu
from jax.sharding import PartitionSpec as P

H = 8


EPS = 1e-05
NEG = -1e30
BF = jnp.bfloat16
F32 = jnp.float32
VMEM_MB = 30
V = True
LOG2_E = 1.4426950408889634
SQRT_2_PI = 0.7978845608028654
CUBIC = 0.044715


def nn(a, b):
    return lax.dot_general(a, b, (((1,), (0,)), ((), ())), preferred_element_type=F32)


def nt(a, b):
    return lax.dot_general(a, b, (((1,), (1,)), ((), ())), preferred_element_type=F32)


def tn(a, b):
    return lax.dot_general(a, b, (((0,), (0,)), ((), ())), preferred_element_type=F32)


def flip(v):
    return jnp.transpose(v)


def hat(v):
    center = v - jnp.mean(v, axis=-1, keepdims=True)
    scale = lax.rsqrt(jnp.mean(center * center, axis=-1, keepdims=True) + EPS)
    return center * scale, scale


def norm_back(dy, v, gain):
    unit, scale = hat(v)
    t = dy * gain
    side = scale * (
        t
        - jnp.mean(t, axis=-1, keepdims=True)
        - unit * jnp.mean(t * unit, axis=-1, keepdims=True)
    )
    return side, jnp.sum(dy * unit, axis=0, keepdims=True), jnp.sum(dy, axis=0, keepdims=True)


def gelu_parts(x):
    square = x * x
    t = jnp.tanh(SQRT_2_PI * x * (1.0 + CUBIC * square))
    half = 0.5 + 0.5 * t
    act = x * half
    slope = half + (0.5 * SQRT_2_PI) * x * (1.0 - t * t) * (1.0 + (3.0 * CUBIC) * square)
    return act, slope


def counts_by_row(nb, fill, rows, groups, block_rows, reads):
    keys = groups * block_rows
    key = lax.broadcasted_iota(jnp.int32, (rows, keys), 1)
    row = lax.broadcasted_iota(jnp.int32, (rows, keys), 0)
    per = rows // groups
    out = jnp.zeros((rows, keys), F32)
    for g in range(groups):
        for m in range(groups):
            times = jnp.int32(0)
            for n in range(reads):
                times = times + (nb[g, n] == m).astype(jnp.int32)
            live = (key >= m * block_rows) & (key < m * block_rows + fill[m])
            here = live & (row >= g * per) & (row < (g + 1) * per)
            out = jnp.where(here, times.astype(F32), out)
    return out


def counts_by_key(nb, fill, rows, groups, block_rows, reads):
    keys = groups * block_rows
    key = lax.broadcasted_iota(jnp.int32, (keys, rows), 0)
    row = lax.broadcasted_iota(jnp.int32, (keys, rows), 1)
    per = rows // groups
    out = jnp.zeros((keys, rows), F32)
    for g in range(groups):
        for m in range(groups):
            times = jnp.int32(0)
            for n in range(reads):
                times = times + (nb[g, n] == m).astype(jnp.int32)
            live = (key >= m * block_rows) & (key < m * block_rows + fill[m])
            here = live & (row >= g * per) & (row < (g + 1) * per)
            out = jnp.where(here, times.astype(F32), out)
    return out


def whole(shape):
    zeros = (0,) * len(shape)
    return pl.BlockSpec(shape, lambda i, *_: zeros)


def near_core(array):
    return pltpu.with_memory_space_constraint(array, pltpu.VMEM)


def far_off(array):
    return pltpu.with_memory_space_constraint(array, pltpu.HBM)


def call(kernel, name, grid, scalars, ins, outs, scratch, vmem=VMEM_MB, after=(), flops=1):
    first = len(scalars) + len(ins)

    def body(*refs):
        kernel(*refs[:first], *refs[first + len(after) :])

    arrays = [near_core(item[0]) if len(item) > 2 else far_off(item[0]) for item in ins]
    shapes = [(pltpu.VMEM if len(item) > 3 else pltpu.HBM)(item[0], item[1]) for item in outs]
    return pl.pallas_call(
        body,
        name=name,
        grid_spec=pltpu.PrefetchScalarGridSpec(
            num_scalar_prefetch=len(scalars),
            grid=(grid,),
            in_specs=[item[1] for item in ins] + [pl.BlockSpec(memory_space=pl.ANY)] * len(after),
            out_specs=[item[2] for item in outs],
            scratch_shapes=scratch,
        ),
        out_shape=shapes,
        compiler_params=pltpu.CompilerParams(
            vmem_limit_bytes=vmem * 1024 * 1024, dimension_semantics=("arbitrary",)
        ),
        cost_estimate=pl.CostEstimate(flops=flops, bytes_accessed=1, transcendentals=0),
    )(*scalars, *arrays, *after)


def tie(array, after):
    spec = pl.BlockSpec(memory_space=pl.ANY)
    array = near_core(array)
    return pl.pallas_call(
        lambda *refs: None,
        name="tie",
        in_specs=[spec] * (1 + len(after)),
        out_specs=spec,
        out_shape=pltpu.VMEM(array.shape, array.dtype),
        input_output_aliases={0: 0},
        compiler_params=pltpu.CompilerParams(vmem_limit_bytes=1024 * 1024),
        cost_estimate=pl.CostEstimate(flops=1, bytes_accessed=1, transcendentals=0),
    )(array, *after)


def cross_forward_kernel(
    groups, reads, nb, fill, lat, blk, lg, lb, bg, bb, sg, sb, wq, wk, wv, wo,
    cq, ck, cv, co, ac, self_in, lat_in, blk_in, acc, cnt,
):
    i = pl.program_id(0)
    rows, width = lat.shape
    keys = blk.shape[0]
    scale = (width // H) ** -0.5
    head = width // H

    @pl.when(i == 0)
    def _():
        lat_in[...] = (hat(lat[...].astype(F32))[0] * lg[...] + lb[...]).astype(BF)
        blk_in[...] = (hat(blk[...].astype(F32))[0] * bg[...] + bb[...]).astype(BF)
        acc[...] = lat[...].astype(F32)
        cnt[...] = counts_by_row(nb, fill, rows, groups, keys // groups, reads)

    q = nn(lat_in[...], wq[...]).astype(BF)
    k = nn(blk_in[...], wk[...]).astype(BF)
    v = nn(blk_in[...], wv[...]).astype(BF)
    cq[...] = q
    ck[...] = k
    cv[...] = v
    times = cnt[...]
    seen = times > 0.0
    mixed = []
    for h in range(q.shape[1] // head):
        cut = slice(h * head, (h + 1) * head)
        s = jnp.where(seen, nt(q[:, cut], k[:, cut]), NEG)
        e = jnp.exp2((s - jnp.max(s, axis=-1, keepdims=True)) * (scale * LOG2_E))
        total = jnp.sum(e * times, axis=-1, keepdims=True)
        p = (e * (1.0 / total)).astype(BF) * times.astype(BF)
        mixed.append(nn(p, v[:, cut]).astype(BF))
    mixed = jnp.concatenate(mixed, axis=1)
    co[...] = mixed
    acc[...] += nn(mixed, wo[...])

    @pl.when(i == pl.num_programs(0) - 1)
    def _():
        after = acc[...]
        ac[...] = after
        self_in[...] = (hat(after)[0] * sg[...] + sb[...]).astype(BF)


def flip_rows_kernel(plan, orders, *refs):
    n = 1 + max(src for src, _ in plan)
    ins, outs, tmp = refs[:n], refs[n : n + len(plan)], refs[n + len(plan) :]
    chunks = orders.shape[1]
    for src, t in zip(ins, tmp, strict=True):
        t[...] = flip(src[...])
    for dst, (src, which) in zip(outs, plan, strict=True):
        t = tmp[src]
        size = t.shape[0] // chunks
        for p in range(chunks):
            at = pl.multiple_of(orders[which, p] * size, size)
            dst[p * size : (p + 1) * size, :] = t[pl.ds(at, size), :]


def self_forward_kernel(ids, a0, a1, a2, a3, wq, wk, wv, q, k, v, o0, o1, o2):
    rows, width = a0.shape
    head = width // H
    scale = head**-0.5
    for j, a in enumerate((a0, a1, a2, a3)):
        here = slice(j * rows, (j + 1) * rows)
        x = a[...]
        q[here, :] = nn(x, wq[...]).astype(BF)
        k[here, :] = nn(x, wk[...]).astype(BF)
        v[here, :] = nn(x, wv[...]).astype(BF)
    for t in range(2):
        mixed = []
        for h in range(q.shape[1] // head):
            cut = slice(h * head, (h + 1) * head)
            s = nt(q[2 * t * rows : 2 * (t + 1) * rows, cut], k[:, cut])
            e = jnp.exp2((s - jnp.max(s, axis=-1, keepdims=True)) * (scale * LOG2_E))
            p = (e * (1.0 / jnp.sum(e, axis=-1, keepdims=True))).astype(BF)
            mixed.append(nn(p, v[:, cut]).astype(BF))
        mixed = jnp.concatenate(mixed, axis=1)
        if t == 0:
            o0[...] = mixed[:rows]
            o1[...] = mixed[rows:]
        else:
            o2[...] = mixed


def self_out_kernel(ids, ac, o0, o1, o2, o3, wo, hg, hb, after, hidden_in, so):
    cols = o0.shape[1]
    for j, o in enumerate((o0, o1, o2, o3)):
        at = pl.multiple_of((ids[1] ^ j) * cols, cols)
        so[:, pl.ds(at, cols)] = o[...]
    v = ac[...] + nn(so[...], wo[...])
    after[...] = v
    hidden_in[...] = (hat(v)[0] * hg[...] + hb[...]).astype(BF)


def cot_back_kernel(gy, wred, out):
    out[...] = nt(gy[...], wred[...])


def cot_units_kernel(ids, *refs):
    gs, wexp, wred = refs[:8], refs[8:12], refs[12:16]
    own, other, we, wr = refs[16:]
    unit = wexp[0].shape[1]
    for q in range(4):
        we[q * unit : (q + 1) * unit, :] = flip(wexp[q][...])
        wr[q * unit : (q + 1) * unit, :] = wred[q][...]
    rows = gs[0].shape[0]
    for k, g in enumerate(gs):
        out = own if k < 4 else other
        at = (k % 4) * rows
        out[:, at : at + rows] = nt(wr[...], g[...])


def ff_local_kernel(
    hidden_in, gy, after, hg, dact, wexp, wred, updated, gate, das, vecs, up, dh
):
    i = pl.program_id(0)

    @pl.when(i == 0)
    def _():
        up[...] = after[...]
        dh[...] = jnp.zeros_like(dh)

    act, slope = gelu_parts(nn(hidden_in[...], wexp[...]))
    up[...] += nn(act.astype(BF), wred[...])
    dh[...] += nt((dact[...] * slope).astype(BF), wexp[...])

    @pl.when(i == pl.num_programs(0) - 1)
    def _():
        updated[...] = up[...].astype(BF)
        side, dg, db = norm_back(dh[...], after[...], hg[...])
        total = gy[...].astype(F32) + side
        das[...] = total
        gate[...] = total.astype(BF)
        vecs[0:1, :] = dg
        vecs[1:2, :] = db


def ff_sums(we, dact, h, g, red, exp, fresh):
    act, slope = gelu_parts(nt(we[...], h))
    dpre = (dact * slope).astype(BF)
    if fresh:
        red[...] = nn(act.astype(BF), g)
        exp[...] = nn(dpre, h)
    else:
        red[...] += nn(act.astype(BF), g)
        exp[...] += nn(dpre, h)


def ff_tokens(refs, dact, we, red, exp, h_all, g_all, sem, fresh):
    hs, gs = refs[:4], refs[4:8]
    rows = hs[0].shape[0]
    copies = [
        pltpu.make_async_copy(piece, dst.at[pl.ds(k * rows, rows)], sem.at[which, k])
        for which, (src, dst) in enumerate(((hs, h_all), (gs, g_all)))
        for k, piece in enumerate(src)
    ]
    for c in copies:
        c.start()
    for t in range(2):
        for k in (2 * t, 2 * t + 1, 2 * t + 4, 2 * t + 5):
            copies[k].wait()
        here = slice(2 * t * rows, 2 * (t + 1) * rows)
        ff_sums(we, dact[:, here], h_all[here, :], g_all[here, :], red, exp, fresh and t == 0)


def ff_weights_a_kernel(*refs):
    dact, we, red, exp, h_all, g_all, sem = refs[8:]
    ff_tokens(refs, dact, we, red, exp, h_all, g_all, sem, True)


def ff_weights_b_kernel(ids, *refs):
    red_in, exp_in, dact, we, keep, send, red, exp, h_all, g_all, sem = refs[8:]
    red[...] = red_in[...]
    exp[...] = exp_in[...]
    ff_tokens(refs, dact, we, red, exp, h_all, g_all, sem, False)
    unit = we.shape[0] // 4
    half = 2 * unit
    width = red.shape[1]
    keep[:, 0:width] = red[0:half, :].astype(BF)
    send[:, 0:width] = red[half:, :].astype(BF)
    span = width // 8
    for p in range(4):
        out = keep if p < 2 else send
        low = (p % 2) * unit
        for q in range(4):
            for z in range(2):
                lanes = pl.ds(pl.multiple_of((ids[8 + p] + 2 * z) * span, span), span)
                to = pl.ds(pl.multiple_of(width + (2 * ids[12 + q] + z) * span, span), span)
                out[low : low + unit, to] = exp[q * unit : (q + 1) * unit, lanes].astype(BF)


def self_backward_kernel(
    ids, g0, g1, g2, g3, q, k, v, wo, wq, wk, wv, flipped, keep, send, do, dq, dk, dv
):
    rows, width = g0.shape
    head = width // H
    scale = head**-0.5
    for j, g in enumerate((g0, g1, g2, g3)):
        do[j * rows : (j + 1) * rows, :] = nt(g[...], wo[...]).astype(BF)
    cols = q.shape[1]
    tile = 512
    for h in range(cols // head):
        cut = slice(h * head, (h + 1) * head)
        kh = k[:, cut]
        vh = v[:, cut]
        kt = flip(kh)
        key_sum = jnp.zeros((k.shape[0], head), F32)
        value_sum = jnp.zeros((k.shape[0], head), F32)
        for t in range(q.shape[0] // tile):
            here = slice(t * tile, (t + 1) * tile)
            qt = q[here, cut]
            dt = do[here, cut]
            s = nt(kh, qt)
            e = jnp.exp2((s - jnp.max(s, axis=0, keepdims=True)) * (scale * LOG2_E))
            p = e * (1.0 / jnp.sum(e, axis=0, keepdims=True))
            dp = nt(vh, dt)
            ds = (p * (dp - jnp.sum(p * dp, axis=0, keepdims=True))).astype(BF)
            value_sum += nn(p.astype(BF), dt)
            key_sum += nn(ds, qt)
            back = (nn(kt, ds) * scale).astype(BF)
            flipped[cut, here] = back
            dq[here, cut] = flip(back)
        dk[:, cut] = (key_sum * scale).astype(BF)
        dv[:, cut] = value_sum.astype(BF)
    flipped[cols : 2 * cols, :] = flip(dk[...])
    flipped[2 * cols : 3 * cols, :] = flip(dv[...])
    for j in range(4):
        here = slice(j * rows, (j + 1) * rows)
        side = nt(dq[here, :], wq[...]) + nt(dk[here, :], wk[...]) + nt(dv[here, :], wv[...])
        out = send if j % 2 else keep
        low = (j // 2) * rows
        out[low : low + rows, :] = side.astype(BF)


def self_weights_kernel(ids, flipped, *refs):
    ins, gates, mixed = refs[0:4], refs[4:8], refs[8:12]
    keep, send, total = refs[12:]
    rows = ins[0].shape[0]
    three = flipped.shape[0]
    for low, high, parts in (
        (0, three, [(flipped[:, j * rows : (j + 1) * rows], ins[j][...]) for j in range(4)]),
        (three, total.shape[0], [(flip(gates[j][...]), mixed[j][...]) for j in range(4)]),
    ):
        acc = None
        for left, right in parts:
            part = nn(left, right)
            acc = part if acc is None else acc + part
        total[low:high, :] = acc
    depth, span = total.shape[0], keep.shape[1]
    blocks = total.shape[1] // span
    for p in range(blocks):
        out = keep if p < blocks // 2 else send
        low = (p % (blocks // 2)) * depth
        lanes = pl.ds(pl.multiple_of(ids[16 + p] * span, span), span)
        out[low : low + depth, :] = total[:, lanes].astype(BF)


def cross_backward_kernel(
    groups, reads, nb, fill, orders, keep, rcv, xr, das, ac, sg, wo, cq, ck, cv, wq, wk, wv, lat, blk, lg, bg, hv,
    gate, dq, dk, dv, dlat, dblk, vec_keep, vec_send, cnt, dac, la, ba, vecs, turned,
):
    i = pl.program_id(0)
    rows, width = das.shape
    keys = ck.shape[0]
    head = width // H
    scale = head**-0.5

    @pl.when(i == 0)
    def _():
        dy = keep[...].astype(F32) + rcv[...].astype(F32) + xr[...].astype(F32)
        side, dg, db = norm_back(dy, ac[...], sg[...])
        total = das[...] + side
        dac[...] = total
        gate[...] = total.astype(BF)
        vecs[...] = jnp.zeros_like(vecs)
        vecs[4:5, :] = dg
        vecs[5:6, :] = db
        vecs[6:8, :] = hv[...]
        la[...] = jnp.zeros_like(la)
        ba[...] = jnp.zeros_like(ba)
        cnt[...] = counts_by_key(nb, fill, rows, groups, keys // groups, reads)

    do = nt(gate[...], wo[...]).astype(BF)
    times = cnt[...]
    seen = times > 0.0
    for h in range(cq.shape[1] // head):
        cut = slice(h * head, (h + 1) * head)
        qh = cq[:, cut]
        kh = ck[:, cut]
        dh = do[:, cut]
        s = jnp.where(seen, nt(kh, qh), NEG)
        e = jnp.exp2((s - jnp.max(s, axis=0, keepdims=True)) * (scale * LOG2_E))
        p = e * (1.0 / jnp.sum(e * times, axis=0, keepdims=True))
        dp = nt(cv[:, cut], dh)
        delta = jnp.sum(p * dp * times, axis=0, keepdims=True)
        ds = (p * (dp - delta)).astype(BF) * times.astype(BF)
        dv[:, cut] = nn(p.astype(BF) * times.astype(BF), dh).astype(BF)
        dk[:, cut] = (nn(ds, qh) * scale).astype(BF)
        dq[:, cut] = flip((nn(flip(kh), ds) * scale).astype(BF))
    la[...] += nt(dq[...], wq[...])
    ba[...] += nt(dk[...], wk[...]) + nt(dv[...], wv[...])

    @pl.when(i == pl.num_programs(0) - 1)
    def _():
        side, dg, db = norm_back(la[...], lat[...].astype(F32), lg[...])
        dlat[...] = (dac[...] + side).astype(BF)
        vecs[0:1, :] = dg
        vecs[1:2, :] = db
        side, dg, db = norm_back(ba[...], blk[...].astype(F32), bg[...])
        dblk[...] = side.astype(BF)
        vecs[2:3, :] = dg
        vecs[3:4, :] = db
        turned[...] = flip(vecs[...])
        chunks = orders.shape[1]
        size = turned.shape[0] // chunks
        half = chunks // 2
        for p in range(chunks):
            at = pl.multiple_of(orders[2, p] * size, size)
            low = (p % half) * size
            out = vec_keep if p < half else vec_send
            out[low : low + size, :] = turned[pl.ds(at, size), :].astype(BF)


def cross_weights_kernel(parts, *refs):
    n = (len(refs) - len(parts) - 1) // 2
    lefts, rights, vecs, outs = refs[:n], refs[n : 2 * n], refs[2 * n], refs[2 * n + 1 :]
    for members, out in zip(parts, outs, strict=True):
        at = 0
        for m in members:
            r = nn(lefts[m][...], rights[m][...])
            out[:, at : at + r.shape[1]] = r.astype(BF)
            at += r.shape[1]
    out[:, at:] = vecs[...]


def combine_kernel(terms, *refs):
    total = sum(sum(parts) for parts in terms)
    ins, outs = refs[: 2 * total], refs[2 * total :]
    n = 0
    for k, parts in enumerate(terms):
        at = 0
        for count in parts:
            tops, lows = ins[n : n + 2 * count : 2], ins[n + 1 : n + 2 * count : 2]
            width = tops[0].shape[1]
            for out, refs_ in ((outs[2 * k], tops), (outs[2 * k + 1], lows)):
                acc = refs_[0][...].astype(F32)
                for ref in refs_[1:]:
                    acc = acc + ref[...].astype(F32)
                out[:, at : at + width] = acc.astype(BF)
            at += width
            n += 2 * count


def combine(name, chains, steps, after=()):
    ins, outs = [], []
    for parts in chains:
        depth = parts[0][0].shape[0]
        part = depth // 2 // steps
        for terms in parts:
            for a in terms:
                top = pl.BlockSpec((part, a.shape[1]), lambda i: (i, 0))
                low = pl.BlockSpec((part, a.shape[1]), lambda i: (i + steps, 0))
                ins += [(a, top, V), (a, low, V)]
        width = sum(terms[0].shape[1] for terms in parts)
        outs += [((depth // 2, width), BF, pl.BlockSpec((part, width), lambda i: (i, 0)), V)] * 2
    counts = tuple(tuple(len(terms) for terms in parts) for parts in chains)
    out = call(
        functools.partial(combine_kernel, counts), name, steps, [], ins, outs, [], after=after
    )
    return [tuple(out[2 * k : 2 * k + 2]) for k in range(len(chains))]


def copy_kernel(a, out):
    out[...] = a[...]


def add_kernel(a, b, out):
    out[...] = (a[...].astype(F32) + b[...].astype(F32)).astype(BF)


def pack_kernel(ff_kept, ff_got, set_kept, set_got, reduce_delta, out):
    unit, width = reduce_delta.shape
    reduce_delta[...] = ff_kept[:, 0:width].astype(F32) + ff_got[:, 0:width].astype(F32)
    rest = ff_kept[:, width:].astype(F32) + ff_got[:, width:].astype(F32)
    devices, chunk, _ = out.shape
    span = devices * chunk
    parts = width // span
    for q in range(parts):
        t = flip(rest[:, q * span : (q + 1) * span]).astype(BF)
        for d in range(devices):
            out[d, :, q * unit : (q + 1) * unit] = t[d * chunk : (d + 1) * chunk, :]
    t = flip(set_kept[...].astype(F32) + set_got[...].astype(F32)).astype(BF)
    n_set = t.shape[0] // chunk
    for d in range(devices):
        at = (d % n_set) * chunk
        out[d, :, parts * unit :] = t[at : at + chunk, :]


def place_kernel(unit, n_set, ids, got, expand, *outs):
    devices, _, width = got.shape
    parts = expand.shape[1] // (devices * unit)
    for q in range(parts):
        for d in range(devices):
            at = ((q // 2) * 2 * devices + (d // n_set) * devices + (q % 2) * n_set + d % n_set) * unit
            expand[:, at : at + unit] = got[d, :, q * unit : (q + 1) * unit].astype(F32)
    cols = (width - parts * unit) // len(outs)
    for d in range(n_set):
        mine = got[ids[3] * n_set + d]
        for m, out in enumerate(outs):
            at = parts * unit + m * cols
            out[:, d * cols : (d + 1) * cols] = mine[:, at : at + cols].astype(F32)


def cross_last_kernel(parts, n, *refs):
    ins, outs, vecs = refs[: 2 * n], refs[2 * n : 2 * n + 4], refs[2 * n + 4 :]
    done = [0] * len(outs)
    for chain, members in enumerate(parts):
        total = ins[2 * chain][...].astype(F32) + ins[2 * chain + 1][...].astype(F32)
        at = 0
        for which, cols in members:
            if which < len(outs):
                outs[which][:, done[which] : done[which] + cols] = total[:, at : at + cols]
                done[which] += cols
            else:
                t = flip(total[:, at : at + cols])
                for k, out in enumerate(vecs):
                    out[...] = t[k : k + 1, :]
            at += cols


def swap(values, axis, bit):
    size = lax.axis_size(axis)
    return lax.ppermute(values, axis, [(i, i ^ bit) for i in range(size)])


CORE = ("lvl", 1)
ACROSS = ("lvl", 2)
BESIDE = ("grp", 1)
NEAR = ("grp", 2)
FAR = ("grp", 4)


def gather_set(own, wait=lambda across: across):
    across = wait(swap(own, *ACROSS))
    return own, swap(own, *CORE), across, swap(across, *CORE)


def places(links, n_lvl):
    weights = [bit * (n_lvl if axis == "grp" else 1) for axis, bit in links]
    n = len(weights)
    return [
        sum(w for k, w in enumerate(weights) if p >> (n - 1 - k) & 1) for p in range(1 << n)
    ]


CHAINS = (
    (CORE, ACROSS, BESIDE, NEAR, FAR),
    (CORE, BESIDE, NEAR, ACROSS, FAR),
    (CORE, NEAR, ACROSS, FAR, BESIDE),
)


def tiled(
    latents, blocks, neighbours, fill, cotangent,
    latent_gain, latent_shift, block_gain, block_shift,
    cross_query, cross_key, cross_value, cross_output,
    self_gain, self_shift, self_query, self_key, self_value, self_output,
    hidden_gain, hidden_shift, hidden_expand, hidden_reduce,
):
    rows, width = latents.shape
    groups, block_rows, _ = blocks.shape
    keys = groups * block_rows
    reads = neighbours.shape[1]
    hidden = hidden_expand.shape[1]
    n_grp, n_lvl = lax.axis_size("grp"), lax.axis_size("lvl")
    n_dev = n_grp * n_lvl
    n_plane = 2 * n_lvl
    g = lax.axis_index("grp").astype(jnp.int32)
    l = lax.axis_index("lvl").astype(jnp.int32)
    me = g * n_lvl + l
    per = n_lvl
    steps = [0, FAR[1], BESIDE[1], FAR[1] | BESIDE[1]]
    bare = g & ~NEAR[1]
    ids = jnp.stack(
        [g, l, me, (g & NEAR[1]) // NEAR[1]]
        + [me ^ (p * per) for p in steps]
        + [bare ^ p for p in steps]
        + [((bare ^ p) // FAR[1]) * 2 + ((bare ^ p) & 1) for p in steps]
        + [g ^ p for p in (0, 4, 1, 5, 2, 6, 3, 7)]
    ).astype(jnp.int32)
    orders = jnp.array([places(links, n_lvl) for links in CHAINS], jnp.int32) ^ me
    unit = hidden // n_dev
    chunk = width // n_dev

    vec = lambda v: v.reshape(1, width)
    vspec = whole((1, width))
    blk = blocks.reshape(keys, width)
    pair = width // 4
    cols = pl.BlockSpec((width, pair), lambda i, *_: (0, i))
    rspec = pl.BlockSpec((pair, width), lambda i, *_: (i, 0))
    mine = pl.BlockSpec((width, pair), lambda i, ids: (0, ids[1]))
    mine_rows = pl.BlockSpec((pair, width), lambda i, ids: (ids[1], 0))
    row_full = whole((rows, width))
    key_full = whole((keys, width))
    row_part = pl.BlockSpec((rows, pair), lambda i, *_: (0, i))
    key_part = pl.BlockSpec((keys, pair), lambda i, *_: (0, i))
    set_rows = n_lvl * rows

    full = lambda a: whole(a.shape)
    cot_across, cot_near = swap(cotangent, *ACROSS), swap(cotangent, *NEAR)

    cq, ck, cv, co, after_cross, self_in, latent_in, block_in = call(
        functools.partial(cross_forward_kernel, groups, reads),
        "cross_forward", 4, [neighbours, fill],
        [(latents, row_full), (blk, key_full)]
        + [(vec(v), vspec) for v in (latent_gain, latent_shift, block_gain, block_shift, self_gain, self_shift)]
        + [(cross_query, cols), (cross_key, cols), (cross_value, cols), (cross_output, rspec)],
        [
            ((rows, width), BF, row_part), ((keys, width), BF, key_part),
            ((keys, width), BF, key_part), ((rows, width), BF, row_part),
            ((rows, width), F32, row_full), ((rows, width), BF, row_full, V),
            ((rows, width), BF, row_full), ((keys, width), BF, key_full),
        ],
        [pltpu.VMEM((rows, width), F32), pltpu.VMEM((rows, keys), F32)],
        after=[ids, orders],
    )

    set_of = lambda pieces: [(a, whole((rows, width)), V) for a in pieces]
    part = (set_rows, pair)
    plan = ((0, 0), (1, 1), (1, 2), (2, 0))
    sources = (latent_in, block_in, co)
    flips = call(
        functools.partial(flip_rows_kernel, plan), "flip_cross", 1, [orders],
        [(a, full(a)) for a in sources],
        [(sources[k].shape[::-1], BF, whole(sources[k].shape[::-1])) for k, _ in plan],
        [pltpu.VMEM(a.shape[::-1], BF) for a in sources],
    )
    cot_corner = swap(cot_across, *NEAR)
    (dact,) = call(
        cot_back_kernel, "cot_back", 4, [],
        [(cotangent, row_full), (hidden_reduce, pl.BlockSpec((hidden // 4, width), lambda i: (i, 0)))],
        [((rows, hidden), F32, pl.BlockSpec((rows, hidden // 4), lambda i: (0, i)), V)],
        [], after=[far_off(flips[0])],
    )
    self_in = tie(self_in, [cot_across, cot_near])
    set_in = gather_set(self_in, lambda across: tie(across, [dact]))
    q, k, v, o0, o1, o2 = call(
        self_forward_kernel, "self_forward", 1, [ids],
        set_of(set_in)
        + [(self_query, mine), (self_key, mine), (self_value, mine)],
        [(part, BF, whole(part))] * 3
        + [((rows, pair), BF, whole((rows, pair)), V)] * 2
        + [((2 * rows, pair), BF, whole((2 * rows, pair)), V)],
        [],
        after=[dact],
    )

    across = swap(tie(o2, [cot_corner]), *ACROSS)
    cots = [cotangent, cot_across, cot_near, cot_corner]
    cots_core = [swap(a, *CORE) for a in cots]
    own_cot = [cotangent, cot_across, cots_core[0], cots_core[1]]
    other_cot = [cot_near, cot_corner, cots_core[2], cots_core[3]]

    def unit_cols(p):
        return pl.BlockSpec((width, unit), lambda i, ids: (0, ids[4 + p]))

    def unit_rows(p):
        return pl.BlockSpec((unit, width), lambda i, ids: (ids[4 + p], 0))

    mine_units = (4 * unit, width)
    by_token = (4 * unit, set_rows)
    dact_own, dact_other, mine_expand = call(
        cot_units_kernel, "cot_units", 1, [ids],
        [(own_cot[0], row_full)] + [(a, row_full, V) for a in own_cot[1:] + other_cot]
        + [(hidden_expand, unit_cols(p)) for p in range(4)]
        + [(hidden_reduce, unit_rows(p)) for p in range(4)],
        [(by_token, F32, whole(by_token), V)] * 2 + [(mine_units, BF, whole(mine_units), V)],
        [pltpu.VMEM(mine_units, BF)], after=[o0],
    )
    second = pl.BlockSpec((rows, pair), lambda i: (1, 0))
    (across_next,) = call(
        copy_kernel, "pass", 1, [], [(across, second, V)], [((rows, pair), BF, whole((rows, pair)), V)], [],
        after=[mine_expand],
    )
    o_spec = whole((rows, pair))
    pieces = (o0, swap(o1, *CORE), across, swap(across_next, *CORE))
    after_self, hidden_in, so = call(
        self_out_kernel, "self_out", 1, [ids],
        [(after_cross, row_full)] + [(p, o_spec, V) for p in pieces]
        + [(self_output, whole((width, width))), (vec(hidden_gain), vspec), (vec(hidden_shift), vspec)],
        [((rows, width), F32, row_full, V), ((rows, width), BF, row_full, V), ((rows, width), BF, row_full, V)],
        [], after=[mine_expand],
    )

    hid_across, hid_near = swap(hidden_in, *ACROSS), swap(hidden_in, *NEAR)
    step = 512
    updated, gate, after_self_delta, hidden_vecs = call(
        ff_local_kernel, "ff_local", hidden // step, [],
        [
            (hidden_in, row_full, V), (cotangent, row_full), (after_self, row_full, V), (vec(hidden_gain), vspec),
            (dact, pl.BlockSpec((rows, step), lambda i: (0, i)), V),
            (hidden_expand, pl.BlockSpec((width, step), lambda i: (0, i))),
            (hidden_reduce, pl.BlockSpec((step, width), lambda i: (i, 0))),
        ],
        [
            ((rows, width), BF, row_full), ((rows, width), BF, row_full, V),
            ((rows, width), F32, row_full), ((2, width), F32, whole((2, width))),
        ],
        [pltpu.VMEM((rows, width), F32)] * 2,
    )
    gate = tie(gate, [hid_across, hid_near])
    hid_across = tie(hid_across, [gate])
    hid_corner = swap(hid_across, *NEAR)

    any_spec = pl.BlockSpec(memory_space=pl.ANY)

    own_hid = [hidden_in, hid_across, swap(hidden_in, *CORE), swap(hid_across, *CORE)]
    copied = [
        pltpu.VMEM((set_rows, width), BF), pltpu.VMEM((set_rows, width), BF), pltpu.SemaphoreType.DMA((2, 4)),
    ]
    ff_part = call(
        ff_weights_a_kernel, "ff_weights_a", 1, [],
        [(a, any_spec, V) for a in own_hid] + [(own_cot[0], any_spec)] + [(a, any_spec, V) for a in own_cot[1:]]
        + [(a, full(a), V) for a in (dact_own, mine_expand)],
        [(mine_units, F32, whole(mine_units), V)] * 2, copied, after=[gate],
    )

    gate_all = gather_set(gate, lambda across: tie(across, [ff_part[0], hid_corner]))
    flipped, self_keep, self_send = call(
        self_backward_kernel, "self_backward", 1, [ids],
        set_of(gate_all) + [(a, whole(part)) for a in (q, k, v)]
        + [(self_output, mine_rows), (self_query, mine), (self_key, mine), (self_value, mine)],
        [((3 * pair, set_rows), BF, whole((3 * pair, set_rows)))]
        + [((2 * rows, width), BF, whole((2 * rows, width)), V)] * 2,
        [pltpu.VMEM(part, BF)] * 4,
    )
    so = tie(so, [gate_all[2]])
    so_across = swap(so, *ACROSS)
    self_send = tie(self_send, [so_across])
    self_got = swap(self_send, *CORE)
    so_all = (so, swap(so, *CORE), so_across, swap(so_across, *CORE))
    lower = pl.BlockSpec((rows // 2, width), lambda i: (i + 2, 0))
    (self_pass,) = call(
        add_kernel, "self_pass", 2, [], [(self_keep, lower, V), (self_got, lower, V)],
        [((rows, width), BF, pl.BlockSpec((rows // 2, width), lambda i: (i, 0)), V)],
        [],
    )
    self_across = swap(self_pass, *ACROSS)

    other_hid = [hid_near, hid_corner, swap(hid_near, *CORE), swap(hid_corner, *CORE)]
    half = (2 * unit, 2 * width)
    ff_keep, ff_send = call(
        ff_weights_b_kernel, "ff_weights_b", 1, [ids],
        [(a, any_spec, V) for a in other_hid + other_cot] + [(a, full(a), V) for a in (*ff_part, dact_other, mine_expand)],
        [(half, BF, whole(half), V)] * 2,
        [pltpu.VMEM(mine_units, F32)] * 2 + copied, after=[self_pass],
    )
    ff_got = swap(ff_send, *BESIDE)

    span = width // n_grp
    stack = (n_grp // 2 * 4 * pair, span)
    stack_keep, stack_send = call(
        self_weights_kernel, "self_weights", 1, [ids],
        [(flipped, full(flipped))] + set_of(set_in)
        + [(a, pl.BlockSpec((rows, pair), lambda i, ids: (0, ids[1])), V) for a in gate_all]
        + set_of(so_all),
        [(stack, BF, whole(stack), V)] * 2,
        [pltpu.VMEM((4 * pair, width), F32)],
        after=[ff_send],
    )
    stack_send = tie(stack_send, [self_across])
    stack_got = swap(stack_send, *NEAR)

    half_rows = pl.BlockSpec((rows, width), lambda i, *_: (0, 0))
    marks = 128
    halved = (width // 2, marks)
    cross_gate, dcq, dck, dcv, latent_delta, block_delta, vec_keep, vec_send = call(
        functools.partial(cross_backward_kernel, groups, reads),
        "cross_backward", 4, [neighbours, fill, orders],
        [
            (self_keep, half_rows, V), (self_got, half_rows, V), (self_across, row_full, V),
            (after_self_delta, row_full), (after_cross, row_full), (vec(self_gain), vspec),
            (cross_output, rspec), (cq, row_part), (ck, key_part), (cv, key_part),
            (cross_query, cols), (cross_key, cols), (cross_value, cols),
            (latents, row_full), (blk, key_full), (vec(latent_gain), vspec), (vec(block_gain), vspec),
            (hidden_vecs, full(hidden_vecs)),
        ],
        [
            ((rows, width), BF, row_full, V),
            ((rows, width), BF, row_part, V), ((keys, width), BF, key_part, V), ((keys, width), BF, key_part, V),
            ((rows, width), BF, row_full), ((keys, width), BF, key_full),
        ]
        + [(halved, BF, whole(halved), V)] * 2,
        [
            pltpu.VMEM((keys, rows), F32), pltpu.VMEM((rows, width), F32), pltpu.VMEM((rows, width), F32),
            pltpu.VMEM((keys, width), F32), pltpu.VMEM((marks, width), F32), pltpu.VMEM((width, marks), F32),
        ],
        after=[stack_send, ff_send],
    )

    lefts = (flips[0], flips[3], flips[1], flips[2])
    rights = [(dcq, full(dcq), V), (cross_gate, full(cross_gate), V), (dck, full(dck), V), (dcv, full(dcv), V)]
    tile = width // 4
    def halves(name, first, vecs):
        return call(
            functools.partial(cross_weights_kernel, ((0, 1), (2,), (3,))), name, 2, [],
            [(a, pl.BlockSpec((tile, a.shape[1]), lambda i: (i + first, 0))) for a in lefts] + rights
            + [(vecs, pl.BlockSpec((tile, marks), lambda i: (i, 0)), V)],
            [
                ((width // 2, n), BF, pl.BlockSpec((tile, n), lambda i: (i, 0)), V)
                for n in (2 * width, width, width + marks)
            ],
            [],
        )

    sent = halves("cross_weights_sent", 2, tie(vec_send, [ff_got, stack_got]))
    got = [swap(a, *CORE) for a in sent]
    kept = halves("cross_weights_kept", 0, tie(vec_keep, [sent[0]]))
    ((ff_keep, ff_send),) = combine("ff_sum", [[(ff_keep, ff_got)]], 1, after=[kept[0]])
    ff_got = swap(ff_send, *FAR)
    ((stack_keep, stack_send),) = combine("self_sum_near", [[(stack_keep, stack_got)]], 2, after=[ff_send])
    stack_got = swap(stack_send, *BESIDE)

    pairs = combine("cross_sum_core", [[p] for p in zip(kept, got)], 4, after=[stack_send, ff_send])
    got = [swap(send, *CHAINS[n][1]) for n, (_, send) in enumerate(pairs)]

    ((stack_keep, stack_send),) = combine("self_sum_y", [[(stack_keep, stack_got)]], 2, after=[pairs[0][1]])
    stack_got = swap(stack_send, *FAR)
    last = [stack_send, ff_got]
    for stage in (2, 3, 4):
        chains = [[(kept, a)] for (kept, _), a in zip(pairs, got)]
        pairs = combine(f"cross_sum_{stage}", chains, 1, after=last)
        got = [swap(send, *CHAINS[n][stage]) for n, (_, send) in enumerate(pairs)]
        last = [pairs[0][1]]
        if stage == 3:
            piece = (unit, width)
            mixed = (n_plane, chunk, 4 * unit + 4 * pair)
            reduce_delta, turned = call(
                pack_kernel, "pack", 1, [],
                [(a, full(a), V) for a in (ff_keep, ff_got, stack_keep, stack_got)],
                [(piece, F32, whole(piece)), (mixed, BF, whole(mixed), V)],
                [], after=last,
            )
            last = [turned]
        if stage == 4:
            planes = [
                [(d ^ z) * n_lvl + k for z in (0, NEAR[1]) for k in range(n_lvl)]
                for d in range(n_grp)
                if not d & NEAR[1]
            ]
            got_all = lax.all_to_all(
                tie(turned, [pairs[0][1]]), ("grp", "lvl"), split_axis=0, concat_axis=0, axis_index_groups=planes, tiled=True
            )
    members = (((0, width), (3, width)), ((1, width),), ((2, width), (4, marks)))
    ins = []
    for (kept, _), a in zip(pairs, got):
        ins += [(kept, full(kept), V), (a, full(a), V)]
    last = call(
        functools.partial(cross_last_kernel, members, 3), "cross_last", 1, [], ins,
        [((chunk, width), F32, whole((chunk, width)))] * 4 + [((1, chunk), F32, whole((1, chunk)))] * 8,
        [], flops=5 * 10**9,
    )
    placed = call(
        functools.partial(place_kernel, unit, n_lvl), "place", 1, [ids], [(got_all, full(got_all), V)],
        [((chunk, hidden), F32, whole((chunk, hidden)))] + [((chunk, width), F32, whole((chunk, width)))] * 4,
        [],
    )
    vecs = [a.reshape(chunk) for a in last[4:]]

    return (
        updated, latent_delta, block_delta.reshape(groups, block_rows, width),
        vecs[0], vecs[1], vecs[2], vecs[3],
        last[0], last[1], last[2], last[3],
        vecs[4], vecs[5],
        placed[1], placed[2], placed[3], placed[4],
        vecs[6], vecs[7],
        placed[0], reduce_delta,
    )


def normed(values, norm_gain, norm_shift):
    center = values - jnp.mean(values, axis=-1, keepdims=True)
    spread = jnp.mean(center * center, axis=-1, keepdims=True)
    return center * lax.rsqrt(spread + EPS) * norm_gain + norm_shift


def to_half(values):
    return values.astype(jnp.bfloat16)


def matmul(left_side, right_side):
    return jnp.dot(left_side, right_side, preferred_element_type=jnp.float32)


def left_outer(left_side, right_side):
    return lax.dot_general(
        left_side, right_side, (((0,), (0,)), ((), ())), preferred_element_type=jnp.float32
    )


def right_outer(left_side, right_side):
    return lax.dot_general(
        left_side, right_side, (((1,), (1,)), ((), ())), preferred_element_type=jnp.float32
    )


def self_forward(query_heads, key_heads, value_heads, score_scale):
    length, local_heads, head_size = query_heads.shape
    block_rows = min(512, length)
    query_blocks = query_heads.reshape(length // block_rows, block_rows, local_heads, head_size)

    def one_block(query_block):
        scores = (
            jnp.einsum("qhd,khd->hqk", query_block, key_heads, preferred_element_type=jnp.float32)
            * score_scale
        )
        row_top = jnp.max(scores, axis=-1, keepdims=True)
        raised = jnp.exp(scores - row_top)
        row_total = jnp.sum(raised, axis=-1, keepdims=True)
        attention = raised / row_total
        mixture = jnp.einsum(
            "hqk,khd->qhd", to_half(attention), value_heads, preferred_element_type=jnp.float32
        )
        return (to_half(mixture), row_top + jnp.log(row_total))

    mixture, log_total = lax.map(one_block, query_blocks)
    return (mixture.reshape(length, local_heads, head_size), log_total)


def self_backward(query_heads, key_heads, value_heads, mixed_delta, log_total, score_scale):
    length, local_heads, head_size = query_heads.shape
    block_rows = min(512, length)
    query_blocks = query_heads.reshape(length // block_rows, block_rows, local_heads, head_size)
    delta_blocks = mixed_delta.reshape(length // block_rows, block_rows, local_heads, head_size)

    def one_block(running, pieces):
        key_sum, value_sum = running
        query_block, delta_block, log_block = pieces
        scores = (
            jnp.einsum("qhd,khd->hqk", query_block, key_heads, preferred_element_type=jnp.float32)
            * score_scale
        )
        attention = jnp.exp(scores - log_block)
        value_sum = value_sum + jnp.einsum(
            "hqk,qhd->khd", to_half(attention), delta_block, preferred_element_type=jnp.float32
        )
        weight_delta = jnp.einsum(
            "qhd,khd->hqk", delta_block, value_heads, preferred_element_type=jnp.float32
        )
        score_delta = to_half(
            attention * (weight_delta - jnp.sum(attention * weight_delta, axis=-1, keepdims=True))
        )
        query_delta = to_half(
            jnp.einsum("hqk,khd->qhd", score_delta, key_heads, preferred_element_type=jnp.float32)
            * score_scale
        )
        key_sum = (
            key_sum
            + jnp.einsum(
                "hqk,qhd->khd", score_delta, query_block, preferred_element_type=jnp.float32
            )
            * score_scale
        )
        return ((key_sum, value_sum), query_delta)

    zero_start = jnp.zeros(key_heads.shape, jnp.float32)
    (key_sum, value_sum), query_delta = lax.scan(
        one_block, (zero_start, zero_start), (query_blocks, delta_blocks, log_total)
    )
    return (
        query_delta.reshape(length, local_heads, head_size),
        to_half(key_sum),
        to_half(value_sum),
    )


def cross_forward(cross_queries, block_keys, block_values, neighbours, fill, score_scale):
    groups, latent_rows, head_count, head_size = cross_queries.shape
    block_rows = block_keys.shape[1]
    reads = neighbours.shape[1]
    picked_keys = block_keys[neighbours].reshape(groups, reads * block_rows, head_count, head_size)
    picked_values = block_values[neighbours].reshape(
        groups, reads * block_rows, head_count, head_size
    )
    positions = jnp.arange(block_rows, dtype=jnp.int32)
    live_keys = (positions[None, None, :] < fill[neighbours][:, :, None]).reshape(
        groups, reads * block_rows
    )
    scores = (
        jnp.einsum(
            "gqhd,gkhd->ghqk", cross_queries, picked_keys, preferred_element_type=jnp.float32
        )
        * score_scale
    )
    scores = jnp.where(live_keys[:, None, None, :], scores, NEG)
    attention = jax.nn.softmax(scores, axis=-1)
    return (attention, picked_keys, picked_values)


def plain(
    latents,
    blocks,
    neighbours,
    fill,
    cotangent,
    latent_gain,
    latent_shift,
    block_gain,
    block_shift,
    cross_query,
    cross_key,
    cross_value,
    cross_output,
    self_gain,
    self_shift,
    self_query,
    self_key,
    self_value,
    self_output,
    hidden_gain,
    hidden_shift,
    hidden_expand,
    hidden_reduce,
):
    rows = latents.shape[0]
    width = latents.shape[1]
    groups = blocks.shape[0]
    block_rows = blocks.shape[1]
    reads = neighbours.shape[1]
    head_size = width // H
    score_scale = head_size ** (-0.5)
    latent_float = latents.astype(jnp.float32)
    latent_norm, latent_pull = jax.vjp(normed, latent_float, latent_gain, latent_shift)
    latent_in = to_half(latent_norm)
    block_float = blocks.reshape(groups * block_rows, width).astype(jnp.float32)
    block_norm, block_pull = jax.vjp(normed, block_float, block_gain, block_shift)
    block_in = to_half(block_norm)
    cross_queries = to_half(matmul(latent_in, cross_query)).reshape(
        groups, rows // groups, H, head_size
    )
    block_keys = to_half(matmul(block_in, cross_key)).reshape(groups, block_rows, H, head_size)
    block_values = to_half(matmul(block_in, cross_value)).reshape(groups, block_rows, H, head_size)
    attention, picked_keys, picked_values = cross_forward(
        cross_queries, block_keys, block_values, neighbours, fill, score_scale
    )
    attention_half = to_half(attention)
    cross_mixed = to_half(
        jnp.einsum(
            "ghqk,gkhd->gqhd", attention_half, picked_values, preferred_element_type=jnp.float32
        )
    ).reshape(rows, width)
    after_cross = latent_float + matmul(cross_mixed, cross_output)
    self_norm, self_pull = jax.vjp(normed, after_cross, self_gain, self_shift)
    self_in = to_half(self_norm)
    self_queries = to_half(matmul(self_in, self_query)).reshape(rows, H, head_size)
    self_keys = to_half(matmul(self_in, self_key)).reshape(rows, H, head_size)
    self_values = to_half(matmul(self_in, self_value)).reshape(rows, H, head_size)
    query_heads, key_heads, value_heads = (
        lax.all_to_all(self_queries, "lvl", split_axis=1, concat_axis=0, tiled=True),
        lax.all_to_all(self_keys, "lvl", split_axis=1, concat_axis=0, tiled=True),
        lax.all_to_all(self_values, "lvl", split_axis=1, concat_axis=0, tiled=True),
    )
    head_mixed, log_total = self_forward(query_heads, key_heads, value_heads, score_scale)
    self_mixed = lax.all_to_all(head_mixed, "lvl", split_axis=0, concat_axis=1, tiled=True).reshape(
        rows, width
    )
    after_self = after_cross + matmul(self_mixed, self_output)
    hidden_norm, hidden_pull = jax.vjp(normed, after_self, hidden_gain, hidden_shift)
    hidden_in = to_half(hidden_norm)
    pre_act = matmul(hidden_in, hidden_expand)
    activated, act_pull = jax.vjp(jax.nn.gelu, pre_act)
    act_half = to_half(activated)
    updated = to_half(after_self + matmul(act_half, hidden_reduce))
    reduce_delta = left_outer(act_half, cotangent)
    act_delta = right_outer(cotangent, hidden_reduce)
    pre_delta = to_half(act_pull(act_delta)[0])
    expand_delta = left_outer(hidden_in, pre_delta)
    hidden_delta = right_outer(pre_delta, hidden_expand)
    self_side, hidden_gain_delta, hidden_shift_delta = hidden_pull(hidden_delta)
    after_self_delta = cotangent.astype(jnp.float32) + self_side
    self_gate = to_half(after_self_delta)
    self_output_delta = left_outer(self_mixed, self_gate)
    mixed_delta = to_half(right_outer(self_gate, self_output)).reshape(rows, H, head_size)
    head_delta = lax.all_to_all(mixed_delta, "lvl", split_axis=1, concat_axis=0, tiled=True)
    query_back, key_back, value_back = self_backward(
        query_heads, key_heads, value_heads, head_delta, log_total, score_scale
    )
    query_local, key_local, value_local = (
        lax.all_to_all(query_back, "lvl", split_axis=0, concat_axis=1, tiled=True),
        lax.all_to_all(key_back, "lvl", split_axis=0, concat_axis=1, tiled=True),
        lax.all_to_all(value_back, "lvl", split_axis=0, concat_axis=1, tiled=True),
    )
    query_local = query_local.reshape(rows, width)
    key_local = key_local.reshape(rows, width)
    value_local = value_local.reshape(rows, width)
    self_query_delta = left_outer(self_in, query_local)
    self_key_delta = left_outer(self_in, key_local)
    self_value_delta = left_outer(self_in, value_local)
    self_delta = (
        right_outer(query_local, self_query)
        + right_outer(key_local, self_key)
        + right_outer(value_local, self_value)
    )
    cross_side, self_gain_delta, self_shift_delta = self_pull(self_delta)
    after_cross_delta = after_self_delta + cross_side
    cross_gate = to_half(after_cross_delta)
    cross_output_delta = left_outer(cross_mixed, cross_gate)
    cross_delta = to_half(right_outer(cross_gate, cross_output)).reshape(
        groups, rows // groups, H, head_size
    )
    weight_delta = jnp.einsum(
        "gqhd,gkhd->ghqk", cross_delta, picked_values, preferred_element_type=jnp.float32
    )
    picked_value_delta = jnp.einsum(
        "ghqk,gqhd->gkhd", attention_half, cross_delta, preferred_element_type=jnp.float32
    )
    score_delta = to_half(
        attention * (weight_delta - jnp.sum(attention * weight_delta, axis=-1, keepdims=True))
    )
    cross_query_back = to_half(
        jnp.einsum("ghqk,gkhd->gqhd", score_delta, picked_keys, preferred_element_type=jnp.float32)
        * score_scale
    ).reshape(rows, width)
    picked_key_delta = (
        jnp.einsum(
            "ghqk,gqhd->gkhd", score_delta, cross_queries, preferred_element_type=jnp.float32
        )
        * score_scale
    )
    chosen = (
        neighbours.reshape(groups * reads)[:, None] == jnp.arange(groups, dtype=jnp.int32)[None, :]
    ).astype(jnp.float32)
    key_rows = picked_key_delta.reshape(groups * reads, block_rows * width)
    value_rows = picked_value_delta.reshape(groups * reads, block_rows * width)
    block_key_back = to_half(left_outer_exact(chosen, key_rows)).reshape(groups * block_rows, width)
    block_value_back = to_half(left_outer_exact(chosen, value_rows)).reshape(
        groups * block_rows, width
    )
    cross_query_delta = left_outer(latent_in, cross_query_back)
    cross_key_delta = left_outer(block_in, block_key_back)
    cross_value_delta = left_outer(block_in, block_value_back)
    block_side = right_outer(block_key_back, cross_key) + right_outer(block_value_back, cross_value)
    block_input_delta, block_gain_delta, block_shift_delta = block_pull(block_side)
    latent_side = right_outer(cross_query_back, cross_query)
    latent_input_delta, latent_gain_delta, latent_shift_delta = latent_pull(latent_side)
    latent_delta = to_half(after_cross_delta + latent_input_delta)
    block_delta = to_half(block_input_delta).reshape(groups, block_rows, width)
    summed = (
        lax.psum_scatter(latent_gain_delta, ("grp", "lvl"), scatter_dimension=0, tiled=True),
        lax.psum_scatter(latent_shift_delta, ("grp", "lvl"), scatter_dimension=0, tiled=True),
        lax.psum_scatter(block_gain_delta, ("grp", "lvl"), scatter_dimension=0, tiled=True),
        lax.psum_scatter(block_shift_delta, ("grp", "lvl"), scatter_dimension=0, tiled=True),
        lax.psum_scatter(cross_query_delta, ("grp", "lvl"), scatter_dimension=0, tiled=True),
        lax.psum_scatter(cross_key_delta, ("grp", "lvl"), scatter_dimension=0, tiled=True),
        lax.psum_scatter(cross_value_delta, ("grp", "lvl"), scatter_dimension=0, tiled=True),
        lax.psum_scatter(cross_output_delta, ("grp", "lvl"), scatter_dimension=0, tiled=True),
        lax.psum_scatter(self_gain_delta, ("grp", "lvl"), scatter_dimension=0, tiled=True),
        lax.psum_scatter(self_shift_delta, ("grp", "lvl"), scatter_dimension=0, tiled=True),
        lax.psum_scatter(self_query_delta, ("grp", "lvl"), scatter_dimension=0, tiled=True),
        lax.psum_scatter(self_key_delta, ("grp", "lvl"), scatter_dimension=0, tiled=True),
        lax.psum_scatter(self_value_delta, ("grp", "lvl"), scatter_dimension=0, tiled=True),
        lax.psum_scatter(self_output_delta, ("grp", "lvl"), scatter_dimension=0, tiled=True),
        lax.psum_scatter(hidden_gain_delta, ("grp", "lvl"), scatter_dimension=0, tiled=True),
        lax.psum_scatter(hidden_shift_delta, ("grp", "lvl"), scatter_dimension=0, tiled=True),
        lax.psum_scatter(expand_delta, ("grp", "lvl"), scatter_dimension=0, tiled=True),
        lax.psum_scatter(reduce_delta, ("grp", "lvl"), scatter_dimension=0, tiled=True),
    )
    return (
        updated,
        latent_delta,
        block_delta,
        summed[0],
        summed[1],
        summed[2],
        summed[3],
        summed[4],
        summed[5],
        summed[6],
        summed[7],
        summed[8],
        summed[9],
        summed[10],
        summed[11],
        summed[12],
        summed[13],
        summed[14],
        summed[15],
        summed[16],
        summed[17],
    )


def left_outer_exact(left_side, right_side):
    return lax.dot_general(
        left_side,
        right_side,
        (((0,), (0,)), ((), ())),
        precision=lax.Precision.HIGHEST,
        preferred_element_type=jnp.float32,
    )

def fits(shape, latents, hidden_expand):
    n_dev = shape["grp"] * shape["lvl"]
    return (
        shape["grp"] == 8
        and shape["lvl"] == 4
        and latents.shape[1] % (16 * n_dev) == 0
        and hidden_expand.shape[1] % (128 * n_dev) == 0
    )


def on_device(shape, *args):
    return (tiled if fits(shape, args[0], args[21]) else plain)(*args)


def solution(mesh):
    placed = (
        P(("grp", "lvl"), None),
        P(("grp", "lvl"), None, None),
        P(("grp", "lvl"), None),
        P(("grp", "lvl")),
        P(("grp", "lvl"), None),
        P(),
        P(),
        P(),
        P(),
        P(),
        P(),
        P(),
        P(),
        P(),
        P(),
        P(),
        P(),
        P(),
        P(),
        P(),
        P(),
        P(),
        P(),
    )
    return jax.shard_map(
        functools.partial(on_device, mesh.shape),
        mesh=mesh,
        in_specs=placed,
        out_specs=(
            P(("grp", "lvl"), None),
            P(("grp", "lvl"), None),
            P(("grp", "lvl"), None, None),
            P(("grp", "lvl")),
            P(("grp", "lvl")),
            P(("grp", "lvl")),
            P(("grp", "lvl")),
            P(("grp", "lvl"), None),
            P(("grp", "lvl"), None),
            P(("grp", "lvl"), None),
            P(("grp", "lvl"), None),
            P(("grp", "lvl")),
            P(("grp", "lvl")),
            P(("grp", "lvl"), None),
            P(("grp", "lvl"), None),
            P(("grp", "lvl"), None),
            P(("grp", "lvl"), None),
            P(("grp", "lvl")),
            P(("grp", "lvl")),
            P(("grp", "lvl"), None),
            P(("grp", "lvl"), None),
        ),
        check_vma=False,
    )
```

```python
import functools

import jax
import jax.numpy as jnp
from jax import lax
from jax.experimental import pallas as pl
from jax.experimental.pallas import tpu as pltpu
from jax.sharding import PartitionSpec as P

H = 8


EPS = 1e-05
NEG = -1e30
BF = jnp.bfloat16
F32 = jnp.float32
VMEM_MB = 30
V = True
LOG2_E = 1.4426950408889634
SQRT_2_PI = 0.7978845608028654
CUBIC = 0.044715


def count_bias(times):
    return jnp.where(times > 0.0, jnp.log(jnp.maximum(times, 1.0)) * LOG2_E, NEG)


def nn(a, b):
    return lax.dot_general(a, b, (((1,), (0,)), ((), ())), preferred_element_type=F32)


def nt(a, b):
    return lax.dot_general(a, b, (((1,), (1,)), ((), ())), preferred_element_type=F32)


def tn(a, b):
    return lax.dot_general(a, b, (((0,), (0,)), ((), ())), preferred_element_type=F32)


def flip(v):
    return jnp.transpose(v)


def hat(v):
    center = v - jnp.mean(v, axis=-1, keepdims=True)
    scale = lax.rsqrt(jnp.mean(center * center, axis=-1, keepdims=True) + EPS)
    return center * scale, scale


def norm_back(dy, v, gain):
    unit, scale = hat(v)
    t = dy * gain
    side = scale * (
        t
        - jnp.mean(t, axis=-1, keepdims=True)
        - unit * jnp.mean(t * unit, axis=-1, keepdims=True)
    )
    return side, jnp.sum(dy * unit, axis=0, keepdims=True), jnp.sum(dy, axis=0, keepdims=True)


def gelu_parts(x):
    square = x * x
    t = jnp.tanh(SQRT_2_PI * x * (1.0 + CUBIC * square))
    half = 0.5 + 0.5 * t
    act = x * half
    slope = half + (0.5 * SQRT_2_PI) * x * (1.0 - t * t) * (1.0 + (3.0 * CUBIC) * square)
    return act, slope


def counts_by_row(nb, fill, rows, groups, block_rows, reads):
    keys = groups * block_rows
    key = lax.broadcasted_iota(jnp.int32, (rows, keys), 1)
    row = lax.broadcasted_iota(jnp.int32, (rows, keys), 0)
    per = rows // groups
    out = jnp.zeros((rows, keys), F32)
    for g in range(groups):
        for m in range(groups):
            times = jnp.int32(0)
            for n in range(reads):
                times = times + (nb[g, n] == m).astype(jnp.int32)
            live = (key >= m * block_rows) & (key < m * block_rows + fill[m])
            here = live & (row >= g * per) & (row < (g + 1) * per)
            out = jnp.where(here, times.astype(F32), out)
    return out


def counts_by_key(nb, fill, rows, groups, block_rows, reads):
    keys = groups * block_rows
    key = lax.broadcasted_iota(jnp.int32, (keys, rows), 0)
    row = lax.broadcasted_iota(jnp.int32, (keys, rows), 1)
    per = rows // groups
    out = jnp.zeros((keys, rows), F32)
    for g in range(groups):
        for m in range(groups):
            times = jnp.int32(0)
            for n in range(reads):
                times = times + (nb[g, n] == m).astype(jnp.int32)
            live = (key >= m * block_rows) & (key < m * block_rows + fill[m])
            here = live & (row >= g * per) & (row < (g + 1) * per)
            out = jnp.where(here, times.astype(F32), out)
    return out


def whole(shape):
    zeros = (0,) * len(shape)
    return pl.BlockSpec(shape, lambda i, *_: zeros)


def near_core(array):
    return pltpu.with_memory_space_constraint(array, pltpu.VMEM)


def far_off(array):
    return pltpu.with_memory_space_constraint(array, pltpu.HBM)


def call(kernel, name, grid, scalars, ins, outs, scratch, vmem=VMEM_MB, after=(), flops=1):
    first = len(scalars) + len(ins)

    def body(*refs):
        kernel(*refs[:first], *refs[first + len(after) :])

    arrays = [near_core(item[0]) if len(item) > 2 else far_off(item[0]) for item in ins]
    shapes = [(pltpu.VMEM if len(item) > 3 else pltpu.HBM)(item[0], item[1]) for item in outs]
    return pl.pallas_call(
        body,
        name=name,
        grid_spec=pltpu.PrefetchScalarGridSpec(
            num_scalar_prefetch=len(scalars),
            grid=(grid,),
            in_specs=[item[1] for item in ins] + [pl.BlockSpec(memory_space=pl.ANY)] * len(after),
            out_specs=[item[2] for item in outs],
            scratch_shapes=scratch,
        ),
        out_shape=shapes,
        compiler_params=pltpu.CompilerParams(
            vmem_limit_bytes=vmem * 1024 * 1024, dimension_semantics=("arbitrary",)
        ),
        cost_estimate=pl.CostEstimate(flops=flops, bytes_accessed=1, transcendentals=0),
    )(*scalars, *arrays, *after)


def tie(array, after):
    spec = pl.BlockSpec(memory_space=pl.ANY)
    array = near_core(array)
    return pl.pallas_call(
        lambda *refs: None,
        name="tie",
        in_specs=[spec] * (1 + len(after)),
        out_specs=spec,
        out_shape=pltpu.VMEM(array.shape, array.dtype),
        input_output_aliases={0: 0},
        compiler_params=pltpu.CompilerParams(vmem_limit_bytes=1024 * 1024),
        cost_estimate=pl.CostEstimate(flops=1, bytes_accessed=1, transcendentals=0),
    )(array, *after)


def cross_forward_kernel(
    groups, reads, nb, fill, lat, blk, lg, lb, bg, bb, sg, sb, wq, wk, wv, wo,
    cq, ck, cv, co, ac, self_in, lat_in, blk_in, acc, cnt,
):
    i = pl.program_id(0)
    rows, width = lat.shape
    keys = blk.shape[0]
    scale = (width // H) ** -0.5
    head = width // H

    @pl.when(i == 0)
    def _():
        lat_in[...] = (hat(lat[...].astype(F32))[0] * lg[...] + lb[...]).astype(BF)
        blk_in[...] = (hat(blk[...].astype(F32))[0] * bg[...] + bb[...]).astype(BF)
        acc[...] = lat[...].astype(F32)
        cnt[...] = count_bias(counts_by_row(nb, fill, rows, groups, keys // groups, reads))

    q = nn(lat_in[...], wq[...]).astype(BF)
    k = nn(blk_in[...], wk[...]).astype(BF)
    v = nn(blk_in[...], wv[...]).astype(BF)
    cq[...] = q
    ck[...] = k
    cv[...] = v
    bias = cnt[...]
    mixed = []
    for h in range(q.shape[1] // head):
        cut = slice(h * head, (h + 1) * head)
        s = nt(q[:, cut], k[:, cut]) * (scale * LOG2_E) + bias
        e = jnp.exp2(s - jnp.max(s, axis=-1, keepdims=True))
        p = (e * (1.0 / jnp.sum(e, axis=-1, keepdims=True))).astype(BF)
        mixed.append(nn(p, v[:, cut]).astype(BF))
    mixed = jnp.concatenate(mixed, axis=1)
    co[...] = mixed
    acc[...] += nn(mixed, wo[...])

    @pl.when(i == pl.num_programs(0) - 1)
    def _():
        after = acc[...]
        ac[...] = after
        self_in[...] = (hat(after)[0] * sg[...] + sb[...]).astype(BF)


def flip_rows_kernel(plan, orders, ids, *refs):
    n = 1 + max(src for src, _ in plan)
    ins, outs, tmp = refs[:n], refs[n : n + len(plan)], refs[n + len(plan) :]
    for src, t in zip(ins, tmp, strict=True):
        t[...] = flip(src[...])
    for dst, (src, which) in zip(outs, plan, strict=True):
        t = tmp[src]
        size = t.shape[0] // len(orders[which])
        for p, distance in enumerate(orders[which]):
            at = pl.multiple_of((ids[2] ^ distance) * size, size)
            dst[p * size : (p + 1) * size, :] = t[pl.ds(at, size), :]


def self_forward_kernel(ids, a0, a1, a2, a3, wq, wk, wv, q, k, v, o0, o1, o2):
    rows, width = a0.shape
    head = width // H
    scale = head**-0.5
    for j, a in enumerate((a0, a1, a2, a3)):
        here = slice(j * rows, (j + 1) * rows)
        x = a[...]
        q[here, :] = nn(x, wq[...]).astype(BF)
        k[here, :] = nn(x, wk[...]).astype(BF)
        v[here, :] = nn(x, wv[...]).astype(BF)
    for t in range(2):
        mixed = []
        for h in range(q.shape[1] // head):
            cut = slice(h * head, (h + 1) * head)
            s = nt(q[2 * t * rows : 2 * (t + 1) * rows, cut], k[:, cut])
            e = jnp.exp2((s - jnp.max(s, axis=-1, keepdims=True)) * (scale * LOG2_E))
            p = (e * (1.0 / jnp.sum(e, axis=-1, keepdims=True))).astype(BF)
            mixed.append(nn(p, v[:, cut]).astype(BF))
        mixed = jnp.concatenate(mixed, axis=1)
        if t == 0:
            o0[...] = mixed[:rows]
            o1[...] = mixed[rows:]
        else:
            o2[...] = mixed


def self_out_kernel(ids, ac, o0, o1, o2, o3, wo, hg, hb, after, hidden_in, so, kept):
    cols = o0.shape[1]
    for j, o in enumerate((o0, o1, o2, o3)):
        at = pl.multiple_of((ids[1] ^ j) * cols, cols)
        so[:, pl.ds(at, cols)] = o[...]
    v = ac[...] + nn(so[...], wo[...])
    after[...] = v
    kept[...] = v
    hidden_in[...] = (hat(v)[0] * hg[...] + hb[...]).astype(BF)


def cot_back_kernel(gy, wred, out):
    out[...] = nt(gy[...], wred[...])


def cot_units_kernel(ids, *refs):
    gs, wexp, wred = refs[:8], refs[8:12], refs[12:16]
    own, other, we, wr = refs[16:]
    unit = wexp[0].shape[1]
    for q in range(4):
        we[q * unit : (q + 1) * unit, :] = flip(wexp[q][...])
        wr[q * unit : (q + 1) * unit, :] = wred[q][...]
    rows = gs[0].shape[0]
    for k, g in enumerate(gs):
        out = own if k < 4 else other
        at = (k % 4) * rows
        out[:, at : at + rows] = nt(wr[...], g[...])


def ff_local_kernel(hidden_in, gy, after, hg, dact, wexp, act_out, gate, das, vecs, dh):
    i = pl.program_id(0)

    @pl.when(i == 0)
    def _():
        dh[...] = jnp.zeros_like(dh)

    act, slope = gelu_parts(nn(hidden_in[...], wexp[...]))
    act_out[...] = act.astype(BF)
    dh[...] += nt((dact[...] * slope).astype(BF), wexp[...])

    @pl.when(i == pl.num_programs(0) - 1)
    def _():
        side, dg, db = norm_back(dh[...], after[...], hg[...])
        total = gy[...].astype(F32) + side
        das[...] = total
        gate[...] = total.astype(BF)
        vecs[0:1, :] = dg
        vecs[1:2, :] = db


def updated_kernel(act, wred, after, out, total):
    i = pl.program_id(0)

    @pl.when(i == 0)
    def _():
        total[...] = after[...]

    total[...] += nn(act[...], wred[...])

    @pl.when(i == pl.num_programs(0) - 1)
    def _():
        out[...] = total[...].astype(BF)


def ff_sums(we, dact, h, g, red, exp, fresh):
    act, slope = gelu_parts(nt(we[...], h))
    dpre = (dact * slope).astype(BF)
    if fresh:
        red[...] = nn(act.astype(BF), g)
        exp[...] = nn(dpre, h)
    else:
        red[...] += nn(act.astype(BF), g)
        exp[...] += nn(dpre, h)


def ff_tokens(refs, dact, we, red, exp, h_all, g_all, sem, fresh):
    hs, gs = refs[:4], refs[4:8]
    rows = hs[0].shape[0]
    copies = [
        pltpu.make_async_copy(piece, dst.at[pl.ds(k * rows, rows)], sem.at[which, k])
        for which, (src, dst) in enumerate(((hs, h_all), (gs, g_all)))
        for k, piece in enumerate(src)
    ]
    for c in copies:
        c.start()
    for t in range(2):
        for k in (2 * t, 2 * t + 1, 2 * t + 4, 2 * t + 5):
            copies[k].wait()
        here = slice(2 * t * rows, 2 * (t + 1) * rows)
        ff_sums(we, dact[:, here], h_all[here, :], g_all[here, :], red, exp, fresh and t == 0)


def ff_weights_a_kernel(*refs):
    dact, we, red, exp, h_all, g_all, sem = refs[8:]
    ff_tokens(refs, dact, we, red, exp, h_all, g_all, sem, True)


def ff_weights_b_kernel(ids, *refs):
    red_in, exp_in, dact, we, keep, send, red, exp, h_all, g_all, sem = refs[8:]
    red[...] = red_in[...]
    exp[...] = exp_in[...]
    ff_tokens(refs, dact, we, red, exp, h_all, g_all, sem, False)
    unit = we.shape[0] // 4
    half = 2 * unit
    width = red.shape[1]
    keep[:, 0:width] = red[0:half, :].astype(BF)
    send[:, 0:width] = red[half:, :].astype(BF)
    span = width // 8
    for p in range(4):
        out = keep if p < 2 else send
        low = (p % 2) * unit
        for q in range(4):
            for z in range(2):
                lanes = pl.ds(pl.multiple_of((ids[8 + p] + 2 * z) * span, span), span)
                to = pl.ds(pl.multiple_of(width + (2 * ids[12 + q] + z) * span, span), span)
                out[low : low + unit, to] = exp[q * unit : (q + 1) * unit, lanes].astype(BF)


def self_backward_kernel(
    ids, g0, g1, g2, g3, q, k, v, wo, wq, wk, wv, flipped, keep, send, do, dq, dk, dv
):
    rows, width = g0.shape
    head = width // H
    scale = head**-0.5
    for j, g in enumerate((g0, g1, g2, g3)):
        do[j * rows : (j + 1) * rows, :] = nt(g[...], wo[...]).astype(BF)
    cols = q.shape[1]
    tile = 512
    for h in range(cols // head):
        cut = slice(h * head, (h + 1) * head)
        kh = k[:, cut]
        vh = v[:, cut]
        kt = flip(kh)
        key_sum = jnp.zeros((k.shape[0], head), F32)
        value_sum = jnp.zeros((k.shape[0], head), F32)
        for t in range(q.shape[0] // tile):
            here = slice(t * tile, (t + 1) * tile)
            qt = q[here, cut]
            dt = do[here, cut]
            s = nt(kh, qt)
            e = jnp.exp2((s - jnp.max(s, axis=0, keepdims=True)) * (scale * LOG2_E))
            p = e * (1.0 / jnp.sum(e, axis=0, keepdims=True))
            dp = nt(vh, dt)
            ds = (p * (dp - jnp.sum(p * dp, axis=0, keepdims=True))).astype(BF)
            value_sum += nn(p.astype(BF), dt)
            key_sum += nn(ds, qt)
            back = (nn(kt, ds) * scale).astype(BF)
            flipped[cut, here] = back
            dq[here, cut] = flip(back)
        dk[:, cut] = (key_sum * scale).astype(BF)
        dv[:, cut] = value_sum.astype(BF)
    flipped[cols : 2 * cols, :] = flip(dk[...])
    flipped[2 * cols : 3 * cols, :] = flip(dv[...])
    for j in range(4):
        here = slice(j * rows, (j + 1) * rows)
        side = nt(dq[here, :], wq[...]) + nt(dk[here, :], wk[...]) + nt(dv[here, :], wv[...])
        out = send if j % 2 else keep
        low = (j // 2) * rows
        out[low : low + rows, :] = side.astype(BF)


def self_weights_kernel(ids, flipped, *refs):
    ins, gates, mixed = refs[0:4], refs[4:8], refs[8:12]
    keep, send, total = refs[12:]
    rows = ins[0].shape[0]
    three = flipped.shape[0]
    for low, high, parts in (
        (0, three, [(flipped[:, j * rows : (j + 1) * rows], ins[j][...]) for j in range(4)]),
        (three, total.shape[0], [(flip(gates[j][...]), mixed[j][...]) for j in range(4)]),
    ):
        acc = None
        for left, right in parts:
            part = nn(left, right)
            acc = part if acc is None else acc + part
        total[low:high, :] = acc
    depth, span = total.shape[0], keep.shape[1]
    blocks = total.shape[1] // span
    for p in range(blocks):
        out = keep if p < blocks // 2 else send
        low = (p % (blocks // 2)) * depth
        lanes = pl.ds(pl.multiple_of(ids[16 + p] * span, span), span)
        out[low : low + depth, :] = total[:, lanes].astype(BF)


def cross_backward_kernel(
    groups, reads, nb, fill, keep, rcv, xr, das, ac, sg, wo, cq, ck, cv, gate, dq, dk, dv, dac, vecs, cnt,
):
    i = pl.program_id(0)
    rows, width = das.shape
    keys = ck.shape[0]
    head = width // H
    scale = head**-0.5

    @pl.when(i == 0)
    def _():
        dy = keep[...].astype(F32) + rcv[...].astype(F32) + xr[...].astype(F32)
        side, dg, db = norm_back(dy, ac[...], sg[...])
        total = das[...] + side
        dac[...] = total
        gate[...] = total.astype(BF)
        vecs[0:1, :] = dg
        vecs[1:2, :] = db
        cnt[...] = count_bias(counts_by_key(nb, fill, rows, groups, keys // groups, reads))

    do = nt(gate[...], wo[...]).astype(BF)
    bias = cnt[...]
    for h in range(cq.shape[1] // head):
        cut = slice(h * head, (h + 1) * head)
        qh = cq[:, cut]
        kh = ck[:, cut]
        dh = do[:, cut]
        s = nt(kh, qh) * (scale * LOG2_E) + bias
        e = jnp.exp2(s - jnp.max(s, axis=0, keepdims=True))
        p = e * (1.0 / jnp.sum(e, axis=0, keepdims=True))
        dp = nt(cv[:, cut], dh)
        ds = (p * (dp - jnp.sum(p * dp, axis=0, keepdims=True))).astype(BF)
        dv[:, cut] = nn(p.astype(BF), dh).astype(BF)
        dk[:, cut] = (nn(ds, qh) * scale).astype(BF)
        dq[:, cut] = flip((nn(flip(kh), ds) * scale).astype(BF))


def cross_inputs_kernel(
    ids, dq, dk, dv, wq, wk, wv, lat, blk, lg, bg, dac, sv, hv, dlat, dblk, keep, send, la, ba, vecs, turned
):
    i = pl.program_id(0)

    @pl.when(i == 0)
    def _():
        la[...] = jnp.zeros_like(la)
        ba[...] = jnp.zeros_like(ba)

    la[...] += nt(dq[...], wq[...])
    ba[...] += nt(dk[...], wk[...]) + nt(dv[...], wv[...])

    @pl.when(i == pl.num_programs(0) - 1)
    def _():
        vecs[...] = jnp.zeros_like(vecs)
        side, dg, db = norm_back(la[...], lat[...].astype(F32), lg[...])
        dlat[...] = (dac[...] + side).astype(BF)
        vecs[0:1, :] = dg
        vecs[1:2, :] = db
        side, dg, db = norm_back(ba[...], blk[...].astype(F32), bg[...])
        dblk[...] = side.astype(BF)
        vecs[2:3, :] = dg
        vecs[3:4, :] = db
        vecs[4:6, :] = sv[...]
        vecs[6:8, :] = hv[...]
        turned[...] = flip(vecs[...])
        devices = 8
        chunk = keep.shape[0] // (2 * devices)
        for p in range(4):
            out = keep if p < 2 else send
            for d in range(devices):
                at = ids[8 + p] * 4 + (d // 4) * 8 + d % 4
                low = ((p % 2) * devices + d) * chunk
                rows = turned[pl.ds(pl.multiple_of(at * chunk, chunk), chunk), :]
                out[low : low + chunk, :] = rows.astype(BF)


def stack_sum_kernel(kept, got, vec_keep, vec_send, keep, send):
    rows = kept.shape[0] // 4
    more = vec_keep.shape[0] // 2
    for p in range(4):
        out, vecs = (keep, vec_keep) if p < 2 else (send, vec_send)
        low = (p % 2) * (rows + more)
        here = slice(p * rows, (p + 1) * rows)
        out[low : low + rows, :] = (kept[here, :].astype(F32) + got[here, :].astype(F32)).astype(BF)
        out[low + rows : low + rows + more, :] = vecs[(p % 2) * more : (p % 2 + 1) * more, :]


def cross_weights_kernel(*refs):
    n = (len(refs) - 2) // 2
    lefts, rights, outs = refs[:n], refs[n : 2 * n], refs[2 * n :]
    for k, (left, right) in enumerate(zip(lefts, rights, strict=True)):
        width = right.shape[1]
        outs[k // 2][:, (k % 2) * width : (k % 2 + 1) * width] = nn(left[...], right[...]).astype(BF)


def combine_kernel(terms, *refs):
    total = sum(sum(parts) for parts in terms)
    ins, outs = refs[: 2 * total], refs[2 * total :]
    n = 0
    for k, parts in enumerate(terms):
        at = 0
        for count in parts:
            tops, lows = ins[n : n + 2 * count : 2], ins[n + 1 : n + 2 * count : 2]
            width = tops[0].shape[1]
            for out, refs_ in ((outs[2 * k], tops), (outs[2 * k + 1], lows)):
                acc = refs_[0][...].astype(F32)
                for ref in refs_[1:]:
                    acc = acc + ref[...].astype(F32)
                out[:, at : at + width] = acc.astype(BF)
            at += width
            n += 2 * count


def combine(name, chains, steps, after=(), parts_of=1, flops=1):
    ins, outs = [], []
    for parts in chains:
        total = 0
        for terms in parts:
            for term in terms:
                a, k = term if parts_of > 1 else (term, 0)
                depth, width = a.shape[0], a.shape[1] // parts_of
                part = depth // 2 // steps
                top = pl.BlockSpec((part, width), lambda i, k=k: (i, k))
                low = pl.BlockSpec((part, width), lambda i, k=k: (i + steps, k))
                ins += [(a, top, V), (a, low, V)]
            total += width
        outs += [((depth // 2, total), BF, pl.BlockSpec((part, total), lambda i: (i, 0)), V)] * 2
    counts = tuple(tuple(len(terms) for terms in parts) for parts in chains)
    out = call(
        functools.partial(combine_kernel, counts), name, steps, [], ins, outs, [], after=after, flops=flops
    )
    return [tuple(out[2 * k : 2 * k + 2]) for k in range(len(chains))]


def copy_kernel(a, out):
    out[...] = a[...]


def add_kernel(a, b, out):
    out[...] = (a[...].astype(F32) + b[...].astype(F32)).astype(BF)


def pack_kernel(ff_kept, ff_got, set_kept, set_got, reduce_delta, out):
    unit, width = reduce_delta.shape
    reduce_delta[...] = ff_kept[:, 0:width].astype(F32) + ff_got[:, 0:width].astype(F32)
    rest = ff_kept[:, width:].astype(F32) + ff_got[:, width:].astype(F32)
    devices, chunk, _ = out.shape
    span = devices * chunk
    parts = width // span
    for q in range(parts):
        t = flip(rest[:, q * span : (q + 1) * span]).astype(BF)
        for d in range(devices):
            out[d, :, q * unit : (q + 1) * unit] = t[d * chunk : (d + 1) * chunk, :]
    total = set_kept[...].astype(F32) + set_got[...].astype(F32)
    cols = total.shape[0] - span
    t = flip(total[:cols, :]).astype(BF)
    n_set = t.shape[0] // chunk
    for d in range(devices):
        at = (d % n_set) * chunk
        out[d, :, parts * unit : parts * unit + cols] = t[at : at + chunk, :]
        out[d, :, parts * unit + cols :] = total[cols + d * chunk : cols + (d + 1) * chunk, :].astype(BF)


def place_kernel(unit, n_set, ids, got, expand, *outs):
    devices, chunk, width = got.shape
    parts = expand.shape[1] // (devices * unit)
    for q in range(parts):
        for d in range(devices):
            at = ((q // 2) * 2 * devices + (d // n_set) * devices + (q % 2) * n_set + d % n_set) * unit
            expand[:, at : at + unit] = got[d, :, q * unit : (q + 1) * unit].astype(F32)
    outs, vecs = outs[:4], outs[4:]
    lanes = width - parts * unit - 4 * outs[0].shape[1] // n_set
    cols = outs[0].shape[1] // n_set
    for d in range(n_set):
        mine = got[ids[3] * n_set + d]
        for m, out in enumerate(outs):
            at = parts * unit + m * cols
            out[:, d * cols : (d + 1) * cols] = mine[:, at : at + cols].astype(F32)
    total = jnp.zeros((chunk, lanes), F32)
    for d in range(devices):
        total += got[d, :, width - lanes :].astype(F32)
    total = flip(total)
    for k, out in enumerate(vecs):
        out[...] = total[k : k + 1, :]


def cross_last_kernel(parts, n, *refs):
    ins, outs = refs[: 2 * n], refs[2 * n :]
    for chain, members in enumerate(parts):
        total = ins[2 * chain][...].astype(F32) + ins[2 * chain + 1][...].astype(F32)
        at = 0
        for which, cols in members:
            outs[which][...] = total[:, at : at + cols]
            at += cols


def swap(values, axis, bit):
    size = lax.axis_size(axis)
    return lax.ppermute(values, axis, [(i, i ^ bit) for i in range(size)])


CORE = ("lvl", 1)
ACROSS = ("lvl", 2)
BESIDE = ("grp", 1)
NEAR = ("grp", 2)
FAR = ("grp", 4)


def gather_set(own, wait=lambda across: across):
    across = wait(swap(own, *ACROSS))
    return own, swap(own, *CORE), across, swap(across, *CORE)


def places(links, n_lvl):
    weights = [bit * (n_lvl if axis == "grp" else 1) for axis, bit in links]
    n = len(weights)
    return [
        sum(w for k, w in enumerate(weights) if p >> (n - 1 - k) & 1) for p in range(1 << n)
    ]


CHAINS = (
    (CORE, ACROSS, BESIDE, NEAR, FAR),
    (CORE, BESIDE, NEAR, ACROSS, FAR),
    (CORE, NEAR, ACROSS, FAR, BESIDE),
)


def tiled(
    latents, blocks, neighbours, fill, cotangent,
    latent_gain, latent_shift, block_gain, block_shift,
    cross_query, cross_key, cross_value, cross_output,
    self_gain, self_shift, self_query, self_key, self_value, self_output,
    hidden_gain, hidden_shift, hidden_expand, hidden_reduce,
):
    rows, width = latents.shape
    groups, block_rows, _ = blocks.shape
    keys = groups * block_rows
    reads = neighbours.shape[1]
    hidden = hidden_expand.shape[1]
    n_grp, n_lvl = lax.axis_size("grp"), lax.axis_size("lvl")
    n_dev = n_grp * n_lvl
    n_plane = 2 * n_lvl
    g = lax.axis_index("grp").astype(jnp.int32)
    l = lax.axis_index("lvl").astype(jnp.int32)
    me = g * n_lvl + l
    per = n_lvl
    steps = [0, FAR[1], BESIDE[1], FAR[1] | BESIDE[1]]
    bare = g & ~NEAR[1]
    ids = jnp.stack(
        [g, l, me, (g & NEAR[1]) // NEAR[1]]
        + [me ^ (p * per) for p in steps]
        + [bare ^ p for p in steps]
        + [((bare ^ p) // FAR[1]) * 2 + ((bare ^ p) & 1) for p in steps]
        + [g ^ p for p in (0, 4, 1, 5, 2, 6, 3, 7)]
    ).astype(jnp.int32)
    orders = tuple(tuple(places(links, n_lvl)) for links in CHAINS)
    unit = hidden // n_dev
    chunk = width // n_dev

    vec = lambda v: v.reshape(1, width)
    vspec = whole((1, width))
    scalars = pl.BlockSpec(memory_space=pltpu.SMEM)
    blk = blocks.reshape(keys, width)
    pair = width // 4
    cols = pl.BlockSpec((width, pair), lambda i, *_: (0, i))
    rspec = pl.BlockSpec((pair, width), lambda i, *_: (i, 0))
    mine = pl.BlockSpec((width, pair), lambda i, ids: (0, ids[1]))
    mine_rows = pl.BlockSpec((pair, width), lambda i, ids: (ids[1], 0))
    row_full = whole((rows, width))
    key_full = whole((keys, width))
    row_part = pl.BlockSpec((rows, pair), lambda i, *_: (0, i))
    key_part = pl.BlockSpec((keys, pair), lambda i, *_: (0, i))
    set_rows = n_lvl * rows

    full = lambda a: whole(a.shape)
    cot_across, cot_near = swap(cotangent, *ACROSS), swap(cotangent, *NEAR)

    cq, ck, cv, co, after_cross, self_in, latent_in, block_in = call(
        functools.partial(cross_forward_kernel, groups, reads),
        "cross_forward", 4, [],
        [(neighbours, scalars), (fill, scalars), (latents, row_full), (blk, key_full)]
        + [(vec(v), vspec) for v in (latent_gain, latent_shift, block_gain, block_shift, self_gain, self_shift)]
        + [(cross_query, cols), (cross_key, cols), (cross_value, cols), (cross_output, rspec)],
        [
            ((rows, width), BF, row_part), ((keys, width), BF, key_part),
            ((keys, width), BF, key_part), ((rows, width), BF, row_part),
            ((rows, width), F32, row_full), ((rows, width), BF, row_full, V),
            ((rows, width), BF, row_full), ((keys, width), BF, key_full),
        ],
        [pltpu.VMEM((rows, width), F32), pltpu.VMEM((rows, keys), F32)],
        after=[ids],
    )

    set_of = lambda pieces: [(a, whole((rows, width)), V) for a in pieces]
    part = (set_rows, pair)
    plan = ((0, 0), (1, 1), (1, 2), (2, 0))
    sources = (latent_in, block_in, co)
    flips = call(
        functools.partial(flip_rows_kernel, plan, orders), "flip_cross", 1, [ids],
        [(a, full(a)) for a in sources],
        [(sources[k].shape[::-1], BF, whole(sources[k].shape[::-1])) for k, _ in plan],
        [pltpu.VMEM(a.shape[::-1], BF) for a in sources],
    )
    cot_corner = swap(cot_across, *NEAR)
    (dact,) = call(
        cot_back_kernel, "cot_back", 4, [],
        [(cotangent, row_full), (hidden_reduce, pl.BlockSpec((hidden // 4, width), lambda i: (i, 0)))],
        [((rows, hidden), F32, pl.BlockSpec((rows, hidden // 4), lambda i: (0, i)), V)],
        [], after=[far_off(flips[0])],
    )
    self_in = tie(self_in, [cot_across, cot_near])
    set_in = gather_set(self_in, lambda across: tie(across, [dact]))
    q, k, v, o0, o1, o2 = call(
        self_forward_kernel, "self_forward", 1, [ids],
        set_of(set_in)
        + [(self_query, mine), (self_key, mine), (self_value, mine)],
        [(part, BF, whole(part))] * 3
        + [((rows, pair), BF, whole((rows, pair)), V)] * 2
        + [((2 * rows, pair), BF, whole((2 * rows, pair)), V)],
        [],
        after=[dact],
    )

    across = swap(tie(o2, [cot_corner]), *ACROSS)
    cots = [cotangent, cot_across, cot_near, cot_corner]
    cots_core = [swap(a, *CORE) for a in cots]
    own_cot = [cotangent, cot_across, cots_core[0], cots_core[1]]
    other_cot = [cot_near, cot_corner, cots_core[2], cots_core[3]]

    def unit_cols(p):
        return pl.BlockSpec((width, unit), lambda i, ids: (0, ids[4 + p]))

    def unit_rows(p):
        return pl.BlockSpec((unit, width), lambda i, ids: (ids[4 + p], 0))

    mine_units = (4 * unit, width)
    by_token = (4 * unit, set_rows)
    dact_own, dact_other, mine_expand = call(
        cot_units_kernel, "cot_units", 1, [ids],
        [(own_cot[0], row_full)] + [(a, row_full, V) for a in own_cot[1:] + other_cot]
        + [(hidden_expand, unit_cols(p)) for p in range(4)]
        + [(hidden_reduce, unit_rows(p)) for p in range(4)],
        [(by_token, F32, whole(by_token), V)] * 2 + [(mine_units, BF, whole(mine_units), V)],
        [pltpu.VMEM(mine_units, BF)], after=[o0],
    )
    second = pl.BlockSpec((rows, pair), lambda i: (1, 0))
    (across_next,) = call(
        copy_kernel, "pass", 1, [], [(across, second, V)], [((rows, pair), BF, whole((rows, pair)), V)], [],
        after=[mine_expand],
    )
    o_spec = whole((rows, pair))
    pieces = (o0, swap(o1, *CORE), across, swap(across_next, *CORE))
    after_self, hidden_in, so, after_self_kept = call(
        self_out_kernel, "self_out", 1, [ids],
        [(after_cross, row_full)] + [(p, o_spec, V) for p in pieces]
        + [(self_output, whole((width, width))), (vec(hidden_gain), vspec), (vec(hidden_shift), vspec)],
        [
            ((rows, width), F32, row_full, V), ((rows, width), BF, row_full, V), ((rows, width), BF, row_full, V),
            ((rows, width), F32, row_full),
        ],
        [], after=[mine_expand],
    )

    hid_across, hid_near = swap(hidden_in, *ACROSS), swap(hidden_in, *NEAR)
    step = 512
    activated, gate, after_self_delta, hidden_vecs = call(
        ff_local_kernel, "ff_local", hidden // step, [],
        [
            (hidden_in, row_full, V), (cotangent, row_full), (after_self, row_full, V), (vec(hidden_gain), vspec),
            (dact, pl.BlockSpec((rows, step), lambda i: (0, i)), V),
            (hidden_expand, pl.BlockSpec((width, step), lambda i: (0, i))),
        ],
        [
            ((rows, hidden), BF, pl.BlockSpec((rows, step), lambda i: (0, i))), ((rows, width), BF, row_full, V),
            ((rows, width), F32, row_full), ((2, width), F32, whole((2, width))),
        ],
        [pltpu.VMEM((rows, width), F32)],
    )
    gate = tie(gate, [hid_across, hid_near])
    hid_across = tie(hid_across, [gate])
    hid_corner = swap(hid_across, *NEAR)

    any_spec = pl.BlockSpec(memory_space=pl.ANY)

    own_hid = [hidden_in, hid_across, swap(hidden_in, *CORE), swap(hid_across, *CORE)]
    copied = [
        pltpu.VMEM((set_rows, width), BF), pltpu.VMEM((set_rows, width), BF), pltpu.SemaphoreType.DMA((2, 4)),
    ]
    ff_part = call(
        ff_weights_a_kernel, "ff_weights_a", 1, [],
        [(a, any_spec, V) for a in own_hid] + [(own_cot[0], any_spec)] + [(a, any_spec, V) for a in own_cot[1:]]
        + [(a, full(a), V) for a in (dact_own, mine_expand)],
        [(mine_units, F32, whole(mine_units), V)] * 2, copied, after=[gate],
    )

    gate_all = gather_set(gate, lambda across: tie(across, [ff_part[0]]))
    flipped, self_keep, self_send = call(
        self_backward_kernel, "self_backward", 1, [ids],
        set_of(gate_all) + [(a, whole(part)) for a in (q, k, v)]
        + [(self_output, mine_rows), (self_query, mine), (self_key, mine), (self_value, mine)],
        [((3 * pair, set_rows), BF, whole((3 * pair, set_rows)))]
        + [((2 * rows, width), BF, whole((2 * rows, width)), V)] * 2,
        [pltpu.VMEM(part, BF)] * 4,
    )
    so = tie(so, [gate_all[2]])
    so_across = swap(so, *ACROSS)
    self_send = tie(self_send, [so_across, hid_corner])
    self_got = swap(self_send, *CORE)
    so_all = (so, swap(so, *CORE), so_across, swap(so_across, *CORE))
    lower = pl.BlockSpec((rows // 2, width), lambda i: (i + 2, 0))
    (self_pass,) = call(
        add_kernel, "self_pass", 2, [], [(self_keep, lower, V), (self_got, lower, V)],
        [((rows, width), BF, pl.BlockSpec((rows // 2, width), lambda i: (i, 0)), V)],
        [],
    )
    self_across = swap(self_pass, *ACROSS)

    other_hid = [hid_near, hid_corner, swap(hid_near, *CORE), swap(hid_corner, *CORE)]
    half = (2 * unit, 2 * width)
    ff_keep, ff_send = call(
        ff_weights_b_kernel, "ff_weights_b", 1, [ids],
        [(a, any_spec, V) for a in other_hid + other_cot] + [(a, full(a), V) for a in (*ff_part, dact_other, mine_expand)],
        [(half, BF, whole(half), V)] * 2,
        [pltpu.VMEM(mine_units, F32)] * 2 + copied, after=[self_pass],
    )
    ff_got = swap(ff_send, *BESIDE)

    span = width // n_grp
    stack = (n_grp // 2 * 4 * pair, span)
    stack_keep, stack_send = call(
        self_weights_kernel, "self_weights", 1, [ids],
        [(flipped, full(flipped))] + set_of(set_in)
        + [(a, pl.BlockSpec((rows, pair), lambda i, ids: (0, ids[1])), V) for a in gate_all]
        + set_of(so_all),
        [(stack, BF, whole(stack), V)] * 2,
        [pltpu.VMEM((4 * pair, width), F32)],
        after=[ff_send],
    )
    stack_send = tie(stack_send, [self_across])
    stack_got = swap(stack_send, *NEAR)

    half_rows = pl.BlockSpec((rows, width), lambda i, *_: (0, 0))
    cross_gate, dcq, dck, dcv, after_cross_delta, self_vecs = call(
        functools.partial(cross_backward_kernel, groups, reads),
        "cross_backward", 4, [],
        [
            (neighbours, scalars), (fill, scalars),
            (self_keep, half_rows, V), (self_got, half_rows, V), (self_across, row_full, V),
            (after_self_delta, row_full), (after_cross, row_full), (vec(self_gain), vspec),
            (cross_output, rspec), (cq, row_part), (ck, key_part), (cv, key_part),
        ],
        [
            ((rows, width), BF, row_full, V),
            ((rows, width), BF, row_part, V), ((keys, width), BF, key_part, V), ((keys, width), BF, key_part, V),
            ((rows, width), F32, row_full), ((2, width), F32, whole((2, width))),
        ],
        [pltpu.VMEM((keys, rows), F32)],
        after=[stack_send, ff_send],
    )

    lefts = (flips[0], flips[3], flips[1], flips[2])
    rights = [(a, full(a), V) for a in (dcq, cross_gate, dck, dcv)]
    tile = width // 4

    def halves(name, first, after, flops):
        return call(
            cross_weights_kernel, name, 2, [],
            [(a, pl.BlockSpec((tile, a.shape[1]), lambda i: (i + first, 0))) for a in lefts] + rights,
            [((width // 2, 2 * width), BF, pl.BlockSpec((tile, 2 * width), lambda i: (i, 0)), V)] * 2,
            [], after=after, flops=flops,
        )

    sent = halves("cross_weights_sent", 2, [ff_send, stack_send], 1)
    kept = halves("cross_weights_kept", 0, [sent[0], ff_send, stack_send], 1)
    cores = [(a, swap(b, *CORE)) for a, b in zip(kept, sent)]
    stack_got = tie(stack_got, [kept[0]])
    ((ff_keep, ff_send),) = combine("ff_sum", [[(ff_keep, ff_got)]], 1, after=[stack_got], flops=2 * 10**10)
    ff_got = swap(ff_send, *FAR)
    pairs = combine(
        "cross_sum_core",
        [
            [tuple((a, 0) for a in cores[0]), tuple((a, 1) for a in cores[0])],
            [tuple((a, 0) for a in cores[1])],
            [tuple((a, 1) for a in cores[1])],
        ],
        4, after=[stack_got, ff_send], parts_of=2,
    )
    got = [swap(send, *CHAINS[n][1]) for n, (_, send) in enumerate(pairs)]

    marks = 128
    part_vecs = (2 * n_plane * chunk, marks)
    latent_delta, block_delta, vec_keep, vec_send = call(
        cross_inputs_kernel, "cross_inputs", 4, [ids],
        [
            (dcq, row_part, V), (dck, key_part, V), (dcv, key_part, V),
            (cross_query, cols), (cross_key, cols), (cross_value, cols),
            (latents, row_full), (blk, key_full), (vec(latent_gain), vspec), (vec(block_gain), vspec),
            (after_cross_delta, row_full), (self_vecs, full(self_vecs)), (hidden_vecs, full(hidden_vecs)),
        ],
        [((rows, width), BF, row_full), ((keys, width), BF, key_full)]
        + [(part_vecs, BF, whole(part_vecs), V)] * 2,
        [
            pltpu.VMEM((rows, width), F32), pltpu.VMEM((keys, width), F32),
            pltpu.VMEM((marks, width), F32), pltpu.VMEM((width, marks), F32),
        ],
        after=[pairs[0][1]],
    )
    joined = (2 * (4 * pair + part_vecs[0] // 2), marks)
    stack_keep, stack_send = call(
        stack_sum_kernel, "self_sum_near", 1, [],
        [(a, full(a), V) for a in (stack_keep, stack_got, vec_keep, vec_send)],
        [(joined, BF, whole(joined), V)] * 2, [],
    )
    stack_got = swap(stack_send, *BESIDE)
    span = hidden // 4
    (updated,) = call(
        updated_kernel, "updated", 4, [],
        [
            (activated, pl.BlockSpec((rows, span), lambda i: (0, i))),
            (hidden_reduce, pl.BlockSpec((span, width), lambda i: (i, 0))), (after_self_kept, row_full),
        ],
        [((rows, width), BF, row_full)], [pltpu.VMEM((rows, width), F32)], after=[stack_send],
    )
    last = [stack_send, ff_got, far_off(updated)]
    for stage in (2, 3, 4):
        chains = [[(kept, a)] for (kept, _), a in zip(pairs, got)]
        pairs = combine(f"cross_sum_{stage}", chains, 1, after=last)
        got = [swap(send, *CHAINS[n][stage]) for n, (_, send) in enumerate(pairs)]
        last = [pairs[0][1]]
        if stage == 2:
            ((stack_keep, stack_send),) = combine(
                "self_sum_y", [[(stack_keep, stack_got)]], 2, after=[pairs[0][1], ff_got]
            )
            stack_got = swap(stack_send, *FAR)
            last = [stack_send]
        if stage == 3:
            piece = (unit, width)
            mixed = (n_plane, chunk, 4 * unit + 4 * pair + marks)
            reduce_delta, turned = call(
                pack_kernel, "pack", 1, [],
                [(a, full(a), V) for a in (ff_keep, ff_got, stack_keep, stack_got)],
                [(piece, F32, whole(piece)), (mixed, BF, whole(mixed), V)],
                [], after=last,
            )
            last = [turned]
        if stage == 4:
            planes = [
                [(d ^ z) * n_lvl + k for z in (0, NEAR[1]) for k in range(n_lvl)]
                for d in range(n_grp)
                if not d & NEAR[1]
            ]
            got_all = lax.all_to_all(
                tie(turned, [pairs[0][1]]), ("grp", "lvl"), split_axis=0, concat_axis=0, axis_index_groups=planes, tiled=True
            )
    members = (((0, width), (3, width)), ((1, width),), ((2, width),))
    ins = []
    for (kept, _), a in zip(pairs, got):
        ins += [(kept, full(kept), V), (a, full(a), V)]
    last = call(
        functools.partial(cross_last_kernel, members, 3), "cross_last", 1, [], ins,
        [((chunk, width), F32, whole((chunk, width)))] * 4,
        [], flops=5 * 10**9,
    )
    placed = call(
        functools.partial(place_kernel, unit, n_lvl), "place", 1, [ids], [(got_all, full(got_all), V)],
        [((chunk, hidden), F32, whole((chunk, hidden)))] + [((chunk, width), F32, whole((chunk, width)))] * 4
        + [((1, chunk), F32, whole((1, chunk)))] * 8,
        [],
    )
    vecs = [a.reshape(chunk) for a in placed[5:]]

    return (
        updated, latent_delta, block_delta.reshape(groups, block_rows, width),
        vecs[0], vecs[1], vecs[2], vecs[3],
        last[0], last[1], last[2], last[3],
        vecs[4], vecs[5],
        placed[1], placed[2], placed[3], placed[4],
        vecs[6], vecs[7],
        placed[0], reduce_delta,
    )


def normed(values, norm_gain, norm_shift):
    center = values - jnp.mean(values, axis=-1, keepdims=True)
    spread = jnp.mean(center * center, axis=-1, keepdims=True)
    return center * lax.rsqrt(spread + EPS) * norm_gain + norm_shift


def to_half(values):
    return values.astype(jnp.bfloat16)


def matmul(left_side, right_side):
    return jnp.dot(left_side, right_side, preferred_element_type=jnp.float32)


def left_outer(left_side, right_side):
    return lax.dot_general(
        left_side, right_side, (((0,), (0,)), ((), ())), preferred_element_type=jnp.float32
    )


def right_outer(left_side, right_side):
    return lax.dot_general(
        left_side, right_side, (((1,), (1,)), ((), ())), preferred_element_type=jnp.float32
    )


def self_forward(query_heads, key_heads, value_heads, score_scale):
    length, local_heads, head_size = query_heads.shape
    block_rows = min(512, length)
    query_blocks = query_heads.reshape(length // block_rows, block_rows, local_heads, head_size)

    def one_block(query_block):
        scores = (
            jnp.einsum("qhd,khd->hqk", query_block, key_heads, preferred_element_type=jnp.float32)
            * score_scale
        )
        row_top = jnp.max(scores, axis=-1, keepdims=True)
        raised = jnp.exp(scores - row_top)
        row_total = jnp.sum(raised, axis=-1, keepdims=True)
        attention = raised / row_total
        mixture = jnp.einsum(
            "hqk,khd->qhd", to_half(attention), value_heads, preferred_element_type=jnp.float32
        )
        return (to_half(mixture), row_top + jnp.log(row_total))

    mixture, log_total = lax.map(one_block, query_blocks)
    return (mixture.reshape(length, local_heads, head_size), log_total)


def self_backward(query_heads, key_heads, value_heads, mixed_delta, log_total, score_scale):
    length, local_heads, head_size = query_heads.shape
    block_rows = min(512, length)
    query_blocks = query_heads.reshape(length // block_rows, block_rows, local_heads, head_size)
    delta_blocks = mixed_delta.reshape(length // block_rows, block_rows, local_heads, head_size)

    def one_block(running, pieces):
        key_sum, value_sum = running
        query_block, delta_block, log_block = pieces
        scores = (
            jnp.einsum("qhd,khd->hqk", query_block, key_heads, preferred_element_type=jnp.float32)
            * score_scale
        )
        attention = jnp.exp(scores - log_block)
        value_sum = value_sum + jnp.einsum(
            "hqk,qhd->khd", to_half(attention), delta_block, preferred_element_type=jnp.float32
        )
        weight_delta = jnp.einsum(
            "qhd,khd->hqk", delta_block, value_heads, preferred_element_type=jnp.float32
        )
        score_delta = to_half(
            attention * (weight_delta - jnp.sum(attention * weight_delta, axis=-1, keepdims=True))
        )
        query_delta = to_half(
            jnp.einsum("hqk,khd->qhd", score_delta, key_heads, preferred_element_type=jnp.float32)
            * score_scale
        )
        key_sum = (
            key_sum
            + jnp.einsum(
                "hqk,qhd->khd", score_delta, query_block, preferred_element_type=jnp.float32
            )
            * score_scale
        )
        return ((key_sum, value_sum), query_delta)

    zero_start = jnp.zeros(key_heads.shape, jnp.float32)
    (key_sum, value_sum), query_delta = lax.scan(
        one_block, (zero_start, zero_start), (query_blocks, delta_blocks, log_total)
    )
    return (
        query_delta.reshape(length, local_heads, head_size),
        to_half(key_sum),
        to_half(value_sum),
    )


def cross_forward(cross_queries, block_keys, block_values, neighbours, fill, score_scale):
    groups, latent_rows, head_count, head_size = cross_queries.shape
    block_rows = block_keys.shape[1]
    reads = neighbours.shape[1]
    picked_keys = block_keys[neighbours].reshape(groups, reads * block_rows, head_count, head_size)
    picked_values = block_values[neighbours].reshape(
        groups, reads * block_rows, head_count, head_size
    )
    positions = jnp.arange(block_rows, dtype=jnp.int32)
    live_keys = (positions[None, None, :] < fill[neighbours][:, :, None]).reshape(
        groups, reads * block_rows
    )
    scores = (
        jnp.einsum(
            "gqhd,gkhd->ghqk", cross_queries, picked_keys, preferred_element_type=jnp.float32
        )
        * score_scale
    )
    scores = jnp.where(live_keys[:, None, None, :], scores, NEG)
    attention = jax.nn.softmax(scores, axis=-1)
    return (attention, picked_keys, picked_values)


def plain(
    latents,
    blocks,
    neighbours,
    fill,
    cotangent,
    latent_gain,
    latent_shift,
    block_gain,
    block_shift,
    cross_query,
    cross_key,
    cross_value,
    cross_output,
    self_gain,
    self_shift,
    self_query,
    self_key,
    self_value,
    self_output,
    hidden_gain,
    hidden_shift,
    hidden_expand,
    hidden_reduce,
):
    rows = latents.shape[0]
    width = latents.shape[1]
    groups = blocks.shape[0]
    block_rows = blocks.shape[1]
    reads = neighbours.shape[1]
    head_size = width // H
    score_scale = head_size ** (-0.5)
    latent_float = latents.astype(jnp.float32)
    latent_norm, latent_pull = jax.vjp(normed, latent_float, latent_gain, latent_shift)
    latent_in = to_half(latent_norm)
    block_float = blocks.reshape(groups * block_rows, width).astype(jnp.float32)
    block_norm, block_pull = jax.vjp(normed, block_float, block_gain, block_shift)
    block_in = to_half(block_norm)
    cross_queries = to_half(matmul(latent_in, cross_query)).reshape(
        groups, rows // groups, H, head_size
    )
    block_keys = to_half(matmul(block_in, cross_key)).reshape(groups, block_rows, H, head_size)
    block_values = to_half(matmul(block_in, cross_value)).reshape(groups, block_rows, H, head_size)
    attention, picked_keys, picked_values = cross_forward(
        cross_queries, block_keys, block_values, neighbours, fill, score_scale
    )
    attention_half = to_half(attention)
    cross_mixed = to_half(
        jnp.einsum(
            "ghqk,gkhd->gqhd", attention_half, picked_values, preferred_element_type=jnp.float32
        )
    ).reshape(rows, width)
    after_cross = latent_float + matmul(cross_mixed, cross_output)
    self_norm, self_pull = jax.vjp(normed, after_cross, self_gain, self_shift)
    self_in = to_half(self_norm)
    self_queries = to_half(matmul(self_in, self_query)).reshape(rows, H, head_size)
    self_keys = to_half(matmul(self_in, self_key)).reshape(rows, H, head_size)
    self_values = to_half(matmul(self_in, self_value)).reshape(rows, H, head_size)
    query_heads, key_heads, value_heads = (
        lax.all_to_all(self_queries, "lvl", split_axis=1, concat_axis=0, tiled=True),
        lax.all_to_all(self_keys, "lvl", split_axis=1, concat_axis=0, tiled=True),
        lax.all_to_all(self_values, "lvl", split_axis=1, concat_axis=0, tiled=True),
    )
    head_mixed, log_total = self_forward(query_heads, key_heads, value_heads, score_scale)
    self_mixed = lax.all_to_all(head_mixed, "lvl", split_axis=0, concat_axis=1, tiled=True).reshape(
        rows, width
    )
    after_self = after_cross + matmul(self_mixed, self_output)
    hidden_norm, hidden_pull = jax.vjp(normed, after_self, hidden_gain, hidden_shift)
    hidden_in = to_half(hidden_norm)
    pre_act = matmul(hidden_in, hidden_expand)
    activated, act_pull = jax.vjp(jax.nn.gelu, pre_act)
    act_half = to_half(activated)
    updated = to_half(after_self + matmul(act_half, hidden_reduce))
    reduce_delta = left_outer(act_half, cotangent)
    act_delta = right_outer(cotangent, hidden_reduce)
    pre_delta = to_half(act_pull(act_delta)[0])
    expand_delta = left_outer(hidden_in, pre_delta)
    hidden_delta = right_outer(pre_delta, hidden_expand)
    self_side, hidden_gain_delta, hidden_shift_delta = hidden_pull(hidden_delta)
    after_self_delta = cotangent.astype(jnp.float32) + self_side
    self_gate = to_half(after_self_delta)
    self_output_delta = left_outer(self_mixed, self_gate)
    mixed_delta = to_half(right_outer(self_gate, self_output)).reshape(rows, H, head_size)
    head_delta = lax.all_to_all(mixed_delta, "lvl", split_axis=1, concat_axis=0, tiled=True)
    query_back, key_back, value_back = self_backward(
        query_heads, key_heads, value_heads, head_delta, log_total, score_scale
    )
    query_local, key_local, value_local = (
        lax.all_to_all(query_back, "lvl", split_axis=0, concat_axis=1, tiled=True),
        lax.all_to_all(key_back, "lvl", split_axis=0, concat_axis=1, tiled=True),
        lax.all_to_all(value_back, "lvl", split_axis=0, concat_axis=1, tiled=True),
    )
    query_local = query_local.reshape(rows, width)
    key_local = key_local.reshape(rows, width)
    value_local = value_local.reshape(rows, width)
    self_query_delta = left_outer(self_in, query_local)
    self_key_delta = left_outer(self_in, key_local)
    self_value_delta = left_outer(self_in, value_local)
    self_delta = (
        right_outer(query_local, self_query)
        + right_outer(key_local, self_key)
        + right_outer(value_local, self_value)
    )
    cross_side, self_gain_delta, self_shift_delta = self_pull(self_delta)
    after_cross_delta = after_self_delta + cross_side
    cross_gate = to_half(after_cross_delta)
    cross_output_delta = left_outer(cross_mixed, cross_gate)
    cross_delta = to_half(right_outer(cross_gate, cross_output)).reshape(
        groups, rows // groups, H, head_size
    )
    weight_delta = jnp.einsum(
        "gqhd,gkhd->ghqk", cross_delta, picked_values, preferred_element_type=jnp.float32
    )
    picked_value_delta = jnp.einsum(
        "ghqk,gqhd->gkhd", attention_half, cross_delta, preferred_element_type=jnp.float32
    )
    score_delta = to_half(
        attention * (weight_delta - jnp.sum(attention * weight_delta, axis=-1, keepdims=True))
    )
    cross_query_back = to_half(
        jnp.einsum("ghqk,gkhd->gqhd", score_delta, picked_keys, preferred_element_type=jnp.float32)
        * score_scale
    ).reshape(rows, width)
    picked_key_delta = (
        jnp.einsum(
            "ghqk,gqhd->gkhd", score_delta, cross_queries, preferred_element_type=jnp.float32
        )
        * score_scale
    )
    chosen = (
        neighbours.reshape(groups * reads)[:, None] == jnp.arange(groups, dtype=jnp.int32)[None, :]
    ).astype(jnp.float32)
    key_rows = picked_key_delta.reshape(groups * reads, block_rows * width)
    value_rows = picked_value_delta.reshape(groups * reads, block_rows * width)
    block_key_back = to_half(left_outer_exact(chosen, key_rows)).reshape(groups * block_rows, width)
    block_value_back = to_half(left_outer_exact(chosen, value_rows)).reshape(
        groups * block_rows, width
    )
    cross_query_delta = left_outer(latent_in, cross_query_back)
    cross_key_delta = left_outer(block_in, block_key_back)
    cross_value_delta = left_outer(block_in, block_value_back)
    block_side = right_outer(block_key_back, cross_key) + right_outer(block_value_back, cross_value)
    block_input_delta, block_gain_delta, block_shift_delta = block_pull(block_side)
    latent_side = right_outer(cross_query_back, cross_query)
    latent_input_delta, latent_gain_delta, latent_shift_delta = latent_pull(latent_side)
    latent_delta = to_half(after_cross_delta + latent_input_delta)
    block_delta = to_half(block_input_delta).reshape(groups, block_rows, width)
    summed = (
        lax.psum_scatter(latent_gain_delta, ("grp", "lvl"), scatter_dimension=0, tiled=True),
        lax.psum_scatter(latent_shift_delta, ("grp", "lvl"), scatter_dimension=0, tiled=True),
        lax.psum_scatter(block_gain_delta, ("grp", "lvl"), scatter_dimension=0, tiled=True),
        lax.psum_scatter(block_shift_delta, ("grp", "lvl"), scatter_dimension=0, tiled=True),
        lax.psum_scatter(cross_query_delta, ("grp", "lvl"), scatter_dimension=0, tiled=True),
        lax.psum_scatter(cross_key_delta, ("grp", "lvl"), scatter_dimension=0, tiled=True),
        lax.psum_scatter(cross_value_delta, ("grp", "lvl"), scatter_dimension=0, tiled=True),
        lax.psum_scatter(cross_output_delta, ("grp", "lvl"), scatter_dimension=0, tiled=True),
        lax.psum_scatter(self_gain_delta, ("grp", "lvl"), scatter_dimension=0, tiled=True),
        lax.psum_scatter(self_shift_delta, ("grp", "lvl"), scatter_dimension=0, tiled=True),
        lax.psum_scatter(self_query_delta, ("grp", "lvl"), scatter_dimension=0, tiled=True),
        lax.psum_scatter(self_key_delta, ("grp", "lvl"), scatter_dimension=0, tiled=True),
        lax.psum_scatter(self_value_delta, ("grp", "lvl"), scatter_dimension=0, tiled=True),
        lax.psum_scatter(self_output_delta, ("grp", "lvl"), scatter_dimension=0, tiled=True),
        lax.psum_scatter(hidden_gain_delta, ("grp", "lvl"), scatter_dimension=0, tiled=True),
        lax.psum_scatter(hidden_shift_delta, ("grp", "lvl"), scatter_dimension=0, tiled=True),
        lax.psum_scatter(expand_delta, ("grp", "lvl"), scatter_dimension=0, tiled=True),
        lax.psum_scatter(reduce_delta, ("grp", "lvl"), scatter_dimension=0, tiled=True),
    )
    return (
        updated,
        latent_delta,
        block_delta,
        summed[0],
        summed[1],
        summed[2],
        summed[3],
        summed[4],
        summed[5],
        summed[6],
        summed[7],
        summed[8],
        summed[9],
        summed[10],
        summed[11],
        summed[12],
        summed[13],
        summed[14],
        summed[15],
        summed[16],
        summed[17],
    )


def left_outer_exact(left_side, right_side):
    return lax.dot_general(
        left_side,
        right_side,
        (((0,), (0,)), ((), ())),
        precision=lax.Precision.HIGHEST,
        preferred_element_type=jnp.float32,
    )

def fits(shape, latents, hidden_expand):
    n_dev = shape["grp"] * shape["lvl"]
    return (
        shape["grp"] == 8
        and shape["lvl"] == 4
        and latents.shape[1] % (16 * n_dev) == 0
        and hidden_expand.shape[1] % (128 * n_dev) == 0
    )


def on_device(shape, *args):
    return (tiled if fits(shape, args[0], args[21]) else plain)(*args)


def solution(mesh):
    placed = (
        P(("grp", "lvl"), None),
        P(("grp", "lvl"), None, None),
        P(("grp", "lvl"), None),
        P(("grp", "lvl")),
        P(("grp", "lvl"), None),
        P(),
        P(),
        P(),
        P(),
        P(),
        P(),
        P(),
        P(),
        P(),
        P(),
        P(),
        P(),
        P(),
        P(),
        P(),
        P(),
        P(),
        P(),
    )
    return jax.shard_map(
        functools.partial(on_device, mesh.shape),
        mesh=mesh,
        in_specs=placed,
        out_specs=(
            P(("grp", "lvl"), None),
            P(("grp", "lvl"), None),
            P(("grp", "lvl"), None, None),
            P(("grp", "lvl")),
            P(("grp", "lvl")),
            P(("grp", "lvl")),
            P(("grp", "lvl")),
            P(("grp", "lvl"), None),
            P(("grp", "lvl"), None),
            P(("grp", "lvl"), None),
            P(("grp", "lvl"), None),
            P(("grp", "lvl")),
            P(("grp", "lvl")),
            P(("grp", "lvl"), None),
            P(("grp", "lvl"), None),
            P(("grp", "lvl"), None),
            P(("grp", "lvl"), None),
            P(("grp", "lvl")),
            P(("grp", "lvl")),
            P(("grp", "lvl"), None),
            P(("grp", "lvl"), None),
        ),
        check_vma=False,
    )
```

```python
import functools

import jax
import jax.numpy as jnp
from jax import lax
from jax.experimental import pallas as pl
from jax.experimental.pallas import tpu as pltpu
from jax.sharding import PartitionSpec as P

H = 8


EPS = 1e-05
NEG = -1e30
BF = jnp.bfloat16
F32 = jnp.float32
VMEM_MB = 30
V = True
LOG2_E = 1.4426950408889634
SQRT_2_PI = 0.7978845608028654
CUBIC = 0.044715


def count_bias(times):
    return jnp.where(times > 0.0, jnp.log(jnp.maximum(times, 1.0)) * LOG2_E, NEG)


def nn(a, b):
    return lax.dot_general(a, b, (((1,), (0,)), ((), ())), preferred_element_type=F32)


def nt(a, b):
    return lax.dot_general(a, b, (((1,), (1,)), ((), ())), preferred_element_type=F32)


def tn(a, b):
    return lax.dot_general(a, b, (((0,), (0,)), ((), ())), preferred_element_type=F32)


def flip(v):
    return jnp.transpose(v)


def hat(v):
    center = v - jnp.mean(v, axis=-1, keepdims=True)
    scale = lax.rsqrt(jnp.mean(center * center, axis=-1, keepdims=True) + EPS)
    return center * scale, scale


def norm_back(dy, v, gain):
    unit, scale = hat(v)
    t = dy * gain
    side = scale * (
        t
        - jnp.mean(t, axis=-1, keepdims=True)
        - unit * jnp.mean(t * unit, axis=-1, keepdims=True)
    )
    return side, jnp.sum(dy * unit, axis=0, keepdims=True), jnp.sum(dy, axis=0, keepdims=True)


def gelu_parts(x):
    square = x * x
    t = jnp.tanh(SQRT_2_PI * x * (1.0 + CUBIC * square))
    half = 0.5 + 0.5 * t
    act = x * half
    slope = half + (0.5 * SQRT_2_PI) * x * (1.0 - t * t) * (1.0 + (3.0 * CUBIC) * square)
    return act, slope


def counts_by_row(nb, fill, rows, groups, block_rows, reads):
    keys = groups * block_rows
    key = lax.broadcasted_iota(jnp.int32, (rows, keys), 1)
    row = lax.broadcasted_iota(jnp.int32, (rows, keys), 0)
    per = rows // groups
    out = jnp.zeros((rows, keys), F32)
    for g in range(groups):
        for m in range(groups):
            times = jnp.int32(0)
            for n in range(reads):
                times = times + (nb[g, n] == m).astype(jnp.int32)
            live = (key >= m * block_rows) & (key < m * block_rows + fill[m])
            here = live & (row >= g * per) & (row < (g + 1) * per)
            out = jnp.where(here, times.astype(F32), out)
    return out


def counts_by_key(nb, fill, rows, groups, block_rows, reads):
    keys = groups * block_rows
    key = lax.broadcasted_iota(jnp.int32, (keys, rows), 0)
    row = lax.broadcasted_iota(jnp.int32, (keys, rows), 1)
    per = rows // groups
    out = jnp.zeros((keys, rows), F32)
    for g in range(groups):
        for m in range(groups):
            times = jnp.int32(0)
            for n in range(reads):
                times = times + (nb[g, n] == m).astype(jnp.int32)
            live = (key >= m * block_rows) & (key < m * block_rows + fill[m])
            here = live & (row >= g * per) & (row < (g + 1) * per)
            out = jnp.where(here, times.astype(F32), out)
    return out


def whole(shape):
    zeros = (0,) * len(shape)
    return pl.BlockSpec(shape, lambda i, *_: zeros)


def near_core(array):
    return pltpu.with_memory_space_constraint(array, pltpu.VMEM)


def far_off(array):
    return pltpu.with_memory_space_constraint(array, pltpu.HBM)


def call(kernel, name, grid, scalars, ins, outs, scratch, vmem=VMEM_MB, after=(), flops=1):
    first = len(scalars) + len(ins)

    def body(*refs):
        kernel(*refs[:first], *refs[first + len(after) :])

    arrays = [near_core(item[0]) if len(item) > 2 else far_off(item[0]) for item in ins]
    shapes = [(pltpu.VMEM if len(item) > 3 else pltpu.HBM)(item[0], item[1]) for item in outs]
    return pl.pallas_call(
        body,
        name=name,
        grid_spec=pltpu.PrefetchScalarGridSpec(
            num_scalar_prefetch=len(scalars),
            grid=(grid,),
            in_specs=[item[1] for item in ins] + [pl.BlockSpec(memory_space=pl.ANY)] * len(after),
            out_specs=[item[2] for item in outs],
            scratch_shapes=scratch,
        ),
        out_shape=shapes,
        compiler_params=pltpu.CompilerParams(
            vmem_limit_bytes=vmem * 1024 * 1024, dimension_semantics=("arbitrary",)
        ),
        cost_estimate=pl.CostEstimate(flops=flops, bytes_accessed=1, transcendentals=0),
    )(*scalars, *arrays, *after)


def tie(array, after):
    spec = pl.BlockSpec(memory_space=pl.ANY)
    array = near_core(array)
    return pl.pallas_call(
        lambda *refs: None,
        name="tie",
        in_specs=[spec] * (1 + len(after)),
        out_specs=spec,
        out_shape=pltpu.VMEM(array.shape, array.dtype),
        input_output_aliases={0: 0},
        compiler_params=pltpu.CompilerParams(vmem_limit_bytes=1024 * 1024),
        cost_estimate=pl.CostEstimate(flops=1, bytes_accessed=1, transcendentals=0),
    )(array, *after)


def cross_forward_kernel(
    groups, reads, nb, fill, lat, blk, lg, lb, bg, bb, sg, sb, wq, wk, wv, wo,
    cq, ck, cv, co, ac, self_in, lat_in, blk_in, acc, cnt,
):
    i = pl.program_id(0)
    rows, width = lat.shape
    keys = blk.shape[0]
    scale = (width // H) ** -0.5
    head = width // H

    @pl.when(i == 0)
    def _():
        lat_in[...] = (hat(lat[...].astype(F32))[0] * lg[...] + lb[...]).astype(BF)
        blk_in[...] = (hat(blk[...].astype(F32))[0] * bg[...] + bb[...]).astype(BF)
        acc[...] = lat[...].astype(F32)
        cnt[...] = count_bias(counts_by_row(nb, fill, rows, groups, keys // groups, reads))

    q = nn(lat_in[...], wq[...]).astype(BF)
    k = nn(blk_in[...], wk[...]).astype(BF)
    v = nn(blk_in[...], wv[...]).astype(BF)
    cq[...] = q
    ck[...] = k
    cv[...] = v
    bias = cnt[...]
    mixed = []
    for h in range(q.shape[1] // head):
        cut = slice(h * head, (h + 1) * head)
        s = nt(q[:, cut], k[:, cut]) * (scale * LOG2_E) + bias
        e = jnp.exp2(s - jnp.max(s, axis=-1, keepdims=True))
        p = (e * (1.0 / jnp.sum(e, axis=-1, keepdims=True))).astype(BF)
        mixed.append(nn(p, v[:, cut]).astype(BF))
    mixed = jnp.concatenate(mixed, axis=1)
    co[...] = mixed
    acc[...] += nn(mixed, wo[...])

    @pl.when(i == pl.num_programs(0) - 1)
    def _():
        after = acc[...]
        ac[...] = after
        self_in[...] = (hat(after)[0] * sg[...] + sb[...]).astype(BF)


def flip_rows_kernel(plan, orders, ids, *refs):
    n = 1 + max(src for src, _ in plan)
    ins, outs, tmp = refs[:n], refs[n : n + len(plan)], refs[n + len(plan) :]
    for src, t in zip(ins, tmp, strict=True):
        t[...] = flip(src[...])
    for dst, (src, which) in zip(outs, plan, strict=True):
        t = tmp[src]
        size = t.shape[0] // len(orders[which])
        for p, distance in enumerate(orders[which]):
            at = pl.multiple_of((ids[2] ^ distance) * size, size)
            dst[p * size : (p + 1) * size, :] = t[pl.ds(at, size), :]


def self_forward_kernel(ids, a0, a1, a2, a3, wq, wk, wv, q, k, v, o0, o1, o2):
    rows, width = a0.shape
    head = width // H
    scale = head**-0.5
    for j, a in enumerate((a0, a1, a2, a3)):
        here = slice(j * rows, (j + 1) * rows)
        x = a[...]
        q[here, :] = nn(x, wq[...]).astype(BF)
        k[here, :] = nn(x, wk[...]).astype(BF)
        v[here, :] = nn(x, wv[...]).astype(BF)
    for t in range(2):
        mixed = []
        for h in range(q.shape[1] // head):
            cut = slice(h * head, (h + 1) * head)
            s = nt(q[2 * t * rows : 2 * (t + 1) * rows, cut], k[:, cut])
            e = jnp.exp2((s - jnp.max(s, axis=-1, keepdims=True)) * (scale * LOG2_E))
            p = (e * (1.0 / jnp.sum(e, axis=-1, keepdims=True))).astype(BF)
            mixed.append(nn(p, v[:, cut]).astype(BF))
        mixed = jnp.concatenate(mixed, axis=1)
        if t == 0:
            o0[...] = mixed[:rows]
            o1[...] = mixed[rows:]
        else:
            o2[...] = mixed


def self_out_kernel(ids, ac, o0, o1, o2, o3, wo, hg, hb, after, hidden_in, so):
    cols = o0.shape[1]
    for j, o in enumerate((o0, o1, o2, o3)):
        at = pl.multiple_of((ids[1] ^ j) * cols, cols)
        so[:, pl.ds(at, cols)] = o[...]
    v = ac[...] + nn(so[...], wo[...])
    after[...] = v
    hidden_in[...] = (hat(v)[0] * hg[...] + hb[...]).astype(BF)


def cot_back_kernel(gy, wred, out):
    out[...] = nt(gy[...], wred[...])


def cot_units_kernel(ids, *refs):
    gs, wexp, wred = refs[:8], refs[8:12], refs[12:16]
    own, other, we, wr = refs[16:]
    unit = wexp[0].shape[1]
    for q in range(4):
        we[q * unit : (q + 1) * unit, :] = flip(wexp[q][...])
        wr[q * unit : (q + 1) * unit, :] = wred[q][...]
    rows = gs[0].shape[0]
    for k, g in enumerate(gs):
        out = own if k < 4 else other
        at = (k % 4) * rows
        out[:, at : at + rows] = nt(wr[...], g[...])


def ff_local_kernel(hidden_in, gy, after, hg, dact, wexp, act_out, gate, das, vecs, dh):
    i = pl.program_id(0)

    @pl.when(i == 0)
    def _():
        dh[...] = jnp.zeros_like(dh)

    act, slope = gelu_parts(nn(hidden_in[...], wexp[...]))
    act_out[...] = act.astype(BF)
    dh[...] += nt((dact[...] * slope).astype(BF), wexp[...])

    @pl.when(i == pl.num_programs(0) - 1)
    def _():
        side, dg, db = norm_back(dh[...], after[...], hg[...])
        total = gy[...].astype(F32) + side
        das[...] = total
        gate[...] = total.astype(BF)
        vecs[0:1, :] = dg
        vecs[1:2, :] = db


def updated_kernel(act, wred, after, out, total):
    i = pl.program_id(0)

    @pl.when(i == 0)
    def _():
        total[...] = after[...]

    total[...] += nn(act[...], wred[...])

    @pl.when(i == pl.num_programs(0) - 1)
    def _():
        out[...] = total[...].astype(BF)


def ff_sums(we, dact, h, g, red, exp, fresh):
    act, slope = gelu_parts(nt(we[...], h))
    dpre = (dact * slope).astype(BF)
    if fresh:
        red[...] = nn(act.astype(BF), g)
        exp[...] = nn(dpre, h)
    else:
        red[...] += nn(act.astype(BF), g)
        exp[...] += nn(dpre, h)


def ff_tokens(refs, dact, we, red, exp, h_all, g_all, sem, fresh):
    hs, gs = refs[:4], refs[4:8]
    rows = hs[0].shape[0]
    copies = [
        pltpu.make_async_copy(piece, dst.at[pl.ds(k * rows, rows)], sem.at[which, k])
        for which, (src, dst) in enumerate(((hs, h_all), (gs, g_all)))
        for k, piece in enumerate(src)
    ]
    for c in copies:
        c.start()
    for t in range(2):
        for k in (2 * t, 2 * t + 1, 2 * t + 4, 2 * t + 5):
            copies[k].wait()
        here = slice(2 * t * rows, 2 * (t + 1) * rows)
        ff_sums(we, dact[:, here], h_all[here, :], g_all[here, :], red, exp, fresh and t == 0)


def ff_weights_a_kernel(*refs):
    dact, we, red, exp, h_all, g_all, sem = refs[8:]
    ff_tokens(refs, dact, we, red, exp, h_all, g_all, sem, True)


def ff_weights_b_kernel(ids, *refs):
    red_in, exp_in, dact, we, keep, send, red, exp, h_all, g_all, sem = refs[8:]
    red[...] = red_in[...]
    exp[...] = exp_in[...]
    ff_tokens(refs, dact, we, red, exp, h_all, g_all, sem, False)
    unit = we.shape[0] // 4
    half = 2 * unit
    width = red.shape[1]
    keep[:, 0:width] = red[0:half, :].astype(BF)
    send[:, 0:width] = red[half:, :].astype(BF)
    span = width // 8
    for p in range(4):
        out = keep if p < 2 else send
        low = (p % 2) * unit
        for q in range(4):
            for z in range(2):
                lanes = pl.ds(pl.multiple_of((ids[8 + p] + 2 * z) * span, span), span)
                to = pl.ds(pl.multiple_of(width + (2 * ids[12 + q] + z) * span, span), span)
                out[low : low + unit, to] = exp[q * unit : (q + 1) * unit, lanes].astype(BF)


def self_backward_kernel(
    ids, g0, g1, g2, g3, q, k, v, wo, wq, wk, wv, flipped, keep, send, do, dq, dk, dv
):
    rows, width = g0.shape
    head = width // H
    scale = head**-0.5
    for j, g in enumerate((g0, g1, g2, g3)):
        do[j * rows : (j + 1) * rows, :] = nt(g[...], wo[...]).astype(BF)
    cols = q.shape[1]
    tile = 512
    for h in range(cols // head):
        cut = slice(h * head, (h + 1) * head)
        kh = k[:, cut]
        vh = v[:, cut]
        kt = flip(kh)
        key_sum = jnp.zeros((k.shape[0], head), F32)
        value_sum = jnp.zeros((k.shape[0], head), F32)
        for t in range(q.shape[0] // tile):
            here = slice(t * tile, (t + 1) * tile)
            qt = q[here, cut]
            dt = do[here, cut]
            s = nt(kh, qt)
            e = jnp.exp2((s - jnp.max(s, axis=0, keepdims=True)) * (scale * LOG2_E))
            p = e * (1.0 / jnp.sum(e, axis=0, keepdims=True))
            dp = nt(vh, dt)
            ds = (p * (dp - jnp.sum(p * dp, axis=0, keepdims=True))).astype(BF)
            value_sum += nn(p.astype(BF), dt)
            key_sum += nn(ds, qt)
            back = (nn(kt, ds) * scale).astype(BF)
            flipped[cut, here] = back
            dq[here, cut] = flip(back)
        dk[:, cut] = (key_sum * scale).astype(BF)
        dv[:, cut] = value_sum.astype(BF)
    flipped[cols : 2 * cols, :] = flip(dk[...])
    flipped[2 * cols : 3 * cols, :] = flip(dv[...])
    for j in range(4):
        here = slice(j * rows, (j + 1) * rows)
        side = nt(dq[here, :], wq[...]) + nt(dk[here, :], wk[...]) + nt(dv[here, :], wv[...])
        out = send if j % 2 else keep
        low = (j // 2) * rows
        out[low : low + rows, :] = side.astype(BF)


def self_weights_kernel(ids, flipped, *refs):
    ins, gates, mixed = refs[0:4], refs[4:8], refs[8:12]
    keep, send, total = refs[12:]
    rows = ins[0].shape[0]
    three = flipped.shape[0]
    for low, high, parts in (
        (0, three, [(flipped[:, j * rows : (j + 1) * rows], ins[j][...]) for j in range(4)]),
        (three, total.shape[0], [(flip(gates[j][...]), mixed[j][...]) for j in range(4)]),
    ):
        acc = None
        for left, right in parts:
            part = nn(left, right)
            acc = part if acc is None else acc + part
        total[low:high, :] = acc
    depth, span = total.shape[0], keep.shape[1]
    blocks = total.shape[1] // span
    for p in range(blocks):
        out = keep if p < blocks // 2 else send
        low = (p % (blocks // 2)) * depth
        lanes = pl.ds(pl.multiple_of(ids[16 + p] * span, span), span)
        out[low : low + depth, :] = total[:, lanes].astype(BF)


def cross_backward_kernel(
    groups, reads, nb, fill, keep, rcv, xr, das, ac, sg, wo, cq, ck, cv, gate, dq, dk, dv, dac, vecs, cnt,
):
    i = pl.program_id(0)
    rows, width = das.shape
    keys = ck.shape[0]
    head = width // H
    scale = head**-0.5

    @pl.when(i == 0)
    def _():
        dy = keep[...].astype(F32) + rcv[...].astype(F32) + xr[...].astype(F32)
        side, dg, db = norm_back(dy, ac[...], sg[...])
        total = das[...] + side
        dac[...] = total
        gate[...] = total.astype(BF)
        vecs[0:1, :] = dg
        vecs[1:2, :] = db
        cnt[...] = count_bias(counts_by_key(nb, fill, rows, groups, keys // groups, reads))

    do = nt(gate[...], wo[...]).astype(BF)
    bias = cnt[...]
    for h in range(cq.shape[1] // head):
        cut = slice(h * head, (h + 1) * head)
        qh = cq[:, cut]
        kh = ck[:, cut]
        dh = do[:, cut]
        s = nt(kh, qh) * (scale * LOG2_E) + bias
        e = jnp.exp2(s - jnp.max(s, axis=0, keepdims=True))
        p = e * (1.0 / jnp.sum(e, axis=0, keepdims=True))
        dp = nt(cv[:, cut], dh)
        ds = (p * (dp - jnp.sum(p * dp, axis=0, keepdims=True))).astype(BF)
        dv[:, cut] = nn(p.astype(BF), dh).astype(BF)
        dk[:, cut] = (nn(ds, qh) * scale).astype(BF)
        dq[:, cut] = flip((nn(flip(kh), ds) * scale).astype(BF))


def cross_inputs_kernel(
    ids, dq, dk, dv, wq, wk, wv, lat, blk, lg, bg, dac, sv, hv, dlat, dblk, keep, send, la, ba, vecs
):
    i = pl.program_id(0)

    @pl.when(i == 0)
    def _():
        la[...] = jnp.zeros_like(la)
        ba[...] = jnp.zeros_like(ba)

    la[...] += nt(dq[...], wq[...])
    ba[...] += nt(dk[...], wk[...]) + nt(dv[...], wv[...])

    @pl.when(i == pl.num_programs(0) - 1)
    def _():
        side, dg, db = norm_back(la[...], lat[...].astype(F32), lg[...])
        dlat[...] = (dac[...] + side).astype(BF)
        vecs[0:1, :] = dg
        vecs[1:2, :] = db
        side, dg, db = norm_back(ba[...], blk[...].astype(F32), bg[...])
        dblk[...] = side.astype(BF)
        vecs[2:3, :] = dg
        vecs[3:4, :] = db
        vecs[4:6, :] = sv[...]
        vecs[6:8, :] = hv[...]
        count, span = vecs.shape[0], keep.shape[1]
        for p in range(4):
            out = keep if p < 2 else send
            parts = [
                vecs[:, pl.ds(pl.multiple_of((ids[8 + p] + 2 * z) * span, span), span)] for z in range(2)
            ]
            low = (p % 2) * 2 * count
            out[low : low + 2 * count, :] = jnp.concatenate(parts, axis=0).astype(BF)


def stack_sum_kernel(kept, got, vec_keep, vec_send, keep, send):
    rows = kept.shape[0] // 4
    more = vec_keep.shape[0] // 2
    for p in range(4):
        out, vecs = (keep, vec_keep) if p < 2 else (send, vec_send)
        low = (p % 2) * (rows + more)
        here = slice(p * rows, (p + 1) * rows)
        out[low : low + rows, :] = (kept[here, :].astype(F32) + got[here, :].astype(F32)).astype(BF)
        out[low + rows : low + rows + more, :] = vecs[(p % 2) * more : (p % 2 + 1) * more, :]


def cross_weights_kernel(*refs):
    n = (len(refs) - 2) // 2
    lefts, rights, outs = refs[:n], refs[n : 2 * n], refs[2 * n :]
    for k, (left, right) in enumerate(zip(lefts, rights, strict=True)):
        width = right.shape[1]
        outs[k // 2][:, (k % 2) * width : (k % 2 + 1) * width] = nn(left[...], right[...]).astype(BF)


def combine_kernel(terms, *refs):
    total = sum(sum(parts) for parts in terms)
    ins, outs = refs[: 2 * total], refs[2 * total :]
    n = 0
    for k, parts in enumerate(terms):
        at = 0
        for count in parts:
            tops, lows = ins[n : n + 2 * count : 2], ins[n + 1 : n + 2 * count : 2]
            width = tops[0].shape[1]
            for out, refs_ in ((outs[2 * k], tops), (outs[2 * k + 1], lows)):
                acc = refs_[0][...].astype(F32)
                for ref in refs_[1:]:
                    acc = acc + ref[...].astype(F32)
                out[:, at : at + width] = acc.astype(BF)
            at += width
            n += 2 * count


def combine(name, chains, steps, after=(), parts_of=1, flops=1):
    ins, outs = [], []
    for parts in chains:
        total = 0
        for terms in parts:
            for term in terms:
                a, k = term if parts_of > 1 else (term, 0)
                depth, width = a.shape[0], a.shape[1] // parts_of
                part = depth // 2 // steps
                top = pl.BlockSpec((part, width), lambda i, k=k: (i, k))
                low = pl.BlockSpec((part, width), lambda i, k=k: (i + steps, k))
                ins += [(a, top, V), (a, low, V)]
            total += width
        outs += [((depth // 2, total), BF, pl.BlockSpec((part, total), lambda i: (i, 0)), V)] * 2
    counts = tuple(tuple(len(terms) for terms in parts) for parts in chains)
    out = call(
        functools.partial(combine_kernel, counts), name, steps, [], ins, outs, [], after=after, flops=flops
    )
    return [tuple(out[2 * k : 2 * k + 2]) for k in range(len(chains))]


def copy_kernel(a, out):
    out[...] = a[...]


def add_kernel(a, b, out):
    out[...] = (a[...].astype(F32) + b[...].astype(F32)).astype(BF)


def pack_kernel(ff_kept, ff_got, set_kept, set_got, reduce_delta, out):
    unit, width = reduce_delta.shape
    reduce_delta[...] = ff_kept[:, 0:width].astype(F32) + ff_got[:, 0:width].astype(F32)
    rest = ff_kept[:, width:].astype(F32) + ff_got[:, width:].astype(F32)
    devices, chunk, _ = out.shape
    span = devices * chunk
    parts = width // span
    for q in range(parts):
        t = flip(rest[:, q * span : (q + 1) * span]).astype(BF)
        for d in range(devices):
            out[d, :, q * unit : (q + 1) * unit] = t[d * chunk : (d + 1) * chunk, :]
    total = set_kept[...].astype(F32) + set_got[...].astype(F32)
    count = 8
    cols = total.shape[0] - 2 * count
    t = flip(total[:cols, :]).astype(BF)
    n_set = t.shape[0] // chunk
    lanes = out.shape[2] - parts * unit - cols
    blank = jnp.zeros((chunk - count, lanes), F32)
    for d in range(devices):
        at = (d % n_set) * chunk
        out[d, :, parts * unit : parts * unit + cols] = t[at : at + chunk, :]
        low = cols + (d // n_set) * count
        mine = jnp.concatenate([total[low : low + count, :], blank], axis=0)
        out[d, :, parts * unit + cols :] = mine.astype(BF)


def place_kernel(unit, n_set, ids, got, expand, *rest):
    outs, turned = rest[:-1], rest[-1]
    devices, chunk, width = got.shape
    parts = expand.shape[1] // (devices * unit)
    for q in range(parts):
        for d in range(devices):
            at = ((q // 2) * 2 * devices + (d // n_set) * devices + (q % 2) * n_set + d % n_set) * unit
            expand[:, at : at + unit] = got[d, :, q * unit : (q + 1) * unit].astype(F32)
    outs, vecs = outs[:4], outs[4:]
    lanes = width - parts * unit - 4 * outs[0].shape[1] // n_set
    cols = outs[0].shape[1] // n_set
    for d in range(n_set):
        mine = got[ids[3] * n_set + d]
        for m, out in enumerate(outs):
            at = parts * unit + m * cols
            out[:, d * cols : (d + 1) * cols] = mine[:, at : at + cols].astype(F32)
    total = jnp.zeros((chunk, lanes), F32)
    for d in range(devices):
        total += got[d, :, width - lanes :].astype(F32)
    turned[...] = flip(jnp.concatenate([total, jnp.zeros((lanes - chunk, lanes), F32)], axis=0))
    total = flip(turned[pl.ds(pl.multiple_of(ids[1] * chunk, chunk), chunk), :])
    for k, out in enumerate(vecs):
        out[...] = total[k : k + 1, :]


def cross_last_kernel(parts, n, *refs):
    ins, outs = refs[: 2 * n], refs[2 * n :]
    for chain, members in enumerate(parts):
        total = ins[2 * chain][...].astype(F32) + ins[2 * chain + 1][...].astype(F32)
        at = 0
        for which, cols in members:
            outs[which][...] = total[:, at : at + cols]
            at += cols


def swap(values, axis, bit):
    size = lax.axis_size(axis)
    return lax.ppermute(values, axis, [(i, i ^ bit) for i in range(size)])


CORE = ("lvl", 1)
ACROSS = ("lvl", 2)
BESIDE = ("grp", 1)
NEAR = ("grp", 2)
FAR = ("grp", 4)


def gather_set(own, wait=lambda across: across):
    across = wait(swap(own, *ACROSS))
    return own, swap(own, *CORE), across, swap(across, *CORE)


def places(links, n_lvl):
    weights = [bit * (n_lvl if axis == "grp" else 1) for axis, bit in links]
    n = len(weights)
    return [
        sum(w for k, w in enumerate(weights) if p >> (n - 1 - k) & 1) for p in range(1 << n)
    ]


CHAINS = (
    (CORE, ACROSS, BESIDE, NEAR, FAR),
    (CORE, BESIDE, NEAR, ACROSS, FAR),
    (CORE, NEAR, ACROSS, FAR, BESIDE),
)


def tiled(
    latents, blocks, neighbours, fill, cotangent,
    latent_gain, latent_shift, block_gain, block_shift,
    cross_query, cross_key, cross_value, cross_output,
    self_gain, self_shift, self_query, self_key, self_value, self_output,
    hidden_gain, hidden_shift, hidden_expand, hidden_reduce,
):
    rows, width = latents.shape
    groups, block_rows, _ = blocks.shape
    keys = groups * block_rows
    reads = neighbours.shape[1]
    hidden = hidden_expand.shape[1]
    n_grp, n_lvl = lax.axis_size("grp"), lax.axis_size("lvl")
    n_dev = n_grp * n_lvl
    n_plane = 2 * n_lvl
    g = lax.axis_index("grp").astype(jnp.int32)
    l = lax.axis_index("lvl").astype(jnp.int32)
    me = g * n_lvl + l
    per = n_lvl
    steps = [0, FAR[1], BESIDE[1], FAR[1] | BESIDE[1]]
    bare = g & ~NEAR[1]
    ids = jnp.stack(
        [g, l, me, (g & NEAR[1]) // NEAR[1]]
        + [me ^ (p * per) for p in steps]
        + [bare ^ p for p in steps]
        + [((bare ^ p) // FAR[1]) * 2 + ((bare ^ p) & 1) for p in steps]
        + [g ^ p for p in (0, 4, 1, 5, 2, 6, 3, 7)]
    ).astype(jnp.int32)
    orders = tuple(tuple(places(links, n_lvl)) for links in CHAINS)
    unit = hidden // n_dev
    chunk = width // n_dev

    vec = lambda v: v.reshape(1, width)
    vspec = whole((1, width))
    scalars = pl.BlockSpec(memory_space=pltpu.SMEM)
    blk = blocks.reshape(keys, width)
    pair = width // 4
    cols = pl.BlockSpec((width, pair), lambda i, *_: (0, i))
    rspec = pl.BlockSpec((pair, width), lambda i, *_: (i, 0))
    mine = pl.BlockSpec((width, pair), lambda i, ids: (0, ids[1]))
    mine_rows = pl.BlockSpec((pair, width), lambda i, ids: (ids[1], 0))
    row_full = whole((rows, width))
    key_full = whole((keys, width))
    row_part = pl.BlockSpec((rows, pair), lambda i, *_: (0, i))
    key_part = pl.BlockSpec((keys, pair), lambda i, *_: (0, i))
    set_rows = n_lvl * rows

    full = lambda a: whole(a.shape)
    cot_across, cot_near = swap(cotangent, *ACROSS), swap(cotangent, *NEAR)

    cq, ck, cv, co, after_cross, self_in, latent_in, block_in = call(
        functools.partial(cross_forward_kernel, groups, reads),
        "cross_forward", 4, [],
        [(neighbours, scalars), (fill, scalars), (latents, row_full), (blk, key_full)]
        + [(vec(v), vspec) for v in (latent_gain, latent_shift, block_gain, block_shift, self_gain, self_shift)]
        + [(cross_query, cols), (cross_key, cols), (cross_value, cols), (cross_output, rspec)],
        [
            ((rows, width), BF, row_part), ((keys, width), BF, key_part),
            ((keys, width), BF, key_part), ((rows, width), BF, row_part),
            ((rows, width), F32, row_full), ((rows, width), BF, row_full, V),
            ((rows, width), BF, row_full), ((keys, width), BF, key_full),
        ],
        [pltpu.VMEM((rows, width), F32), pltpu.VMEM((rows, keys), F32)],
        after=[ids],
    )

    set_of = lambda pieces: [(a, whole((rows, width)), V) for a in pieces]
    part = (set_rows, pair)
    plan = ((0, 0), (1, 1), (1, 2), (2, 0))
    sources = (latent_in, block_in, co)
    flips = call(
        functools.partial(flip_rows_kernel, plan, orders), "flip_cross", 1, [ids],
        [(a, full(a)) for a in sources],
        [(sources[k].shape[::-1], BF, whole(sources[k].shape[::-1])) for k, _ in plan],
        [pltpu.VMEM(a.shape[::-1], BF) for a in sources],
    )
    cot_corner = swap(cot_across, *NEAR)
    (dact,) = call(
        cot_back_kernel, "cot_back", 4, [],
        [(cotangent, row_full), (hidden_reduce, pl.BlockSpec((hidden // 4, width), lambda i: (i, 0)))],
        [((rows, hidden), F32, pl.BlockSpec((rows, hidden // 4), lambda i: (0, i)), V)],
        [], after=[far_off(flips[0])],
    )
    self_in = tie(self_in, [cot_across, cot_near])
    set_in = gather_set(self_in, lambda across: tie(across, [dact]))
    q, k, v, o0, o1, o2 = call(
        self_forward_kernel, "self_forward", 1, [ids],
        set_of(set_in)
        + [(self_query, mine), (self_key, mine), (self_value, mine)],
        [(part, BF, whole(part))] * 3
        + [((rows, pair), BF, whole((rows, pair)), V)] * 2
        + [((2 * rows, pair), BF, whole((2 * rows, pair)), V)],
        [],
        after=[dact],
    )

    across = swap(tie(o2, [cot_corner]), *ACROSS)
    cots = [cotangent, cot_across, cot_near, cot_corner]
    cots_core = [swap(a, *CORE) for a in cots]
    own_cot = [cotangent, cot_across, cots_core[0], cots_core[1]]
    other_cot = [cot_near, cot_corner, cots_core[2], cots_core[3]]

    def unit_cols(p):
        return pl.BlockSpec((width, unit), lambda i, ids: (0, ids[4 + p]))

    def unit_rows(p):
        return pl.BlockSpec((unit, width), lambda i, ids: (ids[4 + p], 0))

    mine_units = (4 * unit, width)
    by_token = (4 * unit, set_rows)
    dact_own, dact_other, mine_expand = call(
        cot_units_kernel, "cot_units", 1, [ids],
        [(own_cot[0], row_full)] + [(a, row_full, V) for a in own_cot[1:] + other_cot]
        + [(hidden_expand, unit_cols(p)) for p in range(4)]
        + [(hidden_reduce, unit_rows(p)) for p in range(4)],
        [(by_token, F32, whole(by_token), V)] * 2 + [(mine_units, BF, whole(mine_units), V)],
        [pltpu.VMEM(mine_units, BF)], after=[o0],
    )
    second = pl.BlockSpec((rows, pair), lambda i: (1, 0))
    (across_next,) = call(
        copy_kernel, "pass", 1, [], [(across, second, V)], [((rows, pair), BF, whole((rows, pair)), V)], [],
        after=[mine_expand],
    )
    o_spec = whole((rows, pair))
    pieces = (o0, swap(o1, *CORE), across, swap(across_next, *CORE))
    after_self, hidden_in, so = call(
        self_out_kernel, "self_out", 1, [ids],
        [(after_cross, row_full)] + [(p, o_spec, V) for p in pieces]
        + [(self_output, whole((width, width))), (vec(hidden_gain), vspec), (vec(hidden_shift), vspec)],
        [((rows, width), F32, row_full), ((rows, width), BF, row_full, V), ((rows, width), BF, row_full, V)],
        [], after=[mine_expand],
    )

    hid_across, hid_near = swap(hidden_in, *ACROSS), swap(hidden_in, *NEAR)
    step = 512
    activated, gate, after_self_delta, hidden_vecs = call(
        ff_local_kernel, "ff_local", hidden // step, [],
        [
            (hidden_in, row_full, V), (cotangent, row_full), (after_self, row_full), (vec(hidden_gain), vspec),
            (dact, pl.BlockSpec((rows, step), lambda i: (0, i)), V),
            (hidden_expand, pl.BlockSpec((width, step), lambda i: (0, i))),
        ],
        [
            ((rows, hidden), BF, pl.BlockSpec((rows, step), lambda i: (0, i))), ((rows, width), BF, row_full, V),
            ((rows, width), F32, row_full), ((2, width), F32, whole((2, width))),
        ],
        [pltpu.VMEM((rows, width), F32)],
    )
    gate = tie(gate, [hid_across, hid_near])
    hid_across = tie(hid_across, [gate])
    hid_corner = swap(hid_across, *NEAR)

    any_spec = pl.BlockSpec(memory_space=pl.ANY)

    own_hid = [hidden_in, hid_across, swap(hidden_in, *CORE), swap(hid_across, *CORE)]
    copied = [
        pltpu.VMEM((set_rows, width), BF), pltpu.VMEM((set_rows, width), BF), pltpu.SemaphoreType.DMA((2, 4)),
    ]
    ff_part = call(
        ff_weights_a_kernel, "ff_weights_a", 1, [],
        [(a, any_spec, V) for a in own_hid] + [(own_cot[0], any_spec)] + [(a, any_spec, V) for a in own_cot[1:]]
        + [(a, full(a), V) for a in (dact_own, mine_expand)],
        [(mine_units, F32, whole(mine_units), V)] * 2, copied, after=[gate],
    )

    gate_all = gather_set(gate, lambda across: tie(across, [ff_part[0]]))
    flipped, self_keep, self_send = call(
        self_backward_kernel, "self_backward", 1, [ids],
        set_of(gate_all) + [(a, whole(part)) for a in (q, k, v)]
        + [(self_output, mine_rows), (self_query, mine), (self_key, mine), (self_value, mine)],
        [((3 * pair, set_rows), BF, whole((3 * pair, set_rows)))]
        + [((2 * rows, width), BF, whole((2 * rows, width)), V)] * 2,
        [pltpu.VMEM(part, BF)] * 4,
    )
    so = tie(so, [gate_all[2]])
    so_across = swap(so, *ACROSS)
    self_send = tie(self_send, [so_across, hid_corner])
    self_got = swap(self_send, *CORE)
    so_all = (so, swap(so, *CORE), so_across, swap(so_across, *CORE))
    lower = pl.BlockSpec((rows // 2, width), lambda i: (i + 2, 0))
    (self_pass,) = call(
        add_kernel, "self_pass", 2, [], [(self_keep, lower, V), (self_got, lower, V)],
        [((rows, width), BF, pl.BlockSpec((rows // 2, width), lambda i: (i, 0)), V)],
        [],
    )
    self_across = swap(self_pass, *ACROSS)

    other_hid = [hid_near, hid_corner, swap(hid_near, *CORE), swap(hid_corner, *CORE)]
    half = (2 * unit, 2 * width)
    ff_keep, ff_send = call(
        ff_weights_b_kernel, "ff_weights_b", 1, [ids],
        [(a, any_spec, V) for a in other_hid + other_cot] + [(a, full(a), V) for a in (*ff_part, dact_other, mine_expand)],
        [(half, BF, whole(half), V)] * 2,
        [pltpu.VMEM(mine_units, F32)] * 2 + copied, after=[self_pass],
    )
    ff_got = swap(ff_send, *BESIDE)

    span = width // n_grp
    stack = (n_grp // 2 * 4 * pair, span)
    stack_keep, stack_send = call(
        self_weights_kernel, "self_weights", 1, [ids],
        [(flipped, full(flipped))] + set_of(set_in)
        + [(a, pl.BlockSpec((rows, pair), lambda i, ids: (0, ids[1])), V) for a in gate_all]
        + set_of(so_all),
        [(stack, BF, whole(stack), V)] * 2,
        [pltpu.VMEM((4 * pair, width), F32)],
        after=[ff_send],
    )
    stack_send = tie(stack_send, [self_across])
    stack_got = swap(stack_send, *NEAR)

    half_rows = pl.BlockSpec((rows, width), lambda i, *_: (0, 0))
    cross_gate, dcq, dck, dcv, after_cross_delta, self_vecs = call(
        functools.partial(cross_backward_kernel, groups, reads),
        "cross_backward", 4, [],
        [
            (neighbours, scalars), (fill, scalars),
            (self_keep, half_rows, V), (self_got, half_rows, V), (self_across, row_full, V),
            (after_self_delta, row_full), (after_cross, row_full), (vec(self_gain), vspec),
            (cross_output, rspec), (cq, row_part), (ck, key_part), (cv, key_part),
        ],
        [
            ((rows, width), BF, row_full, V),
            ((rows, width), BF, row_part, V), ((keys, width), BF, key_part, V), ((keys, width), BF, key_part, V),
            ((rows, width), F32, row_full), ((2, width), F32, whole((2, width))),
        ],
        [pltpu.VMEM((keys, rows), F32)],
        after=[stack_send, ff_send],
    )

    lefts = (flips[0], flips[3], flips[1], flips[2])
    rights = [(a, full(a), V) for a in (dcq, cross_gate, dck, dcv)]
    tile = width // 4

    def halves(name, first, after, flops):
        return call(
            cross_weights_kernel, name, 2, [],
            [(a, pl.BlockSpec((tile, a.shape[1]), lambda i: (i + first, 0))) for a in lefts] + rights,
            [((width // 2, 2 * width), BF, pl.BlockSpec((tile, 2 * width), lambda i: (i, 0)), V)] * 2,
            [], after=after, flops=flops,
        )

    sent = halves("cross_weights_sent", 2, [ff_send, stack_send], 1)
    kept = halves("cross_weights_kept", 0, [sent[0], ff_send, stack_send], 1)
    cores = [(a, swap(b, *CORE)) for a, b in zip(kept, sent)]
    stack_got = tie(stack_got, [kept[0]])
    ((ff_keep, ff_send),) = combine("ff_sum", [[(ff_keep, ff_got)]], 1, after=[stack_got], flops=2 * 10**10)
    ff_got = swap(ff_send, *FAR)
    pairs = combine(
        "cross_sum_core",
        [
            [tuple((a, 0) for a in cores[0]), tuple((a, 1) for a in cores[0])],
            [tuple((a, 0) for a in cores[1])],
            [tuple((a, 1) for a in cores[1])],
        ],
        4, after=[stack_got, ff_send], parts_of=2,
    )
    got = [swap(send, *CHAINS[n][1]) for n, (_, send) in enumerate(pairs)]

    marks = 128
    part_vecs = (2 * 2 * 8, marks)
    latent_delta, block_delta, vec_keep, vec_send = call(
        cross_inputs_kernel, "cross_inputs", 4, [ids],
        [
            (dcq, row_part, V), (dck, key_part, V), (dcv, key_part, V),
            (cross_query, cols), (cross_key, cols), (cross_value, cols),
            (latents, row_full), (blk, key_full), (vec(latent_gain), vspec), (vec(block_gain), vspec),
            (after_cross_delta, row_full), (self_vecs, full(self_vecs)), (hidden_vecs, full(hidden_vecs)),
        ],
        [((rows, width), BF, row_full), ((keys, width), BF, key_full)]
        + [(part_vecs, BF, whole(part_vecs), V)] * 2,
        [
            pltpu.VMEM((rows, width), F32), pltpu.VMEM((keys, width), F32), pltpu.VMEM((8, width), F32),
        ],
        after=[pairs[0][1]],
    )
    joined = (2 * (4 * pair + part_vecs[0] // 2), marks)
    stack_keep, stack_send = call(
        stack_sum_kernel, "self_sum_near", 1, [],
        [(a, full(a), V) for a in (stack_keep, stack_got, vec_keep, vec_send)],
        [(joined, BF, whole(joined), V)] * 2, [],
    )
    stack_got = swap(stack_send, *BESIDE)
    span = hidden // 4
    (updated,) = call(
        updated_kernel, "updated", 4, [],
        [
            (activated, pl.BlockSpec((rows, span), lambda i: (0, i))),
            (hidden_reduce, pl.BlockSpec((span, width), lambda i: (i, 0))), (after_self, row_full),
        ],
        [((rows, width), BF, row_full)], [pltpu.VMEM((rows, width), F32)], after=[stack_send],
    )
    last = [stack_send, ff_got, far_off(updated)]
    for stage in (2, 3, 4):
        chains = [[(kept, a)] for (kept, _), a in zip(pairs, got)]
        pairs = combine(f"cross_sum_{stage}", chains, 1, after=last)
        got = [swap(send, *CHAINS[n][stage]) for n, (_, send) in enumerate(pairs)]
        last = [pairs[0][1]]
        if stage == 2:
            ((stack_keep, stack_send),) = combine(
                "self_sum_y", [[(stack_keep, stack_got)]], 2, after=[pairs[0][1], ff_got]
            )
            stack_got = swap(stack_send, *FAR)
            last = [stack_send]
        if stage == 3:
            piece = (unit, width)
            mixed = (n_plane, chunk, 4 * unit + 4 * pair + marks)
            reduce_delta, turned = call(
                pack_kernel, "pack", 1, [],
                [(a, full(a), V) for a in (ff_keep, ff_got, stack_keep, stack_got)],
                [(piece, F32, whole(piece)), (mixed, BF, whole(mixed), V)],
                [], after=last,
            )
            last = [turned]
            planes = [
                [(d ^ z) * n_lvl + k for z in (0, NEAR[1]) for k in range(n_lvl)]
                for d in range(n_grp)
                if not d & NEAR[1]
            ]
            got_all = lax.all_to_all(
                turned, ("grp", "lvl"), split_axis=0, concat_axis=0, axis_index_groups=planes, tiled=True
            )
    members = (((0, width), (3, width)), ((1, width),), ((2, width),))
    ins = []
    for (kept, _), a in zip(pairs, got):
        ins += [(kept, full(kept), V), (a, full(a), V)]
    last = call(
        functools.partial(cross_last_kernel, members, 3), "cross_last", 1, [], ins,
        [((chunk, width), F32, whole((chunk, width)))] * 4,
        [], flops=14 * 10**9,
    )
    placed = call(
        functools.partial(place_kernel, unit, n_lvl), "place", 1, [ids], [(got_all, full(got_all), V)],
        [((chunk, hidden), F32, whole((chunk, hidden)))] + [((chunk, width), F32, whole((chunk, width)))] * 4
        + [((1, chunk), F32, whole((1, chunk)))] * 8,
        [pltpu.VMEM((marks, marks), F32)],
    )
    vecs = [a.reshape(chunk) for a in placed[5:]]

    return (
        updated, latent_delta, block_delta.reshape(groups, block_rows, width),
        vecs[0], vecs[1], vecs[2], vecs[3],
        last[0], last[1], last[2], last[3],
        vecs[4], vecs[5],
        placed[1], placed[2], placed[3], placed[4],
        vecs[6], vecs[7],
        placed[0], reduce_delta,
    )


def normed(values, norm_gain, norm_shift):
    center = values - jnp.mean(values, axis=-1, keepdims=True)
    spread = jnp.mean(center * center, axis=-1, keepdims=True)
    return center * lax.rsqrt(spread + EPS) * norm_gain + norm_shift


def to_half(values):
    return values.astype(jnp.bfloat16)


def matmul(left_side, right_side):
    return jnp.dot(left_side, right_side, preferred_element_type=jnp.float32)


def left_outer(left_side, right_side):
    return lax.dot_general(
        left_side, right_side, (((0,), (0,)), ((), ())), preferred_element_type=jnp.float32
    )


def right_outer(left_side, right_side):
    return lax.dot_general(
        left_side, right_side, (((1,), (1,)), ((), ())), preferred_element_type=jnp.float32
    )


def self_forward(query_heads, key_heads, value_heads, score_scale):
    length, local_heads, head_size = query_heads.shape
    block_rows = min(512, length)
    query_blocks = query_heads.reshape(length // block_rows, block_rows, local_heads, head_size)

    def one_block(query_block):
        scores = (
            jnp.einsum("qhd,khd->hqk", query_block, key_heads, preferred_element_type=jnp.float32)
            * score_scale
        )
        row_top = jnp.max(scores, axis=-1, keepdims=True)
        raised = jnp.exp(scores - row_top)
        row_total = jnp.sum(raised, axis=-1, keepdims=True)
        attention = raised / row_total
        mixture = jnp.einsum(
            "hqk,khd->qhd", to_half(attention), value_heads, preferred_element_type=jnp.float32
        )
        return (to_half(mixture), row_top + jnp.log(row_total))

    mixture, log_total = lax.map(one_block, query_blocks)
    return (mixture.reshape(length, local_heads, head_size), log_total)


def self_backward(query_heads, key_heads, value_heads, mixed_delta, log_total, score_scale):
    length, local_heads, head_size = query_heads.shape
    block_rows = min(512, length)
    query_blocks = query_heads.reshape(length // block_rows, block_rows, local_heads, head_size)
    delta_blocks = mixed_delta.reshape(length // block_rows, block_rows, local_heads, head_size)

    def one_block(running, pieces):
        key_sum, value_sum = running
        query_block, delta_block, log_block = pieces
        scores = (
            jnp.einsum("qhd,khd->hqk", query_block, key_heads, preferred_element_type=jnp.float32)
            * score_scale
        )
        attention = jnp.exp(scores - log_block)
        value_sum = value_sum + jnp.einsum(
            "hqk,qhd->khd", to_half(attention), delta_block, preferred_element_type=jnp.float32
        )
        weight_delta = jnp.einsum(
            "qhd,khd->hqk", delta_block, value_heads, preferred_element_type=jnp.float32
        )
        score_delta = to_half(
            attention * (weight_delta - jnp.sum(attention * weight_delta, axis=-1, keepdims=True))
        )
        query_delta = to_half(
            jnp.einsum("hqk,khd->qhd", score_delta, key_heads, preferred_element_type=jnp.float32)
            * score_scale
        )
        key_sum = (
            key_sum
            + jnp.einsum(
                "hqk,qhd->khd", score_delta, query_block, preferred_element_type=jnp.float32
            )
            * score_scale
        )
        return ((key_sum, value_sum), query_delta)

    zero_start = jnp.zeros(key_heads.shape, jnp.float32)
    (key_sum, value_sum), query_delta = lax.scan(
        one_block, (zero_start, zero_start), (query_blocks, delta_blocks, log_total)
    )
    return (
        query_delta.reshape(length, local_heads, head_size),
        to_half(key_sum),
        to_half(value_sum),
    )


def cross_forward(cross_queries, block_keys, block_values, neighbours, fill, score_scale):
    groups, latent_rows, head_count, head_size = cross_queries.shape
    block_rows = block_keys.shape[1]
    reads = neighbours.shape[1]
    picked_keys = block_keys[neighbours].reshape(groups, reads * block_rows, head_count, head_size)
    picked_values = block_values[neighbours].reshape(
        groups, reads * block_rows, head_count, head_size
    )
    positions = jnp.arange(block_rows, dtype=jnp.int32)
    live_keys = (positions[None, None, :] < fill[neighbours][:, :, None]).reshape(
        groups, reads * block_rows
    )
    scores = (
        jnp.einsum(
            "gqhd,gkhd->ghqk", cross_queries, picked_keys, preferred_element_type=jnp.float32
        )
        * score_scale
    )
    scores = jnp.where(live_keys[:, None, None, :], scores, NEG)
    attention = jax.nn.softmax(scores, axis=-1)
    return (attention, picked_keys, picked_values)


def plain(
    latents,
    blocks,
    neighbours,
    fill,
    cotangent,
    latent_gain,
    latent_shift,
    block_gain,
    block_shift,
    cross_query,
    cross_key,
    cross_value,
    cross_output,
    self_gain,
    self_shift,
    self_query,
    self_key,
    self_value,
    self_output,
    hidden_gain,
    hidden_shift,
    hidden_expand,
    hidden_reduce,
):
    rows = latents.shape[0]
    width = latents.shape[1]
    groups = blocks.shape[0]
    block_rows = blocks.shape[1]
    reads = neighbours.shape[1]
    head_size = width // H
    score_scale = head_size ** (-0.5)
    latent_float = latents.astype(jnp.float32)
    latent_norm, latent_pull = jax.vjp(normed, latent_float, latent_gain, latent_shift)
    latent_in = to_half(latent_norm)
    block_float = blocks.reshape(groups * block_rows, width).astype(jnp.float32)
    block_norm, block_pull = jax.vjp(normed, block_float, block_gain, block_shift)
    block_in = to_half(block_norm)
    cross_queries = to_half(matmul(latent_in, cross_query)).reshape(
        groups, rows // groups, H, head_size
    )
    block_keys = to_half(matmul(block_in, cross_key)).reshape(groups, block_rows, H, head_size)
    block_values = to_half(matmul(block_in, cross_value)).reshape(groups, block_rows, H, head_size)
    attention, picked_keys, picked_values = cross_forward(
        cross_queries, block_keys, block_values, neighbours, fill, score_scale
    )
    attention_half = to_half(attention)
    cross_mixed = to_half(
        jnp.einsum(
            "ghqk,gkhd->gqhd", attention_half, picked_values, preferred_element_type=jnp.float32
        )
    ).reshape(rows, width)
    after_cross = latent_float + matmul(cross_mixed, cross_output)
    self_norm, self_pull = jax.vjp(normed, after_cross, self_gain, self_shift)
    self_in = to_half(self_norm)
    self_queries = to_half(matmul(self_in, self_query)).reshape(rows, H, head_size)
    self_keys = to_half(matmul(self_in, self_key)).reshape(rows, H, head_size)
    self_values = to_half(matmul(self_in, self_value)).reshape(rows, H, head_size)
    query_heads, key_heads, value_heads = (
        lax.all_to_all(self_queries, "lvl", split_axis=1, concat_axis=0, tiled=True),
        lax.all_to_all(self_keys, "lvl", split_axis=1, concat_axis=0, tiled=True),
        lax.all_to_all(self_values, "lvl", split_axis=1, concat_axis=0, tiled=True),
    )
    head_mixed, log_total = self_forward(query_heads, key_heads, value_heads, score_scale)
    self_mixed = lax.all_to_all(head_mixed, "lvl", split_axis=0, concat_axis=1, tiled=True).reshape(
        rows, width
    )
    after_self = after_cross + matmul(self_mixed, self_output)
    hidden_norm, hidden_pull = jax.vjp(normed, after_self, hidden_gain, hidden_shift)
    hidden_in = to_half(hidden_norm)
    pre_act = matmul(hidden_in, hidden_expand)
    activated, act_pull = jax.vjp(jax.nn.gelu, pre_act)
    act_half = to_half(activated)
    updated = to_half(after_self + matmul(act_half, hidden_reduce))
    reduce_delta = left_outer(act_half, cotangent)
    act_delta = right_outer(cotangent, hidden_reduce)
    pre_delta = to_half(act_pull(act_delta)[0])
    expand_delta = left_outer(hidden_in, pre_delta)
    hidden_delta = right_outer(pre_delta, hidden_expand)
    self_side, hidden_gain_delta, hidden_shift_delta = hidden_pull(hidden_delta)
    after_self_delta = cotangent.astype(jnp.float32) + self_side
    self_gate = to_half(after_self_delta)
    self_output_delta = left_outer(self_mixed, self_gate)
    mixed_delta = to_half(right_outer(self_gate, self_output)).reshape(rows, H, head_size)
    head_delta = lax.all_to_all(mixed_delta, "lvl", split_axis=1, concat_axis=0, tiled=True)
    query_back, key_back, value_back = self_backward(
        query_heads, key_heads, value_heads, head_delta, log_total, score_scale
    )
    query_local, key_local, value_local = (
        lax.all_to_all(query_back, "lvl", split_axis=0, concat_axis=1, tiled=True),
        lax.all_to_all(key_back, "lvl", split_axis=0, concat_axis=1, tiled=True),
        lax.all_to_all(value_back, "lvl", split_axis=0, concat_axis=1, tiled=True),
    )
    query_local = query_local.reshape(rows, width)
    key_local = key_local.reshape(rows, width)
    value_local = value_local.reshape(rows, width)
    self_query_delta = left_outer(self_in, query_local)
    self_key_delta = left_outer(self_in, key_local)
    self_value_delta = left_outer(self_in, value_local)
    self_delta = (
        right_outer(query_local, self_query)
        + right_outer(key_local, self_key)
        + right_outer(value_local, self_value)
    )
    cross_side, self_gain_delta, self_shift_delta = self_pull(self_delta)
    after_cross_delta = after_self_delta + cross_side
    cross_gate = to_half(after_cross_delta)
    cross_output_delta = left_outer(cross_mixed, cross_gate)
    cross_delta = to_half(right_outer(cross_gate, cross_output)).reshape(
        groups, rows // groups, H, head_size
    )
    weight_delta = jnp.einsum(
        "gqhd,gkhd->ghqk", cross_delta, picked_values, preferred_element_type=jnp.float32
    )
    picked_value_delta = jnp.einsum(
        "ghqk,gqhd->gkhd", attention_half, cross_delta, preferred_element_type=jnp.float32
    )
    score_delta = to_half(
        attention * (weight_delta - jnp.sum(attention * weight_delta, axis=-1, keepdims=True))
    )
    cross_query_back = to_half(
        jnp.einsum("ghqk,gkhd->gqhd", score_delta, picked_keys, preferred_element_type=jnp.float32)
        * score_scale
    ).reshape(rows, width)
    picked_key_delta = (
        jnp.einsum(
            "ghqk,gqhd->gkhd", score_delta, cross_queries, preferred_element_type=jnp.float32
        )
        * score_scale
    )
    chosen = (
        neighbours.reshape(groups * reads)[:, None] == jnp.arange(groups, dtype=jnp.int32)[None, :]
    ).astype(jnp.float32)
    key_rows = picked_key_delta.reshape(groups * reads, block_rows * width)
    value_rows = picked_value_delta.reshape(groups * reads, block_rows * width)
    block_key_back = to_half(left_outer_exact(chosen, key_rows)).reshape(groups * block_rows, width)
    block_value_back = to_half(left_outer_exact(chosen, value_rows)).reshape(
        groups * block_rows, width
    )
    cross_query_delta = left_outer(latent_in, cross_query_back)
    cross_key_delta = left_outer(block_in, block_key_back)
    cross_value_delta = left_outer(block_in, block_value_back)
    block_side = right_outer(block_key_back, cross_key) + right_outer(block_value_back, cross_value)
    block_input_delta, block_gain_delta, block_shift_delta = block_pull(block_side)
    latent_side = right_outer(cross_query_back, cross_query)
    latent_input_delta, latent_gain_delta, latent_shift_delta = latent_pull(latent_side)
    latent_delta = to_half(after_cross_delta + latent_input_delta)
    block_delta = to_half(block_input_delta).reshape(groups, block_rows, width)
    summed = (
        lax.psum_scatter(latent_gain_delta, ("grp", "lvl"), scatter_dimension=0, tiled=True),
        lax.psum_scatter(latent_shift_delta, ("grp", "lvl"), scatter_dimension=0, tiled=True),
        lax.psum_scatter(block_gain_delta, ("grp", "lvl"), scatter_dimension=0, tiled=True),
        lax.psum_scatter(block_shift_delta, ("grp", "lvl"), scatter_dimension=0, tiled=True),
        lax.psum_scatter(cross_query_delta, ("grp", "lvl"), scatter_dimension=0, tiled=True),
        lax.psum_scatter(cross_key_delta, ("grp", "lvl"), scatter_dimension=0, tiled=True),
        lax.psum_scatter(cross_value_delta, ("grp", "lvl"), scatter_dimension=0, tiled=True),
        lax.psum_scatter(cross_output_delta, ("grp", "lvl"), scatter_dimension=0, tiled=True),
        lax.psum_scatter(self_gain_delta, ("grp", "lvl"), scatter_dimension=0, tiled=True),
        lax.psum_scatter(self_shift_delta, ("grp", "lvl"), scatter_dimension=0, tiled=True),
        lax.psum_scatter(self_query_delta, ("grp", "lvl"), scatter_dimension=0, tiled=True),
        lax.psum_scatter(self_key_delta, ("grp", "lvl"), scatter_dimension=0, tiled=True),
        lax.psum_scatter(self_value_delta, ("grp", "lvl"), scatter_dimension=0, tiled=True),
        lax.psum_scatter(self_output_delta, ("grp", "lvl"), scatter_dimension=0, tiled=True),
        lax.psum_scatter(hidden_gain_delta, ("grp", "lvl"), scatter_dimension=0, tiled=True),
        lax.psum_scatter(hidden_shift_delta, ("grp", "lvl"), scatter_dimension=0, tiled=True),
        lax.psum_scatter(expand_delta, ("grp", "lvl"), scatter_dimension=0, tiled=True),
        lax.psum_scatter(reduce_delta, ("grp", "lvl"), scatter_dimension=0, tiled=True),
    )
    return (
        updated,
        latent_delta,
        block_delta,
        summed[0],
        summed[1],
        summed[2],
        summed[3],
        summed[4],
        summed[5],
        summed[6],
        summed[7],
        summed[8],
        summed[9],
        summed[10],
        summed[11],
        summed[12],
        summed[13],
        summed[14],
        summed[15],
        summed[16],
        summed[17],
    )


def left_outer_exact(left_side, right_side):
    return lax.dot_general(
        left_side,
        right_side,
        (((0,), (0,)), ((), ())),
        precision=lax.Precision.HIGHEST,
        preferred_element_type=jnp.float32,
    )

def fits(shape, latents, hidden_expand):
    n_dev = shape["grp"] * shape["lvl"]
    return (
        shape["grp"] == 8
        and shape["lvl"] == 4
        and latents.shape[1] % (16 * n_dev) == 0
        and hidden_expand.shape[1] % (128 * n_dev) == 0
    )


def on_device(shape, *args):
    return (tiled if fits(shape, args[0], args[21]) else plain)(*args)


def solution(mesh):
    placed = (
        P(("grp", "lvl"), None),
        P(("grp", "lvl"), None, None),
        P(("grp", "lvl"), None),
        P(("grp", "lvl")),
        P(("grp", "lvl"), None),
        P(),
        P(),
        P(),
        P(),
        P(),
        P(),
        P(),
        P(),
        P(),
        P(),
        P(),
        P(),
        P(),
        P(),
        P(),
        P(),
        P(),
        P(),
    )
    return jax.shard_map(
        functools.partial(on_device, mesh.shape),
        mesh=mesh,
        in_specs=placed,
        out_specs=(
            P(("grp", "lvl"), None),
            P(("grp", "lvl"), None),
            P(("grp", "lvl"), None, None),
            P(("grp", "lvl")),
            P(("grp", "lvl")),
            P(("grp", "lvl")),
            P(("grp", "lvl")),
            P(("grp", "lvl"), None),
            P(("grp", "lvl"), None),
            P(("grp", "lvl"), None),
            P(("grp", "lvl"), None),
            P(("grp", "lvl")),
            P(("grp", "lvl")),
            P(("grp", "lvl"), None),
            P(("grp", "lvl"), None),
            P(("grp", "lvl"), None),
            P(("grp", "lvl"), None),
            P(("grp", "lvl")),
            P(("grp", "lvl")),
            P(("grp", "lvl"), None),
            P(("grp", "lvl"), None),
        ),
        check_vma=False,
    )
```

```python
import functools

import jax
import jax.numpy as jnp
from jax import lax
from jax.experimental import pallas as pl
from jax.experimental.pallas import tpu as pltpu
from jax.sharding import PartitionSpec as P

H = 8


EPS = 1e-05
NEG = -1e30
BF = jnp.bfloat16
F32 = jnp.float32
VMEM_MB = 30
V = True
LOG2_E = 1.4426950408889634
SQRT_2_PI = 0.7978845608028654
CUBIC = 0.044715


def count_bias(times):
    return jnp.where(times > 0.0, jnp.log(jnp.maximum(times, 1.0)) * LOG2_E, NEG)


def nn(a, b):
    return lax.dot_general(a, b, (((1,), (0,)), ((), ())), preferred_element_type=F32)


def nt(a, b):
    return lax.dot_general(a, b, (((1,), (1,)), ((), ())), preferred_element_type=F32)


def tn(a, b):
    return lax.dot_general(a, b, (((0,), (0,)), ((), ())), preferred_element_type=F32)


def flip(v):
    return jnp.transpose(v)


def hat(v):
    center = v - jnp.mean(v, axis=-1, keepdims=True)
    scale = lax.rsqrt(jnp.mean(center * center, axis=-1, keepdims=True) + EPS)
    return center * scale, scale


def norm_back(dy, v, gain):
    unit, scale = hat(v)
    t = dy * gain
    side = scale * (
        t
        - jnp.mean(t, axis=-1, keepdims=True)
        - unit * jnp.mean(t * unit, axis=-1, keepdims=True)
    )
    return side, jnp.sum(dy * unit, axis=0, keepdims=True), jnp.sum(dy, axis=0, keepdims=True)


def gelu_parts(x):
    square = x * x
    t = jnp.tanh(SQRT_2_PI * x * (1.0 + CUBIC * square))
    half = 0.5 + 0.5 * t
    act = x * half
    slope = half + (0.5 * SQRT_2_PI) * x * (1.0 - t * t) * (1.0 + (3.0 * CUBIC) * square)
    return act, slope


def counts_by_row(nb, fill, rows, groups, block_rows, reads):
    keys = groups * block_rows
    key = lax.broadcasted_iota(jnp.int32, (rows, keys), 1)
    row = lax.broadcasted_iota(jnp.int32, (rows, keys), 0)
    per = rows // groups
    out = jnp.zeros((rows, keys), F32)
    for g in range(groups):
        for m in range(groups):
            times = jnp.int32(0)
            for n in range(reads):
                times = times + (nb[g, n] == m).astype(jnp.int32)
            live = (key >= m * block_rows) & (key < m * block_rows + fill[m])
            here = live & (row >= g * per) & (row < (g + 1) * per)
            out = jnp.where(here, times.astype(F32), out)
    return out


def counts_by_key(nb, fill, rows, groups, block_rows, reads):
    keys = groups * block_rows
    key = lax.broadcasted_iota(jnp.int32, (keys, rows), 0)
    row = lax.broadcasted_iota(jnp.int32, (keys, rows), 1)
    per = rows // groups
    out = jnp.zeros((keys, rows), F32)
    for g in range(groups):
        for m in range(groups):
            times = jnp.int32(0)
            for n in range(reads):
                times = times + (nb[g, n] == m).astype(jnp.int32)
            live = (key >= m * block_rows) & (key < m * block_rows + fill[m])
            here = live & (row >= g * per) & (row < (g + 1) * per)
            out = jnp.where(here, times.astype(F32), out)
    return out


def whole(shape):
    zeros = (0,) * len(shape)
    return pl.BlockSpec(shape, lambda i, *_: zeros)


def near_core(array):
    return pltpu.with_memory_space_constraint(array, pltpu.VMEM)


def far_off(array):
    return pltpu.with_memory_space_constraint(array, pltpu.HBM)


def call(kernel, name, grid, scalars, ins, outs, scratch, vmem=VMEM_MB, after=(), flops=1):
    first = len(scalars) + len(ins)

    def body(*refs):
        kernel(*refs[:first], *refs[first + len(after) :])

    arrays = [near_core(item[0]) if len(item) > 2 else far_off(item[0]) for item in ins]
    shapes = [(pltpu.VMEM if len(item) > 3 else pltpu.HBM)(item[0], item[1]) for item in outs]
    return pl.pallas_call(
        body,
        name=name,
        grid_spec=pltpu.PrefetchScalarGridSpec(
            num_scalar_prefetch=len(scalars),
            grid=(grid,),
            in_specs=[item[1] for item in ins] + [pl.BlockSpec(memory_space=pl.ANY)] * len(after),
            out_specs=[item[2] for item in outs],
            scratch_shapes=scratch,
        ),
        out_shape=shapes,
        compiler_params=pltpu.CompilerParams(
            vmem_limit_bytes=vmem * 1024 * 1024, dimension_semantics=("arbitrary",)
        ),
        cost_estimate=pl.CostEstimate(flops=flops, bytes_accessed=1, transcendentals=0),
    )(*scalars, *arrays, *after)


def tie(array, after):
    spec = pl.BlockSpec(memory_space=pl.ANY)
    array = near_core(array)
    return pl.pallas_call(
        lambda *refs: None,
        name="tie",
        in_specs=[spec] * (1 + len(after)),
        out_specs=spec,
        out_shape=pltpu.VMEM(array.shape, array.dtype),
        input_output_aliases={0: 0},
        compiler_params=pltpu.CompilerParams(vmem_limit_bytes=1024 * 1024),
        cost_estimate=pl.CostEstimate(flops=1, bytes_accessed=1, transcendentals=0),
    )(array, *after)


def cross_forward_kernel(
    groups, reads, nb, fill, lat, blk, lg, lb, bg, bb, sg, sb, wq, wk, wv, wo,
    cq, ck, cv, co, ac, self_in, lat_in, blk_in, acc, cnt,
):
    i = pl.program_id(0)
    rows, width = lat.shape
    keys = blk.shape[0]
    scale = (width // H) ** -0.5
    head = width // H

    @pl.when(i == 0)
    def _():
        lat_in[...] = (hat(lat[...].astype(F32))[0] * lg[...] + lb[...]).astype(BF)
        blk_in[...] = (hat(blk[...].astype(F32))[0] * bg[...] + bb[...]).astype(BF)
        acc[...] = lat[...].astype(F32)
        cnt[...] = count_bias(counts_by_row(nb, fill, rows, groups, keys // groups, reads))

    q = nn(lat_in[...], wq[...]).astype(BF)
    k = nn(blk_in[...], wk[...]).astype(BF)
    v = nn(blk_in[...], wv[...]).astype(BF)
    cq[...] = q
    ck[...] = k
    cv[...] = v
    bias = cnt[...]
    mixed = []
    for h in range(q.shape[1] // head):
        cut = slice(h * head, (h + 1) * head)
        s = nt(q[:, cut], k[:, cut]) * (scale * LOG2_E) + bias
        e = jnp.exp2(s - jnp.max(s, axis=-1, keepdims=True))
        p = (e * (1.0 / jnp.sum(e, axis=-1, keepdims=True))).astype(BF)
        mixed.append(nn(p, v[:, cut]).astype(BF))
    mixed = jnp.concatenate(mixed, axis=1)
    co[...] = mixed
    acc[...] += nn(mixed, wo[...])

    @pl.when(i == pl.num_programs(0) - 1)
    def _():
        after = acc[...]
        ac[...] = after
        self_in[...] = (hat(after)[0] * sg[...] + sb[...]).astype(BF)


def flip_rows_kernel(plan, orders, ids, *refs):
    n = 1 + max(src for src, _ in plan)
    ins, outs, tmp = refs[:n], refs[n : n + len(plan)], refs[n + len(plan) :]
    for src, t in zip(ins, tmp, strict=True):
        t[...] = flip(src[...])
    for dst, (src, which) in zip(outs, plan, strict=True):
        t = tmp[src]
        size = t.shape[0] // len(orders[which])
        for p, distance in enumerate(orders[which]):
            at = pl.multiple_of((ids[2] ^ distance) * size, size)
            dst[p * size : (p + 1) * size, :] = t[pl.ds(at, size), :]


def self_forward_kernel(ids, a0, a1, a2, a3, wq, wk, wv, q, k, v, o0, o1, o2):
    rows, width = a0.shape
    head = width // H
    scale = head**-0.5
    for j, a in enumerate((a0, a1, a2, a3)):
        here = slice(j * rows, (j + 1) * rows)
        x = a[...]
        q[here, :] = nn(x, wq[...]).astype(BF)
        k[here, :] = nn(x, wk[...]).astype(BF)
        v[here, :] = nn(x, wv[...]).astype(BF)
    for t in range(2):
        mixed = []
        for h in range(q.shape[1] // head):
            cut = slice(h * head, (h + 1) * head)
            s = nt(q[2 * t * rows : 2 * (t + 1) * rows, cut], k[:, cut])
            e = jnp.exp2((s - jnp.max(s, axis=-1, keepdims=True)) * (scale * LOG2_E))
            p = (e * (1.0 / jnp.sum(e, axis=-1, keepdims=True))).astype(BF)
            mixed.append(nn(p, v[:, cut]).astype(BF))
        mixed = jnp.concatenate(mixed, axis=1)
        if t == 0:
            o0[...] = mixed[:rows]
            o1[...] = mixed[rows:]
        else:
            o2[...] = mixed


def self_out_kernel(ids, ac, o0, o1, o2, o3, wo, hg, hb, after, hidden_in, so):
    cols = o0.shape[1]
    for j, o in enumerate((o0, o1, o2, o3)):
        at = pl.multiple_of((ids[1] ^ j) * cols, cols)
        so[:, pl.ds(at, cols)] = o[...]
    v = ac[...] + nn(so[...], wo[...])
    after[...] = v
    hidden_in[...] = (hat(v)[0] * hg[...] + hb[...]).astype(BF)


def cot_back_kernel(gy, wred, out):
    out[...] = nt(gy[...], wred[...])


def cot_units_kernel(ids, *refs):
    gs, wexp, wred = refs[:8], refs[8:12], refs[12:16]
    own, other, we, wr = refs[16:]
    unit = wexp[0].shape[1]
    for q in range(4):
        we[q * unit : (q + 1) * unit, :] = flip(wexp[q][...])
        wr[q * unit : (q + 1) * unit, :] = wred[q][...]
    rows = gs[0].shape[0]
    for k, g in enumerate(gs):
        out = own if k < 4 else other
        at = (k % 4) * rows
        out[:, at : at + rows] = nt(wr[...], g[...])


def ff_local_kernel(hidden_in, gy, after, hg, dact, wexp, act_out, gate, das, vecs, dh):
    i = pl.program_id(0)

    @pl.when(i == 0)
    def _():
        dh[...] = jnp.zeros_like(dh)

    act, slope = gelu_parts(nn(hidden_in[...], wexp[...]))
    act_out[...] = act.astype(BF)
    dh[...] += nt((dact[...] * slope).astype(BF), wexp[...])

    @pl.when(i == pl.num_programs(0) - 1)
    def _():
        side, dg, db = norm_back(dh[...], after[...], hg[...])
        total = gy[...].astype(F32) + side
        das[...] = total
        gate[...] = total.astype(BF)
        vecs[0:1, :] = dg
        vecs[1:2, :] = db


def updated_kernel(act, wred, after, out, total):
    i = pl.program_id(0)

    @pl.when(i == 0)
    def _():
        total[...] = after[...]

    total[...] += nn(act[...], wred[...])

    @pl.when(i == pl.num_programs(0) - 1)
    def _():
        out[...] = total[...].astype(BF)


def ff_sums(we, dact, h, g, red, exp, fresh):
    act, slope = gelu_parts(nt(we[...], h))
    dpre = (dact * slope).astype(BF)
    if fresh:
        red[...] = nn(act.astype(BF), g)
        exp[...] = nn(dpre, h)
    else:
        red[...] += nn(act.astype(BF), g)
        exp[...] += nn(dpre, h)


def ff_tokens(refs, dact, we, red, exp, h_all, g_all, sem, fresh):
    hs, gs = refs[:4], refs[4:8]
    rows = hs[0].shape[0]
    copies = [
        pltpu.make_async_copy(piece, dst.at[pl.ds(k * rows, rows)], sem.at[which, k])
        for which, (src, dst) in enumerate(((hs, h_all), (gs, g_all)))
        for k, piece in enumerate(src)
    ]
    for c in copies:
        c.start()
    for t in range(2):
        for k in (2 * t, 2 * t + 1, 2 * t + 4, 2 * t + 5):
            copies[k].wait()
        here = slice(2 * t * rows, 2 * (t + 1) * rows)
        ff_sums(we, dact[:, here], h_all[here, :], g_all[here, :], red, exp, fresh and t == 0)


def ff_weights_a_kernel(*refs):
    dact, we, red, exp, h_all, g_all, sem = refs[8:]
    ff_tokens(refs, dact, we, red, exp, h_all, g_all, sem, True)


def ff_weights_b_kernel(ids, *refs):
    red_in, exp_in, dact, we, keep, send, red, exp, h_all, g_all, sem = refs[8:]
    red[...] = red_in[...]
    exp[...] = exp_in[...]
    ff_tokens(refs, dact, we, red, exp, h_all, g_all, sem, False)
    unit = we.shape[0] // 4
    half = 2 * unit
    width = red.shape[1]
    keep[:, 0:width] = red[0:half, :].astype(BF)
    send[:, 0:width] = red[half:, :].astype(BF)
    span = width // 8
    for p in range(4):
        out = keep if p < 2 else send
        low = (p % 2) * unit
        for q in range(4):
            for z in range(2):
                lanes = pl.ds(pl.multiple_of((ids[8 + p] + 2 * z) * span, span), span)
                to = pl.ds(pl.multiple_of(width + (2 * ids[12 + q] + z) * span, span), span)
                out[low : low + unit, to] = exp[q * unit : (q + 1) * unit, lanes].astype(BF)


def self_backward_kernel(
    ids, g0, g1, g2, g3, q, k, v, wo, wq, wk, wv, flipped, keep, send, do, dq, dk, dv
):
    rows, width = g0.shape
    head = width // H
    scale = head**-0.5
    for j, g in enumerate((g0, g1, g2, g3)):
        do[j * rows : (j + 1) * rows, :] = nt(g[...], wo[...]).astype(BF)
    cols = q.shape[1]
    tile = 512
    for h in range(cols // head):
        cut = slice(h * head, (h + 1) * head)
        kh = k[:, cut]
        vh = v[:, cut]
        kt = flip(kh)
        key_sum = jnp.zeros((k.shape[0], head), F32)
        value_sum = jnp.zeros((k.shape[0], head), F32)
        for t in range(q.shape[0] // tile):
            here = slice(t * tile, (t + 1) * tile)
            qt = q[here, cut]
            dt = do[here, cut]
            s = nt(kh, qt)
            e = jnp.exp2((s - jnp.max(s, axis=0, keepdims=True)) * (scale * LOG2_E))
            p = e * (1.0 / jnp.sum(e, axis=0, keepdims=True))
            dp = nt(vh, dt)
            ds = (p * (dp - jnp.sum(p * dp, axis=0, keepdims=True))).astype(BF)
            value_sum += nn(p.astype(BF), dt)
            key_sum += nn(ds, qt)
            back = (nn(kt, ds) * scale).astype(BF)
            flipped[cut, here] = back
            dq[here, cut] = flip(back)
        dk[:, cut] = (key_sum * scale).astype(BF)
        dv[:, cut] = value_sum.astype(BF)
    flipped[cols : 2 * cols, :] = flip(dk[...])
    flipped[2 * cols : 3 * cols, :] = flip(dv[...])
    for j in range(4):
        here = slice(j * rows, (j + 1) * rows)
        side = nt(dq[here, :], wq[...]) + nt(dk[here, :], wk[...]) + nt(dv[here, :], wv[...])
        out = send if j % 2 else keep
        low = (j // 2) * rows
        out[low : low + rows, :] = side.astype(BF)


def self_weights_kernel(ids, flipped, *refs):
    ins, gates, mixed = refs[0:4], refs[4:8], refs[8:12]
    keep, send, total = refs[12:]
    rows = ins[0].shape[0]
    three = flipped.shape[0]
    for low, high, parts in (
        (0, three, [(flipped[:, j * rows : (j + 1) * rows], ins[j][...]) for j in range(4)]),
        (three, total.shape[0], [(flip(gates[j][...]), mixed[j][...]) for j in range(4)]),
    ):
        acc = None
        for left, right in parts:
            part = nn(left, right)
            acc = part if acc is None else acc + part
        total[low:high, :] = acc
    depth, span = total.shape[0], keep.shape[1]
    blocks = total.shape[1] // span
    for p in range(blocks):
        out = keep if p < blocks // 2 else send
        low = (p % (blocks // 2)) * depth
        lanes = pl.ds(pl.multiple_of(ids[16 + p] * span, span), span)
        out[low : low + depth, :] = total[:, lanes].astype(BF)


def cross_backward_kernel(
    groups, reads, nb, fill, keep, rcv, xr, das, ac, sg, wo, cq, ck, cv, gate, dq, dk, dv, dac, vecs, cnt,
):
    i = pl.program_id(0)
    rows, width = das.shape
    keys = ck.shape[0]
    head = width // H
    scale = head**-0.5

    @pl.when(i == 0)
    def _():
        dy = keep[...].astype(F32) + rcv[...].astype(F32) + xr[...].astype(F32)
        side, dg, db = norm_back(dy, ac[...], sg[...])
        total = das[...] + side
        dac[...] = total
        gate[...] = total.astype(BF)
        vecs[0:1, :] = dg
        vecs[1:2, :] = db
        cnt[...] = count_bias(counts_by_key(nb, fill, rows, groups, keys // groups, reads))

    do = nt(gate[...], wo[...]).astype(BF)
    bias = cnt[...]
    for h in range(cq.shape[1] // head):
        cut = slice(h * head, (h + 1) * head)
        qh = cq[:, cut]
        kh = ck[:, cut]
        dh = do[:, cut]
        s = nt(kh, qh) * (scale * LOG2_E) + bias
        e = jnp.exp2(s - jnp.max(s, axis=0, keepdims=True))
        p = e * (1.0 / jnp.sum(e, axis=0, keepdims=True))
        dp = nt(cv[:, cut], dh)
        ds = (p * (dp - jnp.sum(p * dp, axis=0, keepdims=True))).astype(BF)
        dv[:, cut] = nn(p.astype(BF), dh).astype(BF)
        dk[:, cut] = (nn(ds, qh) * scale).astype(BF)
        dq[:, cut] = flip((nn(flip(kh), ds) * scale).astype(BF))


def cross_inputs_kernel(
    ids, dq, dk, dv, wq, wk, wv, lat, blk, lg, bg, dac, sv, hv, dlat, dblk, keep, send, la, ba, vecs
):
    i = pl.program_id(0)

    @pl.when(i == 0)
    def _():
        la[...] = jnp.zeros_like(la)
        ba[...] = jnp.zeros_like(ba)

    la[...] += nt(dq[...], wq[...])
    ba[...] += nt(dk[...], wk[...]) + nt(dv[...], wv[...])

    @pl.when(i == pl.num_programs(0) - 1)
    def _():
        side, dg, db = norm_back(la[...], lat[...].astype(F32), lg[...])
        dlat[...] = (dac[...] + side).astype(BF)
        vecs[0:1, :] = dg
        vecs[1:2, :] = db
        side, dg, db = norm_back(ba[...], blk[...].astype(F32), bg[...])
        dblk[...] = side.astype(BF)
        vecs[2:3, :] = dg
        vecs[3:4, :] = db
        vecs[4:6, :] = sv[...]
        vecs[6:8, :] = hv[...]
        count, span = vecs.shape[0], keep.shape[1]
        for p in range(4):
            out = keep if p < 2 else send
            parts = [
                vecs[:, pl.ds(pl.multiple_of((ids[8 + p] + 2 * z) * span, span), span)] for z in range(2)
            ]
            low = (p % 2) * 2 * count
            out[low : low + 2 * count, :] = jnp.concatenate(parts, axis=0).astype(BF)


def stack_sum_kernel(kept, got, vec_keep, vec_send, keep, send):
    rows = kept.shape[0] // 4
    more = vec_keep.shape[0] // 2
    for p in range(4):
        out, vecs = (keep, vec_keep) if p < 2 else (send, vec_send)
        low = (p % 2) * (rows + more)
        here = slice(p * rows, (p + 1) * rows)
        out[low : low + rows, :] = (kept[here, :].astype(F32) + got[here, :].astype(F32)).astype(BF)
        out[low + rows : low + rows + more, :] = vecs[(p % 2) * more : (p % 2 + 1) * more, :]


def cross_weights_kernel(*refs):
    n = (len(refs) - 2) // 2
    lefts, rights, outs = refs[:n], refs[n : 2 * n], refs[2 * n :]
    for k, (left, right) in enumerate(zip(lefts, rights, strict=True)):
        width = right.shape[1]
        outs[k // 2][:, (k % 2) * width : (k % 2 + 1) * width] = nn(left[...], right[...]).astype(BF)


def combine_kernel(terms, *refs):
    total = sum(sum(parts) for parts in terms)
    ins, outs = refs[: 2 * total], refs[2 * total :]
    n = 0
    for k, parts in enumerate(terms):
        at = 0
        for count in parts:
            tops, lows = ins[n : n + 2 * count : 2], ins[n + 1 : n + 2 * count : 2]
            width = tops[0].shape[1]
            for out, refs_ in ((outs[2 * k], tops), (outs[2 * k + 1], lows)):
                acc = refs_[0][...].astype(F32)
                for ref in refs_[1:]:
                    acc = acc + ref[...].astype(F32)
                out[:, at : at + width] = acc.astype(BF)
            at += width
            n += 2 * count


def combine(name, chains, steps, after=(), parts_of=1, flops=1):
    ins, outs = [], []
    for parts in chains:
        total = 0
        for terms in parts:
            for term in terms:
                a, k = term if parts_of > 1 else (term, 0)
                depth, width = a.shape[0], a.shape[1] // parts_of
                part = depth // 2 // steps
                top = pl.BlockSpec((part, width), lambda i, k=k: (i, k))
                low = pl.BlockSpec((part, width), lambda i, k=k: (i + steps, k))
                ins += [(a, top, V), (a, low, V)]
            total += width
        outs += [((depth // 2, total), BF, pl.BlockSpec((part, total), lambda i: (i, 0)), V)] * 2
    counts = tuple(tuple(len(terms) for terms in parts) for parts in chains)
    out = call(
        functools.partial(combine_kernel, counts), name, steps, [], ins, outs, [], after=after, flops=flops
    )
    return [tuple(out[2 * k : 2 * k + 2]) for k in range(len(chains))]


def copy_kernel(a, out):
    out[...] = a[...]


def add_kernel(a, b, out):
    out[...] = (a[...].astype(F32) + b[...].astype(F32)).astype(BF)


def pack_kernel(ff_kept, ff_got, set_kept, set_got, reduce_delta, out):
    unit, width = reduce_delta.shape
    reduce_delta[...] = ff_kept[:, 0:width].astype(F32) + ff_got[:, 0:width].astype(F32)
    rest = ff_kept[:, width:].astype(F32) + ff_got[:, width:].astype(F32)
    devices, chunk, _ = out.shape
    span = devices * chunk
    parts = width // span
    for q in range(parts):
        t = flip(rest[:, q * span : (q + 1) * span]).astype(BF)
        for d in range(devices):
            out[d, :, q * unit : (q + 1) * unit] = t[d * chunk : (d + 1) * chunk, :]
    total = set_kept[...].astype(F32) + set_got[...].astype(F32)
    count = 8
    cols = total.shape[0] - 2 * count
    t = flip(total[:cols, :]).astype(BF)
    n_set = t.shape[0] // chunk
    lanes = out.shape[2] - parts * unit - cols
    blank = jnp.zeros((chunk - count, lanes), F32)
    for d in range(devices):
        at = (d % n_set) * chunk
        out[d, :, parts * unit : parts * unit + cols] = t[at : at + chunk, :]
        low = cols + (d // n_set) * count
        mine = jnp.concatenate([total[low : low + count, :], blank], axis=0)
        out[d, :, parts * unit + cols :] = mine.astype(BF)


def place_kernel(unit, n_set, ids, got, expand, *rest):
    outs, turned = rest[:-1], rest[-1]
    devices, chunk, width = got.shape
    parts = expand.shape[1] // (devices * unit)
    for q in range(parts):
        for d in range(devices):
            at = ((q // 2) * 2 * devices + (d // n_set) * devices + (q % 2) * n_set + d % n_set) * unit
            expand[:, at : at + unit] = got[d, :, q * unit : (q + 1) * unit].astype(F32)
    outs, vecs = outs[:4], outs[4:]
    lanes = width - parts * unit - 4 * outs[0].shape[1] // n_set
    cols = outs[0].shape[1] // n_set
    for d in range(n_set):
        mine = got[ids[3] * n_set + d]
        for m, out in enumerate(outs):
            at = parts * unit + m * cols
            out[:, d * cols : (d + 1) * cols] = mine[:, at : at + cols].astype(F32)
    total = jnp.zeros((chunk, lanes), F32)
    for d in range(devices):
        total += got[d, :, width - lanes :].astype(F32)
    turned[...] = flip(jnp.concatenate([total, jnp.zeros((lanes - chunk, lanes), F32)], axis=0))
    total = flip(turned[pl.ds(pl.multiple_of(ids[1] * chunk, chunk), chunk), :])
    for k, out in enumerate(vecs):
        out[...] = total[k : k + 1, :]


def cross_last_kernel(parts, n, *refs):
    ins, outs = refs[: 2 * n], refs[2 * n :]
    for chain, members in enumerate(parts):
        total = ins[2 * chain][...].astype(F32) + ins[2 * chain + 1][...].astype(F32)
        at = 0
        for which, cols in members:
            outs[which][...] = total[:, at : at + cols]
            at += cols


def swap(values, axis, bit):
    size = lax.axis_size(axis)
    return lax.ppermute(values, axis, [(i, i ^ bit) for i in range(size)])


CORE = ("lvl", 1)
ACROSS = ("lvl", 2)
BESIDE = ("grp", 1)
NEAR = ("grp", 2)
FAR = ("grp", 4)


def gather_set(own, wait=lambda across: across):
    across = wait(swap(own, *ACROSS))
    return own, swap(own, *CORE), across, swap(across, *CORE)


def places(links, n_lvl):
    weights = [bit * (n_lvl if axis == "grp" else 1) for axis, bit in links]
    n = len(weights)
    return [
        sum(w for k, w in enumerate(weights) if p >> (n - 1 - k) & 1) for p in range(1 << n)
    ]


CHAINS = (
    (CORE, ACROSS, BESIDE, NEAR, FAR),
    (CORE, BESIDE, NEAR, ACROSS, FAR),
    (CORE, NEAR, ACROSS, FAR, BESIDE),
)


def tiled(
    latents, blocks, neighbours, fill, cotangent,
    latent_gain, latent_shift, block_gain, block_shift,
    cross_query, cross_key, cross_value, cross_output,
    self_gain, self_shift, self_query, self_key, self_value, self_output,
    hidden_gain, hidden_shift, hidden_expand, hidden_reduce,
):
    rows, width = latents.shape
    groups, block_rows, _ = blocks.shape
    keys = groups * block_rows
    reads = neighbours.shape[1]
    hidden = hidden_expand.shape[1]
    n_grp, n_lvl = lax.axis_size("grp"), lax.axis_size("lvl")
    n_dev = n_grp * n_lvl
    n_plane = 2 * n_lvl
    g = lax.axis_index("grp").astype(jnp.int32)
    l = lax.axis_index("lvl").astype(jnp.int32)
    me = g * n_lvl + l
    per = n_lvl
    steps = [0, FAR[1], BESIDE[1], FAR[1] | BESIDE[1]]
    bare = g & ~NEAR[1]
    ids = jnp.stack(
        [g, l, me, (g & NEAR[1]) // NEAR[1]]
        + [me ^ (p * per) for p in steps]
        + [bare ^ p for p in steps]
        + [((bare ^ p) // FAR[1]) * 2 + ((bare ^ p) & 1) for p in steps]
        + [g ^ p for p in (0, 4, 1, 5, 2, 6, 3, 7)]
    ).astype(jnp.int32)
    orders = tuple(tuple(places(links, n_lvl)) for links in CHAINS)
    unit = hidden // n_dev
    chunk = width // n_dev

    vec = lambda v: v.reshape(1, width)
    vspec = whole((1, width))
    scalars = pl.BlockSpec(memory_space=pltpu.SMEM)
    blk = blocks.reshape(keys, width)
    pair = width // 4
    cols = pl.BlockSpec((width, pair), lambda i, *_: (0, i))
    rspec = pl.BlockSpec((pair, width), lambda i, *_: (i, 0))
    mine = pl.BlockSpec((width, pair), lambda i, ids: (0, ids[1]))
    mine_rows = pl.BlockSpec((pair, width), lambda i, ids: (ids[1], 0))
    row_full = whole((rows, width))
    key_full = whole((keys, width))
    row_part = pl.BlockSpec((rows, pair), lambda i, *_: (0, i))
    key_part = pl.BlockSpec((keys, pair), lambda i, *_: (0, i))
    set_rows = n_lvl * rows

    full = lambda a: whole(a.shape)
    cot_across, cot_near = swap(cotangent, *ACROSS), swap(cotangent, *NEAR)

    cq, ck, cv, co, after_cross, self_in, latent_in, block_in = call(
        functools.partial(cross_forward_kernel, groups, reads),
        "cross_forward", 4, [],
        [(neighbours, scalars), (fill, scalars), (latents, row_full), (blk, key_full)]
        + [(vec(v), vspec) for v in (latent_gain, latent_shift, block_gain, block_shift, self_gain, self_shift)]
        + [(cross_query, cols), (cross_key, cols), (cross_value, cols), (cross_output, rspec)],
        [
            ((rows, width), BF, row_part), ((keys, width), BF, key_part),
            ((keys, width), BF, key_part), ((rows, width), BF, row_part),
            ((rows, width), F32, row_full), ((rows, width), BF, row_full, V),
            ((rows, width), BF, row_full), ((keys, width), BF, key_full),
        ],
        [pltpu.VMEM((rows, width), F32), pltpu.VMEM((rows, keys), F32)],
        after=[ids],
    )

    set_of = lambda pieces: [(a, whole((rows, width)), V) for a in pieces]
    part = (set_rows, pair)
    plan = ((0, 0), (1, 1), (1, 2), (2, 0))
    sources = (latent_in, block_in, co)
    flips = call(
        functools.partial(flip_rows_kernel, plan, orders), "flip_cross", 1, [ids],
        [(a, full(a)) for a in sources],
        [(sources[k].shape[::-1], BF, whole(sources[k].shape[::-1])) for k, _ in plan],
        [pltpu.VMEM(a.shape[::-1], BF) for a in sources],
    )
    cot_corner = swap(cot_across, *NEAR)
    (dact,) = call(
        cot_back_kernel, "cot_back", 4, [],
        [(cotangent, row_full), (hidden_reduce, pl.BlockSpec((hidden // 4, width), lambda i: (i, 0)))],
        [((rows, hidden), F32, pl.BlockSpec((rows, hidden // 4), lambda i: (0, i)), V)],
        [], after=[far_off(flips[0])],
    )
    self_in = tie(self_in, [cot_across, cot_near])
    set_in = gather_set(self_in, lambda across: tie(across, [dact]))
    q, k, v, o0, o1, o2 = call(
        self_forward_kernel, "self_forward", 1, [ids],
        set_of(set_in)
        + [(self_query, mine), (self_key, mine), (self_value, mine)],
        [(part, BF, whole(part))] * 3
        + [((rows, pair), BF, whole((rows, pair)), V)] * 2
        + [((2 * rows, pair), BF, whole((2 * rows, pair)), V)],
        [],
        after=[dact],
    )

    across = swap(tie(o2, [cot_corner]), *ACROSS)
    cots = [cotangent, cot_across, cot_near, cot_corner]
    cots_core = [swap(a, *CORE) for a in cots]
    own_cot = [cotangent, cot_across, cots_core[0], cots_core[1]]
    other_cot = [cot_near, cot_corner, cots_core[2], cots_core[3]]

    def unit_cols(p):
        return pl.BlockSpec((width, unit), lambda i, ids: (0, ids[4 + p]))

    def unit_rows(p):
        return pl.BlockSpec((unit, width), lambda i, ids: (ids[4 + p], 0))

    mine_units = (4 * unit, width)
    by_token = (4 * unit, set_rows)
    dact_own, dact_other, mine_expand = call(
        cot_units_kernel, "cot_units", 1, [ids],
        [(own_cot[0], row_full)] + [(a, row_full, V) for a in own_cot[1:] + other_cot]
        + [(hidden_expand, unit_cols(p)) for p in range(4)]
        + [(hidden_reduce, unit_rows(p)) for p in range(4)],
        [(by_token, F32, whole(by_token), V)] * 2 + [(mine_units, BF, whole(mine_units), V)],
        [pltpu.VMEM(mine_units, BF)], after=[o0],
    )
    second = pl.BlockSpec((rows, pair), lambda i: (1, 0))
    (across_next,) = call(
        copy_kernel, "pass", 1, [], [(across, second, V)], [((rows, pair), BF, whole((rows, pair)), V)], [],
        after=[mine_expand],
    )
    o_spec = whole((rows, pair))
    pieces = (o0, swap(o1, *CORE), across, swap(across_next, *CORE))
    after_self, hidden_in, so = call(
        self_out_kernel, "self_out", 1, [ids],
        [(after_cross, row_full)] + [(p, o_spec, V) for p in pieces]
        + [(self_output, whole((width, width))), (vec(hidden_gain), vspec), (vec(hidden_shift), vspec)],
        [((rows, width), F32, row_full), ((rows, width), BF, row_full, V), ((rows, width), BF, row_full, V)],
        [], after=[mine_expand],
    )

    hid_across, hid_near = swap(hidden_in, *ACROSS), swap(hidden_in, *NEAR)
    step = 1024
    activated, gate, after_self_delta, hidden_vecs = call(
        ff_local_kernel, "ff_local", hidden // step, [],
        [
            (hidden_in, row_full, V), (cotangent, row_full), (after_self, row_full), (vec(hidden_gain), vspec),
            (dact, pl.BlockSpec((rows, step), lambda i: (0, i)), V),
            (hidden_expand, pl.BlockSpec((width, step), lambda i: (0, i))),
        ],
        [
            ((rows, hidden), BF, pl.BlockSpec((rows, step), lambda i: (0, i))), ((rows, width), BF, row_full, V),
            ((rows, width), F32, row_full), ((2, width), F32, whole((2, width))),
        ],
        [pltpu.VMEM((rows, width), F32)],
    )
    gate = tie(gate, [hid_near])
    hid_across = tie(hid_across, [gate])
    hid_corner = swap(hid_across, *NEAR)

    any_spec = pl.BlockSpec(memory_space=pl.ANY)

    own_hid = [hidden_in, hid_across, swap(hidden_in, *CORE), swap(hid_across, *CORE)]
    copied = [
        pltpu.VMEM((set_rows, width), BF), pltpu.VMEM((set_rows, width), BF), pltpu.SemaphoreType.DMA((2, 4)),
    ]
    ff_part = call(
        ff_weights_a_kernel, "ff_weights_a", 1, [],
        [(a, any_spec, V) for a in own_hid] + [(own_cot[0], any_spec)] + [(a, any_spec, V) for a in own_cot[1:]]
        + [(a, full(a), V) for a in (dact_own, mine_expand)],
        [(mine_units, F32, whole(mine_units), V)] * 2, copied, after=[gate],
    )

    gate_all = gather_set(gate, lambda across: tie(across, [ff_part[0]]))
    flipped, self_keep, self_send = call(
        self_backward_kernel, "self_backward", 1, [ids],
        set_of(gate_all) + [(a, whole(part)) for a in (q, k, v)]
        + [(self_output, mine_rows), (self_query, mine), (self_key, mine), (self_value, mine)],
        [((3 * pair, set_rows), BF, whole((3 * pair, set_rows)))]
        + [((2 * rows, width), BF, whole((2 * rows, width)), V)] * 2,
        [pltpu.VMEM(part, BF)] * 4,
    )
    so = tie(so, [gate_all[2]])
    so_across = swap(so, *ACROSS)
    self_send = tie(self_send, [so_across, hid_corner])
    self_got = swap(self_send, *CORE)
    so_all = (so, swap(so, *CORE), so_across, swap(so_across, *CORE))
    lower = pl.BlockSpec((rows // 2, width), lambda i: (i + 2, 0))
    (self_pass,) = call(
        add_kernel, "self_pass", 2, [], [(self_keep, lower, V), (self_got, lower, V)],
        [((rows, width), BF, pl.BlockSpec((rows // 2, width), lambda i: (i, 0)), V)],
        [],
    )
    self_across = swap(self_pass, *ACROSS)

    other_hid = [hid_near, hid_corner, swap(hid_near, *CORE), swap(hid_corner, *CORE)]
    half = (2 * unit, 2 * width)
    ff_keep, ff_send = call(
        ff_weights_b_kernel, "ff_weights_b", 1, [ids],
        [(a, any_spec, V) for a in other_hid + other_cot] + [(a, full(a), V) for a in (*ff_part, dact_other, mine_expand)],
        [(half, BF, whole(half), V)] * 2,
        [pltpu.VMEM(mine_units, F32)] * 2 + copied, after=[self_pass],
    )
    ff_got = swap(ff_send, *BESIDE)

    span = width // n_grp
    stack = (n_grp // 2 * 4 * pair, span)
    stack_keep, stack_send = call(
        self_weights_kernel, "self_weights", 1, [ids],
        [(flipped, full(flipped))] + set_of(set_in)
        + [(a, pl.BlockSpec((rows, pair), lambda i, ids: (0, ids[1])), V) for a in gate_all]
        + set_of(so_all),
        [(stack, BF, whole(stack), V)] * 2,
        [pltpu.VMEM((4 * pair, width), F32)],
        after=[ff_send],
    )
    stack_send = tie(stack_send, [self_across])
    stack_got = swap(stack_send, *NEAR)

    half_rows = pl.BlockSpec((rows, width), lambda i, *_: (0, 0))
    cross_gate, dcq, dck, dcv, after_cross_delta, self_vecs = call(
        functools.partial(cross_backward_kernel, groups, reads),
        "cross_backward", 4, [],
        [
            (neighbours, scalars), (fill, scalars),
            (self_keep, half_rows, V), (self_got, half_rows, V), (self_across, row_full, V),
            (after_self_delta, row_full), (after_cross, row_full), (vec(self_gain), vspec),
            (cross_output, rspec), (cq, row_part), (ck, key_part), (cv, key_part),
        ],
        [
            ((rows, width), BF, row_full, V),
            ((rows, width), BF, row_part, V), ((keys, width), BF, key_part, V), ((keys, width), BF, key_part, V),
            ((rows, width), F32, row_full), ((2, width), F32, whole((2, width))),
        ],
        [pltpu.VMEM((keys, rows), F32)],
        after=[stack_send, ff_send],
    )

    lefts = (flips[0], flips[3], flips[1], flips[2])
    rights = [(a, full(a), V) for a in (dcq, cross_gate, dck, dcv)]
    tile = width // 4

    def halves(name, first, after, flops):
        return call(
            cross_weights_kernel, name, 2, [],
            [(a, pl.BlockSpec((tile, a.shape[1]), lambda i: (i + first, 0))) for a in lefts] + rights,
            [((width // 2, 2 * width), BF, pl.BlockSpec((tile, 2 * width), lambda i: (i, 0)), V)] * 2,
            [], after=after, flops=flops,
        )

    sent = halves("cross_weights_sent", 2, [ff_send, stack_send], 1)
    kept = halves("cross_weights_kept", 0, [sent[0], ff_send, stack_send], 1)
    cores = [(a, swap(b, *CORE)) for a, b in zip(kept, sent)]
    stack_got = tie(stack_got, [kept[0]])
    ((ff_keep, ff_send),) = combine("ff_sum", [[(ff_keep, ff_got)]], 1, after=[stack_got], flops=2 * 10**10)
    ff_got = swap(ff_send, *FAR)
    pairs = combine(
        "cross_sum_core",
        [
            [tuple((a, 0) for a in cores[0]), tuple((a, 1) for a in cores[0])],
            [tuple((a, 0) for a in cores[1])],
            [tuple((a, 1) for a in cores[1])],
        ],
        2, after=[stack_got, ff_send], parts_of=2,
    )
    got = [swap(send, *CHAINS[n][1]) for n, (_, send) in enumerate(pairs)]

    marks = 128
    part_vecs = (2 * 2 * 8, marks)
    latent_delta, block_delta, vec_keep, vec_send = call(
        cross_inputs_kernel, "cross_inputs", 4, [ids],
        [
            (dcq, row_part, V), (dck, key_part, V), (dcv, key_part, V),
            (cross_query, cols), (cross_key, cols), (cross_value, cols),
            (latents, row_full), (blk, key_full), (vec(latent_gain), vspec), (vec(block_gain), vspec),
            (after_cross_delta, row_full), (self_vecs, full(self_vecs)), (hidden_vecs, full(hidden_vecs)),
        ],
        [((rows, width), BF, row_full), ((keys, width), BF, key_full)]
        + [(part_vecs, BF, whole(part_vecs), V)] * 2,
        [
            pltpu.VMEM((rows, width), F32), pltpu.VMEM((keys, width), F32), pltpu.VMEM((8, width), F32),
        ],
        after=[pairs[0][1]],
    )
    joined = (2 * (4 * pair + part_vecs[0] // 2), marks)
    stack_keep, stack_send = call(
        stack_sum_kernel, "self_sum_near", 1, [],
        [(a, full(a), V) for a in (stack_keep, stack_got, vec_keep, vec_send)],
        [(joined, BF, whole(joined), V)] * 2, [],
    )
    stack_got = swap(stack_send, *BESIDE)
    span = hidden // 4
    (updated,) = call(
        updated_kernel, "updated", 4, [],
        [
            (activated, pl.BlockSpec((rows, span), lambda i: (0, i))),
            (hidden_reduce, pl.BlockSpec((span, width), lambda i: (i, 0))), (after_self, row_full),
        ],
        [((rows, width), BF, row_full)], [pltpu.VMEM((rows, width), F32)], after=[stack_send],
    )
    last = [stack_send, ff_got, far_off(updated)]
    for stage in (2, 3, 4):
        chains = [[(kept, a)] for (kept, _), a in zip(pairs, got)]
        pairs = combine(f"cross_sum_{stage}", chains, 1, after=last)
        got = [swap(send, *CHAINS[n][stage]) for n, (_, send) in enumerate(pairs)]
        last = [pairs[0][1]]
        if stage == 2:
            ((stack_keep, stack_send),) = combine(
                "self_sum_y", [[(stack_keep, stack_got)]], 2, after=[pairs[0][1], ff_got]
            )
            stack_got = swap(stack_send, *FAR)
            last = [stack_send]
        if stage == 3:
            piece = (unit, width)
            mixed = (n_plane, chunk, 4 * unit + 4 * pair + marks)
            reduce_delta, turned = call(
                pack_kernel, "pack", 1, [],
                [(a, full(a), V) for a in (ff_keep, ff_got, stack_keep, stack_got)],
                [(piece, F32, whole(piece)), (mixed, BF, whole(mixed), V)],
                [], after=last,
            )
            last = [turned]
            planes = [
                [(d ^ z) * n_lvl + k for z in (0, NEAR[1]) for k in range(n_lvl)]
                for d in range(n_grp)
                if not d & NEAR[1]
            ]
            got_all = lax.all_to_all(
                turned, ("grp", "lvl"), split_axis=0, concat_axis=0, axis_index_groups=planes, tiled=True
            )
    members = (((0, width), (3, width)), ((1, width),), ((2, width),))
    ins = []
    for (kept, _), a in zip(pairs, got):
        ins += [(kept, full(kept), V), (a, full(a), V)]
    last = call(
        functools.partial(cross_last_kernel, members, 3), "cross_last", 1, [], ins,
        [((chunk, width), F32, whole((chunk, width)))] * 4,
        [], flops=14 * 10**9,
    )
    placed = call(
        functools.partial(place_kernel, unit, n_lvl), "place", 1, [ids], [(got_all, full(got_all), V)],
        [((chunk, hidden), F32, whole((chunk, hidden)))] + [((chunk, width), F32, whole((chunk, width)))] * 4
        + [((1, chunk), F32, whole((1, chunk)))] * 8,
        [pltpu.VMEM((marks, marks), F32)],
    )
    vecs = [a.reshape(chunk) for a in placed[5:]]

    return (
        updated, latent_delta, block_delta.reshape(groups, block_rows, width),
        vecs[0], vecs[1], vecs[2], vecs[3],
        last[0], last[1], last[2], last[3],
        vecs[4], vecs[5],
        placed[1], placed[2], placed[3], placed[4],
        vecs[6], vecs[7],
        placed[0], reduce_delta,
    )


def normed(values, norm_gain, norm_shift):
    center = values - jnp.mean(values, axis=-1, keepdims=True)
    spread = jnp.mean(center * center, axis=-1, keepdims=True)
    return center * lax.rsqrt(spread + EPS) * norm_gain + norm_shift


def to_half(values):
    return values.astype(jnp.bfloat16)


def matmul(left_side, right_side):
    return jnp.dot(left_side, right_side, preferred_element_type=jnp.float32)


def left_outer(left_side, right_side):
    return lax.dot_general(
        left_side, right_side, (((0,), (0,)), ((), ())), preferred_element_type=jnp.float32
    )


def right_outer(left_side, right_side):
    return lax.dot_general(
        left_side, right_side, (((1,), (1,)), ((), ())), preferred_element_type=jnp.float32
    )


def self_forward(query_heads, key_heads, value_heads, score_scale):
    length, local_heads, head_size = query_heads.shape
    block_rows = min(512, length)
    query_blocks = query_heads.reshape(length // block_rows, block_rows, local_heads, head_size)

    def one_block(query_block):
        scores = (
            jnp.einsum("qhd,khd->hqk", query_block, key_heads, preferred_element_type=jnp.float32)
            * score_scale
        )
        row_top = jnp.max(scores, axis=-1, keepdims=True)
        raised = jnp.exp(scores - row_top)
        row_total = jnp.sum(raised, axis=-1, keepdims=True)
        attention = raised / row_total
        mixture = jnp.einsum(
            "hqk,khd->qhd", to_half(attention), value_heads, preferred_element_type=jnp.float32
        )
        return (to_half(mixture), row_top + jnp.log(row_total))

    mixture, log_total = lax.map(one_block, query_blocks)
    return (mixture.reshape(length, local_heads, head_size), log_total)


def self_backward(query_heads, key_heads, value_heads, mixed_delta, log_total, score_scale):
    length, local_heads, head_size = query_heads.shape
    block_rows = min(512, length)
    query_blocks = query_heads.reshape(length // block_rows, block_rows, local_heads, head_size)
    delta_blocks = mixed_delta.reshape(length // block_rows, block_rows, local_heads, head_size)

    def one_block(running, pieces):
        key_sum, value_sum = running
        query_block, delta_block, log_block = pieces
        scores = (
            jnp.einsum("qhd,khd->hqk", query_block, key_heads, preferred_element_type=jnp.float32)
            * score_scale
        )
        attention = jnp.exp(scores - log_block)
        value_sum = value_sum + jnp.einsum(
            "hqk,qhd->khd", to_half(attention), delta_block, preferred_element_type=jnp.float32
        )
        weight_delta = jnp.einsum(
            "qhd,khd->hqk", delta_block, value_heads, preferred_element_type=jnp.float32
        )
        score_delta = to_half(
            attention * (weight_delta - jnp.sum(attention * weight_delta, axis=-1, keepdims=True))
        )
        query_delta = to_half(
            jnp.einsum("hqk,khd->qhd", score_delta, key_heads, preferred_element_type=jnp.float32)
            * score_scale
        )
        key_sum = (
            key_sum
            + jnp.einsum(
                "hqk,qhd->khd", score_delta, query_block, preferred_element_type=jnp.float32
            )
            * score_scale
        )
        return ((key_sum, value_sum), query_delta)

    zero_start = jnp.zeros(key_heads.shape, jnp.float32)
    (key_sum, value_sum), query_delta = lax.scan(
        one_block, (zero_start, zero_start), (query_blocks, delta_blocks, log_total)
    )
    return (
        query_delta.reshape(length, local_heads, head_size),
        to_half(key_sum),
        to_half(value_sum),
    )


def cross_forward(cross_queries, block_keys, block_values, neighbours, fill, score_scale):
    groups, latent_rows, head_count, head_size = cross_queries.shape
    block_rows = block_keys.shape[1]
    reads = neighbours.shape[1]
    picked_keys = block_keys[neighbours].reshape(groups, reads * block_rows, head_count, head_size)
    picked_values = block_values[neighbours].reshape(
        groups, reads * block_rows, head_count, head_size
    )
    positions = jnp.arange(block_rows, dtype=jnp.int32)
    live_keys = (positions[None, None, :] < fill[neighbours][:, :, None]).reshape(
        groups, reads * block_rows
    )
    scores = (
        jnp.einsum(
            "gqhd,gkhd->ghqk", cross_queries, picked_keys, preferred_element_type=jnp.float32
        )
        * score_scale
    )
    scores = jnp.where(live_keys[:, None, None, :], scores, NEG)
    attention = jax.nn.softmax(scores, axis=-1)
    return (attention, picked_keys, picked_values)


def plain(
    latents,
    blocks,
    neighbours,
    fill,
    cotangent,
    latent_gain,
    latent_shift,
    block_gain,
    block_shift,
    cross_query,
    cross_key,
    cross_value,
    cross_output,
    self_gain,
    self_shift,
    self_query,
    self_key,
    self_value,
    self_output,
    hidden_gain,
    hidden_shift,
    hidden_expand,
    hidden_reduce,
):
    rows = latents.shape[0]
    width = latents.shape[1]
    groups = blocks.shape[0]
    block_rows = blocks.shape[1]
    reads = neighbours.shape[1]
    head_size = width // H
    score_scale = head_size ** (-0.5)
    latent_float = latents.astype(jnp.float32)
    latent_norm, latent_pull = jax.vjp(normed, latent_float, latent_gain, latent_shift)
    latent_in = to_half(latent_norm)
    block_float = blocks.reshape(groups * block_rows, width).astype(jnp.float32)
    block_norm, block_pull = jax.vjp(normed, block_float, block_gain, block_shift)
    block_in = to_half(block_norm)
    cross_queries = to_half(matmul(latent_in, cross_query)).reshape(
        groups, rows // groups, H, head_size
    )
    block_keys = to_half(matmul(block_in, cross_key)).reshape(groups, block_rows, H, head_size)
    block_values = to_half(matmul(block_in, cross_value)).reshape(groups, block_rows, H, head_size)
    attention, picked_keys, picked_values = cross_forward(
        cross_queries, block_keys, block_values, neighbours, fill, score_scale
    )
    attention_half = to_half(attention)
    cross_mixed = to_half(
        jnp.einsum(
            "ghqk,gkhd->gqhd", attention_half, picked_values, preferred_element_type=jnp.float32
        )
    ).reshape(rows, width)
    after_cross = latent_float + matmul(cross_mixed, cross_output)
    self_norm, self_pull = jax.vjp(normed, after_cross, self_gain, self_shift)
    self_in = to_half(self_norm)
    self_queries = to_half(matmul(self_in, self_query)).reshape(rows, H, head_size)
    self_keys = to_half(matmul(self_in, self_key)).reshape(rows, H, head_size)
    self_values = to_half(matmul(self_in, self_value)).reshape(rows, H, head_size)
    query_heads, key_heads, value_heads = (
        lax.all_to_all(self_queries, "lvl", split_axis=1, concat_axis=0, tiled=True),
        lax.all_to_all(self_keys, "lvl", split_axis=1, concat_axis=0, tiled=True),
        lax.all_to_all(self_values, "lvl", split_axis=1, concat_axis=0, tiled=True),
    )
    head_mixed, log_total = self_forward(query_heads, key_heads, value_heads, score_scale)
    self_mixed = lax.all_to_all(head_mixed, "lvl", split_axis=0, concat_axis=1, tiled=True).reshape(
        rows, width
    )
    after_self = after_cross + matmul(self_mixed, self_output)
    hidden_norm, hidden_pull = jax.vjp(normed, after_self, hidden_gain, hidden_shift)
    hidden_in = to_half(hidden_norm)
    pre_act = matmul(hidden_in, hidden_expand)
    activated, act_pull = jax.vjp(jax.nn.gelu, pre_act)
    act_half = to_half(activated)
    updated = to_half(after_self + matmul(act_half, hidden_reduce))
    reduce_delta = left_outer(act_half, cotangent)
    act_delta = right_outer(cotangent, hidden_reduce)
    pre_delta = to_half(act_pull(act_delta)[0])
    expand_delta = left_outer(hidden_in, pre_delta)
    hidden_delta = right_outer(pre_delta, hidden_expand)
    self_side, hidden_gain_delta, hidden_shift_delta = hidden_pull(hidden_delta)
    after_self_delta = cotangent.astype(jnp.float32) + self_side
    self_gate = to_half(after_self_delta)
    self_output_delta = left_outer(self_mixed, self_gate)
    mixed_delta = to_half(right_outer(self_gate, self_output)).reshape(rows, H, head_size)
    head_delta = lax.all_to_all(mixed_delta, "lvl", split_axis=1, concat_axis=0, tiled=True)
    query_back, key_back, value_back = self_backward(
        query_heads, key_heads, value_heads, head_delta, log_total, score_scale
    )
    query_local, key_local, value_local = (
        lax.all_to_all(query_back, "lvl", split_axis=0, concat_axis=1, tiled=True),
        lax.all_to_all(key_back, "lvl", split_axis=0, concat_axis=1, tiled=True),
        lax.all_to_all(value_back, "lvl", split_axis=0, concat_axis=1, tiled=True),
    )
    query_local = query_local.reshape(rows, width)
    key_local = key_local.reshape(rows, width)
    value_local = value_local.reshape(rows, width)
    self_query_delta = left_outer(self_in, query_local)
    self_key_delta = left_outer(self_in, key_local)
    self_value_delta = left_outer(self_in, value_local)
    self_delta = (
        right_outer(query_local, self_query)
        + right_outer(key_local, self_key)
        + right_outer(value_local, self_value)
    )
    cross_side, self_gain_delta, self_shift_delta = self_pull(self_delta)
    after_cross_delta = after_self_delta + cross_side
    cross_gate = to_half(after_cross_delta)
    cross_output_delta = left_outer(cross_mixed, cross_gate)
    cross_delta = to_half(right_outer(cross_gate, cross_output)).reshape(
        groups, rows // groups, H, head_size
    )
    weight_delta = jnp.einsum(
        "gqhd,gkhd->ghqk", cross_delta, picked_values, preferred_element_type=jnp.float32
    )
    picked_value_delta = jnp.einsum(
        "ghqk,gqhd->gkhd", attention_half, cross_delta, preferred_element_type=jnp.float32
    )
    score_delta = to_half(
        attention * (weight_delta - jnp.sum(attention * weight_delta, axis=-1, keepdims=True))
    )
    cross_query_back = to_half(
        jnp.einsum("ghqk,gkhd->gqhd", score_delta, picked_keys, preferred_element_type=jnp.float32)
        * score_scale
    ).reshape(rows, width)
    picked_key_delta = (
        jnp.einsum(
            "ghqk,gqhd->gkhd", score_delta, cross_queries, preferred_element_type=jnp.float32
        )
        * score_scale
    )
    chosen = (
        neighbours.reshape(groups * reads)[:, None] == jnp.arange(groups, dtype=jnp.int32)[None, :]
    ).astype(jnp.float32)
    key_rows = picked_key_delta.reshape(groups * reads, block_rows * width)
    value_rows = picked_value_delta.reshape(groups * reads, block_rows * width)
    block_key_back = to_half(left_outer_exact(chosen, key_rows)).reshape(groups * block_rows, width)
    block_value_back = to_half(left_outer_exact(chosen, value_rows)).reshape(
        groups * block_rows, width
    )
    cross_query_delta = left_outer(latent_in, cross_query_back)
    cross_key_delta = left_outer(block_in, block_key_back)
    cross_value_delta = left_outer(block_in, block_value_back)
    block_side = right_outer(block_key_back, cross_key) + right_outer(block_value_back, cross_value)
    block_input_delta, block_gain_delta, block_shift_delta = block_pull(block_side)
    latent_side = right_outer(cross_query_back, cross_query)
    latent_input_delta, latent_gain_delta, latent_shift_delta = latent_pull(latent_side)
    latent_delta = to_half(after_cross_delta + latent_input_delta)
    block_delta = to_half(block_input_delta).reshape(groups, block_rows, width)
    summed = (
        lax.psum_scatter(latent_gain_delta, ("grp", "lvl"), scatter_dimension=0, tiled=True),
        lax.psum_scatter(latent_shift_delta, ("grp", "lvl"), scatter_dimension=0, tiled=True),
        lax.psum_scatter(block_gain_delta, ("grp", "lvl"), scatter_dimension=0, tiled=True),
        lax.psum_scatter(block_shift_delta, ("grp", "lvl"), scatter_dimension=0, tiled=True),
        lax.psum_scatter(cross_query_delta, ("grp", "lvl"), scatter_dimension=0, tiled=True),
        lax.psum_scatter(cross_key_delta, ("grp", "lvl"), scatter_dimension=0, tiled=True),
        lax.psum_scatter(cross_value_delta, ("grp", "lvl"), scatter_dimension=0, tiled=True),
        lax.psum_scatter(cross_output_delta, ("grp", "lvl"), scatter_dimension=0, tiled=True),
        lax.psum_scatter(self_gain_delta, ("grp", "lvl"), scatter_dimension=0, tiled=True),
        lax.psum_scatter(self_shift_delta, ("grp", "lvl"), scatter_dimension=0, tiled=True),
        lax.psum_scatter(self_query_delta, ("grp", "lvl"), scatter_dimension=0, tiled=True),
        lax.psum_scatter(self_key_delta, ("grp", "lvl"), scatter_dimension=0, tiled=True),
        lax.psum_scatter(self_value_delta, ("grp", "lvl"), scatter_dimension=0, tiled=True),
        lax.psum_scatter(self_output_delta, ("grp", "lvl"), scatter_dimension=0, tiled=True),
        lax.psum_scatter(hidden_gain_delta, ("grp", "lvl"), scatter_dimension=0, tiled=True),
        lax.psum_scatter(hidden_shift_delta, ("grp", "lvl"), scatter_dimension=0, tiled=True),
        lax.psum_scatter(expand_delta, ("grp", "lvl"), scatter_dimension=0, tiled=True),
        lax.psum_scatter(reduce_delta, ("grp", "lvl"), scatter_dimension=0, tiled=True),
    )
    return (
        updated,
        latent_delta,
        block_delta,
        summed[0],
        summed[1],
        summed[2],
        summed[3],
        summed[4],
        summed[5],
        summed[6],
        summed[7],
        summed[8],
        summed[9],
        summed[10],
        summed[11],
        summed[12],
        summed[13],
        summed[14],
        summed[15],
        summed[16],
        summed[17],
    )


def left_outer_exact(left_side, right_side):
    return lax.dot_general(
        left_side,
        right_side,
        (((0,), (0,)), ((), ())),
        precision=lax.Precision.HIGHEST,
        preferred_element_type=jnp.float32,
    )

def fits(shape, latents, hidden_expand):
    n_dev = shape["grp"] * shape["lvl"]
    return (
        shape["grp"] == 8
        and shape["lvl"] == 4
        and latents.shape[1] % (16 * n_dev) == 0
        and hidden_expand.shape[1] % (128 * n_dev) == 0
    )


def on_device(shape, *args):
    return (tiled if fits(shape, args[0], args[21]) else plain)(*args)


def solution(mesh):
    placed = (
        P(("grp", "lvl"), None),
        P(("grp", "lvl"), None, None),
        P(("grp", "lvl"), None),
        P(("grp", "lvl")),
        P(("grp", "lvl"), None),
        P(),
        P(),
        P(),
        P(),
        P(),
        P(),
        P(),
        P(),
        P(),
        P(),
        P(),
        P(),
        P(),
        P(),
        P(),
        P(),
        P(),
        P(),
    )
    return jax.shard_map(
        functools.partial(on_device, mesh.shape),
        mesh=mesh,
        in_specs=placed,
        out_specs=(
            P(("grp", "lvl"), None),
            P(("grp", "lvl"), None),
            P(("grp", "lvl"), None, None),
            P(("grp", "lvl")),
            P(("grp", "lvl")),
            P(("grp", "lvl")),
            P(("grp", "lvl")),
            P(("grp", "lvl"), None),
            P(("grp", "lvl"), None),
            P(("grp", "lvl"), None),
            P(("grp", "lvl"), None),
            P(("grp", "lvl")),
            P(("grp", "lvl")),
            P(("grp", "lvl"), None),
            P(("grp", "lvl"), None),
            P(("grp", "lvl"), None),
            P(("grp", "lvl"), None),
            P(("grp", "lvl")),
            P(("grp", "lvl")),
            P(("grp", "lvl"), None),
            P(("grp", "lvl"), None),
        ),
        check_vma=False,
    )
```
